32 devices in a mesh: dp: 8 (over z, core), fsdp: 4 (over y, x).
Axes of the slice: x: 2, y: 2, z: 4, core: 2. Of those that a mesh axis runs over, the one named last changes fastest.
Arguments:
- tokens: bfloat16 [8192, 1024], P(('dp', 'fsdp')), may hold values from -6 to 6
- cotangent: bfloat16 [8192, 1024], P(('dp', 'fsdp')), may hold values from -6 to 6
- lengths: int32 [32, 8], P(('dp', 'fsdp')), may hold values from 0 to 256, as said below
- value_proj: bfloat16 [1024, 2048], P('dp', 'fsdp'), may hold values from -0.1875 to 0.1875
- mix_proj: bfloat16 [1024, 4224], P('dp', 'fsdp'), may hold values from -0.1875 to 0.1875
- merge_proj: bfloat16 [2048, 1024], P('dp', 'fsdp'), may hold values from -0.5 to 0.5
- up_proj: bfloat16 [1024, 4096], P('dp', 'fsdp'), may hold values from -0.1875 to 0.1875
- down_proj: bfloat16 [4096, 1024], P('dp', 'fsdp'), may hold values from -0.09375 to 0.09375
- norm_gains: bfloat16 [3, 1024], P(None, ('dp', 'fsdp')), may hold values from 0.5 to 1.5
- ema_params: bfloat16 [4, 1024, 16], P(None, ('dp', 'fsdp')), may hold values from -6 to 4
- attn_params: bfloat16 [512], P(('dp', 'fsdp')), may hold values from -6 to 6
Outputs:
- result: bfloat16 [8192, 1024], P(('dp', 'fsdp'))
- grad_tokens: bfloat16 [8192, 1024], P(('dp', 'fsdp'))
- grad_value: float32 [1024, 2048], P('dp', 'fsdp')
- grad_mix: float32 [1024, 4224], P('dp', 'fsdp')
- grad_merge: float32 [2048, 1024], P('dp', 'fsdp')
- grad_up: float32 [1024, 4096], P('dp', 'fsdp')
- grad_down: float32 [4096, 1024], P('dp', 'fsdp')
- grad_gains: float32 [3, 1024], P(None, ('dp', 'fsdp'))
- grad_ema: float32 [4, 1024, 16], P(None, ('dp', 'fsdp'))
- grad_attn: float32 [512], P(('dp', 'fsdp'))
The draws below stay inside these ranges and needn't reach their ends.
Inputs may be any that keep to these rules, and one draw needn't show every extreme that they name: Each row lists the lengths of up to 8 sequences packed from the start of one device's buffer of 256 slots. Every nonzero length is 256 times a power of two, a row sums to at most 256, its first entry is nonzero, zeros come only after the nonzero entries, and slots past the row's sum are padding.
All inputs are finite; a program needn't handle non-finite values.
Results may differ from the reference program's by a relative error of at most 0.018.
Values may be sent and summed in bfloat16 or wider, within the bound.
A program may use at most 320 MiB of HBM per device.

```python
import math
import jax
import jax.numpy as jnp
from jax import lax

D = 1024
NDIM = 16
Z = 128
V = 2048
FF = 4096
STRETCH = 128
SEQ_MIN = 256
SLOTS = 8
TOK_DEV = 256
BUFFERS = 32
TOKENS = 8192


def draw_lengths(key, part):
    streams = jax.random.split(key, 3)
    exp_span = (TOK_DEV // SEQ_MIN).bit_length() - 1
    first_exp = jax.random.randint(streams[0], (BUFFERS, SLOTS), 0, exp_span + 1)
    second_exp = jax.random.randint(streams[1], (BUFFERS, SLOTS), 0, exp_span + 1)
    sizes_raw = SEQ_MIN * jnp.left_shift(jnp.ones((BUFFERS, SLOTS), jnp.int32), jnp.minimum(first_exp, second_exp).astype(jnp.int32))
    full_row = jax.random.randint(streams[2], (), 0, BUFFERS)
    row_ids = jnp.arange(BUFFERS)[:, None]
    slot_ids = jnp.arange(SLOTS)[None, :]
    sizes_raw = jnp.where((row_ids == full_row) & (slot_ids == 0), TOK_DEV, sizes_raw)
    running = jnp.cumsum(sizes_raw, axis=1)
    return jnp.where(running <= TOK_DEV, sizes_raw, 0).astype(jnp.int32)


def draw_ema_params(key, part):
    streams = jax.random.split(key, 4)
    shape_one = (D, NDIM)
    low_rate = 0.25 / TOK_DEV
    top_rate = 0.05
    log_rate = jax.random.uniform(streams[0], shape_one, jnp.float32, math.log(low_rate), math.log(top_rate))
    rate_all = jnp.exp(log_rate)
    split_power = jax.random.uniform(streams[1], shape_one, jnp.float32, 0.35, 0.65)
    first_share = rate_all ** split_power
    second_share = rate_all ** (1.0 - split_power)
    first_logit = jnp.log(first_share) - jnp.log1p(-first_share)
    second_logit = jnp.log(second_share) - jnp.log1p(-second_share)
    beta_in = 1.0 + 0.3 * jnp.clip(jax.random.normal(streams[2], shape_one, jnp.float32), -3.0, 3.0)
    gamma_out = jnp.clip(1.5 * jax.random.normal(streams[3], shape_one, jnp.float32), -4.0, 4.0)
    return jnp.stack([first_logit, second_logit, beta_in, gamma_out]).astype(jnp.bfloat16)


def steps_of(key, extent, shards, smallest, high):
    level = 1.0
    for dim, parts in shards:
        steps = jax.random.uniform(jax.random.fold_in(jax.random.fold_in(key, 6), dim), (parts,), jnp.float32, smallest / len(shards), high / len(shards))
        level = level * jnp.repeat(jnp.exp(steps), extent[dim] // parts).reshape((-1,) + (1,) * (len(extent) - 1 - dim))
    return level


def scatter_about(stream_key, shape, scale, bound, shards=(), kind=jnp.bfloat16):
    array = jax.random.normal(stream_key, shape, jnp.float32) * scale
    if len(shards) > 0:
        array = steps_of(stream_key, shape, shards, -0.22, 0.18) * array
    return jnp.clip(array, min=-bound, max=bound).astype(kind)


def setup_inputs(seed: int = 0) -> dict:
    key_of = jax.random.split(jax.random.key(seed), 12)
    return {
        "tokens": scatter_about(key_of[0], (TOKENS, D), 1.0, 6.0, ((0, 32),)),
        "cotangent": scatter_about(key_of[1], (TOKENS, D), 1.0, 6.0, ((0, 32),)),
        "lengths": draw_lengths(jax.random.fold_in(key_of[11], 71), 0),
        "value_proj": scatter_about(key_of[3], (D, V), D ** -0.5, 0.1875, ((0, 8), (1, 4))),
        "mix_proj": scatter_about(key_of[4], (D, 2 * D + Z + V), D ** -0.5, 0.1875, ((0, 8), (1, 4))),
        "merge_proj": scatter_about(key_of[5], (V, D), (V // 16) ** -0.5, 0.5, ((0, 8), (1, 4))),
        "up_proj": scatter_about(key_of[6], (D, FF), D ** -0.5, 0.1875, ((0, 8), (1, 4))),
        "down_proj": scatter_about(key_of[7], (FF, D), FF ** -0.5, 0.09375, ((0, 8), (1, 4))),
        "norm_gains": jnp.clip(1.0 + 0.1 * jax.random.normal(key_of[8], (3, D), jnp.float32), 0.5, 1.5).astype(jnp.bfloat16),
        "ema_params": draw_ema_params(jax.random.fold_in(key_of[11], 71), 0),
        "attn_params": scatter_about(key_of[10], (3 * Z + STRETCH,), 1.5, 6.0, ((0, 32),)),
    }


highest = lax.Precision.HIGHEST

@jax.custom_vjp
def low(v):
    return lax.optimization_barrier(v.astype(jnp.bfloat16)).astype(jnp.float32)

@jax.custom_vjp
def low_back(v):
    return v

def low_keep(v):
    return (low(v), None)

def low_pass(kept, grad):
    return (grad,)

def back_keep(v):
    return (v, None)

def back_low(kept, grad):
    return (low(grad),)
low.defvjp(low_keep, low_pass)
low_back.defvjp(back_keep, back_low)

def layer_norm(values, gain):
    centred = values - lax.optimization_barrier(jnp.mean(values, axis=-1, keepdims=True))
    spread_sq = lax.optimization_barrier(jnp.mean(centred * centred, axis=-1, keepdims=True))
    return centred * lax.rsqrt(spread_sq + 1e-05) * gain

def token_layout(length_row, row_count):
    places = jnp.arange(row_count, dtype=jnp.int32)
    running = jnp.cumsum(length_row).astype(jnp.int32)
    before = (running[None, :] <= places[:, None]).astype(jnp.int32)
    starts = lax.optimization_barrier(jnp.sum(before * length_row[None, :], axis=1)).astype(jnp.int32)
    return (places - starts, places < running[-1])

def ema_apply(normed, ema_float, omega_gain, position):
    row_count = normed.shape[0]
    block_len = STRETCH // 4
    damping = jax.nn.sigmoid(ema_float[0])
    decay_gate = jax.nn.sigmoid(ema_float[1])
    keep_rate = 1.0 - damping * decay_gate
    weights_out = damping * ema_float[2] * ema_float[3] * ema_float.shape[2] ** (-0.5)
    lag_axis = jnp.arange(block_len + 1, dtype=normed.dtype)
    powers = jnp.exp(lag_axis[None, None, :] * jnp.log(keep_rate)[:, :, None])
    kernel = jnp.einsum('cj,cjl->cl', weights_out, powers[:, :, :block_len], precision=highest)
    offsets = jnp.arange(block_len, dtype=jnp.int32)[:, None] - jnp.arange(block_len, dtype=jnp.int32)[None, :]
    toeplitz = jnp.where(offsets[None] >= 0, jnp.take(kernel, jnp.clip(offsets, 0, block_len - 1), axis=1), 0.0)
    leaving = powers[:, :, block_len - 1::-1]
    arriving = weights_out[:, :, None] * powers[:, :, 1:]
    blocks = normed.reshape(row_count // block_len, block_len, normed.shape[1])
    resets = position.reshape(row_count // block_len, block_len)[:, 0] == 0

    def advance(ema_state, inputs):
        block_in, is_reset = inputs
        ema_state = jnp.where(is_reset, 0.0, ema_state)
        inner_part = jnp.einsum('cts,sc->tc', toeplitz, block_in, precision=highest)
        carried = jnp.einsum('cjt,cj->tc', arriving, ema_state, precision=highest)
        ema_state = ema_state * powers[:, :, block_len] + jnp.einsum('cjs,sc->cj', leaving, block_in, precision=highest)
        return (ema_state, inner_part + carried)
    zero_state = jnp.zeros(keep_rate.shape, normed.dtype)
    final_state, mixed_out = lax.scan(advance, zero_state, (blocks, resets))
    return mixed_out.reshape(row_count, normed.shape[1]) + omega_gain * normed

def block_forward(params, tokens_float, length_row):
    value_w, mix_w, merge_w, up_w, down_w, gains_float, ema_float, attn_float = params
    row_count = tokens_float.shape[0]
    position, live_rows = token_layout(length_row, row_count)
    normed = layer_norm(tokens_float, gains_float[0])
    normed_low = low(normed)
    value_pre = low_back(jnp.dot(normed_low, value_w, precision=highest))
    value_low = low(jax.nn.silu(value_pre))
    ema_out = ema_apply(normed, ema_float, gains_float[2], position)
    mixed_low = low(jax.nn.silu(ema_out))
    projected = low_back(jnp.dot(mixed_low, mix_w, precision=highest))
    update_gate = jax.nn.sigmoid(projected[:, :D])
    shared = jax.nn.silu(projected[:, D:D + Z])
    reset_gate = jax.nn.silu(projected[:, D + Z:D + Z + V])
    hidden_x = projected[:, D + Z + V:]
    query_low = low(shared * attn_float[:Z] + attn_float[Z:2 * Z])
    key_low = low(shared * attn_float[2 * Z:3 * Z])
    block_count = row_count // STRETCH
    lag_grid = jnp.arange(STRETCH, dtype=jnp.int32)[:, None] - jnp.arange(STRETCH, dtype=jnp.int32)[None, :]
    one_hot = (lag_grid[:, :, None] == jnp.arange(STRETCH, dtype=jnp.int32)[None, None, :]).astype(tokens_float.dtype)
    bias_grid = jnp.einsum('ijl,l->ij', one_hot, attn_float[3 * Z:], precision=highest)
    raw_scores = jnp.einsum('nik,njk->nij', query_low.reshape(block_count, STRETCH, Z), key_low.reshape(block_count, STRETCH, Z), precision=highest) * Z ** (-0.5) + bias_grid
    scores = low_back(jnp.where(lag_grid >= 0, raw_scores, -1000000000.0))
    probs_low = low(jax.nn.softmax(scores, axis=-1))
    attended = low_back(jnp.einsum('nij,njv->niv', probs_low, value_low.reshape(block_count, STRETCH, V), precision=highest)).reshape(row_count, V)
    gated_low = low(attended * reset_gate)
    merged = low_back(jnp.dot(gated_low, merge_w, precision=highest))
    hidden = jax.nn.silu(merged + hidden_x)
    after_mixer = update_gate * hidden + (1.0 - update_gate) * tokens_float
    normed_two = layer_norm(after_mixer, gains_float[1])
    up_pre = low_back(jnp.dot(low(normed_two), up_w, precision=highest))
    down_out = low_back(jnp.dot(low(jax.nn.silu(up_pre)), down_w, precision=highest))
    return after_mixer + down_out

def reference(tokens, cotangent, lengths, value_proj, mix_proj, merge_proj, up_proj, down_proj, norm_gains, ema_params, attn_params):
    params = tuple((array_in.astype(jnp.float32) for array_in in (value_proj, mix_proj, merge_proj, up_proj, down_proj, norm_gains, ema_params, attn_params)))
    tokens_float = tokens.astype(jnp.float32).reshape(BUFFERS, TOK_DEV, D)

    def live_of(length_row):
        return token_layout(length_row, TOK_DEV)[1]
    live_rows = jax.vmap(live_of)(lengths)
    grad_rows = cotangent.astype(jnp.float32).reshape(BUFFERS, TOK_DEV, D) * live_rows[:, :, None].astype(jnp.float32)

    def forward(params_in, tokens_in):

        def runner(operands):
            return block_forward(params_in, operands[0], operands[1])
        return lax.map(jax.checkpoint(runner), (tokens_in, lengths))
    outputs, pullback = jax.vjp(forward, params, tokens_float)
    grads, grad_input = pullback(grad_rows)
    return (outputs.reshape(TOKENS, D).astype(jnp.bfloat16), grad_input.reshape(TOKENS, D).astype(jnp.bfloat16), grads[0], grads[1], grads[2], grads[3], grads[4], grads[5], grads[6], grads[7])
```

```python
import jax
import jax.numpy as jnp
from jax import lax
from jax.experimental import pallas as pl
from jax.experimental.pallas import tpu as pltpu
from jax.sharding import PartitionSpec as P

D = 1024
Z = 128
V = 2048
STRETCH = 128


highest = lax.Precision.HIGHEST


def layer_norm(values, gain):
    centred = values - jnp.mean(values, axis=-1, keepdims=True)
    spread_sq = jnp.mean(centred * centred, axis=-1, keepdims=True)
    return centred * lax.rsqrt(spread_sq + 1e-05) * gain


def token_layout(length_row, row_count):
    places = jnp.arange(row_count, dtype=jnp.int32)
    running = jnp.cumsum(length_row)
    before = (running[None, :] <= places[:, None]).astype(jnp.int32)
    starts = jnp.sum(before * length_row[None, :], axis=1)
    return (places - starts, places < running[-1])


def ema_coefficients(ema):
    damping = jax.nn.sigmoid(ema[0])
    decay_gate = jax.nn.sigmoid(ema[1])
    keep_rate = 1.0 - damping * decay_gate
    weights_out = damping * ema[2] * ema[3] * ema.shape[1] ** (-0.5)
    return damping, decay_gate, keep_rate, weights_out


CHUNK = 32


def ema_forward_kernel(x_ref, ema_ref, omega_ref, keep_ref, y_ref, mark_ref):
    _, _, rate, weight = ema_coefficients(ema_ref[...])
    omega = omega_ref[...]

    def chunk(k, state):
        state = state * keep_ref[k][None]
        mark_ref[k] = state

        def step(i, state):
            t = k * CHUNK + i
            x = x_ref[t]
            state = rate * state + x[None]
            y_ref[t] = jnp.sum(weight * state, axis=0) + omega * x
            return state

        return lax.fori_loop(0, CHUNK, step, state, unroll=4)

    lax.fori_loop(0, x_ref.shape[0] // CHUNK, chunk, jnp.zeros_like(rate))


def ema_backward_kernel(x_ref, g_ref, ema_ref, omega_ref, keep_ref, mark_ref, dx_ref, dema_ref, domega_ref, h_ref):
    ema = ema_ref[...]
    damping, decay_gate, rate_all, weight_all = ema_coefficients(ema)
    omega = omega_ref[...]
    half = rate_all.shape[0] // 2
    chunks = x_ref.shape[0] // CHUNK
    sums = []
    for part in range(2):
        js = slice(part * half, (part + 1) * half)
        rate, weight = rate_all[js], weight_all[js]
        zero = jnp.zeros_like(rate)

        def chunk(m, carry, js=js, rate=rate, weight=weight, part=part):
            k = chunks - 1 - m
            h_ref[0] = mark_ref[k, js]

            def ahead(i, state):
                state = rate * state + x_ref[k * CHUNK + i][None]
                h_ref[i + 1] = state
                return state

            lax.fori_loop(0, CHUNK, ahead, h_ref[0], unroll=4)

            def back(n, carry):
                s, dw, dr, dom = carry
                i = CHUNK - 1 - n
                t = k * CHUNK + i
                g = g_ref[t]
                s = rate * s + g[None]
                dx = jnp.sum(weight * s, axis=0)
                if part == 0:
                    dx_ref[t] = dx + omega * g
                    dom = dom + g * x_ref[t]
                else:
                    dx_ref[t] = dx_ref[t] + dx
                dw = dw + h_ref[i + 1] * g[None]
                dr = dr + h_ref[i] * s
                return s, dw, dr, dom

            s, dw, dr, dom = lax.fori_loop(0, CHUNK, back, carry, unroll=2)
            return s * keep_ref[k][None], dw, dr, dom

        out = lax.fori_loop(0, chunks, chunk, (zero, zero, zero, jnp.zeros_like(omega)))
        sums.append(out)
    dw = jnp.concatenate([sums[0][1], sums[1][1]], axis=0)
    dr = jnp.concatenate([sums[0][2], sums[1][2]], axis=0) * weight_all
    scale = ema.shape[1] ** (-0.5)
    d_damp = dw * ema[2] * ema[3] * scale - dr * decay_gate
    dema_ref[0] = d_damp * damping * (1.0 - damping)
    dema_ref[1] = -dr * damping * decay_gate * (1.0 - decay_gate)
    dema_ref[2] = dw * damping * ema[3] * scale
    dema_ref[3] = dw * damping * ema[2] * scale
    domega_ref[...] = sums[0][3]


def ema_keep(position):
    starts = position.reshape(-1, CHUNK)[:, 0] != 0
    return jnp.broadcast_to(starts.astype(jnp.float32)[:, None, None], (starts.shape[0], 8, 128))


def ema_apply(x, ema, omega, keep):
    f32 = jnp.float32
    shape = jax.ShapeDtypeStruct
    return pl.pallas_call(
        ema_forward_kernel,
        out_shape=(shape(x.shape, f32), shape((keep.shape[0],) + ema.shape[1:], f32)),
        compiler_params=pltpu.CompilerParams(vmem_limit_bytes=32 << 20),
    )(x, ema, omega, keep)


def ema_reverse(x, g, ema, omega, keep, mark):
    f32 = jnp.float32
    shape = jax.ShapeDtypeStruct
    return pl.pallas_call(
        ema_backward_kernel,
        out_shape=(shape(x.shape, f32), shape(ema.shape, f32), shape(omega.shape, f32)),
        scratch_shapes=[pltpu.VMEM((CHUNK + 1, ema.shape[1] // 2) + ema.shape[2:], f32)],
        compiler_params=pltpu.CompilerParams(vmem_limit_bytes=32 << 20),
    )(x, g, ema, omega, keep, mark)


def silu_slope(values):
    logistic = jax.nn.sigmoid(values)
    return logistic * (1.0 + values * (1.0 - logistic))


def relative_table(rel_bias):
    lag_grid = (
        jnp.arange(STRETCH, dtype=jnp.int32)[:, None]
        - jnp.arange(STRETCH, dtype=jnp.int32)[None, :]
    )
    one_hot = (lag_grid[:, :, None] == jnp.arange(STRETCH, dtype=jnp.int32)[None, None, :]).astype(
        jnp.float32
    )
    bias_grid = jnp.einsum("ijl,l->ij", one_hot, rel_bias, precision=highest)
    return (lag_grid, one_hot, bias_grid)


def gather_forward(value_proj, mix_proj, merge_proj, up_proj, down_proj):
    first = (
        lax.all_gather(value_proj, "dp", axis=0, tiled=True),
        lax.all_gather(mix_proj, "dp", axis=0, tiled=True),
        lax.all_gather(merge_proj, "dp", axis=0, tiled=True),
        lax.all_gather(up_proj, "dp", axis=0, tiled=True),
        lax.all_gather(down_proj, "dp", axis=0, tiled=True),
    )
    return (
        lax.all_gather(first[0], "fsdp", axis=1, tiled=True),
        lax.all_gather(first[1], "fsdp", axis=1, tiled=True),
        lax.all_gather(first[2], "fsdp", axis=1, tiled=True),
        lax.all_gather(first[3], "fsdp", axis=1, tiled=True),
        lax.all_gather(first[4], "fsdp", axis=1, tiled=True),
    )


def reduce_gradients(value_grad, mix_grad, merge_grad, up_grad, down_grad):
    first = (
        lax.psum_scatter(
            value_grad.astype(jnp.bfloat16), "dp", scatter_dimension=0, tiled=True
        ).astype(jnp.float32),
        lax.psum_scatter(
            mix_grad.astype(jnp.bfloat16), "dp", scatter_dimension=0, tiled=True
        ).astype(jnp.float32),
        lax.psum_scatter(
            merge_grad.astype(jnp.bfloat16), "dp", scatter_dimension=0, tiled=True
        ).astype(jnp.float32),
        lax.psum_scatter(
            up_grad.astype(jnp.bfloat16), "dp", scatter_dimension=0, tiled=True
        ).astype(jnp.float32),
        lax.psum_scatter(
            down_grad.astype(jnp.bfloat16), "dp", scatter_dimension=0, tiled=True
        ).astype(jnp.float32),
    )
    return (
        lax.psum_scatter(
            first[0].astype(jnp.bfloat16), "fsdp", scatter_dimension=1, tiled=True
        ).astype(jnp.float32),
        lax.psum_scatter(
            first[1].astype(jnp.bfloat16), "fsdp", scatter_dimension=1, tiled=True
        ).astype(jnp.float32),
        lax.psum_scatter(
            first[2].astype(jnp.bfloat16), "fsdp", scatter_dimension=1, tiled=True
        ).astype(jnp.float32),
        lax.psum_scatter(
            first[3].astype(jnp.bfloat16), "fsdp", scatter_dimension=1, tiled=True
        ).astype(jnp.float32),
        lax.psum_scatter(
            first[4].astype(jnp.bfloat16), "fsdp", scatter_dimension=1, tiled=True
        ).astype(jnp.float32),
    )


def on_device(
    tokens,
    cotangent,
    lengths,
    value_proj,
    mix_proj,
    merge_proj,
    up_proj,
    down_proj,
    norm_gains,
    ema_params,
    attn_params,
):
    gains_full, ema_full, attn_full = (
        lax.all_gather(norm_gains, ("dp", "fsdp"), axis=1, tiled=True),
        lax.all_gather(ema_params, ("dp", "fsdp"), axis=1, tiled=True),
        lax.all_gather(attn_params, ("dp", "fsdp"), axis=0, tiled=True),
    )
    value_full, mix_full, merge_full, up_full, down_full = gather_forward(
        value_proj, mix_proj, merge_proj, up_proj, down_proj
    )
    gains_float = gains_full.astype(jnp.float32)
    ema_float = ema_full.astype(jnp.float32)
    attn_float = attn_full.astype(jnp.float32)
    row_count = tokens.shape[0]
    position, live_rows = token_layout(lengths[0], row_count)
    tokens_float = tokens.astype(jnp.float32)
    normed, norm_back = jax.vjp(layer_norm, tokens_float, gains_float[0])
    normed_low = normed.astype(jnp.bfloat16)
    value_pre = jnp.dot(normed_low, value_full, preferred_element_type=jnp.float32)
    value_low = jax.nn.silu(value_pre).astype(jnp.bfloat16)

    lanes = (8, tokens.shape[1] // 8)
    ema_by_state = jnp.swapaxes(ema_float, 1, 2).reshape(4, -1, *lanes)
    omega = gains_float[2].reshape(lanes)
    keep = ema_keep(position)
    normed_rows = normed.reshape(row_count, *lanes)
    ema_rows, ema_marks = ema_apply(normed_rows, ema_by_state, omega, keep)
    ema_out = ema_rows.reshape(row_count, -1)
    mixed_low = jax.nn.silu(ema_out).astype(jnp.bfloat16)
    projected = jnp.dot(mixed_low, mix_full, preferred_element_type=jnp.float32)
    update_gate = jax.nn.sigmoid(projected[:, :D])
    shared_pre = projected[:, D : D + Z]
    reset_pre = projected[:, D + Z : D + Z + V]
    hidden_x = projected[:, D + Z + V :]
    shared = jax.nn.silu(shared_pre)
    reset_gate = jax.nn.silu(reset_pre)
    query_low = (shared * attn_float[:Z] + attn_float[Z : 2 * Z]).astype(jnp.bfloat16)
    key_low = (shared * attn_float[2 * Z : 3 * Z]).astype(jnp.bfloat16)
    block_count = row_count // STRETCH
    lag_grid, one_hot, bias_grid = relative_table(attn_float[3 * Z :])
    query_blocks = query_low.reshape(block_count, STRETCH, Z)
    key_blocks = key_low.reshape(block_count, STRETCH, Z)
    value_blocks = value_low.reshape(block_count, STRETCH, V)
    score_scale = Z ** (-0.5)

    def block_scores():
        raw_scores = (
            jnp.einsum("nik,njk->nij", query_blocks, key_blocks, preferred_element_type=jnp.float32)
            * score_scale
            + bias_grid
        )
        return jnp.where(lag_grid >= 0, raw_scores, -1000000000.0)

    scores = block_scores()
    row_max = jnp.max(scores, axis=-1, keepdims=True)
    log_total = row_max + jnp.log(jnp.sum(jnp.exp(scores - row_max), axis=-1, keepdims=True))
    probs_low = jnp.exp(scores - log_total).astype(jnp.bfloat16)
    attended = jnp.einsum(
        "nij,njv->niv", probs_low, value_blocks, preferred_element_type=jnp.float32
    ).reshape(row_count, V)
    gated_low = (attended * reset_gate).astype(jnp.bfloat16)
    hidden_in = jnp.dot(gated_low, merge_full, preferred_element_type=jnp.float32) + hidden_x
    hidden = jax.nn.silu(hidden_in)
    after_mixer = update_gate * hidden + (1.0 - update_gate) * tokens_float
    normed_two, norm_two_back = jax.vjp(layer_norm, after_mixer, gains_float[1])
    normed_two_low = normed_two.astype(jnp.bfloat16)
    up_pre = jnp.dot(normed_two_low, up_full, preferred_element_type=jnp.float32)
    up_low = jax.nn.silu(up_pre).astype(jnp.bfloat16)
    result = (after_mixer + jnp.dot(up_low, down_full, preferred_element_type=jnp.float32)).astype(
        jnp.bfloat16
    )
    value_back, mix_back, merge_back, up_back, down_back = (
        value_full, mix_full, merge_full, up_full, down_full
    )
    grad_rows = cotangent.astype(jnp.float32) * live_rows[:, None].astype(jnp.float32)
    grad_down_low = grad_rows.astype(jnp.bfloat16)
    down_grad = jnp.einsum("tf,td->fd", up_low, grad_down_low, preferred_element_type=jnp.float32)
    grad_up_act = jnp.einsum(
        "td,fd->tf", grad_down_low, down_back, preferred_element_type=jnp.float32
    )
    grad_up_low = (grad_up_act * silu_slope(up_pre)).astype(jnp.bfloat16)
    up_grad = jnp.einsum(
        "td,tf->df", normed_two_low, grad_up_low, preferred_element_type=jnp.float32
    )
    grad_normed_two = jnp.einsum(
        "tf,df->td", grad_up_low, up_back, preferred_element_type=jnp.float32
    )
    grad_after_norm, gain_two_grad = norm_two_back(grad_normed_two)
    grad_after = grad_after_norm + grad_rows
    grad_hidden_in = grad_after * update_gate * silu_slope(hidden_in)
    grad_merge_low = grad_hidden_in.astype(jnp.bfloat16)
    merge_grad = jnp.einsum(
        "tv,td->vd", gated_low, grad_merge_low, preferred_element_type=jnp.float32
    )
    grad_gated = jnp.einsum(
        "td,vd->tv", grad_merge_low, merge_back, preferred_element_type=jnp.float32
    )
    grad_reset = grad_gated * attended
    grad_attended_low = (
        (grad_gated * reset_gate).astype(jnp.bfloat16).reshape(block_count, STRETCH, V)
    )
    grad_probs = jnp.einsum(
        "niv,njv->nij", grad_attended_low, value_blocks, preferred_element_type=jnp.float32
    )
    soft_probs = jnp.exp(block_scores() - log_total)
    grad_scores_low = (
        soft_probs * (grad_probs - jnp.sum(soft_probs * grad_probs, axis=-1, keepdims=True))
    ).astype(jnp.bfloat16)
    grad_query = (
        jnp.einsum(
            "nij,njk->nik", grad_scores_low, key_blocks, preferred_element_type=jnp.float32
        ).reshape(row_count, Z)
        * score_scale
    )
    grad_key = (
        jnp.einsum(
            "nij,nik->njk", grad_scores_low, query_blocks, preferred_element_type=jnp.float32
        ).reshape(row_count, Z)
        * score_scale
    )
    grad_value_act = jnp.einsum(
        "nij,niv->njv",
        soft_probs.astype(jnp.bfloat16),
        grad_attended_low,
        preferred_element_type=jnp.float32,
    ).reshape(row_count, V)
    rel_grad = jnp.einsum(
        "ij,ijl->l",
        jnp.sum(grad_scores_low.astype(jnp.float32), axis=0),
        one_hot,
        precision=highest,
    )
    attn_grad = jnp.concatenate(
        [
            jnp.sum(grad_query * shared, axis=0),
            jnp.sum(grad_query, axis=0),
            jnp.sum(grad_key * shared, axis=0),
            rel_grad,
        ]
    )
    grad_shared = grad_query * attn_float[:Z] + grad_key * attn_float[2 * Z : 3 * Z]
    grad_projected_low = jnp.concatenate(
        [
            grad_after * (hidden - tokens_float) * update_gate * (1.0 - update_gate),
            grad_shared * silu_slope(shared_pre),
            grad_reset * silu_slope(reset_pre),
            grad_hidden_in,
        ],
        axis=1,
    ).astype(jnp.bfloat16)
    mix_grad = jnp.einsum(
        "td,tm->dm", mixed_low, grad_projected_low, preferred_element_type=jnp.float32
    )
    grad_mixed = jnp.einsum(
        "tm,dm->td", grad_projected_low, mix_back, preferred_element_type=jnp.float32
    )
    grad_ema_rows = (grad_mixed * silu_slope(ema_out)).reshape(row_count, *lanes)
    grad_normed_rows, ema_grad_rows, omega_grad = ema_reverse(
        normed_rows, grad_ema_rows, ema_by_state, omega, keep, ema_marks
    )
    grad_normed_ema = grad_normed_rows.reshape(row_count, -1)
    ema_grad = jnp.swapaxes(ema_grad_rows.reshape(4, -1, tokens.shape[1]), 1, 2)
    omega_grad = omega_grad.reshape(-1)
    grad_value_low = (grad_value_act * silu_slope(value_pre)).astype(jnp.bfloat16)
    value_grad = jnp.einsum(
        "td,tv->dv", normed_low, grad_value_low, preferred_element_type=jnp.float32
    )
    grad_normed = grad_normed_ema + jnp.einsum(
        "tv,dv->td", grad_value_low, value_back, preferred_element_type=jnp.float32
    )
    grad_input, gain_one_grad = norm_back(grad_normed)
    grad_tokens = (grad_input + grad_after * (1.0 - update_gate)).astype(jnp.bfloat16)
    gains_grad = jnp.stack([gain_one_grad, gain_two_grad, omega_grad])
    small_totals = (
        lax.psum_scatter(gains_grad, ("dp", "fsdp"), scatter_dimension=1, tiled=True),
        lax.psum_scatter(ema_grad, ("dp", "fsdp"), scatter_dimension=1, tiled=True),
        lax.psum_scatter(attn_grad, ("dp", "fsdp"), scatter_dimension=0, tiled=True),
    )
    totals = reduce_gradients(value_grad, mix_grad, merge_grad, up_grad, down_grad)
    return (
        result,
        grad_tokens,
        totals[0],
        totals[1],
        totals[2],
        totals[3],
        totals[4],
        small_totals[0],
        small_totals[1],
        small_totals[2],
    )


def solution(mesh):
    in_specs = (
        P(("dp", "fsdp"), None),
        P(("dp", "fsdp"), None),
        P(("dp", "fsdp"), None),
        P("dp", "fsdp"),
        P("dp", "fsdp"),
        P("dp", "fsdp"),
        P("dp", "fsdp"),
        P("dp", "fsdp"),
        P(None, ("dp", "fsdp")),
        P(None, ("dp", "fsdp"), None),
        P(("dp", "fsdp")),
    )
    out_specs = (
        P(("dp", "fsdp"), None),
        P(("dp", "fsdp"), None),
        P("dp", "fsdp"),
        P("dp", "fsdp"),
        P("dp", "fsdp"),
        P("dp", "fsdp"),
        P("dp", "fsdp"),
        P(None, ("dp", "fsdp")),
        P(None, ("dp", "fsdp"), None),
        P(("dp", "fsdp")),
    )
    return jax.shard_map(
        on_device, mesh=mesh, in_specs=in_specs, out_specs=out_specs, check_vma=False
    )
```

```python
import functools
import types

import jax
import jax.numpy as jnp
from jax import lax
from jax.experimental import pallas as pl
from jax.experimental.pallas import tpu as pltpu
from jax.sharding import PartitionSpec as P

D = 1024
Z = 128
V = 2048
STRETCH = 128


DP, FS = "dp", "fsdp"
highest = lax.Precision.HIGHEST


def layer_norm(values, gain):
    centred = values - jnp.mean(values, axis=-1, keepdims=True)
    spread_sq = jnp.mean(centred * centred, axis=-1, keepdims=True)
    return centred * lax.rsqrt(spread_sq + 1e-05) * gain


def token_layout(length_row, row_count):
    places = jnp.arange(row_count, dtype=jnp.int32)
    running = jnp.cumsum(length_row)
    before = (running[None, :] <= places[:, None]).astype(jnp.int32)
    starts = jnp.sum(before * length_row[None, :], axis=1)
    return (places - starts, places < running[-1])


def ema_coefficients(ema):
    damping = jax.nn.sigmoid(ema[0])
    decay_gate = jax.nn.sigmoid(ema[1])
    keep_rate = 1.0 - damping * decay_gate
    weights_out = damping * ema[2] * ema[3] * ema.shape[1] ** (-0.5)
    return damping, decay_gate, keep_rate, weights_out


CHUNK = 32


def ema_forward_kernel(x_ref, ema_ref, omega_ref, keep_ref, y_ref, mark_ref):
    _, _, rate, weight = ema_coefficients(ema_ref[...])
    omega = omega_ref[...]

    def chunk(k, state):
        state = state * keep_ref[k][None]
        mark_ref[k] = state

        def step(i, state):
            t = k * CHUNK + i
            x = x_ref[t]
            state = rate * state + x[None]
            y_ref[t] = jnp.sum(weight * state, axis=0) + omega * x
            return state

        return lax.fori_loop(0, CHUNK, step, state, unroll=4)

    lax.fori_loop(0, x_ref.shape[0] // CHUNK, chunk, jnp.zeros_like(rate))


def ema_backward_kernel(x_ref, g_ref, ema_ref, omega_ref, keep_ref, mark_ref, dx_ref, dema_ref, domega_ref, h_ref):
    ema = ema_ref[...]
    damping, decay_gate, rate_all, weight_all = ema_coefficients(ema)
    omega = omega_ref[...]
    half = rate_all.shape[0] // 2
    chunks = x_ref.shape[0] // CHUNK
    sums = []
    for part in range(2):
        js = slice(part * half, (part + 1) * half)
        rate, weight = rate_all[js], weight_all[js]
        zero = jnp.zeros_like(rate)

        def chunk(m, carry, js=js, rate=rate, weight=weight, part=part):
            k = chunks - 1 - m
            h_ref[0] = mark_ref[k, js]

            def ahead(i, state):
                state = rate * state + x_ref[k * CHUNK + i][None]
                h_ref[i + 1] = state
                return state

            lax.fori_loop(0, CHUNK, ahead, h_ref[0], unroll=4)

            def back(n, carry):
                s, dw, dr, dom = carry
                i = CHUNK - 1 - n
                t = k * CHUNK + i
                g = g_ref[t]
                s = rate * s + g[None]
                dx = jnp.sum(weight * s, axis=0)
                if part == 0:
                    dx_ref[t] = dx + omega * g
                    dom = dom + g * x_ref[t]
                else:
                    dx_ref[t] = dx_ref[t] + dx
                dw = dw + h_ref[i + 1] * g[None]
                dr = dr + h_ref[i] * s
                return s, dw, dr, dom

            s, dw, dr, dom = lax.fori_loop(0, CHUNK, back, carry, unroll=2)
            return s * keep_ref[k][None], dw, dr, dom

        out = lax.fori_loop(0, chunks, chunk, (zero, zero, zero, jnp.zeros_like(omega)))
        sums.append(out)
    dw = jnp.concatenate([sums[0][1], sums[1][1]], axis=0)
    dr = jnp.concatenate([sums[0][2], sums[1][2]], axis=0) * weight_all
    scale = ema.shape[1] ** (-0.5)
    d_damp = dw * ema[2] * ema[3] * scale - dr * decay_gate
    dema_ref[0] = d_damp * damping * (1.0 - damping)
    dema_ref[1] = -dr * damping * decay_gate * (1.0 - decay_gate)
    dema_ref[2] = dw * damping * ema[3] * scale
    dema_ref[3] = dw * damping * ema[2] * scale
    domega_ref[...] = sums[0][3]


def ema_keep(position):
    starts = position.reshape(-1, CHUNK)[:, 0] != 0
    return jnp.broadcast_to(starts.astype(jnp.float32)[:, None, None], (starts.shape[0], 8, 128))


def ema_apply(x, ema, omega, keep):
    f32 = jnp.float32
    shape = jax.ShapeDtypeStruct
    return pl.pallas_call(
        ema_forward_kernel,
        out_shape=(shape(x.shape, f32), shape((keep.shape[0],) + ema.shape[1:], f32)),
        compiler_params=pltpu.CompilerParams(vmem_limit_bytes=32 << 20),
    )(x, ema, omega, keep)


def ema_reverse(x, g, ema, omega, keep, mark):
    f32 = jnp.float32
    shape = jax.ShapeDtypeStruct
    return pl.pallas_call(
        ema_backward_kernel,
        out_shape=(shape(x.shape, f32), shape(ema.shape, f32), shape(omega.shape, f32)),
        scratch_shapes=[pltpu.VMEM((CHUNK + 1, ema.shape[1] // 2) + ema.shape[2:], f32)],
        compiler_params=pltpu.CompilerParams(vmem_limit_bytes=32 << 20),
    )(x, g, ema, omega, keep, mark)


def silu_slope(values):
    logistic = jax.nn.sigmoid(values)
    return logistic * (1.0 + values * (1.0 - logistic))


def relative_table(rel_bias):
    lag_grid = (
        jnp.arange(STRETCH, dtype=jnp.int32)[:, None]
        - jnp.arange(STRETCH, dtype=jnp.int32)[None, :]
    )
    one_hot = (lag_grid[:, :, None] == jnp.arange(STRETCH, dtype=jnp.int32)[None, None, :]).astype(
        jnp.float32
    )
    bias_grid = jnp.einsum("ijl,l->ij", one_hot, rel_bias, precision=highest)
    return (lag_grid, one_hot, bias_grid)


def gather_forward(value_proj, mix_proj, merge_proj, up_proj, down_proj):
    first = (
        lax.all_gather(value_proj, DP, axis=0, tiled=True),
        lax.all_gather(mix_proj, DP, axis=0, tiled=True),
        lax.all_gather(merge_proj, DP, axis=0, tiled=True),
        lax.all_gather(up_proj, DP, axis=0, tiled=True),
        lax.all_gather(down_proj, DP, axis=0, tiled=True),
    )
    return (
        lax.all_gather(first[0], FS, axis=1, tiled=True),
        lax.all_gather(first[1], FS, axis=1, tiled=True),
        lax.all_gather(first[2], FS, axis=1, tiled=True),
        lax.all_gather(first[3], FS, axis=1, tiled=True),
        lax.all_gather(first[4], FS, axis=1, tiled=True),
    )


def reduce_gradients(value_grad, mix_grad, merge_grad, up_grad, down_grad):
    first = (
        lax.psum_scatter(
            value_grad.astype(jnp.bfloat16), DP, scatter_dimension=0, tiled=True
        ).astype(jnp.float32),
        lax.psum_scatter(
            mix_grad.astype(jnp.bfloat16), DP, scatter_dimension=0, tiled=True
        ).astype(jnp.float32),
        lax.psum_scatter(
            merge_grad.astype(jnp.bfloat16), DP, scatter_dimension=0, tiled=True
        ).astype(jnp.float32),
        lax.psum_scatter(
            up_grad.astype(jnp.bfloat16), DP, scatter_dimension=0, tiled=True
        ).astype(jnp.float32),
        lax.psum_scatter(
            down_grad.astype(jnp.bfloat16), DP, scatter_dimension=0, tiled=True
        ).astype(jnp.float32),
    )
    return (
        lax.psum_scatter(
            first[0].astype(jnp.bfloat16), FS, scatter_dimension=1, tiled=True
        ).astype(jnp.float32),
        lax.psum_scatter(
            first[1].astype(jnp.bfloat16), FS, scatter_dimension=1, tiled=True
        ).astype(jnp.float32),
        lax.psum_scatter(
            first[2].astype(jnp.bfloat16), FS, scatter_dimension=1, tiled=True
        ).astype(jnp.float32),
        lax.psum_scatter(
            first[3].astype(jnp.bfloat16), FS, scatter_dimension=1, tiled=True
        ).astype(jnp.float32),
        lax.psum_scatter(
            first[4].astype(jnp.bfloat16), FS, scatter_dimension=1, tiled=True
        ).astype(jnp.float32),
    )


def on_device(
    tokens,
    cotangent,
    lengths,
    value_proj,
    mix_proj,
    merge_proj,
    up_proj,
    down_proj,
    norm_gains,
    ema_params,
    attn_params,
):
    gains_full, ema_full, attn_full = (
        lax.all_gather(norm_gains, (DP, FS), axis=1, tiled=True),
        lax.all_gather(ema_params, (DP, FS), axis=1, tiled=True),
        lax.all_gather(attn_params, (DP, FS), axis=0, tiled=True),
    )
    value_full, mix_full, merge_full, up_full, down_full = gather_forward(
        value_proj, mix_proj, merge_proj, up_proj, down_proj
    )
    gains_float = gains_full.astype(jnp.float32)
    ema_float = ema_full.astype(jnp.float32)
    attn_float = attn_full.astype(jnp.float32)
    row_count = tokens.shape[0]
    position, live_rows = token_layout(lengths[0], row_count)
    tokens_float = tokens.astype(jnp.float32)
    normed, norm_back = jax.vjp(layer_norm, tokens_float, gains_float[0])
    normed_low = normed.astype(jnp.bfloat16)
    value_pre = jnp.dot(normed_low, value_full, preferred_element_type=jnp.float32)
    value_low = jax.nn.silu(value_pre).astype(jnp.bfloat16)

    lanes = (8, tokens.shape[1] // 8)
    ema_by_state = jnp.swapaxes(ema_float, 1, 2).reshape(4, -1, *lanes)
    omega = gains_float[2].reshape(lanes)
    keep = ema_keep(position)
    normed_rows = normed.reshape(row_count, *lanes)
    ema_rows, ema_marks = ema_apply(normed_rows, ema_by_state, omega, keep)
    ema_out = ema_rows.reshape(row_count, -1)
    mixed_low = jax.nn.silu(ema_out).astype(jnp.bfloat16)
    projected = jnp.dot(mixed_low, mix_full, preferred_element_type=jnp.float32)
    update_gate = jax.nn.sigmoid(projected[:, :D])
    shared_pre = projected[:, D : D + Z]
    reset_pre = projected[:, D + Z : D + Z + V]
    hidden_x = projected[:, D + Z + V :]
    shared = jax.nn.silu(shared_pre)
    reset_gate = jax.nn.silu(reset_pre)
    query_low = (shared * attn_float[:Z] + attn_float[Z : 2 * Z]).astype(jnp.bfloat16)
    key_low = (shared * attn_float[2 * Z : 3 * Z]).astype(jnp.bfloat16)
    block_count = row_count // STRETCH
    lag_grid, one_hot, bias_grid = relative_table(attn_float[3 * Z :])
    query_blocks = query_low.reshape(block_count, STRETCH, Z)
    key_blocks = key_low.reshape(block_count, STRETCH, Z)
    value_blocks = value_low.reshape(block_count, STRETCH, V)
    score_scale = Z ** (-0.5)

    def block_scores():
        raw_scores = (
            jnp.einsum("nik,njk->nij", query_blocks, key_blocks, preferred_element_type=jnp.float32)
            * score_scale
            + bias_grid
        )
        return jnp.where(lag_grid >= 0, raw_scores, -1000000000.0)

    scores = block_scores()
    row_max = jnp.max(scores, axis=-1, keepdims=True)
    log_total = row_max + jnp.log(jnp.sum(jnp.exp(scores - row_max), axis=-1, keepdims=True))
    probs_low = jnp.exp(scores - log_total).astype(jnp.bfloat16)
    attended = jnp.einsum(
        "nij,njv->niv", probs_low, value_blocks, preferred_element_type=jnp.float32
    ).reshape(row_count, V)
    gated_low = (attended * reset_gate).astype(jnp.bfloat16)
    hidden_in = jnp.dot(gated_low, merge_full, preferred_element_type=jnp.float32) + hidden_x
    hidden = jax.nn.silu(hidden_in)
    after_mixer = update_gate * hidden + (1.0 - update_gate) * tokens_float
    normed_two, norm_two_back = jax.vjp(layer_norm, after_mixer, gains_float[1])
    normed_two_low = normed_two.astype(jnp.bfloat16)
    up_pre = jnp.dot(normed_two_low, up_full, preferred_element_type=jnp.float32)
    up_low = jax.nn.silu(up_pre).astype(jnp.bfloat16)
    result = (after_mixer + jnp.dot(up_low, down_full, preferred_element_type=jnp.float32)).astype(
        jnp.bfloat16
    )
    value_back, mix_back, merge_back, up_back, down_back = (
        value_full, mix_full, merge_full, up_full, down_full
    )
    grad_rows = cotangent.astype(jnp.float32) * live_rows[:, None].astype(jnp.float32)
    grad_down_low = grad_rows.astype(jnp.bfloat16)
    down_grad = jnp.einsum("tf,td->fd", up_low, grad_down_low, preferred_element_type=jnp.float32)
    grad_up_act = jnp.einsum(
        "td,fd->tf", grad_down_low, down_back, preferred_element_type=jnp.float32
    )
    grad_up_low = (grad_up_act * silu_slope(up_pre)).astype(jnp.bfloat16)
    up_grad = jnp.einsum(
        "td,tf->df", normed_two_low, grad_up_low, preferred_element_type=jnp.float32
    )
    grad_normed_two = jnp.einsum(
        "tf,df->td", grad_up_low, up_back, preferred_element_type=jnp.float32
    )
    grad_after_norm, gain_two_grad = norm_two_back(grad_normed_two)
    grad_after = grad_after_norm + grad_rows
    grad_hidden_in = grad_after * update_gate * silu_slope(hidden_in)
    grad_merge_low = grad_hidden_in.astype(jnp.bfloat16)
    merge_grad = jnp.einsum(
        "tv,td->vd", gated_low, grad_merge_low, preferred_element_type=jnp.float32
    )
    grad_gated = jnp.einsum(
        "td,vd->tv", grad_merge_low, merge_back, preferred_element_type=jnp.float32
    )
    grad_reset = grad_gated * attended
    grad_attended_low = (
        (grad_gated * reset_gate).astype(jnp.bfloat16).reshape(block_count, STRETCH, V)
    )
    grad_probs = jnp.einsum(
        "niv,njv->nij", grad_attended_low, value_blocks, preferred_element_type=jnp.float32
    )
    soft_probs = jnp.exp(block_scores() - log_total)
    grad_scores_low = (
        soft_probs * (grad_probs - jnp.sum(soft_probs * grad_probs, axis=-1, keepdims=True))
    ).astype(jnp.bfloat16)
    grad_query = (
        jnp.einsum(
            "nij,njk->nik", grad_scores_low, key_blocks, preferred_element_type=jnp.float32
        ).reshape(row_count, Z)
        * score_scale
    )
    grad_key = (
        jnp.einsum(
            "nij,nik->njk", grad_scores_low, query_blocks, preferred_element_type=jnp.float32
        ).reshape(row_count, Z)
        * score_scale
    )
    grad_value_act = jnp.einsum(
        "nij,niv->njv",
        soft_probs.astype(jnp.bfloat16),
        grad_attended_low,
        preferred_element_type=jnp.float32,
    ).reshape(row_count, V)
    rel_grad = jnp.einsum(
        "ij,ijl->l",
        jnp.sum(grad_scores_low.astype(jnp.float32), axis=0),
        one_hot,
        precision=highest,
    )
    attn_grad = jnp.concatenate(
        [
            jnp.sum(grad_query * shared, axis=0),
            jnp.sum(grad_query, axis=0),
            jnp.sum(grad_key * shared, axis=0),
            rel_grad,
        ]
    )
    grad_shared = grad_query * attn_float[:Z] + grad_key * attn_float[2 * Z : 3 * Z]
    grad_projected_low = jnp.concatenate(
        [
            grad_after * (hidden - tokens_float) * update_gate * (1.0 - update_gate),
            grad_shared * silu_slope(shared_pre),
            grad_reset * silu_slope(reset_pre),
            grad_hidden_in,
        ],
        axis=1,
    ).astype(jnp.bfloat16)
    mix_grad = jnp.einsum(
        "td,tm->dm", mixed_low, grad_projected_low, preferred_element_type=jnp.float32
    )
    grad_mixed = jnp.einsum(
        "tm,dm->td", grad_projected_low, mix_back, preferred_element_type=jnp.float32
    )
    grad_ema_rows = (grad_mixed * silu_slope(ema_out)).reshape(row_count, *lanes)
    grad_normed_rows, ema_grad_rows, omega_grad = ema_reverse(
        normed_rows, grad_ema_rows, ema_by_state, omega, keep, ema_marks
    )
    grad_normed_ema = grad_normed_rows.reshape(row_count, -1)
    ema_grad = jnp.swapaxes(ema_grad_rows.reshape(4, -1, tokens.shape[1]), 1, 2)
    omega_grad = omega_grad.reshape(-1)
    grad_value_low = (grad_value_act * silu_slope(value_pre)).astype(jnp.bfloat16)
    value_grad = jnp.einsum(
        "td,tv->dv", normed_low, grad_value_low, preferred_element_type=jnp.float32
    )
    grad_normed = grad_normed_ema + jnp.einsum(
        "tv,dv->td", grad_value_low, value_back, preferred_element_type=jnp.float32
    )
    grad_input, gain_one_grad = norm_back(grad_normed)
    grad_tokens = (grad_input + grad_after * (1.0 - update_gate)).astype(jnp.bfloat16)
    gains_grad = jnp.stack([gain_one_grad, gain_two_grad, omega_grad])
    small_totals = (
        lax.psum_scatter(gains_grad, (DP, FS), scatter_dimension=1, tiled=True),
        lax.psum_scatter(ema_grad, (DP, FS), scatter_dimension=1, tiled=True),
        lax.psum_scatter(attn_grad, (DP, FS), scatter_dimension=0, tiled=True),
    )
    totals = reduce_gradients(value_grad, mix_grad, merge_grad, up_grad, down_grad)
    return (
        result,
        grad_tokens,
        totals[0],
        totals[1],
        totals[2],
        totals[3],
        totals[4],
        small_totals[0],
        small_totals[1],
        small_totals[2],
    )


STRIP = 128
MESH = pl.DeviceIdType.MESH
F32 = jnp.float32
LOW = jnp.bfloat16
SHARDED = VALUE, MIX, MERGE, UP, DOWN = range(5)


def mm(a, b):
    return lax.dot_general(a, b, (((1,), (0,)), ((), ())), preferred_element_type=F32)


def mm_nt(a, b):
    return lax.dot_general(a, b, (((1,), (1,)), ((), ())), preferred_element_type=F32)


def mm_tn(a, b):
    return lax.dot_general(a, b, (((0,), (0,)), ((), ())), preferred_element_type=F32)


def at_rows(start, size, unit=16):
    return pl.ds(pl.multiple_of(start, unit), size)


def row_loop(count, size, body):
    def step(i, carry):
        body(pl.multiple_of(i * size, size))
        return carry

    lax.fori_loop(0, count // size, step, 0)


def slope_of(value, gate):
    return gate * (1.0 + value * (1.0 - gate))


def layer_kernel(trees, depth, *refs):
    ref, at = types.SimpleNamespace(), 0
    for tree in trees:
        ref.__dict__.update(jax.tree.unflatten(tree, refs[at : at + tree.num_leaves]))
        at += tree.num_leaves
    tok, cot, gains, ema_in, omega_in, attn = ref.tok, ref.cot, ref.gains, ref.ema_in, ref.omega_in, ref.attn
    rows, width = tok.shape
    tiles = width // 128
    dp, fs = lax.axis_index(DP), lax.axis_index(FS)
    z, c, y, x = dp // 2, dp % 2, fs // 2, fs % 2
    q = c * 2 + x

    def place(z, c, y, x):
        return (z * 2 + c, y * 2 + x)

    sib, xn, xc, yn = place(z, 1 - c, y, x), place(z, c, y, 1 - x), place(z, 1 - c, y, 1 - x), place(z, c, 1 - y, x)
    zs = [None] + [place((z + d) % depth, c, y, x) for d in range(1, depth)]
    mates = ((sib, 1 - c, x), (xn, c, 1 - x), (xc, 1 - c, 1 - x))
    plane = [(pc, py, px) for pc in range(2) for py in range(2) for px in range(2)][1:]
    plane = [((c + pc) % 2, (y + py) % 2, (x + px) % 2) for pc, py, px in plane]

    barrier = pltpu.get_barrier_semaphore()
    peers = [place(z, *p) for p in plane] + zs[1:]
    for peer in peers:
        pl.semaphore_signal(barrier, inc=1, device_id=peer, device_id_type=MESH)
    pl.semaphore_wait(barrier, len(peers))

    send_sems, recv_sems, local_sems = ref.send_sems, ref.recv_sems, ref.local_sems
    used, used_local, pending = [0], [0], []

    def send(src, dst, peer, slot=None):
        k = used[0]
        used[0] += 1
        copy = pltpu.make_async_remote_copy(
            src_ref=src, dst_ref=dst, send_sem=send_sems.at[k], recv_sem=recv_sems.at[k],
            device_id=peer, device_id_type=MESH,
        )
        copy.start()
        handle = [k, copy, False]
        pending.append(handle)
        return handle

    def sent(handle):
        if not handle[2]:
            handle[1].wait_send()
            handle[2] = True

    def received(handle, landed):
        k = handle[0]
        pltpu.make_async_remote_copy(
            src_ref=landed, dst_ref=landed, send_sem=send_sems.at[k], recv_sem=recv_sems.at[k],
            device_id=sib, device_id_type=MESH,
        ).wait_recv()

    def local(src, dst):
        k = used_local[0]
        used_local[0] += 1
        copy = pltpu.make_async_copy(src, dst, local_sems.at[k])
        copy.start()
        return copy

    lens = ref.lens
    ends, run = [], 0
    for i in range(lens.shape[1]):
        run = run + lens[0, i]
        ends.append(run)

    def kept(k):
        start = 0
        for i, end in enumerate(ends):
            start = start + jnp.where(end <= k * CHUNK, lens[0, i], 0)
        return jnp.where(k * CHUNK - start == 0, 0.0, 1.0)

    def live_rows(r, size):
        places = r + lax.broadcasted_iota(jnp.int32, (size, 1), 0)
        return (places < ends[-1]).astype(F32)

    small_all, packed = ref.small_all, ref.packed
    lane_group = lax.broadcasted_iota(jnp.int32, (1, 128), 1) // 32

    def slot(pc, py, px, pz):
        return (pc * 4 + py * 2 + px) * depth + pz

    def small_start():
        return [send(packed, small_all.at[slot(c, y, x, z)], zs[d]) for d in range(1, depth)]

    def small_relay(handles):
        for d, handle in enumerate(handles):
            received(handle, small_all.at[slot(c, y, x, (z + depth - 1 - d) % depth)])
        small_all[slot(c, y, x, z)] = packed[...]
        mine = small_all.at[pl.ds(slot(c, y, x, 0), depth)]
        return [send(mine, mine, place(z, *p)) for p in plane]

    def small_finish(handles):
        for handle, p in zip(handles, plane):
            received(handle, small_all.at[pl.ds(slot(*p, 0), depth)])
        states = ema_in.shape[0] // (4 * tiles)
        gains[...] = jnp.zeros_like(gains)
        attn[...] = jnp.zeros_like(attn)
        for t in range(tiles):
            pz, pc = t // 2, t % 2
            got = [small_all[slot(pc, f // 2, f % 2, pz)].astype(F32)[0 : states + 8, :] for f in range(4)]
            for p in range(4):
                v = jnp.zeros_like(got[0])
                for f in range(4):
                    turn = (f - p) * 32 % 128
                    v = jnp.where(lane_group == f, pltpu.roll(got[f], turn, 1) if turn else got[f], v)
                ema_in[pl.ds(p * states * tiles + t, states, stride=tiles), :] = v[0:states]
                row = v[states : states + 1]
                if p < 3:
                    gains[p : p + 1, t * 128 : (t + 1) * 128] = row
                    if p == 2:
                        omega_in[t : t + 1, :] = row
                    continue
                for f in range(4):
                    turn = (t % 2 * 64 - f * 16) % 128
                    mine = lax.broadcasted_iota(jnp.int32, (1, 128), 1) // 16 == t % 2 * 4 + f
                    moved = pltpu.roll(row, turn, 1) if turn else row
                    attn[t // 2 : t // 2 + 1, :] += jnp.where(mine, moved, 0.0)

    lane = lax.broadcasted_iota(jnp.int32, (1, 128), 1)
    shift = fs * 32

    def mix_align():
        raw, win = ref.s[MIX], ref.mix_win
        last = raw.shape[1] // 128 * 128

        def step(r):
            at = pl.ds(r, 32)
            before = jnp.zeros((32, 128), F32)
            for t in range(win.shape[1] // 128):
                if t * 128 < last:
                    v = raw[at, t * 128 : (t + 1) * 128].astype(F32)
                else:
                    v = jnp.concatenate(
                        [raw[at, last:].astype(F32), jnp.zeros((32, 128 - raw.shape[1] + last), F32)], axis=1
                    )
                v = pltpu.roll(v, shift, 1)
                win[at, t * 128 : (t + 1) * 128] = jnp.where(lane < shift, before, v).astype(LOW)
                before = v

        row_loop(raw.shape[0], 32, step)

    weights = {m: ref.w[m] for m in SHARDED}
    block_shape = {m: (w.shape[0] // depth, w.shape[1] // 2) for m, w in weights.items()}

    def block(m, zz, yy):
        rb, cb = block_shape[m]
        return weights[m].at[at_rows(zz * rb, rb), at_rows(yy * cb, cb, 128)]

    def piece(m, src_c, src_x):
        rb, cb = block_shape[m]
        half = cb // 2
        if m in (VALUE, UP):
            return weights[m].at[at_rows(z * rb + src_c * (rb // 2), rb // 2), at_rows(y * cb + src_x * half, half, 128)]
        return weights[m].at[at_rows(z * rb, rb), at_rows(y * cb + src_x * half, half, 128)]

    swaps, own_copies = {m: [] for m in SHARDED}, {m: [] for m in SHARDED}

    def swap_start(m):
        shard = ref.s[m] if m != MIX else ref.mix_win
        if m == MIX:
            first, last = 1 - (fs + 2) // 3, fs // 3
            middle = 1 - first - last
            for peer, pc, px in ((None, c, x),) + mates:
                pq = pc * 2 + px
                tiles_at = (
                    first * 2 * pq,
                    (first + last) * (1 + 2 * pq) + middle * (1 + pq),
                    first * 8 + last * (2 + 2 * pq) + middle * (5 + pq),
                )
                for i, tile in enumerate(tiles_at):
                    src = shard.at[:, at_rows(tile * 128, 128, 128)]
                    dst = ref.mix_in.at[x, at_rows(c * 128, 128), pl.ds(i * 128, 128)]
                    if peer is None:
                        own_copies[m].append(local(src, dst))
                    else:
                        swaps[m].append((send(src, dst, peer), pc, px, i))
            return
        if m in (VALUE, UP):
            wide = shard.shape[1] // 4
            for peer, pc, px in ((None, c, x),) + mates:
                src = shard.at[:, at_rows((pc * 2 + px) * wide, wide, 128)]
                if peer is None:
                    own_copies[m].append(local(src, piece(m, c, x)))
                else:
                    swaps[m].append((send(src, piece(m, c, x), peer), pc, px, 0))
            return
        tall = shard.shape[0] // 2
        own_copies[m].append(local(shard.at[at_rows(x * tall, tall), :], piece(m, c, x)))
        swaps[m].append((send(shard.at[at_rows((1 - x) * tall, tall), :], piece(m, c, x), xn), c, 1 - x, 0))

    z_sends, y_sends = {}, {}

    def swap_finish(m):
        for copy in own_copies[m]:
            copy.wait()
        for handle, pc, px, i in swaps[m]:
            if m == MIX:
                received(handle, ref.mix_in.at[px, at_rows(pc * 128, 128), pl.ds(i * 128, 128)])
            else:
                received(handle, piece(m, pc, px))
        if m == MIX:
            only = (q == 3).astype(F32)
            low_y = (y == 0).astype(F32)
            lead = jnp.broadcast_to(jnp.maximum(low_y, only), (1, 128))
            rb, cb = block_shape[m]
            a, b, w = ref.mix_in.at[0], ref.mix_in.at[1], weights[m]

            def combine(r):
                at = pl.ds(r, 64)
                to = at_rows(z * rb + r, 64)

                def put(i, v):
                    w[to, at_rows(y * cb + i * 128, 128, 128)] = v.astype(LOW)

                put(0, a[at, 0:128].astype(F32) * lead)
                put(1, a[at, 128:256])
                put(2, a[at, 256:384].astype(F32) + b[at, 0:128].astype(F32) * lead)
                put(3, b[at, 128:256])
                put(4, b[at, 256:384])

            row_loop(rb, 64, combine)

    def y_own(m):
        y_sends[m] = [send(block(m, z, y), block(m, z, y), yn)]

    def z_start(m):
        z_sends[m] = [None] + [send(block(m, z, y), block(m, z, y), zs[d]) for d in range(1, depth)]

    def y_forward(m, steps=range(1, depth)):
        for d in steps:
            zz = (z + depth - d) % depth
            received(z_sends[m][d], block(m, zz, y))
            y_sends[m].append(send(block(m, zz, y), block(m, zz, y), yn))

    def y_finish(m):
        for d in range(depth):
            received(y_sends[m][d], block(m, (z + depth - d) % depth, 1 - y))

    def group_rows(c, x):
        return at_rows((c * 2 + x) * rows, rows)

    def gather_start(buf):
        own = buf.at[group_rows(c, x), :]
        return [send(own, own, xn), send(own, own, sib)]

    def gather_relay(buf, handles):
        other = buf.at[group_rows(c, 1 - x), :]
        received(handles[0], other)
        handles.append(send(other, other, sib))

    def gather_finish(buf, handles):
        received(handles[1], buf.at[group_rows(1 - c, x), :])
        received(handles[2], buf.at[group_rows(1 - c, 1 - x), :])

    total = ref.total
    stage = ref.stage
    staged = [None, None, None]

    def stage_out(k, extra=None):
        if staged[k] is not None:
            sent(staged[k])

        def put(r):
            at = pl.ds(r, 32)
            v = total[at, :]
            if extra is not None:
                v = v + extra[at, :].astype(F32)
            stage[k, at, :] = v.astype(LOW)

        row_loop(rows, 32, put)

    def reduce_early(partial, sibs, cross):
        partial(1 - c, 1 - x)
        stage_out(0)
        h0 = staged[0] = send(stage.at[0], sibs.at[0], sib)
        partial(1 - c, x)
        stage_out(1)
        h1 = staged[1] = send(stage.at[1], sibs.at[1], sib)
        partial(c, 1 - x)
        received(h0, sibs.at[0])
        stage_out(2, sibs.at[0])
        h2 = staged[2] = send(stage.at[2], cross, xn)
        return h1, h2

    def reduce_late(partial, sibs, cross, handles):
        partial(c, x)
        received(handles[0], sibs.at[1])
        received(handles[1], cross)

    def reduced(r, size, sibs, cross):
        at = pl.ds(r, size)
        return total[at, :] + sibs[1, at, :].astype(F32) + cross[at, :].astype(F32)

    sibs_a, cross_a, sibs_b, cross_b = ref.sibs_a, ref.cross_a, ref.sibs_b, ref.cross_b

    w_up = weights[UP]
    y_out = {
        DOWN: ref.yo[1],
        UP: ref.yo[0],
        MERGE: ref.gc.at[0 : weights[MERGE].shape[0], 0 : block_shape[MERGE][1]],
        MIX: w_up.at[:, 0 : block_shape[MIX][1]],
        VALUE: w_up.at[:, block_shape[MIX][1] : block_shape[MIX][1] + block_shape[VALUE][1]],
    }
    y_in = {m: ref.yi[m] for m in SHARDED}
    z_in = {m: ref.zi[m] for m in SHARDED}
    f_in = {m: ref.fi[m] for m in SHARDED}
    gy, gz, gf = {}, {}, {}

    def y_grad_send(m, product):
        rb, cb = block_shape[m]
        gy[m] = []
        for d in list(range(1, depth)) + [0]:
            zz = (z + d) % depth
            at = at_rows(zz * rb, rb)
            y_out[m][at, :] = product(zz, 1 - y).astype(LOW)
            gy[m].append(send(y_out[m].at[at, :], y_in[m].at[at, :], yn))

    def y_grad_add(m, product, steps=(*range(1, depth), 0)):
        rb, cb = block_shape[m]
        gz.setdefault(m, [])
        for d in steps:
            zz = (z + d) % depth
            at = at_rows(zz * rb, rb)
            own = product(zz, y)
            received(gy[m][(d - 1) % depth], y_in[m].at[at, :])
            y_in[m][at, :] = (own + y_in[m][at, :].astype(F32)).astype(LOW)
            if d:
                gz[m].append(send(y_in[m].at[at, :], z_in[m].at[d - 1], zs[d]))

    def z_grad_add(m):
        rb, cb = block_shape[m]
        for d in range(1, depth):
            received(gz[m][d - 1], z_in[m].at[d - 1])

        def add(r):
            at = at_rows(z * rb + r, 64)
            v = y_in[m][at, :].astype(F32)
            for d in range(1, depth):
                v = v + z_in[m][d - 1, pl.ds(r, 64), :].astype(F32)
            y_in[m][at, :] = v.astype(LOW)

        row_loop(rb, 64, add)
        gf[m] = []
        if m in (MERGE, DOWN):
            land = f_in[m].at[at_rows(x * rb, rb), :]

            def part(px):
                return y_in[m].at[at_rows(z * rb, rb), at_rows(px * (cb // 2), cb // 2, 128)]

            gf[m].append((send(part(1 - x), land, xn), f_in[m].at[at_rows((1 - x) * rb, rb), :]))
            gf[m].append((local(part(x), land), None))
            return
        half = rb // 2

        def land_at(pc, px):
            if m == MIX:
                return f_in[m].at[pc * 2 + px]
            wide = f_in[m].shape[1] // 4
            return f_in[m].at[:, at_rows((pc * 2 + px) * wide, wide, 128)]

        def part(pc, px):
            if m == MIX:
                return y_in[m].at[at_rows(z * rb + pc * half, half), at_rows(px * 256, 384, 128)]
            return y_in[m].at[at_rows(z * rb + pc * half, half), at_rows(px * (cb // 2), cb // 2, 128)]

        for peer, pc, px in mates:
            gf[m].append((send(part(pc, px), land_at(c, x), peer), land_at(pc, px)))
        gf[m].append((local(part(c, x), land_at(c, x)), None))

    def grad_out(m):
        for handle, landed in gf[m]:
            if landed is None:
                handle.wait()
            else:
                received(handle, landed)
        if m != MIX:
            return
        out, src = ref.g_mix, f_in[MIX]
        first, last = (fs == 0).astype(F32), (fs == 3).astype(F32)
        mid = 1.0 - first - last
        first, last, mid = (jnp.broadcast_to(v, (1, 128)) for v in (first, last, mid))

        def write(r):
            at = pl.ds(r, 16)

            def get(p, t):
                return src[p, at, t * 128 : (t + 1) * 128].astype(F32)

            turned = []
            for tile in range(9):
                v = first * (get(tile // 2, tile % 2) if tile < 8 else src[q, at, 256:384].astype(F32))
                if tile == 0:
                    v = v + (mid + last) * get(3, 0)
                else:
                    v = v + mid * get((tile - 1) % 4, 1 + (tile - 1) // 4)
                    v = v + last * get((tile - 1) // 2, 1 + (tile - 1) % 2)
                turned.append(pltpu.roll(v, (128 - shift) % 128, 1))
            for tile in range(9):
                v = turned[tile]
                if tile < 8:
                    v = jnp.where(lane < 128 - shift, v, turned[tile + 1])
                wide = min(128, out.shape[1] - tile * 128)
                out[at, tile * 128 : tile * 128 + wide] = v[:, :wide].astype(LOW)

        row_loop(out.shape[0], 16, write)

    h_small = small_start()
    swap_start(VALUE)
    mix_align()
    h_small = small_relay(h_small)
    swap_start(MIX)
    swap_start(MERGE)
    swap_finish(VALUE)
    y_own(VALUE)
    z_start(VALUE)

    nl, ml, n2, gc, gm = (ref.nl, ref.ml, ref.n2, ref.gc, ref.gm)
    by_time, out_time, back_time = ref.by_time, ref.out_time, ref.back_time

    def centre(v):
        cen = v - jnp.mean(v, axis=-1, keepdims=True)
        return cen, lax.rsqrt(jnp.mean(cen * cen, axis=-1, keepdims=True) + 1e-05)

    def norm_one(r):
        cen, rate = centre(tok[pl.ds(r, 16), :].astype(F32))
        v = cen * rate * gains[0:1, :]
        nl[at_rows(q * rows + r, 16), :] = v.astype(LOW)
        for s in range(tiles):
            by_time[pl.ds(r * tiles + s, 16, stride=tiles), :] = v[:, s * 128 : (s + 1) * 128]

    small_finish(h_small)
    row_loop(rows, 16, norm_one)
    h_nl = gather_start(nl)
    swap_start(UP)
    swap_finish(MIX)
    y_own(MIX)
    z_start(MIX)
    swap_finish(MERGE)
    y_own(MERGE)
    z_start(MERGE)

    def cot_low(r):
        at = pl.ds(r, 32)
        gc[at_rows(q * rows + r, 32), :] = (cot[at, :].astype(F32) * live_rows(r, 32)).astype(LOW)

    def load_ema():
        return ema_in[...].reshape(4, -1, tiles, 128)

    _, _, rate_all, weight_all = ema_coefficients(load_ema())
    omega = omega_in[...]
    marks = ref.marks

    def at_time(t):
        return at_rows(t * tiles, tiles, 8)

    def ema_chunk(k, state):
        state = state * kept(k)
        marks[k] = state

        def step(i, state):
            t = k * CHUNK + i
            v = by_time[at_time(t), :]
            state = rate_all * state + v[None]
            out_time[at_time(t), :] = jnp.sum(weight_all * state, axis=0) + omega * v
            return state

        return lax.fori_loop(0, CHUNK, step, state, unroll=4)

    lax.fori_loop(0, rows // CHUNK, ema_chunk, jnp.zeros_like(rate_all))

    def mixed(r):
        for s in range(tiles):
            at = pl.ds(r * tiles + s, 16, stride=tiles)
            v = out_time[at, :]
            gate = jax.nn.sigmoid(v)
            ml[at_rows(q * rows + r, 16), s * 128 : (s + 1) * 128] = (v * gate).astype(LOW)
            out_time[at, :] = slope_of(v, gate)

    row_loop(rows, 16, mixed)
    h_ml = gather_start(ml)
    swap_start(DOWN)
    swap_finish(UP)
    z_start(UP)
    row_loop(rows, 32, cot_low)
    y_forward(VALUE)
    y_own(UP)
    gather_relay(nl, h_nl)
    h_gc = gather_start(gc)
    swap_finish(DOWN)
    z_start(DOWN)
    gather_finish(nl, h_nl)
    y_finish(VALUE)

    value_low, value_slope = ref.value_low, ref.value_slope
    vq = value_low.shape[1]

    def value_block(r):
        total[:, :vq] = mm(nl[pl.ds(r, rows), :], weights[VALUE][...])

        def act(s):
            v = total[pl.ds(s, 32), :vq]
            gate = jax.nn.sigmoid(v)
            value_low[at_rows(r + s, 32), :] = (v * gate).astype(LOW)
            value_slope[at_rows(r + s, 32), :] = slope_of(v, gate).astype(LOW)

        row_loop(rows, 32, act)

    row_loop(4 * rows, rows, value_block)
    gather_relay(ml, h_ml)
    y_forward(MIX)
    y_own(DOWN)
    gather_finish(ml, h_ml)
    gather_relay(gc, h_gc)
    y_finish(MIX)

    w_mix, reset_w = weights[MIX], ref.reset_w
    half_mix = w_mix.shape[1] // 2

    def fix_reset(r):
        at = pl.ds(r, 64)
        reset_w[at, 0:128] = w_mix[at, 384:512]
        reset_w[at, 128:256] = (w_mix[at, 512:640].astype(F32) + w_mix[at, half_mix : half_mix + 128].astype(F32)).astype(LOW)

    row_loop(width, 64, fix_reset)

    def w_update():
        return w_mix[:, 0:256]

    def w_shared():
        return w_mix[:, 256:384]

    def w_late():
        return w_mix[:, half_mix + 128 : half_mix + 384]

    def w_hidden():
        return w_mix[:, half_mix + 384 : half_mix + 640]

    scale = float(STRETCH) ** -0.5
    stretch = STRETCH
    shared_pre, query, key, probs = ref.shared_pre, ref.query, ref.key, ref.probs
    probs_low = ref.probs_low
    shared_pre[...] = mm(ml[group_rows(c, x), :], w_shared())
    sv = shared_pre[...]
    shared = sv * jax.nn.sigmoid(sv)
    query[...] = (shared * attn[0:1, :] + attn[1:2, :]).astype(LOW)
    key[...] = (shared * attn[2:3, :]).astype(LOW)
    bias = pltpu.roll(jnp.broadcast_to(attn[3:4, :], (stretch, stretch)), 0, 1, stride=1, stride_axis=0).T
    row_id = lax.broadcasted_iota(jnp.int32, (stretch, stretch), 0)
    col_id = lax.broadcasted_iota(jnp.int32, (stretch, stretch), 1)
    for n in range(rows // stretch):
        at = pl.ds(n * stretch, stretch)
        scores = mm_nt(query[at, :], key[at, :]) * scale + bias
        scores = jnp.where(row_id >= col_id, scores, -1000000000.0)
        ex = jnp.exp(scores - jnp.max(scores, axis=-1, keepdims=True))
        pr = ex / jnp.sum(ex, axis=-1, keepdims=True)
        probs[at, :] = pr
        probs_low[at_rows(q * rows + n * stretch, stretch), :] = pr.astype(LOW)
    own_probs = probs_low.at[group_rows(c, x), :]
    h_probs = [send(own_probs, own_probs, peer) for peer, _, _ in mates]

    mix_pack, update_in = ref.mix_pack, ref.update_in
    hidden_at = pl.ds(mix_pack.shape[1] - 256, 256)
    update_out = mix_pack.at[:, hidden_at]

    def update_block(r):
        update_out[pl.ds(r, rows), :] = mm(ml[pl.ds(r, rows), :], w_update()).astype(LOW)

    row_loop(4 * rows, rows, update_block)
    part_w = width // 4
    own_cols = at_rows(q * part_w, part_w, 128)
    h_update = [
        send(update_out.at[group_rows(pc, px), :], update_in.at[:, own_cols], peer) for peer, pc, px in mates
    ]
    update_in[:, own_cols] = update_out[group_rows(c, x), :]

    reset_gate, reset_slope = ref.reset_gate, ref.reset_slope

    def reset_block(r):
        at = pl.ds(r, rows)
        total[:, 0:256] = mm(ml[at, :], reset_w[...])
        total[:, 256:512] = mm(ml[at, :], w_late())

        def act(s):
            v = total[pl.ds(s, 32), :vq]
            gate = jax.nn.sigmoid(v)
            reset_gate[at_rows(r + s, 32), :] = (v * gate).astype(LOW)
            reset_slope[at_rows(r + s, 32), :] = slope_of(v, gate).astype(LOW)

        row_loop(rows, 32, act)

    row_loop(4 * rows, rows, reset_block)
    y_forward(MERGE)
    for handle, (_, pc, px) in zip(h_probs, mates):
        received(handle, probs_low.at[group_rows(pc, px), :])

    gated = ref.gated

    def attend(r):
        at = pl.ds(r, stretch)
        total[0:stretch, :vq] = mm(probs_low[at, :], value_low[at, :])

        def act(s):
            v = total[pl.ds(s, 32), :vq]
            to = at_rows(r + s, 32)
            gated[to, :] = (v * reset_gate[to, :].astype(F32)).astype(LOW)
            reset_slope[to, :] = (v * reset_slope[to, :].astype(F32)).astype(LOW)

        row_loop(stretch, 32, act)

    row_loop(4 * rows, stretch, attend)
    y_forward(UP, (1,))
    y_finish(MERGE)

    def merge_partial(c, x):
        at = group_rows(c, x)
        total[...] = mm(gated[at, :], weights[MERGE][...])
        total[:, own_cols] += mm(ml[at, :], w_hidden())

    h_red = reduce_early(merge_partial, sibs_a, cross_a)
    for handle, (_, pc, px) in zip(h_update, mates):
        received(handle, update_in.at[:, at_rows((pc * 2 + px) * part_w, part_w, 128)])
    gather_finish(gc, h_gc)
    y_forward(UP, (2, 3))
    reduce_late(merge_partial, sibs_a, cross_a, h_red)

    after, hidden_mul, update_mul = ref.after, ref.hidden_mul, ref.update_mul

    def norm_two(r):
        at = pl.ds(r, 16)
        v = reduced(r, 16, sibs_a, cross_a)
        gate = jax.nn.sigmoid(v)
        hidden = v * gate
        u = jax.nn.sigmoid(update_in[at, :].astype(F32))
        xv = tok[at, :].astype(F32)
        av = u * hidden + (1.0 - u) * xv
        after[at, :] = av
        hidden_mul[at, :] = (u * slope_of(v, gate)).astype(LOW)
        update_mul[at, :] = ((hidden - xv) * u * (1.0 - u)).astype(LOW)
        cen, rate = centre(av)
        n2[at_rows(q * rows + r, 16), :] = (cen * rate * gains[1:2, :]).astype(LOW)

    row_loop(rows, 16, norm_two)
    h_n2 = gather_start(n2)
    y_forward(DOWN, (1,))
    gather_relay(n2, h_n2)
    y_forward(DOWN, (2,))
    gather_finish(n2, h_n2)
    y_forward(DOWN, (3,))
    y_finish(UP)

    up_low, up_slope = ref.up_low, ref.up_slope

    def up_block(r):
        total[...] = mm(n2[pl.ds(r, rows), :], weights[UP][...])

        def act(s):
            v = total[pl.ds(s, 16), :]
            gate = jax.nn.sigmoid(v)
            up_low[at_rows(r + s, 16), :] = (v * gate).astype(LOW)
            up_slope[at_rows(r + s, 16), :] = slope_of(v, gate).astype(LOW)

        row_loop(rows, 16, act)

    row_loop(4 * rows, rows, up_block)

    def cols_of(m, yy):
        cb = block_shape[m][1]
        return at_rows(yy * cb, cb, 128)

    def rows_of(m, zz):
        rb = block_shape[m][0]
        return at_rows(zz * rb, rb, 128)

    def down_product(zz, yy):
        return mm_tn(up_low[:, rows_of(DOWN, zz)], gc[:, cols_of(DOWN, yy)])

    y_grad_send(DOWN, down_product)
    y_finish(DOWN)

    def up_back(r):
        at = pl.ds(r, rows)
        total[...] = mm_nt(gc[at, :], weights[DOWN][...])

        def act(s):
            to = at_rows(r + s, 16)
            up_slope[to, :] = (total[pl.ds(s, 16), :] * up_slope[to, :].astype(F32)).astype(LOW)

        row_loop(rows, 16, act)

    row_loop(4 * rows, rows, up_back)
    grad_up = up_slope

    def two_partial(c, x):
        total[...] = mm_nt(grad_up[group_rows(c, x), :], weights[UP][...])

    def down_partial(c, x):
        total[...] = mm(up_low[group_rows(c, x), :], weights[DOWN][...])

    def up_product(zz, yy):
        return mm_tn(n2[:, rows_of(UP, zz)], grad_up[:, cols_of(UP, yy)])

    h_red = reduce_early(two_partial, sibs_a, cross_a)
    y_grad_send(UP, up_product)
    y_grad_add(DOWN, down_product)
    reduce_late(two_partial, sibs_a, cross_a, h_red)

    gain_sum, update_back = ref.gain_sum, hidden_mul
    gain_sum[...] = jnp.zeros_like(gain_sum)

    def norm_two_back(r):
        at = pl.ds(r, 16)
        g = reduced(r, 16, sibs_a, cross_a)
        cen, rate = centre(after[at, :])
        unit = cen * rate
        gain_sum[1] += g * unit
        g = g * gains[1:2, :]
        back = rate * (g - jnp.mean(g, axis=-1, keepdims=True) - unit * jnp.mean(g * unit, axis=-1, keepdims=True))
        back = back + cot[at, :].astype(F32) * live_rows(r, 16)
        gm[at_rows(q * rows + r, 16), :] = (back * hidden_mul[at, :].astype(F32)).astype(LOW)
        hidden_mul[at, :] = (back * update_mul[at, :].astype(F32)).astype(LOW)
        u = jax.nn.sigmoid(update_in[at, :].astype(F32))
        update_mul[at, :] = (back * (1.0 - u)).astype(LOW)

    row_loop(rows, 16, norm_two_back)
    h_gm = gather_start(gm)
    for handle in h_update:
        sent(handle)
    update_grad = mix_pack.at[:, 0:256]
    own_rows = group_rows(c, x)
    h_update = [
        send(update_back.at[:, at_rows((pc * 2 + px) * part_w, part_w, 128)], update_grad.at[own_rows, :], peer)
        for peer, pc, px in mates
    ]
    update_grad[own_rows, :] = update_back[:, own_cols]

    h_red = reduce_early(down_partial, sibs_b, cross_b)
    y_grad_add(UP, up_product, (1, 2))
    gather_relay(gm, h_gm)
    y_grad_add(UP, up_product, (3,))
    gather_finish(gm, h_gm)

    def merge_product(zz, yy):
        return mm_tn(gated[:, rows_of(MERGE, zz)], gm[:, cols_of(MERGE, yy)])

    for handle in z_sends[UP][1:] + y_sends[UP] + h_gc:
        sent(handle)
    y_grad_send(MERGE, merge_product)

    grad_probs, probs_in = ref.grad_probs, ref.probs_in

    def gated_back(r):
        at = pl.ds(r, rows)
        total[:, :vq] = mm_nt(gm[at, :], weights[MERGE][...])

        def act(s):
            to = at_rows(r + s, 32)
            g = total[pl.ds(s, 32), :vq]
            back = (g * reset_slope[to, :].astype(F32)).astype(LOW)
            mix_pack[to, 384:640] = back[:, 0:256]
            mix_pack[to, 640:768] = back[:, 128:256]
            mix_pack[to, 768:1024] = back[:, 256:512]
            mix_pack[to, hidden_at] = gm[to, own_cols]
            reset_gate[to, :] = (g * reset_gate[to, :].astype(F32)).astype(LOW)

        row_loop(rows, 32, act)

    row_loop(4 * rows, rows, gated_back)
    grad_att = reset_gate

    def probs_back(r):
        at = pl.ds(r, stretch)
        grad_probs[at, :] = mm_nt(grad_att[at, :], value_low[at, :])

    row_loop(4 * rows, stretch, probs_back)
    h_probs = [
        send(grad_probs.at[group_rows(pc, px), :], probs_in.at[i], peer) for i, (peer, pc, px) in enumerate(mates)
    ]
    for handle, (_, pc, px) in zip(h_update, mates):
        received(handle, update_grad.at[group_rows(pc, px), :])

    shared_grad = mix_pack.at[:, 256:384]

    def mixed_partial(cc, xx):
        at = group_rows(cc, xx)
        total[...] = (
            mm_nt(update_grad[at, :], w_update())
            + mm_nt(mix_pack[at, 384:640], reset_w[...])
            + mm_nt(mix_pack[at, 768:1024], w_late())
            + mm_nt(mix_pack[at, hidden_at], w_hidden())
        )

    y_grad_add(UP, up_product, (0,))
    h_mixed = reduce_early(mixed_partial, sibs_a, cross_a)
    z_grad_add(DOWN)

    def value_back(r):
        at = pl.ds(r, stretch)
        total[0:stretch, :vq] = mm_tn(probs_low[at, :], grad_att[at, :])

        def act(s):
            to = at_rows(r + s, 32)
            value_slope[to, :] = (total[pl.ds(s, 32), :vq] * value_slope[to, :].astype(F32)).astype(LOW)

        row_loop(stretch, 32, act)

    row_loop(4 * rows, stretch, value_back)
    grad_value = value_slope

    def value_product(zz, yy):
        return mm_tn(nl[:, rows_of(VALUE, zz)], grad_value[:, cols_of(VALUE, yy)])

    y_grad_send(VALUE, value_product)
    y_grad_add(MERGE, merge_product, (1,))
    reduce_late(down_partial, sibs_b, cross_b, h_red)

    def finish(r):
        at = pl.ds(r, 16)
        ref.result[at, :] = (after[at, :] + reduced(r, 16, sibs_b, cross_b)).astype(LOW)

    row_loop(rows, 16, finish)

    for i, handle in enumerate(h_probs):
        received(handle, probs_in.at[i])
    anti = (row_id + col_id == stretch - 1).astype(LOW)
    lag_sum = jnp.zeros((1, stretch), F32)
    grads_q = jnp.zeros((1, stretch), F32)
    grads_o = jnp.zeros((1, stretch), F32)
    grads_k = jnp.zeros((1, stretch), F32)
    for n in range(rows // stretch):
        at = pl.ds(n * stretch, stretch)
        to = at_rows(q * rows + n * stretch, stretch)
        g = grad_probs[to, :] + probs_in[0, at, :] + probs_in[1, at, :] + probs_in[2, at, :]
        pr = probs[at, :]
        gs = (pr * (g - jnp.sum(pr * g, axis=-1, keepdims=True))).astype(LOW)
        gq = mm(gs, key[at, :]) * scale
        gk = mm_tn(gs, query[at, :]) * scale
        lags = pltpu.roll(mm_nt(anti, gs), 1, 1, stride=1, stride_axis=0)
        lag_sum += jnp.sum(lags, axis=0, keepdims=True)
        sv = shared_pre[at, :]
        gate = jax.nn.sigmoid(sv)
        sh = sv * gate
        grads_q += jnp.sum(gq * sh, axis=0, keepdims=True)
        grads_o += jnp.sum(gq, axis=0, keepdims=True)
        grads_k += jnp.sum(gk * sh, axis=0, keepdims=True)
        gsh = gq * attn[0:1, :] + gk * attn[2:3, :]
        shared_grad[to, :] = (gsh * slope_of(sv, gate)).astype(LOW)
    attn_rows = (grads_q, grads_o, grads_k, lag_sum)
    own_shared = shared_grad.at[own_rows, :]
    h_shared = [send(own_shared, own_shared, peer) for peer, _, _ in mates]

    y_grad_add(MERGE, merge_product, (2, 3, 0))
    for handle, (_, pc, px) in zip(h_shared, mates):
        received(handle, shared_grad.at[group_rows(pc, px), :])

    def mix_product(zz, yy):
        return mm_tn(ml[:, rows_of(MIX, zz)], mix_pack[:, cols_of(MIX, yy)])

    y_grad_send(MIX, mix_product)

    def mixed_own(cc, xx):
        mixed_partial(cc, xx)
        total[...] += mm_nt(shared_grad[own_rows, :], w_shared())

    reduce_late(mixed_own, sibs_a, cross_a, h_mixed)

    def to_time(r):
        v = reduced(r, 16, sibs_a, cross_a)
        for s in range(tiles):
            at = pl.ds(r * tiles + s, 16, stride=tiles)
            out_time[at, :] = out_time[at, :] * v[:, s * 128 : (s + 1) * 128]

    row_loop(rows, 16, to_time)

    def value_partial(cc, xx):
        total[...] = mm_nt(grad_value[group_rows(cc, xx), :], weights[VALUE][...])

    h_red = reduce_early(value_partial, sibs_b, cross_b)
    y_grad_add(VALUE, value_product)
    z_grad_add(UP)

    held = ref.held
    ema = load_ema()
    damping, decay_gate, rate_all, weight_all = ema_coefficients(ema)
    omega = omega_in[...]
    half = rate_all.shape[0] // 2
    chunks = rows // CHUNK
    sums = []
    for part in range(2):
        js = slice(part * half, (part + 1) * half)
        rate, weight = rate_all[js], weight_all[js]

        def chunk(m, carry, js=js, rate=rate, weight=weight, part=part):
            k = chunks - 1 - m
            held[0] = marks[k, js]

            def ahead(i, state):
                state = rate * state + by_time[at_time(k * CHUNK + i), :][None]
                held[i + 1] = state
                return state

            lax.fori_loop(0, CHUNK, ahead, held[0], unroll=4)

            def back(n, carry):
                s, dw, dr, dom = carry
                i = CHUNK - 1 - n
                t = at_time(k * CHUNK + i)
                g = out_time[t, :]
                s = rate * s + g[None]
                dx = jnp.sum(weight * s, axis=0)
                if part == 0:
                    back_time[t, :] = dx + omega * g
                    dom = dom + g * by_time[t, :]
                else:
                    back_time[t, :] = back_time[t, :] + dx
                return s, dw + held[i + 1] * g[None], dr + held[i] * s, dom

            s, dw, dr, dom = lax.fori_loop(0, CHUNK, back, carry, unroll=2)
            return s * kept(k), dw, dr, dom

        zero = jnp.zeros_like(rate)
        sums.append(lax.fori_loop(0, chunks, chunk, (zero, zero, zero, jnp.zeros_like(omega))))
    small = ref.small_by_time
    rate_scale = ema.shape[1] ** (-0.5)
    for part in range(2):
        js = slice(part * half, (part + 1) * half)
        dw, dr = sums[part][1], sums[part][2] * weight_all[js]
        d_damp = dw * ema[2, js] * ema[3, js] * rate_scale - dr * decay_gate[js]
        parts = (
            d_damp * damping[js] * (1.0 - damping[js]),
            -dr * damping[js] * decay_gate[js] * (1.0 - decay_gate[js]),
            dw * damping[js] * ema[3, js] * rate_scale,
            dw * damping[js] * ema[2, js] * rate_scale,
        )
        for p in range(4):
            for j in range(half):
                small[pl.ds((p * 2 * half + part * half + j) * tiles, tiles), :] = parts[p][j]

    y_grad_add(MIX, mix_product, (1,))
    reduce_late(value_partial, sibs_b, cross_b, h_red)

    def norm_one_back(r):
        at = pl.ds(r, 16)
        ema_part = jnp.concatenate(
            [back_time[pl.ds(r * tiles + s, 16, stride=tiles), :] for s in range(tiles)], axis=1
        )
        g = reduced(r, 16, sibs_b, cross_b) + ema_part
        cen, rate = centre(tok[at, :].astype(F32))
        unit = cen * rate
        gain_sum[0] += g * unit
        g = g * gains[0:1, :]
        back = rate * (g - jnp.mean(g, axis=-1, keepdims=True) - unit * jnp.mean(g * unit, axis=-1, keepdims=True))
        ref.grad_tokens[at, :] = (back + update_mul[at, :].astype(F32)).astype(LOW)

    row_loop(rows, 16, norm_one_back)
    y_grad_add(MIX, mix_product, (2,))

    tile_rows = ref.tile_rows
    states = 4 * ema.shape[1]
    gain_one = jnp.sum(gain_sum[0], axis=0, keepdims=True)
    gain_two = jnp.sum(gain_sum[1], axis=0, keepdims=True)
    for t in range(tiles):
        at = (t % 2) * depth + t // 2
        tile_rows[at, 0:states, :] = small[pl.ds(t, states, stride=tiles), :]
        tail = jnp.concatenate(
            [
                gain_one[:, t * 128 : (t + 1) * 128],
                gain_two[:, t * 128 : (t + 1) * 128],
                sums[0][3][t : t + 1],
                attn_rows[t // 2],
                jnp.zeros((4, 128), F32),
            ],
            axis=0,
        )
        tile_rows[at, states : states + 8, :] = tail
    sib_in, z_small, x_small, y_small = ref.sib_in, ref.z_small, ref.x_small, ref.y_small
    h_sib = send(tile_rows.at[pl.ds((1 - c) * depth, depth)], sib_in, sib)
    y_grad_add(MIX, mix_product, (3, 0))
    z_grad_add(MERGE)
    received(h_sib, sib_in)
    sib_in[...] += tile_rows[pl.ds(c * depth, depth)]
    h_zs = [send(sib_in.at[(z + d) % depth], z_small.at[d - 1], zs[d]) for d in range(1, depth)]
    z_grad_add(VALUE)
    for d, handle in enumerate(h_zs):
        received(handle, z_small.at[d])
    x_small[0] = sib_in[z] + z_small[0] + z_small[1] + z_small[2]
    h_x = send(x_small.at[0], x_small.at[1], xn)
    z_grad_add(MIX)
    received(h_x, x_small.at[1])
    y_small[0] = x_small[0] + x_small[1]
    h_y = send(y_small.at[0], y_small.at[1], yn)
    for m in (DOWN, UP, MERGE, VALUE, MIX):
        grad_out(m)
    received(h_y, y_small.at[1])
    totals = y_small[0] + y_small[1]
    states = 4 * ema.shape[1]
    ref.small_out[...] = pltpu.roll(totals, (128 - shift) % 128, 1)
    ref.attn_out[...] = pltpu.roll(totals[states : states + 8], (128 - c * 64 - fs * 16) % 128, 1)
    for handle in pending:
        sent(handle)


def pack_small(norm_gains, ema_params, attn_params):
    states, mine = ema_params.shape[2], ema_params.shape[1]
    last = jnp.pad(attn_params, (0, mine - attn_params.shape[0]))
    rows = [
        jnp.transpose(ema_params, (2, 0, 1)).reshape(states, 4 * mine),
        jnp.concatenate([norm_gains.reshape(-1), last])[None],
        jnp.zeros((32 - states - 1, 4 * mine), LOW),
    ]
    return jnp.concatenate(rows, axis=0)


def finish_kernel(result, grad_tokens, value, mix, merge, up, down, small, attn, *outs):
    for src, out in zip((result, grad_tokens, value, mix, merge, up, down), outs):

        def widen(r, src=src, out=out):
            out[pl.ds(r, 32), :] = src[pl.ds(r, 32), :].astype(out.dtype)

        row_loop(out.shape[0], 32, widen)
    gains, ema, per = outs[7:]
    mine, states = ema.shape[1:]
    gains[...] = small[4 * states : 4 * states + 3, :mine]
    turned = small[0 : 4 * states, :].T
    for p in range(4):
        ema[p] = turned[:mine, p * states : (p + 1) * states]
    per[...] = attn[3:4, : per.shape[1]]


def layer_on_device(depth, tokens, cotangent, lengths, value_proj, mix_proj, merge_proj, up_proj, down_proj, norm_gains, ema_params, attn_params):
    rows, width = tokens.shape
    fs = lax.axis_index(FS)
    window = -(-mix_proj.shape[1] // 128) * 128
    group = 4 * rows
    vq = value_proj.shape[1]
    fq = up_proj.shape[1]
    quarters = ((width, vq), (width, 10 * STRIP), (vq, width), (width, fq), (fq, width))
    tiles = width // 128
    states = ema_params.shape[2]
    small_rows = 4 * states + 8
    shape = jax.ShapeDtypeStruct
    shards = (value_proj, mix_proj, merge_proj, up_proj, down_proj)
    inputs = dict(
        tok=tokens,
        cot=cotangent,
        lens=lengths,
        packed=pack_small(norm_gains, ema_params, attn_params),
        s=shards,
    )
    landings = [w.shape for w in shards]
    landings[MIX] = (4, mix_proj.shape[0], 3 * STRIP)
    outputs = dict(
        result=shape((rows, width), LOW),
        grad_tokens=shape((rows, width), LOW),
        fi=tuple(shape(d, LOW) for d in landings),
        g_mix=shape(mix_proj.shape, LOW),
        small_out=shape((small_rows, 128), F32),
        attn_out=shape((8, 128), F32),
    )
    copies = pltpu.SemaphoreType.DMA((200,))

    def low(*dims):
        return pltpu.VMEM(dims, LOW)

    def full(*dims):
        return pltpu.VMEM(dims, F32)

    scratch = dict(
        send_sems=copies,
        recv_sems=copies,
        local_sems=pltpu.SemaphoreType.DMA((24,)),
        w=tuple(low(*d) for d in quarters),
        yo=tuple(low(quarters[m][0], quarters[m][1] // 2) for m in (UP, DOWN)),
        yi=tuple(low(r, k // 2) for r, k in quarters),
        zi=tuple(low(depth - 1, r // depth, k // 2) for r, k in quarters),
        mix_win=low(mix_proj.shape[0], window),
        small_all=low(8 * depth, 32, 128),
        ema_in=full(4 * states * tiles, 128),
        omega_in=full(tiles, 128),
        gains=full(8, width),
        attn=full(8, 128),
        nl=low(group, width),
        ml=low(group, width),
        n2=low(group, width),
        gc=low(group, width),
        gm=low(group, width),
        mix_in=low(2, 2 * mix_proj.shape[0], 3 * STRIP),
        reset_w=low(width, 256),
        value_low=low(group, vq),
        value_slope=low(group, vq),
        reset_gate=low(group, vq),
        reset_slope=low(group, vq),
        gated=low(group, vq),
        up_low=low(group, fq),
        up_slope=low(group, fq),
        update_in=low(rows, width),
        probs_low=low(group, STRETCH),
        probs=full(rows, STRETCH),
        shared_pre=full(rows, Z),
        query=low(rows, Z),
        key=low(rows, Z),
        grad_probs=full(group, STRETCH),
        probs_in=full(3, rows, STRETCH),
        mix_pack=low(group, 10 * STRIP),
        by_time=full(rows * tiles, 128),
        out_time=full(rows * tiles, 128),
        back_time=full(rows * tiles, 128),
        marks=full(rows // CHUNK, states, tiles, 128),
        held=full(CHUNK + 1, states // 2, tiles, 128),
        total=full(rows, width),
        stage=low(3, rows, width),
        sibs_a=low(2, rows, width),
        sibs_b=low(2, rows, width),
        cross_a=low(rows, width),
        cross_b=low(rows, width),
        after=full(rows, width),
        hidden_mul=low(rows, width),
        update_mul=low(rows, width),
        gain_sum=full(2, 16, width),
        small_by_time=full(4 * states * tiles, 128),
        tile_rows=full(tiles, small_rows, 128),
        sib_in=full(depth, small_rows, 128),
        z_small=full(depth - 1, small_rows, 128),
        x_small=full(2, small_rows, 128),
        y_small=full(2, small_rows, 128),
    )
    in_vmem = pl.BlockSpec(memory_space=pltpu.VMEM)
    specs = jax.tree.map(lambda _: in_vmem, inputs)
    anywhere = pl.BlockSpec(memory_space=pl.ANY)
    specs.update(
        lens=pl.BlockSpec(memory_space=pltpu.SMEM), s=tuple(in_vmem if m == MIX else anywhere for m in SHARDED)
    )
    in_leaves, in_tree = jax.tree.flatten(inputs)
    out_leaves, out_tree = jax.tree.flatten(outputs)
    scratch_leaves, scratch_tree = jax.tree.flatten(scratch, is_leaf=lambda v: not isinstance(v, (dict, tuple)))
    outs = pl.pallas_call(
        functools.partial(layer_kernel, (in_tree, out_tree, scratch_tree), depth),
        out_shape=tuple(out_leaves),
        in_specs=jax.tree.leaves(specs),
        out_specs=tuple(in_vmem for _ in out_leaves),
        scratch_shapes=scratch_leaves,
        compiler_params=pltpu.CompilerParams(collective_id=0, has_side_effects=True, vmem_limit_bytes=VMEM_BYTES),
        name="layer",
    )(*in_leaves)
    by = types.SimpleNamespace(**jax.tree.unflatten(out_tree, outs))
    grads = list(by.fi)
    grads[MIX] = by.g_mix
    wide = [shape(g.shape, F32) for g in (*grads, norm_gains, ema_params)]
    *finals, attn_grad = pl.pallas_call(
        finish_kernel,
        out_shape=(shape((rows, width), LOW), shape((rows, width), LOW), *wide, shape((1, attn_params.shape[0]), F32)),
        in_specs=[in_vmem] * 9,
        out_specs=(in_vmem,) * 10,
        compiler_params=pltpu.CompilerParams(vmem_limit_bytes=32 << 20),
        name="finish",
    )(by.result, by.grad_tokens, *grads, by.small_out, by.attn_out)
    return (*finals, attn_grad[0])


VMEM_BYTES = 64 << 20


def solution(mesh):
    in_specs = (
        P((DP, FS), None),
        P((DP, FS), None),
        P((DP, FS), None),
        P(DP, FS),
        P(DP, FS),
        P(DP, FS),
        P(DP, FS),
        P(DP, FS),
        P(None, (DP, FS)),
        P(None, (DP, FS), None),
        P((DP, FS)),
    )
    out_specs = (
        P((DP, FS), None),
        P((DP, FS), None),
        P(DP, FS),
        P(DP, FS),
        P(DP, FS),
        P(DP, FS),
        P(DP, FS),
        P(None, (DP, FS)),
        P(None, (DP, FS), None),
        P((DP, FS)),
    )
    fits = mesh.shape[DP] // 2 * 4 * STRIP == V and mesh.shape[FS] * 4 * STRIP == V
    body = functools.partial(layer_on_device, mesh.shape[DP] // 2) if fits else on_device
    return jax.shard_map(body, mesh=mesh, in_specs=in_specs, out_specs=out_specs, check_vma=False)
```

```python
import functools
import types

import jax
import jax.numpy as jnp
from jax import lax
from jax.experimental import pallas as pl
from jax.experimental.pallas import tpu as pltpu
from jax.sharding import PartitionSpec as P

D = 1024
Z = 128
V = 2048
STRETCH = 128


DP, FS = "dp", "fsdp"
highest = lax.Precision.HIGHEST


def layer_norm(values, gain):
    centred = values - jnp.mean(values, axis=-1, keepdims=True)
    spread_sq = jnp.mean(centred * centred, axis=-1, keepdims=True)
    return centred * lax.rsqrt(spread_sq + 1e-05) * gain


def token_layout(length_row, row_count):
    places = jnp.arange(row_count, dtype=jnp.int32)
    running = jnp.cumsum(length_row)
    before = (running[None, :] <= places[:, None]).astype(jnp.int32)
    starts = jnp.sum(before * length_row[None, :], axis=1)
    return (places - starts, places < running[-1])


def ema_coefficients(ema):
    damping = jax.nn.sigmoid(ema[0])
    decay_gate = jax.nn.sigmoid(ema[1])
    keep_rate = 1.0 - damping * decay_gate
    weights_out = damping * ema[2] * ema[3] * ema.shape[1] ** (-0.5)
    return damping, decay_gate, keep_rate, weights_out


CHUNK = 32


def ema_forward_kernel(x_ref, ema_ref, omega_ref, keep_ref, y_ref, mark_ref):
    _, _, rate, weight = ema_coefficients(ema_ref[...])
    omega = omega_ref[...]

    def chunk(k, state):
        state = state * keep_ref[k][None]
        mark_ref[k] = state

        def step(i, state):
            t = k * CHUNK + i
            x = x_ref[t]
            state = rate * state + x[None]
            y_ref[t] = jnp.sum(weight * state, axis=0) + omega * x
            return state

        return lax.fori_loop(0, CHUNK, step, state, unroll=4)

    lax.fori_loop(0, x_ref.shape[0] // CHUNK, chunk, jnp.zeros_like(rate))


def ema_backward_kernel(x_ref, g_ref, ema_ref, omega_ref, keep_ref, mark_ref, dx_ref, dema_ref, domega_ref, h_ref):
    ema = ema_ref[...]
    damping, decay_gate, rate_all, weight_all = ema_coefficients(ema)
    omega = omega_ref[...]
    half = rate_all.shape[0] // 2
    chunks = x_ref.shape[0] // CHUNK
    sums = []
    for part in range(2):
        js = slice(part * half, (part + 1) * half)
        rate, weight = rate_all[js], weight_all[js]
        zero = jnp.zeros_like(rate)

        def chunk(m, carry, js=js, rate=rate, weight=weight, part=part):
            k = chunks - 1 - m
            h_ref[0] = mark_ref[k, js]

            def ahead(i, state):
                state = rate * state + x_ref[k * CHUNK + i][None]
                h_ref[i + 1] = state
                return state

            lax.fori_loop(0, CHUNK, ahead, h_ref[0], unroll=4)

            def back(n, carry):
                s, dw, dr, dom = carry
                i = CHUNK - 1 - n
                t = k * CHUNK + i
                g = g_ref[t]
                s = rate * s + g[None]
                dx = jnp.sum(weight * s, axis=0)
                if part == 0:
                    dx_ref[t] = dx + omega * g
                    dom = dom + g * x_ref[t]
                else:
                    dx_ref[t] = dx_ref[t] + dx
                dw = dw + h_ref[i + 1] * g[None]
                dr = dr + h_ref[i] * s
                return s, dw, dr, dom

            s, dw, dr, dom = lax.fori_loop(0, CHUNK, back, carry, unroll=2)
            return s * keep_ref[k][None], dw, dr, dom

        out = lax.fori_loop(0, chunks, chunk, (zero, zero, zero, jnp.zeros_like(omega)))
        sums.append(out)
    dw = jnp.concatenate([sums[0][1], sums[1][1]], axis=0)
    dr = jnp.concatenate([sums[0][2], sums[1][2]], axis=0) * weight_all
    scale = ema.shape[1] ** (-0.5)
    d_damp = dw * ema[2] * ema[3] * scale - dr * decay_gate
    dema_ref[0] = d_damp * damping * (1.0 - damping)
    dema_ref[1] = -dr * damping * decay_gate * (1.0 - decay_gate)
    dema_ref[2] = dw * damping * ema[3] * scale
    dema_ref[3] = dw * damping * ema[2] * scale
    domega_ref[...] = sums[0][3]


def ema_keep(position):
    starts = position.reshape(-1, CHUNK)[:, 0] != 0
    return jnp.broadcast_to(starts.astype(jnp.float32)[:, None, None], (starts.shape[0], 8, 128))


def ema_apply(x, ema, omega, keep):
    f32 = jnp.float32
    shape = jax.ShapeDtypeStruct
    return pl.pallas_call(
        ema_forward_kernel,
        out_shape=(shape(x.shape, f32), shape((keep.shape[0],) + ema.shape[1:], f32)),
        compiler_params=pltpu.CompilerParams(vmem_limit_bytes=32 << 20),
    )(x, ema, omega, keep)


def ema_reverse(x, g, ema, omega, keep, mark):
    f32 = jnp.float32
    shape = jax.ShapeDtypeStruct
    return pl.pallas_call(
        ema_backward_kernel,
        out_shape=(shape(x.shape, f32), shape(ema.shape, f32), shape(omega.shape, f32)),
        scratch_shapes=[pltpu.VMEM((CHUNK + 1, ema.shape[1] // 2) + ema.shape[2:], f32)],
        compiler_params=pltpu.CompilerParams(vmem_limit_bytes=32 << 20),
    )(x, g, ema, omega, keep, mark)


def silu_slope(values):
    logistic = jax.nn.sigmoid(values)
    return logistic * (1.0 + values * (1.0 - logistic))


def relative_table(rel_bias):
    lag_grid = (
        jnp.arange(STRETCH, dtype=jnp.int32)[:, None]
        - jnp.arange(STRETCH, dtype=jnp.int32)[None, :]
    )
    one_hot = (lag_grid[:, :, None] == jnp.arange(STRETCH, dtype=jnp.int32)[None, None, :]).astype(
        jnp.float32
    )
    bias_grid = jnp.einsum("ijl,l->ij", one_hot, rel_bias, precision=highest)
    return (lag_grid, one_hot, bias_grid)


def gather_forward(value_proj, mix_proj, merge_proj, up_proj, down_proj):
    first = (
        lax.all_gather(value_proj, DP, axis=0, tiled=True),
        lax.all_gather(mix_proj, DP, axis=0, tiled=True),
        lax.all_gather(merge_proj, DP, axis=0, tiled=True),
        lax.all_gather(up_proj, DP, axis=0, tiled=True),
        lax.all_gather(down_proj, DP, axis=0, tiled=True),
    )
    return (
        lax.all_gather(first[0], FS, axis=1, tiled=True),
        lax.all_gather(first[1], FS, axis=1, tiled=True),
        lax.all_gather(first[2], FS, axis=1, tiled=True),
        lax.all_gather(first[3], FS, axis=1, tiled=True),
        lax.all_gather(first[4], FS, axis=1, tiled=True),
    )


def reduce_gradients(value_grad, mix_grad, merge_grad, up_grad, down_grad):
    first = (
        lax.psum_scatter(
            value_grad.astype(jnp.bfloat16), DP, scatter_dimension=0, tiled=True
        ).astype(jnp.float32),
        lax.psum_scatter(
            mix_grad.astype(jnp.bfloat16), DP, scatter_dimension=0, tiled=True
        ).astype(jnp.float32),
        lax.psum_scatter(
            merge_grad.astype(jnp.bfloat16), DP, scatter_dimension=0, tiled=True
        ).astype(jnp.float32),
        lax.psum_scatter(
            up_grad.astype(jnp.bfloat16), DP, scatter_dimension=0, tiled=True
        ).astype(jnp.float32),
        lax.psum_scatter(
            down_grad.astype(jnp.bfloat16), DP, scatter_dimension=0, tiled=True
        ).astype(jnp.float32),
    )
    return (
        lax.psum_scatter(
            first[0].astype(jnp.bfloat16), FS, scatter_dimension=1, tiled=True
        ).astype(jnp.float32),
        lax.psum_scatter(
            first[1].astype(jnp.bfloat16), FS, scatter_dimension=1, tiled=True
        ).astype(jnp.float32),
        lax.psum_scatter(
            first[2].astype(jnp.bfloat16), FS, scatter_dimension=1, tiled=True
        ).astype(jnp.float32),
        lax.psum_scatter(
            first[3].astype(jnp.bfloat16), FS, scatter_dimension=1, tiled=True
        ).astype(jnp.float32),
        lax.psum_scatter(
            first[4].astype(jnp.bfloat16), FS, scatter_dimension=1, tiled=True
        ).astype(jnp.float32),
    )


def on_device(
    tokens,
    cotangent,
    lengths,
    value_proj,
    mix_proj,
    merge_proj,
    up_proj,
    down_proj,
    norm_gains,
    ema_params,
    attn_params,
):
    gains_full, ema_full, attn_full = (
        lax.all_gather(norm_gains, (DP, FS), axis=1, tiled=True),
        lax.all_gather(ema_params, (DP, FS), axis=1, tiled=True),
        lax.all_gather(attn_params, (DP, FS), axis=0, tiled=True),
    )
    value_full, mix_full, merge_full, up_full, down_full = gather_forward(
        value_proj, mix_proj, merge_proj, up_proj, down_proj
    )
    gains_float = gains_full.astype(jnp.float32)
    ema_float = ema_full.astype(jnp.float32)
    attn_float = attn_full.astype(jnp.float32)
    row_count = tokens.shape[0]
    position, live_rows = token_layout(lengths[0], row_count)
    tokens_float = tokens.astype(jnp.float32)
    normed, norm_back = jax.vjp(layer_norm, tokens_float, gains_float[0])
    normed_low = normed.astype(jnp.bfloat16)
    value_pre = jnp.dot(normed_low, value_full, preferred_element_type=jnp.float32)
    value_low = jax.nn.silu(value_pre).astype(jnp.bfloat16)

    lanes = (8, tokens.shape[1] // 8)
    ema_by_state = jnp.swapaxes(ema_float, 1, 2).reshape(4, -1, *lanes)
    omega = gains_float[2].reshape(lanes)
    keep = ema_keep(position)
    normed_rows = normed.reshape(row_count, *lanes)
    ema_rows, ema_marks = ema_apply(normed_rows, ema_by_state, omega, keep)
    ema_out = ema_rows.reshape(row_count, -1)
    mixed_low = jax.nn.silu(ema_out).astype(jnp.bfloat16)
    projected = jnp.dot(mixed_low, mix_full, preferred_element_type=jnp.float32)
    update_gate = jax.nn.sigmoid(projected[:, :D])
    shared_pre = projected[:, D : D + Z]
    reset_pre = projected[:, D + Z : D + Z + V]
    hidden_x = projected[:, D + Z + V :]
    shared = jax.nn.silu(shared_pre)
    reset_gate = jax.nn.silu(reset_pre)
    query_low = (shared * attn_float[:Z] + attn_float[Z : 2 * Z]).astype(jnp.bfloat16)
    key_low = (shared * attn_float[2 * Z : 3 * Z]).astype(jnp.bfloat16)
    block_count = row_count // STRETCH
    lag_grid, one_hot, bias_grid = relative_table(attn_float[3 * Z :])
    query_blocks = query_low.reshape(block_count, STRETCH, Z)
    key_blocks = key_low.reshape(block_count, STRETCH, Z)
    value_blocks = value_low.reshape(block_count, STRETCH, V)
    score_scale = Z ** (-0.5)

    def block_scores():
        raw_scores = (
            jnp.einsum("nik,njk->nij", query_blocks, key_blocks, preferred_element_type=jnp.float32)
            * score_scale
            + bias_grid
        )
        return jnp.where(lag_grid >= 0, raw_scores, -1000000000.0)

    scores = block_scores()
    row_max = jnp.max(scores, axis=-1, keepdims=True)
    log_total = row_max + jnp.log(jnp.sum(jnp.exp(scores - row_max), axis=-1, keepdims=True))
    probs_low = jnp.exp(scores - log_total).astype(jnp.bfloat16)
    attended = jnp.einsum(
        "nij,njv->niv", probs_low, value_blocks, preferred_element_type=jnp.float32
    ).reshape(row_count, V)
    gated_low = (attended * reset_gate).astype(jnp.bfloat16)
    hidden_in = jnp.dot(gated_low, merge_full, preferred_element_type=jnp.float32) + hidden_x
    hidden = jax.nn.silu(hidden_in)
    after_mixer = update_gate * hidden + (1.0 - update_gate) * tokens_float
    normed_two, norm_two_back = jax.vjp(layer_norm, after_mixer, gains_float[1])
    normed_two_low = normed_two.astype(jnp.bfloat16)
    up_pre = jnp.dot(normed_two_low, up_full, preferred_element_type=jnp.float32)
    up_low = jax.nn.silu(up_pre).astype(jnp.bfloat16)
    result = (after_mixer + jnp.dot(up_low, down_full, preferred_element_type=jnp.float32)).astype(
        jnp.bfloat16
    )
    value_back, mix_back, merge_back, up_back, down_back = (
        value_full, mix_full, merge_full, up_full, down_full
    )
    grad_rows = cotangent.astype(jnp.float32) * live_rows[:, None].astype(jnp.float32)
    grad_down_low = grad_rows.astype(jnp.bfloat16)
    down_grad = jnp.einsum("tf,td->fd", up_low, grad_down_low, preferred_element_type=jnp.float32)
    grad_up_act = jnp.einsum(
        "td,fd->tf", grad_down_low, down_back, preferred_element_type=jnp.float32
    )
    grad_up_low = (grad_up_act * silu_slope(up_pre)).astype(jnp.bfloat16)
    up_grad = jnp.einsum(
        "td,tf->df", normed_two_low, grad_up_low, preferred_element_type=jnp.float32
    )
    grad_normed_two = jnp.einsum(
        "tf,df->td", grad_up_low, up_back, preferred_element_type=jnp.float32
    )
    grad_after_norm, gain_two_grad = norm_two_back(grad_normed_two)
    grad_after = grad_after_norm + grad_rows
    grad_hidden_in = grad_after * update_gate * silu_slope(hidden_in)
    grad_merge_low = grad_hidden_in.astype(jnp.bfloat16)
    merge_grad = jnp.einsum(
        "tv,td->vd", gated_low, grad_merge_low, preferred_element_type=jnp.float32
    )
    grad_gated = jnp.einsum(
        "td,vd->tv", grad_merge_low, merge_back, preferred_element_type=jnp.float32
    )
    grad_reset = grad_gated * attended
    grad_attended_low = (
        (grad_gated * reset_gate).astype(jnp.bfloat16).reshape(block_count, STRETCH, V)
    )
    grad_probs = jnp.einsum(
        "niv,njv->nij", grad_attended_low, value_blocks, preferred_element_type=jnp.float32
    )
    soft_probs = jnp.exp(block_scores() - log_total)
    grad_scores_low = (
        soft_probs * (grad_probs - jnp.sum(soft_probs * grad_probs, axis=-1, keepdims=True))
    ).astype(jnp.bfloat16)
    grad_query = (
        jnp.einsum(
            "nij,njk->nik", grad_scores_low, key_blocks, preferred_element_type=jnp.float32
        ).reshape(row_count, Z)
        * score_scale
    )
    grad_key = (
        jnp.einsum(
            "nij,nik->njk", grad_scores_low, query_blocks, preferred_element_type=jnp.float32
        ).reshape(row_count, Z)
        * score_scale
    )
    grad_value_act = jnp.einsum(
        "nij,niv->njv",
        soft_probs.astype(jnp.bfloat16),
        grad_attended_low,
        preferred_element_type=jnp.float32,
    ).reshape(row_count, V)
    rel_grad = jnp.einsum(
        "ij,ijl->l",
        jnp.sum(grad_scores_low.astype(jnp.float32), axis=0),
        one_hot,
        precision=highest,
    )
    attn_grad = jnp.concatenate(
        [
            jnp.sum(grad_query * shared, axis=0),
            jnp.sum(grad_query, axis=0),
            jnp.sum(grad_key * shared, axis=0),
            rel_grad,
        ]
    )
    grad_shared = grad_query * attn_float[:Z] + grad_key * attn_float[2 * Z : 3 * Z]
    grad_projected_low = jnp.concatenate(
        [
            grad_after * (hidden - tokens_float) * update_gate * (1.0 - update_gate),
            grad_shared * silu_slope(shared_pre),
            grad_reset * silu_slope(reset_pre),
            grad_hidden_in,
        ],
        axis=1,
    ).astype(jnp.bfloat16)
    mix_grad = jnp.einsum(
        "td,tm->dm", mixed_low, grad_projected_low, preferred_element_type=jnp.float32
    )
    grad_mixed = jnp.einsum(
        "tm,dm->td", grad_projected_low, mix_back, preferred_element_type=jnp.float32
    )
    grad_ema_rows = (grad_mixed * silu_slope(ema_out)).reshape(row_count, *lanes)
    grad_normed_rows, ema_grad_rows, omega_grad = ema_reverse(
        normed_rows, grad_ema_rows, ema_by_state, omega, keep, ema_marks
    )
    grad_normed_ema = grad_normed_rows.reshape(row_count, -1)
    ema_grad = jnp.swapaxes(ema_grad_rows.reshape(4, -1, tokens.shape[1]), 1, 2)
    omega_grad = omega_grad.reshape(-1)
    grad_value_low = (grad_value_act * silu_slope(value_pre)).astype(jnp.bfloat16)
    value_grad = jnp.einsum(
        "td,tv->dv", normed_low, grad_value_low, preferred_element_type=jnp.float32
    )
    grad_normed = grad_normed_ema + jnp.einsum(
        "tv,dv->td", grad_value_low, value_back, preferred_element_type=jnp.float32
    )
    grad_input, gain_one_grad = norm_back(grad_normed)
    grad_tokens = (grad_input + grad_after * (1.0 - update_gate)).astype(jnp.bfloat16)
    gains_grad = jnp.stack([gain_one_grad, gain_two_grad, omega_grad])
    small_totals = (
        lax.psum_scatter(gains_grad, (DP, FS), scatter_dimension=1, tiled=True),
        lax.psum_scatter(ema_grad, (DP, FS), scatter_dimension=1, tiled=True),
        lax.psum_scatter(attn_grad, (DP, FS), scatter_dimension=0, tiled=True),
    )
    totals = reduce_gradients(value_grad, mix_grad, merge_grad, up_grad, down_grad)
    return (
        result,
        grad_tokens,
        totals[0],
        totals[1],
        totals[2],
        totals[3],
        totals[4],
        small_totals[0],
        small_totals[1],
        small_totals[2],
    )


STRIP = 128
MESH = pl.DeviceIdType.MESH
F32 = jnp.float32
LOW = jnp.bfloat16
SHARDED = VALUE, MIX, MERGE, UP, DOWN = range(5)


def mm(a, b):
    return lax.dot_general(a, b, (((1,), (0,)), ((), ())), preferred_element_type=F32)


def mm_nt(a, b):
    return lax.dot_general(a, b, (((1,), (1,)), ((), ())), preferred_element_type=F32)


def mm_tn(a, b):
    return lax.dot_general(a, b, (((0,), (0,)), ((), ())), preferred_element_type=F32)


def at_rows(start, size, unit=16):
    return pl.ds(pl.multiple_of(start, unit), size)


def row_loop(count, size, body, first=0, unroll=1):
    def step(i, carry):
        body(pl.multiple_of(first + i * size, size))
        return carry

    lax.fori_loop(0, count // size, step, 0, unroll=unroll)


def slope_of(value, gate):
    return gate * (1.0 + value * (1.0 - gate))


def layer_kernel(trees, depth, *refs):
    ref, at = types.SimpleNamespace(), 0
    for tree in trees:
        ref.__dict__.update(jax.tree.unflatten(tree, refs[at : at + tree.num_leaves]))
        at += tree.num_leaves
    tok, cot, gains, ema_in, omega_in, attn = ref.tok, ref.cot, ref.gains, ref.ema_in, ref.omega_in, ref.attn
    rows, width = tok.shape
    tiles = width // 128
    dp, fs = lax.axis_index(DP), lax.axis_index(FS)
    z, c, y, x = dp // 2, dp % 2, fs // 2, fs % 2
    q = c * 2 + x

    def place(z, c, y, x):
        return (z * 2 + c, y * 2 + x)

    sib, xn, xc, yn = place(z, 1 - c, y, x), place(z, c, y, 1 - x), place(z, 1 - c, y, 1 - x), place(z, c, 1 - y, x)
    half_z = z // 2
    partner, far_mid, far_end = z + 1 - 2 * (z % 2), 2 - half_z, 3 * (1 - half_z)
    middle = (z % 2 + half_z) % 2 == 1
    outer = (z % 2 + half_z) % 2 == 0
    line = (far_end, far_mid, partner, z)
    zs = [None] + [place((z + d) % depth, c, y, x) for d in range(1, depth)]
    mates = ((sib, 1 - c, x), (xn, c, 1 - x), (xc, 1 - c, 1 - x))
    plane = [(pc, py, px) for pc in range(2) for py in range(2) for px in range(2)][1:]
    plane = [((c + pc) % 2, (y + py) % 2, (x + px) % 2) for pc, py, px in plane]

    barrier = pltpu.get_barrier_semaphore()
    peers = [place(z, *p) for p in plane] + zs[1:]
    for peer in peers:
        pl.semaphore_signal(barrier, inc=1, device_id=peer, device_id_type=MESH)
    pl.semaphore_wait(barrier, len(peers))

    send_sems, recv_sems, local_sems = ref.send_sems, ref.recv_sems, ref.local_sems
    used, used_local, pending = [0], [0], []

    def new_id():
        used[0] += 1
        return used[0] - 1

    def send(src, dst, peer, arrives=None, when=None):
        k = new_id()
        copy = pltpu.make_async_remote_copy(
            src_ref=src, dst_ref=dst, send_sem=send_sems.at[k], recv_sem=recv_sems.at[k if arrives is None else arrives],
            device_id=peer, device_id_type=MESH,
        )
        if when is None:
            copy.start()
        else:
            pl.when(when)(copy.start)
        handle = [k, copy, False, when]
        pending.append(handle)
        return handle

    def sent(handle):
        if not handle[2]:
            if handle[3] is None:
                handle[1].wait_send()
            else:
                pl.when(handle[3])(handle[1].wait_send)
            handle[2] = True

    def received(handle, landed):
        k = handle if isinstance(handle, int) else handle[0]
        pltpu.make_async_remote_copy(
            src_ref=landed, dst_ref=landed, send_sem=send_sems.at[k], recv_sem=recv_sems.at[k],
            device_id=sib, device_id_type=MESH,
        ).wait_recv()

    def local(src, dst):
        k = used_local[0]
        used_local[0] += 1
        copy = pltpu.make_async_copy(src, dst, local_sems.at[k])
        copy.start()
        return copy

    lens = ref.lens
    ends, run = [], 0
    for i in range(lens.shape[1]):
        run = run + lens[0, i]
        ends.append(run)

    def kept(k):
        start = 0
        for i, end in enumerate(ends):
            start = start + jnp.where(end <= k * CHUNK, lens[0, i], 0)
        return jnp.where(k * CHUNK - start == 0, 0.0, 1.0)

    def live_rows(r, size):
        places = r + lax.broadcasted_iota(jnp.int32, (size, 1), 0)
        return (places < ends[-1]).astype(F32)

    small_all, packed = ref.small_all, ref.packed
    lane_group = lax.broadcasted_iota(jnp.int32, (1, 128), 1) // 32

    def slot(pc, py, px, pz):
        return (pc * 4 + py * 2 + px) * depth + pz

    def small_start():
        return [send(packed, small_all.at[slot(c, y, x, z)], zs[d]) for d in range(1, depth)]

    def small_relay(handles):
        for d, handle in enumerate(handles):
            received(handle, small_all.at[slot(c, y, x, (z + depth - 1 - d) % depth)])
        small_all[slot(c, y, x, z)] = packed[...]
        mine = small_all.at[pl.ds(slot(c, y, x, 0), depth)]
        return [send(mine, mine, place(z, *p)) for p in plane]

    def small_finish(handles):
        for handle, p in zip(handles, plane):
            received(handle, small_all.at[pl.ds(slot(*p, 0), depth)])
        states = ema_in.shape[0] // (4 * tiles)
        gains[...] = jnp.zeros_like(gains)
        attn[...] = jnp.zeros_like(attn)
        for t in range(tiles):
            pz, pc = t // 2, t % 2
            got = [small_all[slot(pc, f // 2, f % 2, pz)].astype(F32)[0 : states + 8, :] for f in range(4)]
            for p in range(4):
                v = jnp.zeros_like(got[0])
                for f in range(4):
                    turn = (f - p) * 32 % 128
                    v = jnp.where(lane_group == f, pltpu.roll(got[f], turn, 1) if turn else got[f], v)
                ema_in[pl.ds(p * states * tiles + t, states, stride=tiles), :] = v[0:states]
                row = v[states : states + 1]
                if p < 3:
                    gains[p : p + 1, t * 128 : (t + 1) * 128] = row
                    if p == 2:
                        omega_in[t : t + 1, :] = row
                    continue
                for f in range(4):
                    turn = (t % 2 * 64 - f * 16) % 128
                    mine = lax.broadcasted_iota(jnp.int32, (1, 128), 1) // 16 == t % 2 * 4 + f
                    moved = pltpu.roll(row, turn, 1) if turn else row
                    attn[t // 2 : t // 2 + 1, :] += jnp.where(mine, moved, 0.0)

    lane = lax.broadcasted_iota(jnp.int32, (1, 128), 1)
    shift = fs * 32

    def mix_align():
        raw, win = ref.s[MIX], ref.mix_win
        last = raw.shape[1] // 128 * 128

        def step(r):
            at = pl.ds(r, 32)
            before = jnp.zeros((32, 128), F32)
            for t in range(win.shape[1] // 128):
                if t * 128 < last:
                    v = raw[at, t * 128 : (t + 1) * 128].astype(F32)
                else:
                    v = jnp.concatenate(
                        [raw[at, last:].astype(F32), jnp.zeros((32, 128 - raw.shape[1] + last), F32)], axis=1
                    )
                v = pltpu.roll(v, shift, 1)
                win[at, t * 128 : (t + 1) * 128] = jnp.where(lane < shift, before, v).astype(LOW)
                before = v

        row_loop(raw.shape[0], 32, step)

    weights = {m: ref.w[m] for m in SHARDED}
    block_shape = {m: (w.shape[0] // depth, w.shape[1] // 2) for m, w in weights.items()}

    def block(m, zz, yy):
        rb, cb = block_shape[m]
        return weights[m].at[at_rows(zz * rb, rb), at_rows(yy * cb, cb, 128)]

    def piece(m, src_c, src_x):
        rb, cb = block_shape[m]
        half = cb // 2
        if m in (VALUE, UP):
            return weights[m].at[at_rows(z * rb + src_c * (rb // 2), rb // 2), at_rows(y * cb + src_x * half, half, 128)]
        return weights[m].at[at_rows(z * rb, rb), at_rows(y * cb + src_x * half, half, 128)]

    def move(src, dst):
        rows_at_once = 32

        def step(r):
            dst[pl.ds(r, rows_at_once), :] = src[pl.ds(r, rows_at_once), :]

        row_loop(src.shape[0], rows_at_once, step)

    spare, near, loads, top = ref.up_low, {MIX: ref.mix_win}, {}, 0
    for m in (VALUE, MERGE, UP, DOWN):
        tall, wide = ref.s[m].shape
        near[m] = spare.at[top : top + tall, 0:wide]
        loads[m] = local(ref.s[m], near[m])
        top += tall
    for m in loads:
        loads[m].wait()

    swaps = {m: [] for m in SHARDED}

    def swap_start(m):
        shard = near[m]
        if m == MIX:
            first, last = 1 - (fs + 2) // 3, fs // 3
            middle = 1 - first - last
            for peer, pc, px in mates + ((None, c, x),):
                pq = pc * 2 + px
                tiles_at = (
                    first * 2 * pq,
                    (first + last) * (1 + 2 * pq) + middle * (1 + pq),
                    first * 8 + last * (2 + 2 * pq) + middle * (5 + pq),
                )
                for i, tile in enumerate(tiles_at):
                    src = shard.at[:, at_rows(tile * 128, 128, 128)]
                    dst = ref.mix_in.at[x, at_rows(c * 128, 128), pl.ds(i * 128, 128)]
                    if peer is None:
                        move(src, dst)
                    else:
                        swaps[m].append((send(src, dst, peer), pc, px, i))
            return
        if m in (VALUE, UP):
            wide = shard.shape[1] // 4
            for peer, pc, px in mates + ((None, c, x),):
                src = shard.at[:, at_rows((pc * 2 + px) * wide, wide, 128)]
                if peer is None:
                    move(src, piece(m, c, x))
                else:
                    swaps[m].append((send(src, piece(m, c, x), peer), pc, px, 0))
            return
        tall = shard.shape[0] // 2
        swaps[m].append((send(shard.at[at_rows((1 - x) * tall, tall), :], piece(m, c, x), xn), c, 1 - x, 0))
        move(shard.at[at_rows(x * tall, tall), :], piece(m, c, x))

    z_ids, z_sends, y_sends = {}, {}, {}

    def swap_finish(m):
        for handle, pc, px, i in swaps[m]:
            if m == MIX:
                received(handle, ref.mix_in.at[px, at_rows(pc * 128, 128), pl.ds(i * 128, 128)])
            else:
                received(handle, piece(m, pc, px))
        if m == MIX:
            only = (q == 3).astype(F32)
            low_y = (y == 0).astype(F32)
            lead = jnp.broadcast_to(jnp.maximum(low_y, only), (1, 128))
            rb, cb = block_shape[m]
            a, b, w = ref.mix_in.at[0], ref.mix_in.at[1], weights[m]

            def combine(r):
                at = pl.ds(r, 64)
                to = at_rows(z * rb + r, 64)

                def put(i, v):
                    w[to, at_rows(y * cb + i * 128, 128, 128)] = v.astype(LOW)

                put(0, a[at, 0:128].astype(F32) * lead)
                put(1, a[at, 128:256])
                put(2, a[at, 256:384].astype(F32) + b[at, 0:128].astype(F32) * lead)
                put(3, b[at, 128:256])
                put(4, b[at, 256:384])

            row_loop(rb, 64, combine)

    def y_own(m):
        y_sends[m] = [(3, send(block(m, z, y), block(m, z, y), yn))]

    def z_start(m):
        own = block(m, z, y)
        ids = [new_id() for _ in range(3)]
        z_ids[m] = ids
        z_sends[m] = [
            send(own, own, place(partner, c, y, x), ids[2]),
            send(own, own, place(far_mid, c, y, x), ids[1], middle),
            send(own, own, place(far_mid, c, y, x), ids[0], outer),
        ]

    def z_pass(m, steps=(1, 0)):
        for i in steps:
            there = block(m, line[i], y)
            pl.when(middle)(functools.partial(received, z_ids[m][i], there))
            z_sends[m].append(send(there, there, place(partner, c, y, x), z_ids[m][i], middle))

    def y_forward(m, steps=(2, 1, 0)):
        for i in steps:
            there = block(m, line[i], y)
            if i == 2:
                received(z_ids[m][i], there)
            else:
                pl.when(outer)(functools.partial(received, z_ids[m][i], there))
            y_sends[m].append((i, send(there, there, yn)))

    def y_finish(m):
        for i, handle in y_sends[m]:
            received(handle, block(m, line[i], 1 - y))

    def group_rows(c, x):
        return at_rows((c * 2 + x) * rows, rows)

    def part_rows(c, x, first, count):
        return at_rows((c * 2 + x) * rows + first, count)

    def gather_start(buf, first=0, count=None):
        count = rows if count is None else count
        own = buf.at[part_rows(c, x, first, count), :]
        return [(first, count), send(own, own, xn), send(own, own, sib)]

    def gather_relay(buf, handles):
        other = buf.at[part_rows(c, 1 - x, *handles[0]), :]
        received(handles[1], other)
        handles.append(send(other, other, sib))

    def gather_finish(buf, handles):
        received(handles[2], buf.at[part_rows(1 - c, x, *handles[0]), :])
        received(handles[3], buf.at[part_rows(1 - c, 1 - x, *handles[0]), :])

    total = ref.total
    stage = [ref.stage.at[0], ref.stage.at[1], ref.stage.at[2], ref.hidden_mul]
    staged = [[], [], [], []]

    def stage_out(k, first, count, extra=None):
        def put(r):
            at = pl.ds(r, 32)
            v = total[at, :]
            if extra is not None:
                v = v + extra[at, :].astype(F32)
            stage[k][at, :] = v.astype(LOW)

        row_loop(count, 32, put, first)

    def stage_free(k):
        for handle in staged[k]:
            sent(handle)
        staged[k] = []

    def reduce_early(partial, sibs, cross, slot=2):
        halves = (pl.ds(0, rows // 2), pl.ds(rows // 2, rows // 2))
        for k, px in ((0, 1 - x), (1, x)):
            partial(1 - c, px)
            stage_free(k)
            stage_out(k, 0, rows)
            staged[k] = [send(stage[k], sibs[k], sib)]
        first, second = staged[0][0], staged[1][0]
        partial(c, 1 - x)
        received(first, sibs[0])
        stage_free(slot)
        for i, half in enumerate(halves):
            stage_out(slot, i * (rows // 2), rows // 2, sibs[0])
            staged[slot].append(send(stage[slot].at[half, :], cross.at[half, :], xn))
        return second, list(zip(staged[slot], (cross.at[half, :] for half in halves)))

    def reduce_late(partial, sibs, cross, handles, consume):
        partial(c, x)
        received(handles[0], sibs[1])
        for i, (handle, half) in enumerate(handles[1]):
            received(handle, half)
            consume(i * (rows // 2), rows // 2)

    def reduced(r, size, sibs, cross):
        at = pl.ds(r, size)
        return total[at, :] + sibs[1][at, :].astype(F32) + cross[at, :].astype(F32)

    sibs_a, sibs_b = ((r.at[0], r.at[1]) for r in (ref.sibs_a, ref.sibs_b))
    cross_a, cross_b = ref.cross_a, ref.cross_b
    sibs_c, cross_c = (ref.gc.at[2 * rows : 3 * rows, :], ref.gc.at[3 * rows : 4 * rows, :]), ref.update_in

    w_up = weights[UP]
    y_out = {
        DOWN: ref.yo[1],
        UP: ref.yo[0],
        MERGE: ref.gc.at[0 : weights[MERGE].shape[0], 0 : block_shape[MERGE][1]],
        MIX: w_up.at[:, 0 : block_shape[MIX][1]],
        VALUE: w_up.at[:, block_shape[MIX][1] : block_shape[MIX][1] + block_shape[VALUE][1]],
    }
    y_in = {m: ref.yi[m] for m in SHARDED}
    z_in = {m: ref.zi[m] for m in SHARDED}
    f_in = {m: ref.fi[m] for m in SHARDED}
    gy, gz, gf = {}, {}, {}

    def y_grad_send(m, product, steps=(0, 1, 2, 3)):
        rb, cb = block_shape[m]
        if m not in gy:
            gy[m], gz[m] = {}, [new_id() for _ in range(4)]
        for i in steps:
            at = at_rows(line[i] * rb, rb)
            y_out[m][at, :] = product(line[i], 1 - y).astype(LOW)
            gy[m][i] = send(y_out[m].at[at, :], y_in[m].at[at, :], yn)

    def y_grad_add(m, product, steps=(0, 1, 2, 3)):
        rb, cb = block_shape[m]
        for i in steps:
            at = at_rows(line[i] * rb, rb)
            own = product(line[i], y)
            received(gy[m][i], y_in[m].at[at, :])
            y_in[m][at, :] = (own + y_in[m][at, :].astype(F32)).astype(LOW)
            if i < 3:
                send(
                    y_in[m].at[at, :], z_in[m].at[i], place(partner, c, y, x), gz[m][i], outer if i < 2 else None
                )

    def z_relay(m, steps=(0, 1)):
        rb, cb = block_shape[m]
        for i in steps:
            at = at_rows(line[i] * rb, rb)

            @pl.when(middle)
            def _(i=i, at=at):
                received(gz[m][i], z_in[m].at[i])
                y_in[m][at, :] = (y_in[m][at, :].astype(F32) + z_in[m][i].astype(F32)).astype(LOW)

            send(y_in[m].at[at, :], z_in[m].at[3], place(line[i], c, y, x), gz[m][3], middle)

    def z_grad_add(m):
        rb, cb = block_shape[m]
        for i in (2, 3):
            received(gz[m][i], z_in[m].at[i])

        def add(r):
            at = at_rows(z * rb + r, 64)
            v = y_in[m][at, :].astype(F32)
            for i in (2, 3):
                v = v + z_in[m][i, pl.ds(r, 64), :].astype(F32)
            y_in[m][at, :] = v.astype(LOW)

        row_loop(rb, 64, add)
        gf[m] = []
        if m in (MERGE, DOWN):
            land = f_in[m].at[at_rows(x * rb, rb), :]

            def part(px):
                return y_in[m].at[at_rows(z * rb, rb), at_rows(px * (cb // 2), cb // 2, 128)]

            gf[m].append((send(part(1 - x), land, xn), f_in[m].at[at_rows((1 - x) * rb, rb), :]))
            move(part(x), land)
            return
        half = rb // 2

        def land_at(pc, px):
            if m == MIX:
                return f_in[m].at[pc * 2 + px]
            wide = f_in[m].shape[1] // 4
            return f_in[m].at[:, at_rows((pc * 2 + px) * wide, wide, 128)]

        def part(pc, px):
            if m == MIX:
                return y_in[m].at[at_rows(z * rb + pc * half, half), at_rows(px * 256, 384, 128)]
            return y_in[m].at[at_rows(z * rb + pc * half, half), at_rows(px * (cb // 2), cb // 2, 128)]

        for peer, pc, px in mates:
            gf[m].append((send(part(pc, px), land_at(c, x), peer), land_at(pc, px)))
        move(part(c, x), land_at(c, x))

    def grad_out(m):
        for handle, landed in gf[m]:
            received(handle, landed)
        if m != MIX:
            return
        out, src = ref.g_mix, f_in[MIX]
        first, last = (fs == 0).astype(F32), (fs == 3).astype(F32)
        mid = 1.0 - first - last
        first, last, mid = (jnp.broadcast_to(v, (1, 128)) for v in (first, last, mid))

        def write(r):
            at = pl.ds(r, 16)

            def get(p, t):
                return src[p, at, t * 128 : (t + 1) * 128].astype(F32)

            turned = []
            for tile in range(9):
                v = first * (get(tile // 2, tile % 2) if tile < 8 else src[q, at, 256:384].astype(F32))
                if tile == 0:
                    v = v + (mid + last) * get(3, 0)
                else:
                    v = v + mid * get((tile - 1) % 4, 1 + (tile - 1) // 4)
                    v = v + last * get((tile - 1) // 2, 1 + (tile - 1) % 2)
                turned.append(pltpu.roll(v, (128 - shift) % 128, 1))
            for tile in range(9):
                v = turned[tile]
                if tile < 8:
                    v = jnp.where(lane < 128 - shift, v, turned[tile + 1])
                wide = min(128, out.shape[1] - tile * 128)
                out[at, tile * 128 : tile * 128 + wide] = v[:, :wide].astype(LOW)

        row_loop(out.shape[0], 16, write)

    h_small = small_start()
    swap_start(VALUE)
    mix_align()
    h_small = small_relay(h_small)
    swap_start(MERGE)
    swap_start(MIX)
    swap_finish(VALUE)
    y_own(VALUE)
    z_start(VALUE)

    nl, ml, n2, gc, gm = (ref.nl, ref.ml, ref.n2, ref.gc, ref.gm)
    by_time, out_time, back_time = ref.by_time, ref.out_time, ref.back_time

    def centre(v):
        cen = v - jnp.mean(v, axis=-1, keepdims=True)
        return cen, lax.rsqrt(jnp.mean(cen * cen, axis=-1, keepdims=True) + 1e-05)

    def norm_one(r):
        cen, rate = centre(tok[pl.ds(r, 16), :].astype(F32))
        v = cen * rate * gains[0:1, :]
        nl[at_rows(q * rows + r, 16), :] = v.astype(LOW)
        for s in range(tiles):
            by_time[pl.ds(r * tiles + s, 16, stride=tiles), :] = v[:, s * 128 : (s + 1) * 128]

    small_finish(h_small)
    row_loop(rows, 16, norm_one)
    h_nl = gather_start(nl)
    swap_start(UP)
    swap_finish(MERGE)
    y_own(MERGE)
    swap_finish(MIX)
    y_own(MIX)
    z_pass(VALUE)
    z_start(MIX)
    z_start(MERGE)

    def cot_low(r):
        at = pl.ds(r, 32)
        gc[at_rows(q * rows + r, 32), :] = (cot[at, :].astype(F32) * live_rows(r, 32)).astype(LOW)

    def load_ema():
        return ema_in[...].reshape(4, -1, tiles, 128)

    _, _, rate_all, weight_all = ema_coefficients(load_ema())
    omega = omega_in[...]
    marks = ref.marks

    def at_time(t):
        return at_rows(t * tiles, tiles, 8)

    def ema_chunk(k, state):
        state = state * kept(k)
        marks[k] = state

        def step(i, state):
            t = k * CHUNK + i
            v = by_time[at_time(t), :]
            state = rate_all * state + v[None]
            out_time[at_time(t), :] = jnp.sum(weight_all * state, axis=0) + omega * v
            return state

        return lax.fori_loop(0, CHUNK, step, state, unroll=4)

    lax.fori_loop(0, rows // CHUNK, ema_chunk, jnp.zeros_like(rate_all))

    def mixed(r):
        for s in range(tiles):
            at = pl.ds(r * tiles + s, 16, stride=tiles)
            v = out_time[at, :]
            gate = jax.nn.sigmoid(v)
            ml[at_rows(q * rows + r, 16), s * 128 : (s + 1) * 128] = (v * gate).astype(LOW)
            out_time[at, :] = slope_of(v, gate)

    row_loop(rows, 16, mixed)
    h_ml = gather_start(ml)
    swap_start(DOWN)
    row_loop(rows, 32, cot_low)
    y_forward(VALUE)
    z_pass(MIX, (1,))
    gather_relay(nl, h_nl)
    h_gc = gather_start(gc)
    y_forward(MIX, [2])
    z_pass(MIX, (0,))
    gather_finish(nl, h_nl)
    swap_finish(UP)
    z_start(UP)
    y_forward(MIX, [1])
    y_own(UP)
    z_pass(MERGE)
    y_finish(VALUE)

    value_low, value_slope = ref.value_low, ref.value_slope
    vq = value_low.shape[1]

    def value_block(r):
        total[:, :vq] = mm(nl[pl.ds(r, rows), :], weights[VALUE][...])

        def act(s):
            v = total[pl.ds(s, 32), :vq]
            gate = jax.nn.sigmoid(v)
            value_low[at_rows(r + s, 32), :] = (v * gate).astype(LOW)
            value_slope[at_rows(r + s, 32), :] = slope_of(v, gate).astype(LOW)

        row_loop(rows, 32, act)

    row_loop(4 * rows, rows, value_block)
    y_forward(MIX, [0])
    gather_relay(ml, h_ml)
    y_forward(MERGE)
    swap_finish(DOWN)
    z_start(DOWN)
    gather_finish(ml, h_ml)
    z_pass(UP, (1,))
    y_own(DOWN)
    gather_relay(gc, h_gc)
    z_pass(UP, (0,))
    y_finish(MIX)

    w_mix, reset_w = weights[MIX], ref.reset_w
    half_mix = w_mix.shape[1] // 2

    def fix_reset(r):
        at = pl.ds(r, 64)
        reset_w[at, 0:128] = w_mix[at, 384:512]
        reset_w[at, 128:256] = (w_mix[at, 512:640].astype(F32) + w_mix[at, half_mix : half_mix + 128].astype(F32)).astype(LOW)

    row_loop(width, 64, fix_reset)

    def w_update():
        return w_mix[:, 0:256]

    def w_shared():
        return w_mix[:, 256:384]

    def w_late():
        return w_mix[:, half_mix + 128 : half_mix + 384]

    def w_hidden():
        return w_mix[:, half_mix + 384 : half_mix + 640]

    scale = float(STRETCH) ** -0.5
    stretch = STRETCH
    shared_pre, query, key, probs = ref.shared_pre, ref.query, ref.key, ref.probs
    probs_low = ref.probs_low
    shared_pre[...] = mm(ml[group_rows(c, x), :], w_shared())
    sv = shared_pre[...]
    shared = sv * jax.nn.sigmoid(sv)
    query[...] = (shared * attn[0:1, :] + attn[1:2, :]).astype(LOW)
    key[...] = (shared * attn[2:3, :]).astype(LOW)
    bias = pltpu.roll(jnp.broadcast_to(attn[3:4, :], (stretch, stretch)), 0, 1, stride=1, stride_axis=0).T
    row_id = lax.broadcasted_iota(jnp.int32, (stretch, stretch), 0)
    col_id = lax.broadcasted_iota(jnp.int32, (stretch, stretch), 1)
    for n in range(rows // stretch):
        at = pl.ds(n * stretch, stretch)
        scores = mm_nt(query[at, :], key[at, :]) * scale + bias
        scores = jnp.where(row_id >= col_id, scores, -1000000000.0)
        ex = jnp.exp(scores - jnp.max(scores, axis=-1, keepdims=True))
        pr = ex / jnp.sum(ex, axis=-1, keepdims=True)
        probs[at, :] = pr
        probs_low[at_rows(q * rows + n * stretch, stretch), :] = pr.astype(LOW)
    own_probs = probs_low.at[group_rows(c, x), :]
    h_probs = [send(own_probs, own_probs, peer) for peer, _, _ in mates]

    mix_pack, update_in = ref.mix_pack, ref.update_in
    hidden_at = pl.ds(mix_pack.shape[1] - 256, 256)
    update_out = mix_pack.at[:, hidden_at]

    def update_block(r):
        update_out[pl.ds(r, rows), :] = mm(ml[pl.ds(r, rows), :], w_update()).astype(LOW)

    row_loop(4 * rows, rows, update_block)
    part_w = width // 4
    own_cols = at_rows(q * part_w, part_w, 128)
    h_update = [
        send(update_out.at[group_rows(pc, px), :], update_in.at[:, own_cols], peer) for peer, pc, px in mates
    ]
    update_in[:, own_cols] = update_out[group_rows(c, x), :]

    reset_gate, reset_slope = ref.reset_gate, ref.reset_slope

    def reset_block(r):
        at = pl.ds(r, rows)
        total[:, 0:256] = mm(ml[at, :], reset_w[...])
        total[:, 256:512] = mm(ml[at, :], w_late())

        def act(s):
            v = total[pl.ds(s, 32), :vq]
            gate = jax.nn.sigmoid(v)
            reset_gate[at_rows(r + s, 32), :] = (v * gate).astype(LOW)
            reset_slope[at_rows(r + s, 32), :] = slope_of(v, gate).astype(LOW)

        row_loop(rows, 32, act)

    row_loop(4 * rows, rows, reset_block)
    y_forward(UP, [2])
    z_pass(DOWN, (1,))
    for handle, (_, pc, px) in zip(h_probs, mates):
        received(handle, probs_low.at[group_rows(pc, px), :])

    gated = ref.gated

    def attend(r):
        at = pl.ds(r, stretch)
        total[0:stretch, :vq] = mm(probs_low[at, :], value_low[at, :])

        def act(s):
            v = total[pl.ds(s, 32), :vq]
            to = at_rows(r + s, 32)
            gated[to, :] = (v * reset_gate[to, :].astype(F32)).astype(LOW)
            reset_slope[to, :] = (v * reset_slope[to, :].astype(F32)).astype(LOW)

        row_loop(stretch, 32, act)

    row_loop(4 * rows, stretch, attend)
    y_forward(UP, [1])
    z_pass(DOWN, (0,))
    y_finish(MERGE)

    def merge_partial(c, x):
        at = group_rows(c, x)
        total[...] = mm(gated[at, :], weights[MERGE][...])
        total[:, own_cols] += mm(ml[at, :], w_hidden())

    h_red = reduce_early(merge_partial, sibs_a, cross_a)
    y_forward(UP, [0])
    for handle, (_, pc, px) in zip(h_update, mates):
        received(handle, update_in.at[:, at_rows((pc * 2 + px) * part_w, part_w, 128)])
    gather_finish(gc, h_gc)
    y_forward(DOWN, [2])

    after, hidden_mul, update_mul = ref.after, ref.hidden_mul, ref.update_mul

    def norm_two(r):
        at = pl.ds(r, 16)
        v = reduced(r, 16, sibs_a, cross_a)
        gate = jax.nn.sigmoid(v)
        hidden = v * gate
        u = jax.nn.sigmoid(update_in[at, :].astype(F32))
        xv = tok[at, :].astype(F32)
        av = u * hidden + (1.0 - u) * xv
        after[at, :] = av
        hidden_mul[at, :] = (u * slope_of(v, gate)).astype(LOW)
        update_mul[at, :] = ((hidden - xv) * u * (1.0 - u)).astype(LOW)
        cen, rate = centre(av)
        n2[at_rows(q * rows + r, 16), :] = (cen * rate * gains[1:2, :]).astype(LOW)

    h_n2 = []

    def take_merge(first, count):
        row_loop(count, 16, norm_two, first, 2)
        h_n2.append(gather_start(n2, first, count))

    reduce_late(merge_partial, sibs_a, cross_a, h_red, take_merge)
    y_forward(DOWN, [1])
    gather_relay(n2, h_n2[0])
    y_forward(DOWN, [0])
    gather_relay(n2, h_n2[1])
    for handles in h_n2:
        gather_finish(n2, handles)
    y_finish(UP)

    up_low, up_slope = ref.up_low, ref.up_slope
    for m in SHARDED:
        for swap in swaps[m]:
            sent(swap[0])

    def up_block(r):
        total[...] = mm(n2[pl.ds(r, rows), :], weights[UP][...])

        def act(s):
            v = total[pl.ds(s, 16), :]
            gate = jax.nn.sigmoid(v)
            up_low[at_rows(r + s, 16), :] = (v * gate).astype(LOW)
            up_slope[at_rows(r + s, 16), :] = slope_of(v, gate).astype(LOW)

        row_loop(rows, 16, act)

    row_loop(4 * rows, rows, up_block)

    def cols_of(m, yy):
        cb = block_shape[m][1]
        return at_rows(yy * cb, cb, 128)

    def rows_of(m, zz):
        rb = block_shape[m][0]
        return at_rows(zz * rb, rb, 128)

    def down_product(zz, yy):
        return mm_tn(up_low[:, rows_of(DOWN, zz)], gc[:, cols_of(DOWN, yy)])

    y_grad_send(DOWN, down_product)
    y_finish(DOWN)

    def down_partial(c, x):
        total[...] = mm(up_low[group_rows(c, x), :], weights[DOWN][...])

    def up_back(r):
        at = pl.ds(r, rows)
        total[...] = mm_nt(gc[at, :], weights[DOWN][...])

        def act(s):
            to = at_rows(r + s, 16)
            up_slope[to, :] = (total[pl.ds(s, 16), :] * up_slope[to, :].astype(F32)).astype(LOW)

        row_loop(rows, 16, act)

    row_loop(4 * rows, rows, up_back)
    grad_up = up_slope

    def two_partial(c, x):
        total[...] = mm_nt(grad_up[group_rows(c, x), :], weights[UP][...])

    def up_product(zz, yy):
        return mm_tn(n2[:, rows_of(UP, zz)], grad_up[:, cols_of(UP, yy)])

    h_red = reduce_early(two_partial, sibs_a, cross_a)
    y_grad_send(UP, up_product)
    y_grad_add(DOWN, down_product, (0, 1))
    for handle in h_gc[1:]:
        sent(handle)

    gain_sum, update_back = ref.gain_sum, hidden_mul
    gain_sum[...] = jnp.zeros_like(gain_sum)

    def norm_two_back(r):
        at = pl.ds(r, 16)
        g = reduced(r, 16, sibs_a, cross_a)
        cen, rate = centre(after[at, :])
        unit = cen * rate
        gain_sum[1] += g * unit
        g = g * gains[1:2, :]
        back = rate * (g - jnp.mean(g, axis=-1, keepdims=True) - unit * jnp.mean(g * unit, axis=-1, keepdims=True))
        back = back + cot[at, :].astype(F32) * live_rows(r, 16)
        gm[at_rows(q * rows + r, 16), :] = (back * hidden_mul[at, :].astype(F32)).astype(LOW)
        hidden_mul[at, :] = (back * update_mul[at, :].astype(F32)).astype(LOW)
        u = jax.nn.sigmoid(update_in[at, :].astype(F32))
        update_mul[at, :] = (back * (1.0 - u)).astype(LOW)

    h_gm = []

    def take_two(first, count):
        row_loop(count, 16, norm_two_back, first, 2)
        h_gm.append(gather_start(gm, first, count))

    reduce_late(two_partial, sibs_a, cross_a, h_red, take_two)
    for handle in h_update:
        sent(handle)
    update_grad = mix_pack.at[:, 0:256]
    own_rows = group_rows(c, x)
    h_update = [
        send(update_back.at[:, at_rows((pc * 2 + px) * part_w, part_w, 128)], update_grad.at[own_rows, :], peer)
        for peer, pc, px in mates
    ]
    update_grad[own_rows, :] = update_back[:, own_cols]

    y_grad_add(DOWN, down_product, (2, 3))
    z_relay(DOWN)
    y_grad_add(UP, up_product, (0, 1))
    gather_relay(gm, h_gm[0])
    gather_relay(gm, h_gm[1])
    y_grad_add(UP, up_product, (2,))
    for handles in h_gm:
        gather_finish(gm, handles)

    def merge_product(zz, yy):
        return mm_tn(gated[:, rows_of(MERGE, zz)], gm[:, cols_of(MERGE, yy)])

    for handle in z_sends[UP] + [h for _, h in y_sends[UP]]:
        sent(handle)
    y_grad_send(MERGE, merge_product)

    grad_probs, probs_in = ref.grad_probs, ref.probs_in

    def gated_back(r):
        at = pl.ds(r, rows)
        total[:, :vq] = mm_nt(gm[at, :], weights[MERGE][...])

        def act(s):
            to = at_rows(r + s, 32)
            g = total[pl.ds(s, 32), :vq]
            back = (g * reset_slope[to, :].astype(F32)).astype(LOW)
            mix_pack[to, 384:640] = back[:, 0:256]
            mix_pack[to, 640:768] = back[:, 128:256]
            mix_pack[to, 768:1024] = back[:, 256:512]
            mix_pack[to, hidden_at] = gm[to, own_cols]
            reset_gate[to, :] = (g * reset_gate[to, :].astype(F32)).astype(LOW)

        row_loop(rows, 32, act)

    row_loop(4 * rows, rows, gated_back)
    grad_att = reset_gate

    def probs_back(r):
        at = pl.ds(r, stretch)
        grad_probs[at, :] = mm_nt(grad_att[at, :], value_low[at, :]).astype(LOW)

    row_loop(4 * rows, stretch, probs_back)
    h_probs = [
        send(grad_probs.at[group_rows(pc, px), :], probs_in.at[i], peer) for i, (peer, pc, px) in enumerate(mates)
    ]
    for handle, (_, pc, px) in zip(h_update, mates):
        received(handle, update_grad.at[group_rows(pc, px), :])

    shared_grad = mix_pack.at[:, 256:384]

    def mixed_partial(cc, xx):
        at = group_rows(cc, xx)
        total[...] = (
            mm_nt(update_grad[at, :], w_update())
            + mm_nt(mix_pack[at, 384:640], reset_w[...])
            + mm_nt(mix_pack[at, 768:1024], w_late())
            + mm_nt(mix_pack[at, hidden_at], w_hidden())
        )


    def value_back(r):
        at = pl.ds(r, stretch)
        total[0:stretch, :vq] = mm_tn(probs_low[at, :], grad_att[at, :])

        def act(s):
            to = at_rows(r + s, 32)
            value_slope[to, :] = (total[pl.ds(s, 32), :vq] * value_slope[to, :].astype(F32)).astype(LOW)

        row_loop(stretch, 32, act)

    row_loop(4 * rows, stretch, value_back)
    grad_value = value_slope

    def value_product(zz, yy):
        return mm_tn(nl[:, rows_of(VALUE, zz)], grad_value[:, cols_of(VALUE, yy)])

    y_grad_send(VALUE, value_product, (0, 1))
    y_grad_add(UP, up_product, (3,))
    z_relay(UP)

    for i, handle in enumerate(h_probs):
        received(handle, probs_in.at[i])
    anti = (row_id + col_id == stretch - 1).astype(LOW)
    lag_sum = jnp.zeros((1, stretch), F32)
    grads_q = jnp.zeros((1, stretch), F32)
    grads_o = jnp.zeros((1, stretch), F32)
    grads_k = jnp.zeros((1, stretch), F32)
    for n in range(rows // stretch):
        at = pl.ds(n * stretch, stretch)
        to = at_rows(q * rows + n * stretch, stretch)
        g = grad_probs[to, :].astype(F32)
        for i in range(3):
            g = g + probs_in[i, at, :].astype(F32)
        pr = probs[at, :]
        gs = (pr * (g - jnp.sum(pr * g, axis=-1, keepdims=True))).astype(LOW)
        gq = mm(gs, key[at, :]) * scale
        gk = mm_tn(gs, query[at, :]) * scale
        lags = pltpu.roll(mm_nt(anti, gs), 1, 1, stride=1, stride_axis=0)
        lag_sum += jnp.sum(lags, axis=0, keepdims=True)
        sv = shared_pre[at, :]
        gate = jax.nn.sigmoid(sv)
        sh = sv * gate
        grads_q += jnp.sum(gq * sh, axis=0, keepdims=True)
        grads_o += jnp.sum(gq, axis=0, keepdims=True)
        grads_k += jnp.sum(gk * sh, axis=0, keepdims=True)
        gsh = gq * attn[0:1, :] + gk * attn[2:3, :]
        shared_grad[to, :] = (gsh * slope_of(sv, gate)).astype(LOW)
    attn_rows = (grads_q, grads_o, grads_k, lag_sum)
    own_shared = shared_grad.at[own_rows, :]
    h_shared = [send(own_shared, own_shared, peer) for peer, _, _ in mates]
    h_mixed = reduce_early(mixed_partial, sibs_a, cross_a)


    for handle, (_, pc, px) in zip(h_shared, mates):
        received(handle, shared_grad.at[group_rows(pc, px), :])

    def mix_product(zz, yy):
        return mm_tn(ml[:, rows_of(MIX, zz)], mix_pack[:, cols_of(MIX, yy)])

    y_grad_send(MIX, mix_product)
    y_grad_add(MERGE, merge_product)
    y_grad_send(VALUE, value_product, (2, 3))
    y_grad_add(VALUE, value_product, (0, 1))
    z_grad_add(DOWN)

    def mixed_own(cc, xx):
        mixed_partial(cc, xx)
        total[...] += mm_nt(shared_grad[own_rows, :], w_shared())


    def to_time(r):
        v = reduced(r, 16, sibs_a, cross_a)
        for s in range(tiles):
            at = pl.ds(r * tiles + s, 16, stride=tiles)
            out_time[at, :] = out_time[at, :] * v[:, s * 128 : (s + 1) * 128]

    reduce_late(mixed_own, sibs_a, cross_a, h_mixed, lambda first, count: row_loop(count, 16, to_time, first, 2))

    def value_partial(cc, xx):
        total[...] = mm_nt(grad_value[group_rows(cc, xx), :], weights[VALUE][...])

    h_red = reduce_early(value_partial, sibs_b, cross_b)
    z_relay(MERGE)
    y_grad_add(MIX, mix_product, (0,))

    held = ref.held
    ema = load_ema()
    damping, decay_gate, rate_all, weight_all = ema_coefficients(ema)
    omega = omega_in[...]
    half = rate_all.shape[0] // 2
    chunks = rows // CHUNK
    sums = []
    for part in range(2):
        js = slice(part * half, (part + 1) * half)
        rate, weight = rate_all[js], weight_all[js]

        def chunk(m, carry, js=js, rate=rate, weight=weight, part=part):
            k = chunks - 1 - m
            held[0] = marks[k, js]

            def ahead(i, state):
                state = rate * state + by_time[at_time(k * CHUNK + i), :][None]
                held[i + 1] = state
                return state

            lax.fori_loop(0, CHUNK, ahead, held[0], unroll=4)

            def back(n, carry):
                s, dw, dr, dom = carry
                i = CHUNK - 1 - n
                t = at_time(k * CHUNK + i)
                g = out_time[t, :]
                s = rate * s + g[None]
                dx = jnp.sum(weight * s, axis=0)
                if part == 0:
                    back_time[t, :] = dx + omega * g
                    dom = dom + g * by_time[t, :]
                else:
                    back_time[t, :] = back_time[t, :] + dx
                return s, dw + held[i + 1] * g[None], dr + held[i] * s, dom

            s, dw, dr, dom = lax.fori_loop(0, CHUNK, back, carry, unroll=2)
            return s * kept(k), dw, dr, dom

        if part:
            y_grad_add(MIX, mix_product, (1,))
            z_relay(VALUE)
            z_relay(MIX, (0,))
        zero = jnp.zeros_like(rate)
        sums.append(lax.fori_loop(0, chunks, chunk, (zero, zero, zero, jnp.zeros_like(omega))))
    small = ref.small_by_time
    rate_scale = ema.shape[1] ** (-0.5)
    for part in range(2):
        js = slice(part * half, (part + 1) * half)
        dw, dr = sums[part][1], sums[part][2] * weight_all[js]
        d_damp = dw * ema[2, js] * ema[3, js] * rate_scale - dr * decay_gate[js]
        parts = (
            d_damp * damping[js] * (1.0 - damping[js]),
            -dr * damping[js] * decay_gate[js] * (1.0 - decay_gate[js]),
            dw * damping[js] * ema[3, js] * rate_scale,
            dw * damping[js] * ema[2, js] * rate_scale,
        )
        for p in range(4):
            for j in range(half):
                small[pl.ds((p * 2 * half + part * half + j) * tiles, tiles), :] = parts[p][j]

    tile_rows = ref.tile_rows
    states = 4 * ema.shape[1]
    gain_two = jnp.sum(gain_sum[1], axis=0, keepdims=True)
    for t in range(tiles):
        at = (t % 2) * depth + t // 2
        tile_rows[at, 0:states, :] = small[pl.ds(t, states, stride=tiles), :]
        tail = jnp.concatenate(
            [
                jnp.zeros((1, 128), F32),
                gain_two[:, t * 128 : (t + 1) * 128],
                sums[0][3][t : t + 1],
                attn_rows[t // 2],
                jnp.zeros((4, 128), F32),
            ],
            axis=0,
        )
        tile_rows[at, states : states + 8, :] = tail
    sib_in, z_small, x_small, y_small = ref.sib_in, ref.z_small, ref.x_small, ref.y_small
    h_sib = send(tile_rows.at[pl.ds((1 - c) * depth, depth)], sib_in, sib)
    y_grad_add(MIX, mix_product, (2,))
    z_relay(MIX, (1,))
    received(h_sib, sib_in)
    sib_in[...] += tile_rows[pl.ds(c * depth, depth)]
    h_zs = [send(sib_in.at[(z + d) % depth], z_small.at[d - 1], zs[d]) for d in range(1, depth)]

    def norm_one_back(r):
        at = pl.ds(r, 16)
        ema_part = jnp.concatenate(
            [back_time[pl.ds(r * tiles + s, 16, stride=tiles), :] for s in range(tiles)], axis=1
        )
        g = reduced(r, 16, sibs_b, cross_b) + ema_part
        cen, rate = centre(tok[at, :].astype(F32))
        unit = cen * rate
        gain_sum[0] += g * unit
        g = g * gains[0:1, :]
        back = rate * (g - jnp.mean(g, axis=-1, keepdims=True) - unit * jnp.mean(g * unit, axis=-1, keepdims=True))
        ref.grad_tokens[at, :] = (back + update_mul[at, :].astype(F32)).astype(LOW)

    reduce_late(
        value_partial, sibs_b, cross_b, h_red, lambda first, count: row_loop(count, 16, norm_one_back, first, 2)
    )
    for handle in h_update:
        sent(handle)
    h_down = reduce_early(down_partial, sibs_c, cross_c, 3)
    z_grad_add(UP)
    one_rows, one_z, one_sum, one_plane = ref.one_rows, ref.one_z, ref.one_sum, ref.one_plane
    gain_one = jnp.sum(gain_sum[0], axis=0, keepdims=True)
    for t in range(tiles):
        one_rows[t] = jnp.broadcast_to(gain_one[:, t * 128 : (t + 1) * 128], (8, 128))
    h_one = [send(one_rows.at[pl.ds((z + d) % depth * 2, 2)], one_z.at[d - 1], zs[d]) for d in range(1, depth)]
    for d, handle in enumerate(h_zs):
        received(handle, z_small.at[d])
    x_small[0] = sib_in[z] + z_small[0] + z_small[1] + z_small[2]
    h_x = send(x_small.at[0], x_small.at[1], xn)
    y_grad_add(MIX, mix_product, (3,))
    z_grad_add(MERGE)
    for d, handle in enumerate(h_one):
        received(handle, one_z.at[d])
    one_sum[...] = one_rows[pl.ds(z * 2, 2)] + one_z[0] + one_z[1] + one_z[2]
    h_one = [send(one_sum.at[p[0]], one_plane.at[i], place(z, *p)) for i, p in enumerate(plane)]
    received(h_x, x_small.at[1])
    y_small[0] = x_small[0] + x_small[1]
    h_y = send(y_small.at[0], y_small.at[1], yn)
    y_grad_add(VALUE, value_product, (2, 3))
    z_grad_add(MIX)
    z_grad_add(VALUE)

    def finish(r):
        at = pl.ds(r, 16)
        ref.result[at, :] = (after[at, :] + reduced(r, 16, sibs_c, cross_c)).astype(LOW)

    reduce_late(down_partial, sibs_c, cross_c, h_down, lambda first, count: row_loop(count, 16, finish, first, 2))
    for m in (DOWN, UP, MERGE):
        grad_out(m)
    received(h_y, y_small.at[1])
    totals = y_small[0] + y_small[1]
    ref.small_out[...] = pltpu.roll(totals, (128 - shift) % 128, 1)
    one = one_sum[c]
    for i, handle in enumerate(h_one):
        received(handle, one_plane.at[i])
        one = one + one_plane[i]
    ref.small_out[states : states + 1, :] = pltpu.roll(one, (128 - shift) % 128, 1)[0:1]
    for m in (MIX, VALUE):
        grad_out(m)
    ref.attn_out[...] = pltpu.roll(totals[states : states + 8], (128 - c * 64 - fs * 16) % 128, 1)
    for handle in pending:
        sent(handle)
    assert used[0] <= COPIES


def pack_small(norm_gains, ema_params, attn_params):
    states, mine = ema_params.shape[2], ema_params.shape[1]
    last = jnp.pad(attn_params, (0, mine - attn_params.shape[0]))
    rows = [
        jnp.transpose(ema_params, (2, 0, 1)).reshape(states, 4 * mine),
        jnp.concatenate([norm_gains.reshape(-1), last])[None],
        jnp.zeros((32 - states - 1, 4 * mine), LOW),
    ]
    return jnp.concatenate(rows, axis=0)


def finish_kernel(result, grad_tokens, value, mix, merge, up, down, small, attn, *outs):
    for src, out in zip((result, grad_tokens, value, mix, merge, up, down), outs):

        def widen(r, src=src, out=out):
            out[pl.ds(r, 32), :] = src[pl.ds(r, 32), :].astype(out.dtype)

        row_loop(out.shape[0], 32, widen)
    gains, ema, per = outs[7:]
    mine, states = ema.shape[1:]
    gains[...] = small[4 * states : 4 * states + 3, :mine]
    turned = small[0 : 4 * states, :].T
    for p in range(4):
        ema[p] = turned[:mine, p * states : (p + 1) * states]
    per[...] = attn[3:4, : per.shape[1]]


def layer_on_device(depth, tokens, cotangent, lengths, value_proj, mix_proj, merge_proj, up_proj, down_proj, norm_gains, ema_params, attn_params):
    rows, width = tokens.shape
    fs = lax.axis_index(FS)
    window = -(-mix_proj.shape[1] // 128) * 128
    group = 4 * rows
    vq = value_proj.shape[1]
    fq = up_proj.shape[1]
    quarters = ((width, vq), (width, 10 * STRIP), (vq, width), (width, fq), (fq, width))
    tiles = width // 128
    states = ema_params.shape[2]
    small_rows = 4 * states + 8
    shape = jax.ShapeDtypeStruct
    shards = (value_proj, mix_proj, merge_proj, up_proj, down_proj)
    inputs = dict(
        tok=tokens,
        cot=cotangent,
        lens=lengths,
        packed=pack_small(norm_gains, ema_params, attn_params),
        s=shards,
    )
    landings = [w.shape for w in shards]
    landings[MIX] = (4, mix_proj.shape[0], 3 * STRIP)
    outputs = dict(
        result=shape((rows, width), LOW),
        grad_tokens=shape((rows, width), LOW),
        fi=tuple(shape(d, LOW) for d in landings),
        g_mix=shape(mix_proj.shape, LOW),
        small_out=shape((small_rows, 128), F32),
        attn_out=shape((8, 128), F32),
    )
    copies = pltpu.SemaphoreType.DMA((COPIES,))

    def low(*dims):
        return pltpu.VMEM(dims, LOW)

    def full(*dims):
        return pltpu.VMEM(dims, F32)

    scratch = dict(
        send_sems=copies,
        recv_sems=copies,
        local_sems=pltpu.SemaphoreType.DMA((32,)),
        w=tuple(low(*d) for d in quarters),
        yo=tuple(low(quarters[m][0], quarters[m][1] // 2) for m in (UP, DOWN)),
        yi=tuple(low(r, k // 2) for r, k in quarters),
        zi=tuple(low(4, r // depth, k // 2) for r, k in quarters),
        mix_win=low(mix_proj.shape[0], window),
        small_all=low(8 * depth, 32, 128),
        ema_in=full(4 * states * tiles, 128),
        omega_in=full(tiles, 128),
        gains=full(8, width),
        attn=full(8, 128),
        nl=low(group, width),
        ml=low(group, width),
        n2=low(group, width),
        gc=low(group, width),
        gm=low(group, width),
        mix_in=low(2, 2 * mix_proj.shape[0], 3 * STRIP),
        reset_w=low(width, 256),
        value_low=low(group, vq),
        value_slope=low(group, vq),
        reset_gate=low(group, vq),
        reset_slope=low(group, vq),
        gated=low(group, vq),
        up_low=low(group, fq),
        up_slope=low(group, fq),
        update_in=low(rows, width),
        probs_low=low(group, STRETCH),
        probs=full(rows, STRETCH),
        shared_pre=full(rows, Z),
        query=low(rows, Z),
        key=low(rows, Z),
        grad_probs=low(group, STRETCH),
        probs_in=low(3, rows, STRETCH),
        mix_pack=low(group, 10 * STRIP),
        by_time=full(rows * tiles, 128),
        out_time=full(rows * tiles, 128),
        back_time=full(rows * tiles, 128),
        marks=full(rows // CHUNK, states, tiles, 128),
        held=full(CHUNK + 1, states // 2, tiles, 128),
        total=full(rows, width),
        stage=low(3, rows, width),
        sibs_a=low(2, rows, width),
        sibs_b=low(2, rows, width),
        cross_a=low(rows, width),
        cross_b=low(rows, width),
        after=full(rows, width),
        hidden_mul=low(rows, width),
        update_mul=low(rows, width),
        gain_sum=full(2, 16, width),
        small_by_time=full(4 * states * tiles, 128),
        tile_rows=full(tiles, small_rows, 128),
        sib_in=full(depth, small_rows, 128),
        z_small=full(depth - 1, small_rows, 128),
        x_small=full(2, small_rows, 128),
        y_small=full(2, small_rows, 128),
        one_rows=full(tiles, 8, 128),
        one_z=full(depth - 1, 2, 8, 128),
        one_sum=full(2, 8, 128),
        one_plane=full(7, 8, 128),
    )
    in_vmem = pl.BlockSpec(memory_space=pltpu.VMEM)
    specs = jax.tree.map(lambda _: in_vmem, inputs)
    anywhere = pl.BlockSpec(memory_space=pl.ANY)
    specs.update(
        lens=pl.BlockSpec(memory_space=pltpu.SMEM), s=tuple(in_vmem if m == MIX else anywhere for m in SHARDED)
    )
    in_leaves, in_tree = jax.tree.flatten(inputs)
    out_leaves, out_tree = jax.tree.flatten(outputs)
    scratch_leaves, scratch_tree = jax.tree.flatten(scratch, is_leaf=lambda v: not isinstance(v, (dict, tuple)))
    outs = pl.pallas_call(
        functools.partial(layer_kernel, (in_tree, out_tree, scratch_tree), depth),
        out_shape=tuple(out_leaves),
        in_specs=jax.tree.leaves(specs),
        out_specs=tuple(in_vmem for _ in out_leaves),
        scratch_shapes=scratch_leaves,
        compiler_params=pltpu.CompilerParams(collective_id=0, has_side_effects=True, vmem_limit_bytes=VMEM_BYTES),
        name="layer",
    )(*in_leaves)
    by = types.SimpleNamespace(**jax.tree.unflatten(out_tree, outs))
    grads = list(by.fi)
    grads[MIX] = by.g_mix
    wide = [shape(g.shape, F32) for g in (*grads, norm_gains, ema_params)]
    *finals, attn_grad = pl.pallas_call(
        finish_kernel,
        out_shape=(shape((rows, width), LOW), shape((rows, width), LOW), *wide, shape((1, attn_params.shape[0]), F32)),
        in_specs=[in_vmem] * 9,
        out_specs=(in_vmem,) * 10,
        compiler_params=pltpu.CompilerParams(vmem_limit_bytes=32 << 20),
        name="finish",
    )(by.result, by.grad_tokens, *grads, by.small_out, by.attn_out)
    return (*finals, attn_grad[0])


VMEM_BYTES = 64 << 20
COPIES = 256


def solution(mesh):
    in_specs = (
        P((DP, FS), None),
        P((DP, FS), None),
        P((DP, FS), None),
        P(DP, FS),
        P(DP, FS),
        P(DP, FS),
        P(DP, FS),
        P(DP, FS),
        P(None, (DP, FS)),
        P(None, (DP, FS), None),
        P((DP, FS)),
    )
    out_specs = (
        P((DP, FS), None),
        P((DP, FS), None),
        P(DP, FS),
        P(DP, FS),
        P(DP, FS),
        P(DP, FS),
        P(DP, FS),
        P(None, (DP, FS)),
        P(None, (DP, FS), None),
        P((DP, FS)),
    )
    fits = mesh.shape[DP] == 8 and mesh.shape[DP] // 2 * 4 * STRIP == V and mesh.shape[FS] * 4 * STRIP == V
    body = functools.partial(layer_on_device, mesh.shape[DP] // 2) if fits else on_device
    return jax.shard_map(body, mesh=mesh, in_specs=in_specs, out_specs=out_specs, check_vma=False)
```

```python
import functools
import types

import jax
import jax.numpy as jnp
from jax import lax
from jax.experimental import pallas as pl
from jax.experimental.pallas import tpu as pltpu
from jax.sharding import PartitionSpec as P

D = 1024
Z = 128
V = 2048
STRETCH = 128


DP, FS = "dp", "fsdp"
highest = lax.Precision.HIGHEST


def layer_norm(values, gain):
    centred = values - jnp.mean(values, axis=-1, keepdims=True)
    spread_sq = jnp.mean(centred * centred, axis=-1, keepdims=True)
    return centred * lax.rsqrt(spread_sq + 1e-05) * gain


def token_layout(length_row, row_count):
    places = jnp.arange(row_count, dtype=jnp.int32)
    running = jnp.cumsum(length_row)
    before = (running[None, :] <= places[:, None]).astype(jnp.int32)
    starts = jnp.sum(before * length_row[None, :], axis=1)
    return (places - starts, places < running[-1])


def ema_coefficients(ema):
    damping = jax.nn.sigmoid(ema[0])
    decay_gate = jax.nn.sigmoid(ema[1])
    keep_rate = 1.0 - damping * decay_gate
    weights_out = damping * ema[2] * ema[3] * ema.shape[1] ** (-0.5)
    return damping, decay_gate, keep_rate, weights_out


CHUNK = 32


def ema_forward_kernel(x_ref, ema_ref, omega_ref, keep_ref, y_ref, mark_ref):
    _, _, rate, weight = ema_coefficients(ema_ref[...])
    omega = omega_ref[...]

    def chunk(k, state):
        state = state * keep_ref[k][None]
        mark_ref[k] = state

        def step(i, state):
            t = k * CHUNK + i
            x = x_ref[t]
            state = rate * state + x[None]
            y_ref[t] = jnp.sum(weight * state, axis=0) + omega * x
            return state

        return lax.fori_loop(0, CHUNK, step, state, unroll=4)

    lax.fori_loop(0, x_ref.shape[0] // CHUNK, chunk, jnp.zeros_like(rate))


def ema_backward_kernel(x_ref, g_ref, ema_ref, omega_ref, keep_ref, mark_ref, dx_ref, dema_ref, domega_ref, h_ref):
    ema = ema_ref[...]
    damping, decay_gate, rate_all, weight_all = ema_coefficients(ema)
    omega = omega_ref[...]
    half = rate_all.shape[0] // 2
    chunks = x_ref.shape[0] // CHUNK
    sums = []
    for part in range(2):
        js = slice(part * half, (part + 1) * half)
        rate, weight = rate_all[js], weight_all[js]
        zero = jnp.zeros_like(rate)

        def chunk(m, carry, js=js, rate=rate, weight=weight, part=part):
            k = chunks - 1 - m
            h_ref[0] = mark_ref[k, js]

            def ahead(i, state):
                state = rate * state + x_ref[k * CHUNK + i][None]
                h_ref[i + 1] = state
                return state

            lax.fori_loop(0, CHUNK, ahead, h_ref[0], unroll=4)

            def back(n, carry):
                s, dw, dr, dom = carry
                i = CHUNK - 1 - n
                t = k * CHUNK + i
                g = g_ref[t]
                s = rate * s + g[None]
                dx = jnp.sum(weight * s, axis=0)
                if part == 0:
                    dx_ref[t] = dx + omega * g
                    dom = dom + g * x_ref[t]
                else:
                    dx_ref[t] = dx_ref[t] + dx
                dw = dw + h_ref[i + 1] * g[None]
                dr = dr + h_ref[i] * s
                return s, dw, dr, dom

            s, dw, dr, dom = lax.fori_loop(0, CHUNK, back, carry, unroll=2)
            return s * keep_ref[k][None], dw, dr, dom

        out = lax.fori_loop(0, chunks, chunk, (zero, zero, zero, jnp.zeros_like(omega)))
        sums.append(out)
    dw = jnp.concatenate([sums[0][1], sums[1][1]], axis=0)
    dr = jnp.concatenate([sums[0][2], sums[1][2]], axis=0) * weight_all
    scale = ema.shape[1] ** (-0.5)
    d_damp = dw * ema[2] * ema[3] * scale - dr * decay_gate
    dema_ref[0] = d_damp * damping * (1.0 - damping)
    dema_ref[1] = -dr * damping * decay_gate * (1.0 - decay_gate)
    dema_ref[2] = dw * damping * ema[3] * scale
    dema_ref[3] = dw * damping * ema[2] * scale
    domega_ref[...] = sums[0][3]


def ema_keep(position):
    starts = position.reshape(-1, CHUNK)[:, 0] != 0
    return jnp.broadcast_to(starts.astype(jnp.float32)[:, None, None], (starts.shape[0], 8, 128))


def ema_apply(x, ema, omega, keep):
    f32 = jnp.float32
    shape = jax.ShapeDtypeStruct
    return pl.pallas_call(
        ema_forward_kernel,
        out_shape=(shape(x.shape, f32), shape((keep.shape[0],) + ema.shape[1:], f32)),
        compiler_params=pltpu.CompilerParams(vmem_limit_bytes=32 << 20),
    )(x, ema, omega, keep)


def ema_reverse(x, g, ema, omega, keep, mark):
    f32 = jnp.float32
    shape = jax.ShapeDtypeStruct
    return pl.pallas_call(
        ema_backward_kernel,
        out_shape=(shape(x.shape, f32), shape(ema.shape, f32), shape(omega.shape, f32)),
        scratch_shapes=[pltpu.VMEM((CHUNK + 1, ema.shape[1] // 2) + ema.shape[2:], f32)],
        compiler_params=pltpu.CompilerParams(vmem_limit_bytes=32 << 20),
    )(x, g, ema, omega, keep, mark)


def silu_slope(values):
    logistic = jax.nn.sigmoid(values)
    return logistic * (1.0 + values * (1.0 - logistic))


def relative_table(rel_bias):
    lag_grid = (
        jnp.arange(STRETCH, dtype=jnp.int32)[:, None]
        - jnp.arange(STRETCH, dtype=jnp.int32)[None, :]
    )
    one_hot = (lag_grid[:, :, None] == jnp.arange(STRETCH, dtype=jnp.int32)[None, None, :]).astype(
        jnp.float32
    )
    bias_grid = jnp.einsum("ijl,l->ij", one_hot, rel_bias, precision=highest)
    return (lag_grid, one_hot, bias_grid)


def gather_forward(value_proj, mix_proj, merge_proj, up_proj, down_proj):
    first = (
        lax.all_gather(value_proj, DP, axis=0, tiled=True),
        lax.all_gather(mix_proj, DP, axis=0, tiled=True),
        lax.all_gather(merge_proj, DP, axis=0, tiled=True),
        lax.all_gather(up_proj, DP, axis=0, tiled=True),
        lax.all_gather(down_proj, DP, axis=0, tiled=True),
    )
    return (
        lax.all_gather(first[0], FS, axis=1, tiled=True),
        lax.all_gather(first[1], FS, axis=1, tiled=True),
        lax.all_gather(first[2], FS, axis=1, tiled=True),
        lax.all_gather(first[3], FS, axis=1, tiled=True),
        lax.all_gather(first[4], FS, axis=1, tiled=True),
    )


def reduce_gradients(value_grad, mix_grad, merge_grad, up_grad, down_grad):
    first = (
        lax.psum_scatter(
            value_grad.astype(jnp.bfloat16), DP, scatter_dimension=0, tiled=True
        ).astype(jnp.float32),
        lax.psum_scatter(
            mix_grad.astype(jnp.bfloat16), DP, scatter_dimension=0, tiled=True
        ).astype(jnp.float32),
        lax.psum_scatter(
            merge_grad.astype(jnp.bfloat16), DP, scatter_dimension=0, tiled=True
        ).astype(jnp.float32),
        lax.psum_scatter(
            up_grad.astype(jnp.bfloat16), DP, scatter_dimension=0, tiled=True
        ).astype(jnp.float32),
        lax.psum_scatter(
            down_grad.astype(jnp.bfloat16), DP, scatter_dimension=0, tiled=True
        ).astype(jnp.float32),
    )
    return (
        lax.psum_scatter(
            first[0].astype(jnp.bfloat16), FS, scatter_dimension=1, tiled=True
        ).astype(jnp.float32),
        lax.psum_scatter(
            first[1].astype(jnp.bfloat16), FS, scatter_dimension=1, tiled=True
        ).astype(jnp.float32),
        lax.psum_scatter(
            first[2].astype(jnp.bfloat16), FS, scatter_dimension=1, tiled=True
        ).astype(jnp.float32),
        lax.psum_scatter(
            first[3].astype(jnp.bfloat16), FS, scatter_dimension=1, tiled=True
        ).astype(jnp.float32),
        lax.psum_scatter(
            first[4].astype(jnp.bfloat16), FS, scatter_dimension=1, tiled=True
        ).astype(jnp.float32),
    )


def on_device(
    tokens,
    cotangent,
    lengths,
    value_proj,
    mix_proj,
    merge_proj,
    up_proj,
    down_proj,
    norm_gains,
    ema_params,
    attn_params,
):
    gains_full, ema_full, attn_full = (
        lax.all_gather(norm_gains, (DP, FS), axis=1, tiled=True),
        lax.all_gather(ema_params, (DP, FS), axis=1, tiled=True),
        lax.all_gather(attn_params, (DP, FS), axis=0, tiled=True),
    )
    value_full, mix_full, merge_full, up_full, down_full = gather_forward(
        value_proj, mix_proj, merge_proj, up_proj, down_proj
    )
    gains_float = gains_full.astype(jnp.float32)
    ema_float = ema_full.astype(jnp.float32)
    attn_float = attn_full.astype(jnp.float32)
    row_count = tokens.shape[0]
    position, live_rows = token_layout(lengths[0], row_count)
    tokens_float = tokens.astype(jnp.float32)
    normed, norm_back = jax.vjp(layer_norm, tokens_float, gains_float[0])
    normed_low = normed.astype(jnp.bfloat16)
    value_pre = jnp.dot(normed_low, value_full, preferred_element_type=jnp.float32)
    value_low = jax.nn.silu(value_pre).astype(jnp.bfloat16)

    lanes = (8, tokens.shape[1] // 8)
    ema_by_state = jnp.swapaxes(ema_float, 1, 2).reshape(4, -1, *lanes)
    omega = gains_float[2].reshape(lanes)
    keep = ema_keep(position)
    normed_rows = normed.reshape(row_count, *lanes)
    ema_rows, ema_marks = ema_apply(normed_rows, ema_by_state, omega, keep)
    ema_out = ema_rows.reshape(row_count, -1)
    mixed_low = jax.nn.silu(ema_out).astype(jnp.bfloat16)
    projected = jnp.dot(mixed_low, mix_full, preferred_element_type=jnp.float32)
    update_gate = jax.nn.sigmoid(projected[:, :D])
    shared_pre = projected[:, D : D + Z]
    reset_pre = projected[:, D + Z : D + Z + V]
    hidden_x = projected[:, D + Z + V :]
    shared = jax.nn.silu(shared_pre)
    reset_gate = jax.nn.silu(reset_pre)
    query_low = (shared * attn_float[:Z] + attn_float[Z : 2 * Z]).astype(jnp.bfloat16)
    key_low = (shared * attn_float[2 * Z : 3 * Z]).astype(jnp.bfloat16)
    block_count = row_count // STRETCH
    lag_grid, one_hot, bias_grid = relative_table(attn_float[3 * Z :])
    query_blocks = query_low.reshape(block_count, STRETCH, Z)
    key_blocks = key_low.reshape(block_count, STRETCH, Z)
    value_blocks = value_low.reshape(block_count, STRETCH, V)
    score_scale = Z ** (-0.5)

    def block_scores():
        raw_scores = (
            jnp.einsum("nik,njk->nij", query_blocks, key_blocks, preferred_element_type=jnp.float32)
            * score_scale
            + bias_grid
        )
        return jnp.where(lag_grid >= 0, raw_scores, -1000000000.0)

    scores = block_scores()
    row_max = jnp.max(scores, axis=-1, keepdims=True)
    log_total = row_max + jnp.log(jnp.sum(jnp.exp(scores - row_max), axis=-1, keepdims=True))
    probs_low = jnp.exp(scores - log_total).astype(jnp.bfloat16)
    attended = jnp.einsum(
        "nij,njv->niv", probs_low, value_blocks, preferred_element_type=jnp.float32
    ).reshape(row_count, V)
    gated_low = (attended * reset_gate).astype(jnp.bfloat16)
    hidden_in = jnp.dot(gated_low, merge_full, preferred_element_type=jnp.float32) + hidden_x
    hidden = jax.nn.silu(hidden_in)
    after_mixer = update_gate * hidden + (1.0 - update_gate) * tokens_float
    normed_two, norm_two_back = jax.vjp(layer_norm, after_mixer, gains_float[1])
    normed_two_low = normed_two.astype(jnp.bfloat16)
    up_pre = jnp.dot(normed_two_low, up_full, preferred_element_type=jnp.float32)
    up_low = jax.nn.silu(up_pre).astype(jnp.bfloat16)
    result = (after_mixer + jnp.dot(up_low, down_full, preferred_element_type=jnp.float32)).astype(
        jnp.bfloat16
    )
    value_back, mix_back, merge_back, up_back, down_back = (
        value_full, mix_full, merge_full, up_full, down_full
    )
    grad_rows = cotangent.astype(jnp.float32) * live_rows[:, None].astype(jnp.float32)
    grad_down_low = grad_rows.astype(jnp.bfloat16)
    down_grad = jnp.einsum("tf,td->fd", up_low, grad_down_low, preferred_element_type=jnp.float32)
    grad_up_act = jnp.einsum(
        "td,fd->tf", grad_down_low, down_back, preferred_element_type=jnp.float32
    )
    grad_up_low = (grad_up_act * silu_slope(up_pre)).astype(jnp.bfloat16)
    up_grad = jnp.einsum(
        "td,tf->df", normed_two_low, grad_up_low, preferred_element_type=jnp.float32
    )
    grad_normed_two = jnp.einsum(
        "tf,df->td", grad_up_low, up_back, preferred_element_type=jnp.float32
    )
    grad_after_norm, gain_two_grad = norm_two_back(grad_normed_two)
    grad_after = grad_after_norm + grad_rows
    grad_hidden_in = grad_after * update_gate * silu_slope(hidden_in)
    grad_merge_low = grad_hidden_in.astype(jnp.bfloat16)
    merge_grad = jnp.einsum(
        "tv,td->vd", gated_low, grad_merge_low, preferred_element_type=jnp.float32
    )
    grad_gated = jnp.einsum(
        "td,vd->tv", grad_merge_low, merge_back, preferred_element_type=jnp.float32
    )
    grad_reset = grad_gated * attended
    grad_attended_low = (
        (grad_gated * reset_gate).astype(jnp.bfloat16).reshape(block_count, STRETCH, V)
    )
    grad_probs = jnp.einsum(
        "niv,njv->nij", grad_attended_low, value_blocks, preferred_element_type=jnp.float32
    )
    soft_probs = jnp.exp(block_scores() - log_total)
    grad_scores_low = (
        soft_probs * (grad_probs - jnp.sum(soft_probs * grad_probs, axis=-1, keepdims=True))
    ).astype(jnp.bfloat16)
    grad_query = (
        jnp.einsum(
            "nij,njk->nik", grad_scores_low, key_blocks, preferred_element_type=jnp.float32
        ).reshape(row_count, Z)
        * score_scale
    )
    grad_key = (
        jnp.einsum(
            "nij,nik->njk", grad_scores_low, query_blocks, preferred_element_type=jnp.float32
        ).reshape(row_count, Z)
        * score_scale
    )
    grad_value_act = jnp.einsum(
        "nij,niv->njv",
        soft_probs.astype(jnp.bfloat16),
        grad_attended_low,
        preferred_element_type=jnp.float32,
    ).reshape(row_count, V)
    rel_grad = jnp.einsum(
        "ij,ijl->l",
        jnp.sum(grad_scores_low.astype(jnp.float32), axis=0),
        one_hot,
        precision=highest,
    )
    attn_grad = jnp.concatenate(
        [
            jnp.sum(grad_query * shared, axis=0),
            jnp.sum(grad_query, axis=0),
            jnp.sum(grad_key * shared, axis=0),
            rel_grad,
        ]
    )
    grad_shared = grad_query * attn_float[:Z] + grad_key * attn_float[2 * Z : 3 * Z]
    grad_projected_low = jnp.concatenate(
        [
            grad_after * (hidden - tokens_float) * update_gate * (1.0 - update_gate),
            grad_shared * silu_slope(shared_pre),
            grad_reset * silu_slope(reset_pre),
            grad_hidden_in,
        ],
        axis=1,
    ).astype(jnp.bfloat16)
    mix_grad = jnp.einsum(
        "td,tm->dm", mixed_low, grad_projected_low, preferred_element_type=jnp.float32
    )
    grad_mixed = jnp.einsum(
        "tm,dm->td", grad_projected_low, mix_back, preferred_element_type=jnp.float32
    )
    grad_ema_rows = (grad_mixed * silu_slope(ema_out)).reshape(row_count, *lanes)
    grad_normed_rows, ema_grad_rows, omega_grad = ema_reverse(
        normed_rows, grad_ema_rows, ema_by_state, omega, keep, ema_marks
    )
    grad_normed_ema = grad_normed_rows.reshape(row_count, -1)
    ema_grad = jnp.swapaxes(ema_grad_rows.reshape(4, -1, tokens.shape[1]), 1, 2)
    omega_grad = omega_grad.reshape(-1)
    grad_value_low = (grad_value_act * silu_slope(value_pre)).astype(jnp.bfloat16)
    value_grad = jnp.einsum(
        "td,tv->dv", normed_low, grad_value_low, preferred_element_type=jnp.float32
    )
    grad_normed = grad_normed_ema + jnp.einsum(
        "tv,dv->td", grad_value_low, value_back, preferred_element_type=jnp.float32
    )
    grad_input, gain_one_grad = norm_back(grad_normed)
    grad_tokens = (grad_input + grad_after * (1.0 - update_gate)).astype(jnp.bfloat16)
    gains_grad = jnp.stack([gain_one_grad, gain_two_grad, omega_grad])
    small_totals = (
        lax.psum_scatter(gains_grad, (DP, FS), scatter_dimension=1, tiled=True),
        lax.psum_scatter(ema_grad, (DP, FS), scatter_dimension=1, tiled=True),
        lax.psum_scatter(attn_grad, (DP, FS), scatter_dimension=0, tiled=True),
    )
    totals = reduce_gradients(value_grad, mix_grad, merge_grad, up_grad, down_grad)
    return (
        result,
        grad_tokens,
        totals[0],
        totals[1],
        totals[2],
        totals[3],
        totals[4],
        small_totals[0],
        small_totals[1],
        small_totals[2],
    )


STRIP = 128
MESH = pl.DeviceIdType.MESH
F32 = jnp.float32
LOW = jnp.bfloat16
SHARDED = VALUE, MIX, MERGE, UP, DOWN = range(5)
TOK, COT = 5, 6


def mm(a, b):
    return lax.dot_general(a, b, (((1,), (0,)), ((), ())), preferred_element_type=F32)


def mm_nt(a, b):
    return lax.dot_general(a, b, (((1,), (1,)), ((), ())), preferred_element_type=F32)


def mm_tn(a, b):
    return lax.dot_general(a, b, (((0,), (0,)), ((), ())), preferred_element_type=F32)


def at_rows(start, size, unit=16):
    return pl.ds(pl.multiple_of(start, unit), size)


def row_loop(count, size, body, first=0, unroll=1):
    def step(i, carry):
        body(pl.multiple_of(first + i * size, size))
        return carry

    lax.fori_loop(0, count // size, step, 0, unroll=unroll)


def slope_of(value, gate):
    return gate * (1.0 + value * (1.0 - gate))


def layer_kernel(trees, depth, *refs):
    ref, at = types.SimpleNamespace(), 0
    for tree in trees:
        ref.__dict__.update(jax.tree.unflatten(tree, refs[at : at + tree.num_leaves]))
        at += tree.num_leaves
    tok, cot, gains, ema_in, omega_in, attn = ref.tok, ref.cot, ref.gains, ref.ema_in, ref.omega_in, ref.attn
    rows, width = tok.shape
    tiles = width // 128
    dp, fs = lax.axis_index(DP), lax.axis_index(FS)
    z, c, y, x = dp // 2, dp % 2, fs // 2, fs % 2
    q = c * 2 + x

    def place(z, c, y, x):
        return (z * 2 + c, y * 2 + x)

    sib, xn, xc, yn = place(z, 1 - c, y, x), place(z, c, y, 1 - x), place(z, 1 - c, y, 1 - x), place(z, c, 1 - y, x)
    half_z = z // 2
    partner, far_mid, far_end = z + 1 - 2 * (z % 2), 2 - half_z, 3 * (1 - half_z)
    middle = (z % 2 + half_z) % 2 == 1
    outer = (z % 2 + half_z) % 2 == 0
    line = (far_end, far_mid, partner, z)
    zs = [None] + [place((z + d) % depth, c, y, x) for d in range(1, depth)]
    mates = ((sib, 1 - c, x), (xn, c, 1 - x), (xc, 1 - c, 1 - x))
    plane = [(pc, py, px) for pc in range(2) for py in range(2) for px in range(2)][1:]
    plane = [((c + pc) % 2, (y + py) % 2, (x + px) % 2) for pc, py, px in plane]

    send_sems, recv_sems, local_sems = ref.send_sems, ref.recv_sems, ref.local_sems
    used, used_local, pending = [0], [0], []

    def new_id():
        used[0] += 1
        return used[0] - 1

    def send(src, dst, peer, arrives=None, when=None):
        k = new_id()
        copy = pltpu.make_async_remote_copy(
            src_ref=src, dst_ref=dst, send_sem=send_sems.at[k], recv_sem=recv_sems.at[k if arrives is None else arrives],
            device_id=peer, device_id_type=MESH,
        )
        if when is None:
            copy.start()
        else:
            pl.when(when)(copy.start)
        handle = [k, copy, False, when]
        pending.append(handle)
        return handle

    def sent(handle):
        if not handle[2]:
            if handle[3] is None:
                handle[1].wait_send()
            else:
                pl.when(handle[3])(handle[1].wait_send)
            handle[2] = True

    def received(handle, landed):
        k = handle if isinstance(handle, int) else handle[0]
        pltpu.make_async_remote_copy(
            src_ref=landed, dst_ref=landed, send_sem=send_sems.at[k], recv_sem=recv_sems.at[k],
            device_id=sib, device_id_type=MESH,
        ).wait_recv()

    def local(src, dst):
        k = used_local[0]
        used_local[0] += 1
        copy = pltpu.make_async_copy(src, dst, local_sems.at[k])
        copy.start()
        return copy

    lens = ref.lens
    ends, run = [], 0
    for i in range(lens.shape[1]):
        run = run + lens[0, i]
        ends.append(run)

    def kept(k):
        start = 0
        for i, end in enumerate(ends):
            start = start + jnp.where(end <= k * CHUNK, lens[0, i], 0)
        return jnp.where(k * CHUNK - start == 0, 0.0, 1.0)

    def live_rows(r, size):
        places = r + lax.broadcasted_iota(jnp.int32, (size, 1), 0)
        return (places < ends[-1]).astype(F32)

    small_all, packed = ref.small_all, ref.packed
    states_at = ref.ema_params.shape[1]
    params = jnp.zeros((states_at, 128), F32)
    for p in range(4):
        v = ref.ema_params[p].astype(F32)
        v = jnp.concatenate([v, jnp.zeros((states_at, 128 - v.shape[1]), F32)], axis=1)
        params = params + (pltpu.roll(v, p * 32, 1) if p else v)
    packed[0:states_at, :] = params.astype(LOW)
    singles = [ref.norm_gains[p : p + 1, :] for p in range(3)] + [ref.attn_params[...]]
    row = jnp.zeros((1, 128), F32)
    for p, v in enumerate(singles):
        v = jnp.concatenate([v.astype(F32), jnp.zeros((1, 128 - v.shape[1]), F32)], axis=1)
        row = row + (pltpu.roll(v, p * 32, 1) if p else v)
    packed[16:32, :] = jnp.broadcast_to(row, (16, 128)).astype(LOW)
    lane_group = lax.broadcasted_iota(jnp.int32, (1, 128), 1) // 32

    def slot(pc, py, px, pz):
        return (pc * 4 + py * 2 + px) * depth + pz

    def small_start():
        return [send(packed, small_all.at[slot(c, y, x, z)], zs[d]) for d in range(1, depth)]

    def small_relay(handles):
        for d, handle in enumerate(handles):
            received(handle, small_all.at[slot(c, y, x, (z + depth - 1 - d) % depth)])
        small_all[slot(c, y, x, z)] = packed[...]
        mine = small_all.at[pl.ds(slot(c, y, x, 0), depth)]
        return [send(mine, mine, place(z, *p)) for p in plane]

    def small_finish(handles):
        for handle, p in zip(handles, plane):
            received(handle, small_all.at[pl.ds(slot(*p, 0), depth)])
        states = ema_in.shape[0] // (4 * tiles)
        gains[...] = jnp.zeros_like(gains)
        attn[...] = jnp.zeros_like(attn)
        for t in range(tiles):
            pz, pc = t // 2, t % 2
            got = [small_all[slot(pc, f // 2, f % 2, pz)].astype(F32)[0 : states + 8, :] for f in range(4)]
            for p in range(4):
                v = jnp.zeros_like(got[0])
                for f in range(4):
                    turn = (f - p) * 32 % 128
                    v = jnp.where(lane_group == f, pltpu.roll(got[f], turn, 1) if turn else got[f], v)
                ema_in[pl.ds(p * states * tiles + t, states, stride=tiles), :] = v[0:states]
                row = v[states : states + 1]
                if p < 3:
                    gains[p : p + 1, t * 128 : (t + 1) * 128] = row
                    if p == 2:
                        omega_in[t : t + 1, :] = row
                    continue
                for f in range(4):
                    turn = (t % 2 * 64 - f * 16) % 128
                    mine = lax.broadcasted_iota(jnp.int32, (1, 128), 1) // 16 == t % 2 * 4 + f
                    moved = pltpu.roll(row, turn, 1) if turn else row
                    attn[t // 2 : t // 2 + 1, :] += jnp.where(mine, moved, 0.0)

    lane = lax.broadcasted_iota(jnp.int32, (1, 128), 1)
    shift = fs * 32

    def mix_align():
        raw, win, line_up = ref.s[MIX], ref.mix_win, ref.by_time
        line_up[0 : win.shape[1], :] = jnp.zeros((win.shape[1], 128), F32)

        def load(r):
            line_up[at_rows(shift + r, 32, 32), :] = raw[pl.ds(r, 32), :].astype(F32)

        row_loop(raw.shape[0], 32, load)
        for t in range(win.shape[1] // 128):
            win[:, t * 128 : (t + 1) * 128] = line_up[t * 128 : (t + 1) * 128, :].T.astype(LOW)

    weights = {m: ref.w[m] for m in SHARDED}
    block_shape = {m: (w.shape[0] // depth, w.shape[1] // 2) for m, w in weights.items()}

    def block(m, zz, yy):
        rb, cb = block_shape[m]
        return weights[m].at[at_rows(zz * rb, rb), at_rows(yy * cb, cb, 128)]

    def piece(m, src_c, src_x):
        rb, cb = block_shape[m]
        half = cb // 2
        if m in (VALUE, UP):
            return weights[m].at[at_rows(z * rb + src_c * (rb // 2), rb // 2), at_rows(y * cb + src_x * half, half, 128)]
        return weights[m].at[at_rows(z * rb, rb), at_rows(y * cb + src_x * half, half, 128)]

    def move(src, dst):
        rows_at_once = 32

        def step(r):
            dst[pl.ds(r, rows_at_once), :] = src[pl.ds(r, rows_at_once), :]

        row_loop(src.shape[0], rows_at_once, step)

    spare, near, loads, top = ref.up_low, {MIX: ref.mix_win}, {}, 0
    for m in (VALUE, MERGE, UP, DOWN):
        tall, wide = ref.s[m].shape
        near[m] = spare.at[top : top + tall, 0:wide]
        loads[m] = local(ref.s[m], near[m])
        top += tall
    for k in (TOK, COT):
        loads[k] = local(ref.acts[k - TOK], (tok, cot)[k - TOK])
    barrier = pltpu.get_barrier_semaphore()
    peers = [place(z, *p) for p in plane] + zs[1:]
    for peer in peers:
        pl.semaphore_signal(barrier, inc=1, device_id=peer, device_id_type=MESH)
    pl.semaphore_wait(barrier, len(peers))

    swaps = {m: [] for m in SHARDED}

    def swap_start(m):
        shard = near[m]
        if m in loads:
            loads[m].wait()
        if m == MIX:
            first, last = 1 - (fs + 2) // 3, fs // 3
            middle = 1 - first - last
            for peer, pc, px in mates + ((None, c, x),):
                pq = pc * 2 + px
                tiles_at = (
                    first * 2 * pq,
                    (first + last) * (1 + 2 * pq) + middle * (1 + pq),
                    first * 8 + last * (2 + 2 * pq) + middle * (5 + pq),
                )
                for i, tile in enumerate(tiles_at):
                    src = shard.at[:, at_rows(tile * 128, 128, 128)]
                    dst = ref.mix_in.at[x, at_rows(c * 128, 128), pl.ds(i * 128, 128)]
                    if peer is None:
                        move(src, dst)
                    else:
                        swaps[m].append((send(src, dst, peer), pc, px, i))
            return
        if m in (VALUE, UP):
            wide = shard.shape[1] // 4
            for peer, pc, px in mates + ((None, c, x),):
                src = shard.at[:, at_rows((pc * 2 + px) * wide, wide, 128)]
                if peer is None:
                    move(src, piece(m, c, x))
                else:
                    swaps[m].append((send(src, piece(m, c, x), peer), pc, px, 0))
            return
        tall = shard.shape[0] // 2
        swaps[m].append((send(shard.at[at_rows((1 - x) * tall, tall), :], piece(m, c, x), xn), c, 1 - x, 0))
        move(shard.at[at_rows(x * tall, tall), :], piece(m, c, x))

    z_ids, z_sends, y_sends = {}, {}, {}

    def swap_finish(m):
        for handle, pc, px, i in swaps[m]:
            if m == MIX:
                received(handle, ref.mix_in.at[px, at_rows(pc * 128, 128), pl.ds(i * 128, 128)])
            else:
                received(handle, piece(m, pc, px))
        if m == MIX:
            only = (q == 3).astype(F32)
            low_y = (y == 0).astype(F32)
            lead = jnp.broadcast_to(jnp.maximum(low_y, only), (1, 128))
            rb, cb = block_shape[m]
            a, b, w = ref.mix_in.at[0], ref.mix_in.at[1], weights[m]

            def combine(r):
                at = pl.ds(r, 64)
                to = at_rows(z * rb + r, 64)

                def put(i, v):
                    w[to, at_rows(y * cb + i * 128, 128, 128)] = v.astype(LOW)

                put(0, a[at, 0:128].astype(F32) * lead)
                put(1, a[at, 128:256])
                put(2, a[at, 256:384].astype(F32) + b[at, 0:128].astype(F32) * lead)
                put(3, b[at, 128:256])
                put(4, b[at, 256:384])

            row_loop(rb, 64, combine)

    def y_own(m):
        y_sends[m] = [(3, send(block(m, z, y), block(m, z, y), yn))]

    def z_start(m):
        own = block(m, z, y)
        ids = [new_id() for _ in range(3)]
        z_ids[m] = ids
        z_sends[m] = [
            send(own, own, place(partner, c, y, x), ids[2]),
            send(own, own, place(far_mid, c, y, x), ids[1], middle),
            send(own, own, place(far_mid, c, y, x), ids[0], outer),
        ]

    def z_pass(m, steps=(1, 0)):
        for i in steps:
            there = block(m, line[i], y)
            pl.when(middle)(functools.partial(received, z_ids[m][i], there))
            z_sends[m].append(send(there, there, place(partner, c, y, x), z_ids[m][i], middle))

    def y_forward(m, steps=(2, 1, 0)):
        for i in steps:
            there = block(m, line[i], y)
            if i == 2:
                received(z_ids[m][i], there)
            else:
                pl.when(outer)(functools.partial(received, z_ids[m][i], there))
            y_sends[m].append((i, send(there, there, yn)))

    def y_finish(m):
        for i, handle in y_sends[m]:
            received(handle, block(m, line[i], 1 - y))

    def group_rows(c, x):
        return at_rows((c * 2 + x) * rows, rows)

    def part_rows(c, x, first, count):
        return at_rows((c * 2 + x) * rows + first, count)

    def gather_start(buf, first=0, count=None):
        count = rows if count is None else count
        own = buf.at[part_rows(c, x, first, count), :]
        return [(first, count), send(own, own, xn), send(own, own, sib)]

    def gather_relay(buf, handles):
        other = buf.at[part_rows(c, 1 - x, *handles[0]), :]
        received(handles[1], other)
        handles.append(send(other, other, sib))

    def gather_finish(buf, handles):
        received(handles[2], buf.at[part_rows(1 - c, x, *handles[0]), :])
        received(handles[3], buf.at[part_rows(1 - c, 1 - x, *handles[0]), :])

    total = ref.total
    stage = [ref.stage.at[0], ref.stage.at[1], ref.stage.at[2], ref.hidden_mul]
    staged = [[], [], [], []]

    def stage_out(k, first, count, extra=None):
        def put(r):
            at = pl.ds(r, 32)
            v = total[at, :]
            if extra is not None:
                v = v + extra[at, :].astype(F32)
            stage[k][at, :] = v.astype(LOW)

        row_loop(count, 32, put, first)

    def stage_free(k):
        for handle in staged[k]:
            sent(handle)
        staged[k] = []

    def reduce_early(partial, sibs, cross, slot=2):
        halves = (pl.ds(0, rows // 2), pl.ds(rows // 2, rows // 2))
        for k, px in ((0, 1 - x), (1, x)):
            partial(1 - c, px)
            stage_free(k)
            stage_out(k, 0, rows)
            staged[k] = [send(stage[k], sibs[k], sib)]
        first, second = staged[0][0], staged[1][0]
        partial(c, 1 - x)
        received(first, sibs[0])
        stage_free(slot)
        for i, half in enumerate(halves):
            stage_out(slot, i * (rows // 2), rows // 2, sibs[0])
            staged[slot].append(send(stage[slot].at[half, :], cross.at[half, :], xn))
        return second, list(zip(staged[slot], (cross.at[half, :] for half in halves)))

    def reduce_late(partial, sibs, cross, handles, consume):
        partial(c, x)
        received(handles[0], sibs[1])
        for i, (handle, half) in enumerate(handles[1]):
            received(handle, half)
            consume(i * (rows // 2), rows // 2)

    def reduced(r, size, sibs, cross):
        at = pl.ds(r, size)
        return total[at, :] + sibs[1][at, :].astype(F32) + cross[at, :].astype(F32)

    sibs_a, sibs_b = ((r.at[0], r.at[1]) for r in (ref.sibs_a, ref.sibs_b))
    cross_a, cross_b = ref.cross_a, ref.cross_b
    sibs_c, cross_c = (ref.gc.at[2 * rows : 3 * rows, :], ref.gc.at[3 * rows : 4 * rows, :]), ref.update_in

    w_up = weights[UP]
    y_out = {
        DOWN: ref.yo[1],
        UP: ref.yo[0],
        MERGE: ref.gc.at[0 : weights[MERGE].shape[0], 0 : block_shape[MERGE][1]],
        MIX: w_up.at[:, 0 : block_shape[MIX][1]],
        VALUE: w_up.at[:, block_shape[MIX][1] : block_shape[MIX][1] + block_shape[VALUE][1]],
    }
    y_in = {m: ref.yi[m] for m in SHARDED}
    z_in = {m: ref.zi[m] for m in SHARDED}
    f_in = {m: ref.fi[m] for m in SHARDED}
    gy, gz, gf = {}, {}, {}

    def y_grad_send(m, product, steps=(0, 1, 2, 3)):
        rb, cb = block_shape[m]
        if m not in gy:
            gy[m], gz[m] = {}, [new_id() for _ in range(4)]
        for i in steps:
            at = at_rows(line[i] * rb, rb)
            y_out[m][at, :] = product(line[i], 1 - y).astype(LOW)
            gy[m][i] = send(y_out[m].at[at, :], y_in[m].at[at, :], yn)

    def y_grad_add(m, product, steps=(0, 1, 2, 3)):
        rb, cb = block_shape[m]
        for i in steps:
            at = at_rows(line[i] * rb, rb)
            own = product(line[i], y)
            received(gy[m][i], y_in[m].at[at, :])
            y_in[m][at, :] = (own + y_in[m][at, :].astype(F32)).astype(LOW)
            if i < 3:
                send(
                    y_in[m].at[at, :], z_in[m].at[i], place(partner, c, y, x), gz[m][i], outer if i < 2 else None
                )

    def z_relay(m, steps=(0, 1)):
        rb, cb = block_shape[m]
        for i in steps:
            at = at_rows(line[i] * rb, rb)

            @pl.when(middle)
            def _(i=i, at=at):
                received(gz[m][i], z_in[m].at[i])
                y_in[m][at, :] = (y_in[m][at, :].astype(F32) + z_in[m][i].astype(F32)).astype(LOW)

            send(y_in[m].at[at, :], z_in[m].at[3], place(line[i], c, y, x), gz[m][3], middle)

    def z_grad_add(m):
        rb, cb = block_shape[m]
        for i in (2, 3):
            received(gz[m][i], z_in[m].at[i])

        def add(r):
            at = at_rows(z * rb + r, 64)
            v = y_in[m][at, :].astype(F32)
            for i in (2, 3):
                v = v + z_in[m][i, pl.ds(r, 64), :].astype(F32)
            y_in[m][at, :] = v.astype(LOW)

        row_loop(rb, 64, add)
        gf[m] = []
        if m in (MERGE, DOWN):
            land = f_in[m].at[at_rows(x * rb, rb), :]

            def part(px):
                return y_in[m].at[at_rows(z * rb, rb), at_rows(px * (cb // 2), cb // 2, 128)]

            gf[m].append((send(part(1 - x), land, xn), f_in[m].at[at_rows((1 - x) * rb, rb), :]))
            move(part(x), land)
            return
        half = rb // 2

        def land_at(pc, px):
            if m == MIX:
                return f_in[m].at[pc * 2 + px]
            wide = f_in[m].shape[1] // 4
            return f_in[m].at[:, at_rows((pc * 2 + px) * wide, wide, 128)]

        def part(pc, px):
            if m == MIX:
                return y_in[m].at[at_rows(z * rb + pc * half, half), at_rows(px * 256, 384, 128)]
            return y_in[m].at[at_rows(z * rb + pc * half, half), at_rows(px * (cb // 2), cb // 2, 128)]

        for peer, pc, px in mates:
            gf[m].append((send(part(pc, px), land_at(c, x), peer), land_at(pc, px)))
        move(part(c, x), land_at(c, x))

    def grad_out(m):
        for handle, landed in gf[m]:
            received(handle, landed)
        if m != MIX:
            return
        out, src, line_up = ref.g_mix, f_in[MIX], ref.by_time
        first, last = (fs == 0).astype(F32), (fs == 3).astype(F32)
        mid = 1.0 - first - last
        first, last, mid = (jnp.broadcast_to(v, (1, 128)) for v in (first, last, mid))

        def get(p, t):
            return src[p, :, t * 128 : (t + 1) * 128].astype(F32)

        for tile in range(9):
            v = first * (get(tile // 2, tile % 2) if tile < 8 else src[q, :, 256:384].astype(F32))
            if tile == 0:
                v = v + (mid + last) * get(3, 0)
            else:
                v = v + mid * get((tile - 1) % 4, 1 + (tile - 1) // 4)
                v = v + last * get((tile - 1) // 2, 1 + (tile - 1) % 2)
            line_up[tile * 128 : (tile + 1) * 128, :] = v.T

        def write(r):
            out[pl.ds(r, 32), :] = line_up[at_rows(shift + r, 32, 32), :].astype(LOW)

        row_loop(out.shape[0], 32, write)

    h_small = small_start()
    swap_start(VALUE)
    mix_align()
    h_small = small_relay(h_small)
    swap_start(MERGE)
    swap_start(MIX)
    swap_finish(VALUE)
    y_own(VALUE)
    z_start(VALUE)

    nl, ml, n2, gc, gm = (ref.nl, ref.ml, ref.n2, ref.gc, ref.gm)
    by_time, out_time, back_time = ref.by_time, ref.out_time, ref.back_time

    def centre(v):
        cen = v - jnp.mean(v, axis=-1, keepdims=True)
        return cen, lax.rsqrt(jnp.mean(cen * cen, axis=-1, keepdims=True) + 1e-05)

    def norm_one(r):
        cen, rate = centre(tok[pl.ds(r, 16), :].astype(F32))
        v = cen * rate * gains[0:1, :]
        nl[at_rows(q * rows + r, 16), :] = v.astype(LOW)
        for s in range(tiles):
            by_time[pl.ds(r * tiles + s, 16, stride=tiles), :] = v[:, s * 128 : (s + 1) * 128]

    small_finish(h_small)
    loads[TOK].wait()
    row_loop(rows, 16, norm_one)
    h_nl = gather_start(nl)
    swap_start(UP)
    swap_finish(MERGE)
    y_own(MERGE)
    swap_finish(MIX)
    y_own(MIX)
    z_pass(VALUE)
    z_start(MIX)
    z_start(MERGE)

    def cot_low(r):
        at = pl.ds(r, 32)
        gc[at_rows(q * rows + r, 32), :] = (cot[at, :].astype(F32) * live_rows(r, 32)).astype(LOW)

    def load_ema():
        return ema_in[...].reshape(4, -1, tiles, 128)

    _, _, rate_all, weight_all = ema_coefficients(load_ema())
    omega = omega_in[...]
    marks = ref.marks

    def at_time(t):
        return at_rows(t * tiles, tiles, 8)

    def ema_chunk(k, state):
        state = state * kept(k)
        marks[k] = state

        def step(i, state):
            t = k * CHUNK + i
            v = by_time[at_time(t), :]
            state = rate_all * state + v[None]
            out_time[at_time(t), :] = jnp.sum(weight_all * state, axis=0) + omega * v
            return state

        return lax.fori_loop(0, CHUNK, step, state, unroll=4)

    lax.fori_loop(0, rows // CHUNK, ema_chunk, jnp.zeros_like(rate_all))

    def mixed(r):
        for s in range(tiles):
            at = pl.ds(r * tiles + s, 16, stride=tiles)
            v = out_time[at, :]
            gate = jax.nn.sigmoid(v)
            ml[at_rows(q * rows + r, 16), s * 128 : (s + 1) * 128] = (v * gate).astype(LOW)
            out_time[at, :] = slope_of(v, gate)

    row_loop(rows, 16, mixed)
    h_ml = gather_start(ml)
    swap_start(DOWN)
    loads[COT].wait()
    row_loop(rows, 32, cot_low)
    y_forward(VALUE)
    z_pass(MIX, (1,))
    gather_relay(nl, h_nl)
    h_gc = gather_start(gc)
    y_forward(MIX, [2])
    z_pass(MIX, (0,))
    gather_finish(nl, h_nl)
    swap_finish(UP)
    z_start(UP)
    y_forward(MIX, [1])
    z_pass(MERGE)
    y_finish(VALUE)

    value_low, value_slope = ref.value_low, ref.value_slope
    vq = value_low.shape[1]

    def value_block(r):
        total[:, :vq] = mm(nl[pl.ds(r, rows), :], weights[VALUE][...])

        def act(s):
            v = total[pl.ds(s, 32), :vq]
            gate = jax.nn.sigmoid(v)
            value_low[at_rows(r + s, 32), :] = (v * gate).astype(LOW)
            value_slope[at_rows(r + s, 32), :] = slope_of(v, gate).astype(LOW)

        row_loop(rows, 32, act)

    row_loop(4 * rows, rows, value_block)
    y_forward(MIX, [0])
    y_own(UP)
    gather_relay(ml, h_ml)
    y_forward(MERGE)
    swap_finish(DOWN)
    z_start(DOWN)
    gather_finish(ml, h_ml)
    z_pass(UP, (1,))
    y_own(DOWN)
    gather_relay(gc, h_gc)
    z_pass(UP, (0,))
    y_finish(MIX)

    w_mix, reset_w = weights[MIX], ref.reset_w
    half_mix = w_mix.shape[1] // 2

    def fix_reset(r):
        at = pl.ds(r, 64)
        reset_w[at, 0:128] = w_mix[at, 384:512]
        reset_w[at, 128:256] = (w_mix[at, 512:640].astype(F32) + w_mix[at, half_mix : half_mix + 128].astype(F32)).astype(LOW)

    row_loop(width, 64, fix_reset)

    def w_update():
        return w_mix[:, 0:256]

    def w_shared():
        return w_mix[:, 256:384]

    def w_late():
        return w_mix[:, half_mix + 128 : half_mix + 384]

    def w_hidden():
        return w_mix[:, half_mix + 384 : half_mix + 640]

    scale = float(STRETCH) ** -0.5
    stretch = STRETCH
    shared_pre, query, key, probs = ref.shared_pre, ref.query, ref.key, ref.probs
    probs_low = ref.probs_low
    shared_pre[...] = mm(ml[group_rows(c, x), :], w_shared())
    sv = shared_pre[...]
    shared = sv * jax.nn.sigmoid(sv)
    query[...] = (shared * attn[0:1, :] + attn[1:2, :]).astype(LOW)
    key[...] = (shared * attn[2:3, :]).astype(LOW)
    bias = pltpu.roll(jnp.broadcast_to(attn[3:4, :], (stretch, stretch)), 0, 1, stride=1, stride_axis=0).T
    row_id = lax.broadcasted_iota(jnp.int32, (stretch, stretch), 0)
    col_id = lax.broadcasted_iota(jnp.int32, (stretch, stretch), 1)
    for n in range(rows // stretch):
        at = pl.ds(n * stretch, stretch)
        scores = mm_nt(query[at, :], key[at, :]) * scale + bias
        scores = jnp.where(row_id >= col_id, scores, -1000000000.0)
        ex = jnp.exp(scores - jnp.max(scores, axis=-1, keepdims=True))
        pr = ex / jnp.sum(ex, axis=-1, keepdims=True)
        probs[at, :] = pr
        probs_low[at_rows(q * rows + n * stretch, stretch), :] = pr.astype(LOW)
    own_probs = probs_low.at[group_rows(c, x), :]
    h_probs = [send(own_probs, own_probs, peer) for peer, _, _ in mates]

    mix_pack, update_in = ref.mix_pack, ref.update_in
    hidden_at = pl.ds(mix_pack.shape[1] - 256, 256)
    update_out = mix_pack.at[:, hidden_at]

    def update_block(r):
        update_out[pl.ds(r, rows), :] = mm(ml[pl.ds(r, rows), :], w_update()).astype(LOW)

    row_loop(4 * rows, rows, update_block)
    part_w = width // 4
    own_cols = at_rows(q * part_w, part_w, 128)
    h_update = [
        send(update_out.at[group_rows(pc, px), :], update_in.at[:, own_cols], peer) for peer, pc, px in mates
    ]
    update_in[:, own_cols] = update_out[group_rows(c, x), :]

    reset_gate, reset_slope = ref.reset_gate, ref.reset_slope

    def reset_block(r):
        at = pl.ds(r, rows)
        total[:, 0:256] = mm(ml[at, :], reset_w[...])
        total[:, 256:512] = mm(ml[at, :], w_late())

        def act(s):
            v = total[pl.ds(s, 32), :vq]
            gate = jax.nn.sigmoid(v)
            reset_gate[at_rows(r + s, 32), :] = (v * gate).astype(LOW)
            reset_slope[at_rows(r + s, 32), :] = slope_of(v, gate).astype(LOW)

        row_loop(rows, 32, act)

    row_loop(4 * rows, rows, reset_block)
    y_forward(UP, [2])
    z_pass(DOWN, (1,))
    for handle, (_, pc, px) in zip(h_probs, mates):
        received(handle, probs_low.at[group_rows(pc, px), :])

    gated = ref.gated

    def attend(r):
        at = pl.ds(r, stretch)
        total[0:stretch, :vq] = mm(probs_low[at, :], value_low[at, :])

        def act(s):
            v = total[pl.ds(s, 32), :vq]
            to = at_rows(r + s, 32)
            gated[to, :] = (v * reset_gate[to, :].astype(F32)).astype(LOW)
            reset_slope[to, :] = (v * reset_slope[to, :].astype(F32)).astype(LOW)

        row_loop(stretch, 32, act)

    row_loop(4 * rows, stretch, attend)
    y_forward(UP, [1])
    z_pass(DOWN, (0,))
    y_finish(MERGE)

    def merge_partial(c, x):
        at = group_rows(c, x)
        total[...] = mm(gated[at, :], weights[MERGE][...])
        total[:, own_cols] += mm(ml[at, :], w_hidden())

    h_red = reduce_early(merge_partial, sibs_a, cross_a)
    y_forward(UP, [0])
    for handle, (_, pc, px) in zip(h_update, mates):
        received(handle, update_in.at[:, at_rows((pc * 2 + px) * part_w, part_w, 128)])
    gather_finish(gc, h_gc)
    y_forward(DOWN, [2])

    after, hidden_mul, update_mul = ref.after, ref.hidden_mul, ref.update_mul

    def norm_two(r):
        at = pl.ds(r, 16)
        v = reduced(r, 16, sibs_a, cross_a)
        gate = jax.nn.sigmoid(v)
        hidden = v * gate
        u = jax.nn.sigmoid(update_in[at, :].astype(F32))
        xv = tok[at, :].astype(F32)
        av = u * hidden + (1.0 - u) * xv
        after[at, :] = av
        hidden_mul[at, :] = (u * slope_of(v, gate)).astype(LOW)
        update_mul[at, :] = ((hidden - xv) * u * (1.0 - u)).astype(LOW)
        cen, rate = centre(av)
        n2[at_rows(q * rows + r, 16), :] = (cen * rate * gains[1:2, :]).astype(LOW)

    h_n2 = []

    def take_merge(first, count):
        row_loop(count, 16, norm_two, first, 2)
        h_n2.append(gather_start(n2, first, count))

    reduce_late(merge_partial, sibs_a, cross_a, h_red, take_merge)
    y_forward(DOWN, [1])
    gather_relay(n2, h_n2[0])
    y_forward(DOWN, [0])
    gather_relay(n2, h_n2[1])
    for handles in h_n2:
        gather_finish(n2, handles)
    y_finish(UP)

    up_low, up_slope = ref.up_low, ref.up_slope
    for m in SHARDED:
        for swap in swaps[m]:
            sent(swap[0])

    def up_block(r):
        total[...] = mm(n2[pl.ds(r, rows), :], weights[UP][...])

        def act(s):
            v = total[pl.ds(s, 16), :]
            gate = jax.nn.sigmoid(v)
            up_low[at_rows(r + s, 16), :] = (v * gate).astype(LOW)
            up_slope[at_rows(r + s, 16), :] = slope_of(v, gate).astype(LOW)

        row_loop(rows, 16, act)

    row_loop(4 * rows, rows, up_block)

    def cols_of(m, yy):
        cb = block_shape[m][1]
        return at_rows(yy * cb, cb, 128)

    def rows_of(m, zz):
        rb = block_shape[m][0]
        return at_rows(zz * rb, rb, 128)

    def down_product(zz, yy):
        return mm_tn(up_low[:, rows_of(DOWN, zz)], gc[:, cols_of(DOWN, yy)])

    y_grad_send(DOWN, down_product)
    y_finish(DOWN)

    def down_partial(c, x):
        total[...] = mm(up_low[group_rows(c, x), :], weights[DOWN][...])

    def up_back(r):
        at = pl.ds(r, rows)
        total[...] = mm_nt(gc[at, :], weights[DOWN][...])

        def act(s):
            to = at_rows(r + s, 16)
            up_slope[to, :] = (total[pl.ds(s, 16), :] * up_slope[to, :].astype(F32)).astype(LOW)

        row_loop(rows, 16, act)

    row_loop(4 * rows, rows, up_back)
    grad_up = up_slope

    def two_partial(c, x):
        total[...] = mm_nt(grad_up[group_rows(c, x), :], weights[UP][...])

    def up_product(zz, yy):
        return mm_tn(n2[:, rows_of(UP, zz)], grad_up[:, cols_of(UP, yy)])

    h_red = reduce_early(two_partial, sibs_a, cross_a)
    y_grad_send(UP, up_product)
    y_grad_add(DOWN, down_product, (0, 1))
    for handle in h_gc[1:]:
        sent(handle)

    gain_sum, update_back = ref.gain_sum, hidden_mul
    gain_sum[...] = jnp.zeros_like(gain_sum)

    def norm_two_back(r):
        at = pl.ds(r, 16)
        g = reduced(r, 16, sibs_a, cross_a)
        cen, rate = centre(after[at, :])
        unit = cen * rate
        gain_sum[1] += g * unit
        g = g * gains[1:2, :]
        back = rate * (g - jnp.mean(g, axis=-1, keepdims=True) - unit * jnp.mean(g * unit, axis=-1, keepdims=True))
        back = back + cot[at, :].astype(F32) * live_rows(r, 16)
        gm[at_rows(q * rows + r, 16), :] = (back * hidden_mul[at, :].astype(F32)).astype(LOW)
        hidden_mul[at, :] = (back * update_mul[at, :].astype(F32)).astype(LOW)
        u = jax.nn.sigmoid(update_in[at, :].astype(F32))
        update_mul[at, :] = (back * (1.0 - u)).astype(LOW)

    h_gm = []

    def take_two(first, count):
        row_loop(count, 16, norm_two_back, first, 2)
        h_gm.append(gather_start(gm, first, count))

    reduce_late(two_partial, sibs_a, cross_a, h_red, take_two)
    for handle in h_update:
        sent(handle)
    update_grad = mix_pack.at[:, 0:256]
    own_rows = group_rows(c, x)
    h_update = [
        send(update_back.at[:, at_rows((pc * 2 + px) * part_w, part_w, 128)], update_grad.at[own_rows, :], peer)
        for peer, pc, px in mates
    ]
    update_grad[own_rows, :] = update_back[:, own_cols]

    y_grad_add(DOWN, down_product, (2, 3))
    z_relay(DOWN)
    y_grad_add(UP, up_product, (0, 1))
    gather_relay(gm, h_gm[0])
    gather_relay(gm, h_gm[1])
    y_grad_add(UP, up_product, (2,))
    for handles in h_gm:
        gather_finish(gm, handles)

    def merge_product(zz, yy):
        return mm_tn(gated[:, rows_of(MERGE, zz)], gm[:, cols_of(MERGE, yy)])

    for handle in z_sends[UP] + [h for _, h in y_sends[UP]]:
        sent(handle)
    y_grad_send(MERGE, merge_product)

    grad_probs, probs_in = ref.grad_probs, ref.probs_in

    def gated_back(r):
        at = pl.ds(r, rows)
        total[:, :vq] = mm_nt(gm[at, :], weights[MERGE][...])

        def act(s):
            to = at_rows(r + s, 32)
            g = total[pl.ds(s, 32), :vq]
            back = (g * reset_slope[to, :].astype(F32)).astype(LOW)
            mix_pack[to, 384:640] = back[:, 0:256]
            mix_pack[to, 640:768] = back[:, 128:256]
            mix_pack[to, 768:1024] = back[:, 256:512]
            mix_pack[to, hidden_at] = gm[to, own_cols]
            reset_gate[to, :] = (g * reset_gate[to, :].astype(F32)).astype(LOW)

        row_loop(rows, 32, act)

    row_loop(4 * rows, rows, gated_back)
    grad_att = reset_gate

    def probs_back(r):
        at = pl.ds(r, stretch)
        grad_probs[at, :] = mm_nt(grad_att[at, :], value_low[at, :]).astype(LOW)

    row_loop(4 * rows, stretch, probs_back)
    h_probs = [
        send(grad_probs.at[group_rows(pc, px), :], probs_in.at[i], peer) for i, (peer, pc, px) in enumerate(mates)
    ]
    for handle, (_, pc, px) in zip(h_update, mates):
        received(handle, update_grad.at[group_rows(pc, px), :])

    shared_grad = mix_pack.at[:, 256:384]

    def mixed_partial(cc, xx):
        at = group_rows(cc, xx)
        total[...] = (
            mm_nt(update_grad[at, :], w_update())
            + mm_nt(mix_pack[at, 384:640], reset_w[...])
            + mm_nt(mix_pack[at, 768:1024], w_late())
            + mm_nt(mix_pack[at, hidden_at], w_hidden())
        )


    def value_back(r):
        at = pl.ds(r, stretch)
        total[0:stretch, :vq] = mm_tn(probs_low[at, :], grad_att[at, :])

        def act(s):
            to = at_rows(r + s, 32)
            value_slope[to, :] = (total[pl.ds(s, 32), :vq] * value_slope[to, :].astype(F32)).astype(LOW)

        row_loop(stretch, 32, act)

    row_loop(4 * rows, stretch, value_back)
    grad_value = value_slope

    def value_product(zz, yy):
        return mm_tn(nl[:, rows_of(VALUE, zz)], grad_value[:, cols_of(VALUE, yy)])

    y_grad_send(VALUE, value_product, (0, 1))
    y_grad_add(UP, up_product, (3,))
    z_relay(UP)

    for i, handle in enumerate(h_probs):
        received(handle, probs_in.at[i])
    anti = (row_id + col_id == stretch - 1).astype(LOW)
    lag_sum = jnp.zeros((1, stretch), F32)
    grads_q = jnp.zeros((1, stretch), F32)
    grads_o = jnp.zeros((1, stretch), F32)
    grads_k = jnp.zeros((1, stretch), F32)
    for n in range(rows // stretch):
        at = pl.ds(n * stretch, stretch)
        to = at_rows(q * rows + n * stretch, stretch)
        g = grad_probs[to, :].astype(F32)
        for i in range(3):
            g = g + probs_in[i, at, :].astype(F32)
        pr = probs[at, :]
        gs = (pr * (g - jnp.sum(pr * g, axis=-1, keepdims=True))).astype(LOW)
        gq = mm(gs, key[at, :]) * scale
        gk = mm_tn(gs, query[at, :]) * scale
        lags = pltpu.roll(mm_nt(anti, gs), 1, 1, stride=1, stride_axis=0)
        lag_sum += jnp.sum(lags, axis=0, keepdims=True)
        sv = shared_pre[at, :]
        gate = jax.nn.sigmoid(sv)
        sh = sv * gate
        grads_q += jnp.sum(gq * sh, axis=0, keepdims=True)
        grads_o += jnp.sum(gq, axis=0, keepdims=True)
        grads_k += jnp.sum(gk * sh, axis=0, keepdims=True)
        gsh = gq * attn[0:1, :] + gk * attn[2:3, :]
        shared_grad[to, :] = (gsh * slope_of(sv, gate)).astype(LOW)
    attn_rows = (grads_q, grads_o, grads_k, lag_sum)
    own_shared = shared_grad.at[own_rows, :]
    h_shared = [send(own_shared, own_shared, peer) for peer, _, _ in mates]
    h_mixed = reduce_early(mixed_partial, sibs_a, cross_a)


    for handle, (_, pc, px) in zip(h_shared, mates):
        received(handle, shared_grad.at[group_rows(pc, px), :])

    def mix_product(zz, yy):
        return mm_tn(ml[:, rows_of(MIX, zz)], mix_pack[:, cols_of(MIX, yy)])

    y_grad_send(MIX, mix_product)
    y_grad_add(MERGE, merge_product)
    y_grad_send(VALUE, value_product, (2, 3))
    y_grad_add(VALUE, value_product, (0, 1))
    z_grad_add(DOWN)

    def mixed_own(cc, xx):
        mixed_partial(cc, xx)
        total[...] += mm_nt(shared_grad[own_rows, :], w_shared())


    def to_time(r):
        v = reduced(r, 16, sibs_a, cross_a)
        for s in range(tiles):
            at = pl.ds(r * tiles + s, 16, stride=tiles)
            out_time[at, :] = out_time[at, :] * v[:, s * 128 : (s + 1) * 128]

    reduce_late(mixed_own, sibs_a, cross_a, h_mixed, lambda first, count: row_loop(count, 16, to_time, first, 2))

    def value_partial(cc, xx):
        total[...] = mm_nt(grad_value[group_rows(cc, xx), :], weights[VALUE][...])

    h_red = reduce_early(value_partial, sibs_b, cross_b)
    z_relay(MERGE)
    y_grad_add(MIX, mix_product, (0,))

    held = ref.held
    ema = load_ema()
    damping, decay_gate, rate_all, weight_all = ema_coefficients(ema)
    omega = omega_in[...]
    half = rate_all.shape[0] // 2
    chunks = rows // CHUNK
    sums = []
    for part in range(2):
        js = slice(part * half, (part + 1) * half)
        rate, weight = rate_all[js], weight_all[js]

        def chunk(m, carry, js=js, rate=rate, weight=weight, part=part):
            k = chunks - 1 - m
            held[0] = marks[k, js]

            def ahead(i, state):
                state = rate * state + by_time[at_time(k * CHUNK + i), :][None]
                held[i + 1] = state
                return state

            lax.fori_loop(0, CHUNK, ahead, held[0], unroll=4)

            def back(n, carry):
                s, dw, dr, dom = carry
                i = CHUNK - 1 - n
                t = at_time(k * CHUNK + i)
                g = out_time[t, :]
                s = rate * s + g[None]
                dx = jnp.sum(weight * s, axis=0)
                if part == 0:
                    back_time[t, :] = dx + omega * g
                    dom = dom + g * by_time[t, :]
                else:
                    back_time[t, :] = back_time[t, :] + dx
                return s, dw + held[i + 1] * g[None], dr + held[i] * s, dom

            s, dw, dr, dom = lax.fori_loop(0, CHUNK, back, carry, unroll=2)
            return s * kept(k), dw, dr, dom

        if part:
            y_grad_add(MIX, mix_product, (1,))
            z_relay(VALUE)
            for handle in h_update:
                sent(handle)
            h_down = reduce_early(down_partial, sibs_c, cross_c, 3)
        zero = jnp.zeros_like(rate)
        sums.append(lax.fori_loop(0, chunks, chunk, (zero, zero, zero, jnp.zeros_like(omega))))
    small = ref.small_by_time
    rate_scale = ema.shape[1] ** (-0.5)
    for part in range(2):
        js = slice(part * half, (part + 1) * half)
        dw, dr = sums[part][1], sums[part][2] * weight_all[js]
        d_damp = dw * ema[2, js] * ema[3, js] * rate_scale - dr * decay_gate[js]
        parts = (
            d_damp * damping[js] * (1.0 - damping[js]),
            -dr * damping[js] * decay_gate[js] * (1.0 - decay_gate[js]),
            dw * damping[js] * ema[3, js] * rate_scale,
            dw * damping[js] * ema[2, js] * rate_scale,
        )
        for p in range(4):
            for j in range(half):
                small[pl.ds((p * 2 * half + part * half + j) * tiles, tiles), :] = parts[p][j]

    tile_rows = ref.tile_rows
    states = 4 * ema.shape[1]
    gain_two = jnp.sum(gain_sum[1], axis=0, keepdims=True)
    for t in range(tiles):
        at = (t % 2) * depth + t // 2
        tile_rows[at, 0:states, :] = small[pl.ds(t, states, stride=tiles), :]
        tail = jnp.concatenate(
            [
                jnp.zeros((1, 128), F32),
                gain_two[:, t * 128 : (t + 1) * 128],
                sums[0][3][t : t + 1],
                attn_rows[t // 2],
                jnp.zeros((4, 128), F32),
            ],
            axis=0,
        )
        tile_rows[at, states : states + 8, :] = tail
    sib_in, z_small, x_small, y_small = ref.sib_in, ref.z_small, ref.x_small, ref.y_small
    h_sib = send(tile_rows.at[pl.ds((1 - c) * depth, depth)], sib_in, sib)
    y_grad_add(MIX, mix_product, (2,))
    received(h_sib, sib_in)
    sib_in[...] += tile_rows[pl.ds(c * depth, depth)]
    h_zs = [send(sib_in.at[(z + d) % depth], z_small.at[d - 1], zs[d]) for d in range(1, depth)]
    z_relay(MIX)

    def norm_one_back(r):
        at = pl.ds(r, 16)
        ema_part = jnp.concatenate(
            [back_time[pl.ds(r * tiles + s, 16, stride=tiles), :] for s in range(tiles)], axis=1
        )
        g = reduced(r, 16, sibs_b, cross_b) + ema_part
        cen, rate = centre(tok[at, :].astype(F32))
        unit = cen * rate
        gain_sum[0] += g * unit
        g = g * gains[0:1, :]
        back = rate * (g - jnp.mean(g, axis=-1, keepdims=True) - unit * jnp.mean(g * unit, axis=-1, keepdims=True))
        ref.grad_tokens[at, :] = (back + update_mul[at, :].astype(F32)).astype(LOW)

    reduce_late(
        value_partial, sibs_b, cross_b, h_red, lambda first, count: row_loop(count, 16, norm_one_back, first, 2)
    )
    one_rows, one_z, one_sum, one_plane = ref.one_rows, ref.one_z, ref.one_sum, ref.one_plane
    gain_one = jnp.sum(gain_sum[0], axis=0, keepdims=True)
    for t in range(tiles):
        one_rows[t] = jnp.broadcast_to(gain_one[:, t * 128 : (t + 1) * 128], (8, 128))
    h_one = [send(one_rows.at[pl.ds((z + d) % depth * 2, 2)], one_z.at[d - 1], zs[d]) for d in range(1, depth)]
    y_grad_add(MIX, mix_product, (3,))
    z_grad_add(UP)
    z_grad_add(MERGE)
    y_grad_add(VALUE, value_product, (2, 3))
    for d, handle in enumerate(h_zs):
        received(handle, z_small.at[d])
    x_small[0] = sib_in[z] + z_small[0] + z_small[1] + z_small[2]
    h_x = send(x_small.at[0], x_small.at[1], xn)
    z_grad_add(MIX)
    for d, handle in enumerate(h_one):
        received(handle, one_z.at[d])
    one_sum[...] = one_rows[pl.ds(z * 2, 2)] + one_z[0] + one_z[1] + one_z[2]
    h_one = [send(one_sum.at[p[0]], one_plane.at[i], place(z, *p)) for i, p in enumerate(plane)]
    received(h_x, x_small.at[1])
    y_small[0] = x_small[0] + x_small[1]
    h_y = send(y_small.at[0], y_small.at[1], yn)
    z_grad_add(VALUE)

    def finish(r):
        at = pl.ds(r, 16)
        ref.result[at, :] = (after[at, :] + reduced(r, 16, sibs_c, cross_c)).astype(LOW)

    reduce_late(down_partial, sibs_c, cross_c, h_down, lambda first, count: row_loop(count, 16, finish, first, 2))
    for m in (DOWN, UP, MERGE):
        grad_out(m)
    received(h_y, y_small.at[1])
    totals = y_small[0] + y_small[1]
    ref.small_out[...] = pltpu.roll(totals, (128 - shift) % 128, 1)
    one = one_sum[c]
    for i, handle in enumerate(h_one):
        received(handle, one_plane.at[i])
        one = one + one_plane[i]
    ref.small_out[states : states + 1, :] = pltpu.roll(one, (128 - shift) % 128, 1)[0:1]
    for m in (MIX, VALUE):
        grad_out(m)
    ref.attn_out[...] = pltpu.roll(totals[states : states + 8], (128 - c * 64 - fs * 16) % 128, 1)
    for handle in pending:
        sent(handle)
    assert used[0] <= COPIES


def finish_kernel(result, grad_tokens, value, mix, merge, up, down, small, attn, *outs):
    for src, out in zip((result, grad_tokens, value, mix, merge, up, down), outs):

        def widen(r, src=src, out=out):
            out[pl.ds(r, 32), :] = src[pl.ds(r, 32), :].astype(out.dtype)

        row_loop(out.shape[0], 32, widen)
    gains, ema, per = outs[7:]
    states, mine = ema.shape[1:]
    gains[...] = small[4 * states : 4 * states + 3, :mine]
    for p in range(4):
        ema[p] = small[p * states : (p + 1) * states, :mine]
    per[...] = attn[3:4, : per.shape[1]]


def layer_on_device(depth, tokens, cotangent, lengths, value_proj, mix_proj, merge_proj, up_proj, down_proj, norm_gains, ema_params, attn_params):
    rows, width = tokens.shape
    fs = lax.axis_index(FS)
    window = -(-mix_proj.shape[1] // 128) * 128
    group = 4 * rows
    vq = value_proj.shape[1]
    fq = up_proj.shape[1]
    quarters = ((width, vq), (width, 10 * STRIP), (vq, width), (width, fq), (fq, width))
    tiles = width // 128
    states = ema_params.shape[2]
    small_rows = 4 * states + 8
    shape = jax.ShapeDtypeStruct
    mix_turned = mix_proj.T
    ema_turned = jnp.swapaxes(ema_params, 1, 2)
    shards = (value_proj, mix_turned, merge_proj, up_proj, down_proj)
    inputs = dict(
        acts=(tokens, cotangent),
        lens=lengths,
        norm_gains=norm_gains,
        ema_params=ema_turned,
        attn_params=attn_params[None],
        s=shards,
    )
    landings = [w.shape for w in shards]
    landings[MIX] = (4, mix_proj.shape[0], 3 * STRIP)
    outputs = dict(
        result=shape((rows, width), LOW),
        grad_tokens=shape((rows, width), LOW),
        fi=tuple(shape(d, LOW) for d in landings),
        g_mix=shape(mix_turned.shape, LOW),
        small_out=shape((small_rows, 128), F32),
        attn_out=shape((8, 128), F32),
    )
    copies = pltpu.SemaphoreType.DMA((COPIES,))

    def low(*dims):
        return pltpu.VMEM(dims, LOW)

    def full(*dims):
        return pltpu.VMEM(dims, F32)

    scratch = dict(
        send_sems=copies,
        recv_sems=copies,
        local_sems=pltpu.SemaphoreType.DMA((32,)),
        w=tuple(low(*d) for d in quarters),
        yo=tuple(low(quarters[m][0], quarters[m][1] // 2) for m in (UP, DOWN)),
        yi=tuple(low(r, k // 2) for r, k in quarters),
        zi=tuple(low(4, r // depth, k // 2) for r, k in quarters),
        mix_win=low(mix_proj.shape[0], window),
        small_all=low(8 * depth, 32, 128),
        packed=low(32, 128),
        ema_in=full(4 * states * tiles, 128),
        omega_in=full(tiles, 128),
        gains=full(8, width),
        attn=full(8, 128),
        tok=low(rows, width),
        cot=low(rows, width),
        nl=low(group, width),
        ml=low(group, width),
        n2=low(group, width),
        gc=low(group, width),
        gm=low(group, width),
        mix_in=low(2, 2 * mix_proj.shape[0], 3 * STRIP),
        reset_w=low(width, 256),
        value_low=low(group, vq),
        value_slope=low(group, vq),
        reset_gate=low(group, vq),
        reset_slope=low(group, vq),
        gated=low(group, vq),
        up_low=low(group, fq),
        up_slope=low(group, fq),
        update_in=low(rows, width),
        probs_low=low(group, STRETCH),
        probs=full(rows, STRETCH),
        shared_pre=full(rows, Z),
        query=low(rows, Z),
        key=low(rows, Z),
        grad_probs=low(group, STRETCH),
        probs_in=low(3, rows, STRETCH),
        mix_pack=low(group, 10 * STRIP),
        by_time=full(rows * tiles, 128),
        out_time=full(rows * tiles, 128),
        back_time=full(rows * tiles, 128),
        marks=full(rows // CHUNK, states, tiles, 128),
        held=full(CHUNK + 1, states // 2, tiles, 128),
        total=full(rows, width),
        stage=low(3, rows, width),
        sibs_a=low(2, rows, width),
        sibs_b=low(2, rows, width),
        cross_a=low(rows, width),
        cross_b=low(rows, width),
        after=full(rows, width),
        hidden_mul=low(rows, width),
        update_mul=low(rows, width),
        gain_sum=full(2, 16, width),
        small_by_time=full(4 * states * tiles, 128),
        tile_rows=full(tiles, small_rows, 128),
        sib_in=full(depth, small_rows, 128),
        z_small=full(depth - 1, small_rows, 128),
        x_small=full(2, small_rows, 128),
        y_small=full(2, small_rows, 128),
        one_rows=full(tiles, 8, 128),
        one_z=full(depth - 1, 2, 8, 128),
        one_sum=full(2, 8, 128),
        one_plane=full(7, 8, 128),
    )
    in_vmem = pl.BlockSpec(memory_space=pltpu.VMEM)
    specs = jax.tree.map(lambda _: in_vmem, inputs)
    anywhere = pl.BlockSpec(memory_space=pl.ANY)
    specs.update(
        lens=pl.BlockSpec(memory_space=pltpu.SMEM), acts=(anywhere,) * 2, s=tuple(in_vmem if m == MIX else anywhere for m in SHARDED)
    )
    in_leaves, in_tree = jax.tree.flatten(inputs)
    out_leaves, out_tree = jax.tree.flatten(outputs)
    scratch_leaves, scratch_tree = jax.tree.flatten(scratch, is_leaf=lambda v: not isinstance(v, (dict, tuple)))
    outs = pl.pallas_call(
        functools.partial(layer_kernel, (in_tree, out_tree, scratch_tree), depth),
        out_shape=tuple(out_leaves),
        in_specs=jax.tree.leaves(specs),
        out_specs=tuple(in_vmem for _ in out_leaves),
        scratch_shapes=scratch_leaves,
        compiler_params=pltpu.CompilerParams(collective_id=0, has_side_effects=True, vmem_limit_bytes=VMEM_BYTES),
        name="layer",
    )(*in_leaves)
    by = types.SimpleNamespace(**jax.tree.unflatten(out_tree, outs))
    grads = list(by.fi)
    grads[MIX] = by.g_mix
    wide = [shape(g.shape, F32) for g in (*grads, norm_gains, ema_turned)]
    *finals, attn_grad = pl.pallas_call(
        finish_kernel,
        out_shape=(shape((rows, width), LOW), shape((rows, width), LOW), *wide, shape((1, attn_params.shape[0]), F32)),
        in_specs=[in_vmem] * 9,
        out_specs=(in_vmem,) * 10,
        compiler_params=pltpu.CompilerParams(vmem_limit_bytes=VMEM_BYTES),
        name="finish",
    )(by.result, by.grad_tokens, *grads, by.small_out, by.attn_out)
    finals[2 + MIX] = finals[2 + MIX].T
    finals[-1] = jnp.swapaxes(finals[-1], 1, 2)
    return (*finals, attn_grad[0])


VMEM_BYTES = 64 << 20
COPIES = 256


def solution(mesh):
    in_specs = (
        P((DP, FS), None),
        P((DP, FS), None),
        P((DP, FS), None),
        P(DP, FS),
        P(DP, FS),
        P(DP, FS),
        P(DP, FS),
        P(DP, FS),
        P(None, (DP, FS)),
        P(None, (DP, FS), None),
        P((DP, FS)),
    )
    out_specs = (
        P((DP, FS), None),
        P((DP, FS), None),
        P(DP, FS),
        P(DP, FS),
        P(DP, FS),
        P(DP, FS),
        P(DP, FS),
        P(None, (DP, FS)),
        P(None, (DP, FS), None),
        P((DP, FS)),
    )
    fits = mesh.shape[DP] == 8 and mesh.shape[DP] // 2 * 4 * STRIP == V and mesh.shape[FS] * 4 * STRIP == V
    body = functools.partial(layer_on_device, mesh.shape[DP] // 2) if fits else on_device
    return jax.shard_map(body, mesh=mesh, in_specs=in_specs, out_specs=out_specs, check_vma=False)
```

```python
import functools
import types

import jax
import jax.numpy as jnp
from jax import lax
from jax.experimental import pallas as pl
from jax.experimental.pallas import tpu as pltpu
from jax.sharding import PartitionSpec as P

D = 1024
Z = 128
V = 2048
STRETCH = 128


DP, FS = "dp", "fsdp"
highest = lax.Precision.HIGHEST


def layer_norm(values, gain):
    centred = values - jnp.mean(values, axis=-1, keepdims=True)
    spread_sq = jnp.mean(centred * centred, axis=-1, keepdims=True)
    return centred * lax.rsqrt(spread_sq + 1e-05) * gain


def token_layout(length_row, row_count):
    places = jnp.arange(row_count, dtype=jnp.int32)
    running = jnp.cumsum(length_row)
    before = (running[None, :] <= places[:, None]).astype(jnp.int32)
    starts = jnp.sum(before * length_row[None, :], axis=1)
    return (places - starts, places < running[-1])


def ema_coefficients(ema):
    damping = jax.nn.sigmoid(ema[0])
    decay_gate = jax.nn.sigmoid(ema[1])
    keep_rate = 1.0 - damping * decay_gate
    weights_out = damping * ema[2] * ema[3] * ema.shape[1] ** (-0.5)
    return damping, decay_gate, keep_rate, weights_out


CHUNK = 32


def ema_forward_kernel(x_ref, ema_ref, omega_ref, keep_ref, y_ref, mark_ref):
    _, _, rate, weight = ema_coefficients(ema_ref[...])
    omega = omega_ref[...]

    def chunk(k, state):
        state = state * keep_ref[k][None]
        mark_ref[k] = state

        def step(i, state):
            t = k * CHUNK + i
            x = x_ref[t]
            state = rate * state + x[None]
            y_ref[t] = jnp.sum(weight * state, axis=0) + omega * x
            return state

        return lax.fori_loop(0, CHUNK, step, state, unroll=4)

    lax.fori_loop(0, x_ref.shape[0] // CHUNK, chunk, jnp.zeros_like(rate))


def ema_backward_kernel(x_ref, g_ref, ema_ref, omega_ref, keep_ref, mark_ref, dx_ref, dema_ref, domega_ref, h_ref):
    ema = ema_ref[...]
    damping, decay_gate, rate_all, weight_all = ema_coefficients(ema)
    omega = omega_ref[...]
    half = rate_all.shape[0] // 2
    chunks = x_ref.shape[0] // CHUNK
    sums = []
    for part in range(2):
        js = slice(part * half, (part + 1) * half)
        rate, weight = rate_all[js], weight_all[js]
        zero = jnp.zeros_like(rate)

        def chunk(m, carry, js=js, rate=rate, weight=weight, part=part):
            k = chunks - 1 - m
            h_ref[0] = mark_ref[k, js]

            def ahead(i, state):
                state = rate * state + x_ref[k * CHUNK + i][None]
                h_ref[i + 1] = state
                return state

            lax.fori_loop(0, CHUNK, ahead, h_ref[0], unroll=4)

            def back(n, carry):
                s, dw, dr, dom = carry
                i = CHUNK - 1 - n
                t = k * CHUNK + i
                g = g_ref[t]
                s = rate * s + g[None]
                dx = jnp.sum(weight * s, axis=0)
                if part == 0:
                    dx_ref[t] = dx + omega * g
                    dom = dom + g * x_ref[t]
                else:
                    dx_ref[t] = dx_ref[t] + dx
                dw = dw + h_ref[i + 1] * g[None]
                dr = dr + h_ref[i] * s
                return s, dw, dr, dom

            s, dw, dr, dom = lax.fori_loop(0, CHUNK, back, carry, unroll=2)
            return s * keep_ref[k][None], dw, dr, dom

        out = lax.fori_loop(0, chunks, chunk, (zero, zero, zero, jnp.zeros_like(omega)))
        sums.append(out)
    dw = jnp.concatenate([sums[0][1], sums[1][1]], axis=0)
    dr = jnp.concatenate([sums[0][2], sums[1][2]], axis=0) * weight_all
    scale = ema.shape[1] ** (-0.5)
    d_damp = dw * ema[2] * ema[3] * scale - dr * decay_gate
    dema_ref[0] = d_damp * damping * (1.0 - damping)
    dema_ref[1] = -dr * damping * decay_gate * (1.0 - decay_gate)
    dema_ref[2] = dw * damping * ema[3] * scale
    dema_ref[3] = dw * damping * ema[2] * scale
    domega_ref[...] = sums[0][3]


def ema_keep(position):
    starts = position.reshape(-1, CHUNK)[:, 0] != 0
    return jnp.broadcast_to(starts.astype(jnp.float32)[:, None, None], (starts.shape[0], 8, 128))


def ema_apply(x, ema, omega, keep):
    f32 = jnp.float32
    shape = jax.ShapeDtypeStruct
    return pl.pallas_call(
        ema_forward_kernel,
        out_shape=(shape(x.shape, f32), shape((keep.shape[0],) + ema.shape[1:], f32)),
        compiler_params=pltpu.CompilerParams(vmem_limit_bytes=32 << 20),
    )(x, ema, omega, keep)


def ema_reverse(x, g, ema, omega, keep, mark):
    f32 = jnp.float32
    shape = jax.ShapeDtypeStruct
    return pl.pallas_call(
        ema_backward_kernel,
        out_shape=(shape(x.shape, f32), shape(ema.shape, f32), shape(omega.shape, f32)),
        scratch_shapes=[pltpu.VMEM((CHUNK + 1, ema.shape[1] // 2) + ema.shape[2:], f32)],
        compiler_params=pltpu.CompilerParams(vmem_limit_bytes=32 << 20),
    )(x, g, ema, omega, keep, mark)


def silu_slope(values):
    logistic = jax.nn.sigmoid(values)
    return logistic * (1.0 + values * (1.0 - logistic))


def relative_table(rel_bias):
    lag_grid = (
        jnp.arange(STRETCH, dtype=jnp.int32)[:, None]
        - jnp.arange(STRETCH, dtype=jnp.int32)[None, :]
    )
    one_hot = (lag_grid[:, :, None] == jnp.arange(STRETCH, dtype=jnp.int32)[None, None, :]).astype(
        jnp.float32
    )
    bias_grid = jnp.einsum("ijl,l->ij", one_hot, rel_bias, precision=highest)
    return (lag_grid, one_hot, bias_grid)


def gather_forward(value_proj, mix_proj, merge_proj, up_proj, down_proj):
    first = (
        lax.all_gather(value_proj, DP, axis=0, tiled=True),
        lax.all_gather(mix_proj, DP, axis=0, tiled=True),
        lax.all_gather(merge_proj, DP, axis=0, tiled=True),
        lax.all_gather(up_proj, DP, axis=0, tiled=True),
        lax.all_gather(down_proj, DP, axis=0, tiled=True),
    )
    return (
        lax.all_gather(first[0], FS, axis=1, tiled=True),
        lax.all_gather(first[1], FS, axis=1, tiled=True),
        lax.all_gather(first[2], FS, axis=1, tiled=True),
        lax.all_gather(first[3], FS, axis=1, tiled=True),
        lax.all_gather(first[4], FS, axis=1, tiled=True),
    )


def reduce_gradients(value_grad, mix_grad, merge_grad, up_grad, down_grad):
    first = (
        lax.psum_scatter(
            value_grad.astype(jnp.bfloat16), DP, scatter_dimension=0, tiled=True
        ).astype(jnp.float32),
        lax.psum_scatter(
            mix_grad.astype(jnp.bfloat16), DP, scatter_dimension=0, tiled=True
        ).astype(jnp.float32),
        lax.psum_scatter(
            merge_grad.astype(jnp.bfloat16), DP, scatter_dimension=0, tiled=True
        ).astype(jnp.float32),
        lax.psum_scatter(
            up_grad.astype(jnp.bfloat16), DP, scatter_dimension=0, tiled=True
        ).astype(jnp.float32),
        lax.psum_scatter(
            down_grad.astype(jnp.bfloat16), DP, scatter_dimension=0, tiled=True
        ).astype(jnp.float32),
    )
    return (
        lax.psum_scatter(
            first[0].astype(jnp.bfloat16), FS, scatter_dimension=1, tiled=True
        ).astype(jnp.float32),
        lax.psum_scatter(
            first[1].astype(jnp.bfloat16), FS, scatter_dimension=1, tiled=True
        ).astype(jnp.float32),
        lax.psum_scatter(
            first[2].astype(jnp.bfloat16), FS, scatter_dimension=1, tiled=True
        ).astype(jnp.float32),
        lax.psum_scatter(
            first[3].astype(jnp.bfloat16), FS, scatter_dimension=1, tiled=True
        ).astype(jnp.float32),
        lax.psum_scatter(
            first[4].astype(jnp.bfloat16), FS, scatter_dimension=1, tiled=True
        ).astype(jnp.float32),
    )


def on_device(
    tokens,
    cotangent,
    lengths,
    value_proj,
    mix_proj,
    merge_proj,
    up_proj,
    down_proj,
    norm_gains,
    ema_params,
    attn_params,
):
    gains_full, ema_full, attn_full = (
        lax.all_gather(norm_gains, (DP, FS), axis=1, tiled=True),
        lax.all_gather(ema_params, (DP, FS), axis=1, tiled=True),
        lax.all_gather(attn_params, (DP, FS), axis=0, tiled=True),
    )
    value_full, mix_full, merge_full, up_full, down_full = gather_forward(
        value_proj, mix_proj, merge_proj, up_proj, down_proj
    )
    gains_float = gains_full.astype(jnp.float32)
    ema_float = ema_full.astype(jnp.float32)
    attn_float = attn_full.astype(jnp.float32)
    row_count = tokens.shape[0]
    position, live_rows = token_layout(lengths[0], row_count)
    tokens_float = tokens.astype(jnp.float32)
    normed, norm_back = jax.vjp(layer_norm, tokens_float, gains_float[0])
    normed_low = normed.astype(jnp.bfloat16)
    value_pre = jnp.dot(normed_low, value_full, preferred_element_type=jnp.float32)
    value_low = jax.nn.silu(value_pre).astype(jnp.bfloat16)

    lanes = (8, tokens.shape[1] // 8)
    ema_by_state = jnp.swapaxes(ema_float, 1, 2).reshape(4, -1, *lanes)
    omega = gains_float[2].reshape(lanes)
    keep = ema_keep(position)
    normed_rows = normed.reshape(row_count, *lanes)
    ema_rows, ema_marks = ema_apply(normed_rows, ema_by_state, omega, keep)
    ema_out = ema_rows.reshape(row_count, -1)
    mixed_low = jax.nn.silu(ema_out).astype(jnp.bfloat16)
    projected = jnp.dot(mixed_low, mix_full, preferred_element_type=jnp.float32)
    update_gate = jax.nn.sigmoid(projected[:, :D])
    shared_pre = projected[:, D : D + Z]
    reset_pre = projected[:, D + Z : D + Z + V]
    hidden_x = projected[:, D + Z + V :]
    shared = jax.nn.silu(shared_pre)
    reset_gate = jax.nn.silu(reset_pre)
    query_low = (shared * attn_float[:Z] + attn_float[Z : 2 * Z]).astype(jnp.bfloat16)
    key_low = (shared * attn_float[2 * Z : 3 * Z]).astype(jnp.bfloat16)
    block_count = row_count // STRETCH
    lag_grid, one_hot, bias_grid = relative_table(attn_float[3 * Z :])
    query_blocks = query_low.reshape(block_count, STRETCH, Z)
    key_blocks = key_low.reshape(block_count, STRETCH, Z)
    value_blocks = value_low.reshape(block_count, STRETCH, V)
    score_scale = Z ** (-0.5)

    def block_scores():
        raw_scores = (
            jnp.einsum("nik,njk->nij", query_blocks, key_blocks, preferred_element_type=jnp.float32)
            * score_scale
            + bias_grid
        )
        return jnp.where(lag_grid >= 0, raw_scores, -1000000000.0)

    scores = block_scores()
    row_max = jnp.max(scores, axis=-1, keepdims=True)
    log_total = row_max + jnp.log(jnp.sum(jnp.exp(scores - row_max), axis=-1, keepdims=True))
    probs_low = jnp.exp(scores - log_total).astype(jnp.bfloat16)
    attended = jnp.einsum(
        "nij,njv->niv", probs_low, value_blocks, preferred_element_type=jnp.float32
    ).reshape(row_count, V)
    gated_low = (attended * reset_gate).astype(jnp.bfloat16)
    hidden_in = jnp.dot(gated_low, merge_full, preferred_element_type=jnp.float32) + hidden_x
    hidden = jax.nn.silu(hidden_in)
    after_mixer = update_gate * hidden + (1.0 - update_gate) * tokens_float
    normed_two, norm_two_back = jax.vjp(layer_norm, after_mixer, gains_float[1])
    normed_two_low = normed_two.astype(jnp.bfloat16)
    up_pre = jnp.dot(normed_two_low, up_full, preferred_element_type=jnp.float32)
    up_low = jax.nn.silu(up_pre).astype(jnp.bfloat16)
    result = (after_mixer + jnp.dot(up_low, down_full, preferred_element_type=jnp.float32)).astype(
        jnp.bfloat16
    )
    value_back, mix_back, merge_back, up_back, down_back = (
        value_full, mix_full, merge_full, up_full, down_full
    )
    grad_rows = cotangent.astype(jnp.float32) * live_rows[:, None].astype(jnp.float32)
    grad_down_low = grad_rows.astype(jnp.bfloat16)
    down_grad = jnp.einsum("tf,td->fd", up_low, grad_down_low, preferred_element_type=jnp.float32)
    grad_up_act = jnp.einsum(
        "td,fd->tf", grad_down_low, down_back, preferred_element_type=jnp.float32
    )
    grad_up_low = (grad_up_act * silu_slope(up_pre)).astype(jnp.bfloat16)
    up_grad = jnp.einsum(
        "td,tf->df", normed_two_low, grad_up_low, preferred_element_type=jnp.float32
    )
    grad_normed_two = jnp.einsum(
        "tf,df->td", grad_up_low, up_back, preferred_element_type=jnp.float32
    )
    grad_after_norm, gain_two_grad = norm_two_back(grad_normed_two)
    grad_after = grad_after_norm + grad_rows
    grad_hidden_in = grad_after * update_gate * silu_slope(hidden_in)
    grad_merge_low = grad_hidden_in.astype(jnp.bfloat16)
    merge_grad = jnp.einsum(
        "tv,td->vd", gated_low, grad_merge_low, preferred_element_type=jnp.float32
    )
    grad_gated = jnp.einsum(
        "td,vd->tv", grad_merge_low, merge_back, preferred_element_type=jnp.float32
    )
    grad_reset = grad_gated * attended
    grad_attended_low = (
        (grad_gated * reset_gate).astype(jnp.bfloat16).reshape(block_count, STRETCH, V)
    )
    grad_probs = jnp.einsum(
        "niv,njv->nij", grad_attended_low, value_blocks, preferred_element_type=jnp.float32
    )
    soft_probs = jnp.exp(block_scores() - log_total)
    grad_scores_low = (
        soft_probs * (grad_probs - jnp.sum(soft_probs * grad_probs, axis=-1, keepdims=True))
    ).astype(jnp.bfloat16)
    grad_query = (
        jnp.einsum(
            "nij,njk->nik", grad_scores_low, key_blocks, preferred_element_type=jnp.float32
        ).reshape(row_count, Z)
        * score_scale
    )
    grad_key = (
        jnp.einsum(
            "nij,nik->njk", grad_scores_low, query_blocks, preferred_element_type=jnp.float32
        ).reshape(row_count, Z)
        * score_scale
    )
    grad_value_act = jnp.einsum(
        "nij,niv->njv",
        soft_probs.astype(jnp.bfloat16),
        grad_attended_low,
        preferred_element_type=jnp.float32,
    ).reshape(row_count, V)
    rel_grad = jnp.einsum(
        "ij,ijl->l",
        jnp.sum(grad_scores_low.astype(jnp.float32), axis=0),
        one_hot,
        precision=highest,
    )
    attn_grad = jnp.concatenate(
        [
            jnp.sum(grad_query * shared, axis=0),
            jnp.sum(grad_query, axis=0),
            jnp.sum(grad_key * shared, axis=0),
            rel_grad,
        ]
    )
    grad_shared = grad_query * attn_float[:Z] + grad_key * attn_float[2 * Z : 3 * Z]
    grad_projected_low = jnp.concatenate(
        [
            grad_after * (hidden - tokens_float) * update_gate * (1.0 - update_gate),
            grad_shared * silu_slope(shared_pre),
            grad_reset * silu_slope(reset_pre),
            grad_hidden_in,
        ],
        axis=1,
    ).astype(jnp.bfloat16)
    mix_grad = jnp.einsum(
        "td,tm->dm", mixed_low, grad_projected_low, preferred_element_type=jnp.float32
    )
    grad_mixed = jnp.einsum(
        "tm,dm->td", grad_projected_low, mix_back, preferred_element_type=jnp.float32
    )
    grad_ema_rows = (grad_mixed * silu_slope(ema_out)).reshape(row_count, *lanes)
    grad_normed_rows, ema_grad_rows, omega_grad = ema_reverse(
        normed_rows, grad_ema_rows, ema_by_state, omega, keep, ema_marks
    )
    grad_normed_ema = grad_normed_rows.reshape(row_count, -1)
    ema_grad = jnp.swapaxes(ema_grad_rows.reshape(4, -1, tokens.shape[1]), 1, 2)
    omega_grad = omega_grad.reshape(-1)
    grad_value_low = (grad_value_act * silu_slope(value_pre)).astype(jnp.bfloat16)
    value_grad = jnp.einsum(
        "td,tv->dv", normed_low, grad_value_low, preferred_element_type=jnp.float32
    )
    grad_normed = grad_normed_ema + jnp.einsum(
        "tv,dv->td", grad_value_low, value_back, preferred_element_type=jnp.float32
    )
    grad_input, gain_one_grad = norm_back(grad_normed)
    grad_tokens = (grad_input + grad_after * (1.0 - update_gate)).astype(jnp.bfloat16)
    gains_grad = jnp.stack([gain_one_grad, gain_two_grad, omega_grad])
    small_totals = (
        lax.psum_scatter(gains_grad, (DP, FS), scatter_dimension=1, tiled=True),
        lax.psum_scatter(ema_grad, (DP, FS), scatter_dimension=1, tiled=True),
        lax.psum_scatter(attn_grad, (DP, FS), scatter_dimension=0, tiled=True),
    )
    totals = reduce_gradients(value_grad, mix_grad, merge_grad, up_grad, down_grad)
    return (
        result,
        grad_tokens,
        totals[0],
        totals[1],
        totals[2],
        totals[3],
        totals[4],
        small_totals[0],
        small_totals[1],
        small_totals[2],
    )


STRIP = 128
MESH = pl.DeviceIdType.MESH
F32 = jnp.float32
LOW = jnp.bfloat16
SHARDED = VALUE, MIX, MERGE, UP, DOWN = range(5)
TOK, COT = 5, 6


def mm(a, b):
    return lax.dot_general(a, b, (((1,), (0,)), ((), ())), preferred_element_type=F32)


def mm_nt(a, b):
    return lax.dot_general(a, b, (((1,), (1,)), ((), ())), preferred_element_type=F32)


def mm_tn(a, b):
    return lax.dot_general(a, b, (((0,), (0,)), ((), ())), preferred_element_type=F32)


def at_rows(start, size, unit=16):
    return pl.ds(pl.multiple_of(start, unit), size)


def row_loop(count, size, body, first=0, unroll=1):
    def step(i, carry):
        body(pl.multiple_of(first + i * size, size))
        return carry

    lax.fori_loop(0, count // size, step, 0, unroll=unroll)


def slope_of(value, gate):
    return gate * (1.0 + value * (1.0 - gate))


def layer_kernel(trees, depth, *refs):
    ref, at = types.SimpleNamespace(), 0
    for tree in trees:
        ref.__dict__.update(jax.tree.unflatten(tree, refs[at : at + tree.num_leaves]))
        at += tree.num_leaves
    tok, cot, gains, ema_in, omega_in, attn = ref.tok, ref.cot, ref.gains, ref.ema_in, ref.omega_in, ref.attn
    rows, width = tok.shape
    tiles = width // 128
    dp, fs = lax.axis_index(DP), lax.axis_index(FS)
    z, c, y, x = dp // 2, dp % 2, fs // 2, fs % 2
    q = c * 2 + x

    def place(z, c, y, x):
        return (z * 2 + c, y * 2 + x)

    sib, xn, xc, yn = place(z, 1 - c, y, x), place(z, c, y, 1 - x), place(z, 1 - c, y, 1 - x), place(z, c, 1 - y, x)
    half_z = z // 2
    partner, far_mid, far_end = z + 1 - 2 * (z % 2), 2 - half_z, 3 * (1 - half_z)
    middle = (z % 2 + half_z) % 2 == 1
    outer = (z % 2 + half_z) % 2 == 0
    line = (far_end, far_mid, partner, z)
    zs = [None] + [place((z + d) % depth, c, y, x) for d in range(1, depth)]
    mates = ((sib, 1 - c, x), (xn, c, 1 - x), (xc, 1 - c, 1 - x))
    plane = [(pc, py, px) for pc in range(2) for py in range(2) for px in range(2)][1:]
    plane = [((c + pc) % 2, (y + py) % 2, (x + px) % 2) for pc, py, px in plane]

    send_sems, recv_sems, local_sems = ref.send_sems, ref.recv_sems, ref.local_sems
    used, used_local, pending = [0], [0], []

    def new_id():
        used[0] += 1
        return used[0] - 1

    def send(src, dst, peer, arrives=None, when=None):
        k = new_id()
        copy = pltpu.make_async_remote_copy(
            src_ref=src, dst_ref=dst, send_sem=send_sems.at[k], recv_sem=recv_sems.at[k if arrives is None else arrives],
            device_id=peer, device_id_type=MESH,
        )
        if when is None:
            copy.start()
        else:
            pl.when(when)(copy.start)
        handle = [k, copy, False, when]
        pending.append(handle)
        return handle

    def sent(handle):
        if not handle[2]:
            if handle[3] is None:
                handle[1].wait_send()
            else:
                pl.when(handle[3])(handle[1].wait_send)
            handle[2] = True

    def received(handle, landed):
        k = handle if isinstance(handle, int) else handle[0]
        pltpu.make_async_remote_copy(
            src_ref=landed, dst_ref=landed, send_sem=send_sems.at[k], recv_sem=recv_sems.at[k],
            device_id=sib, device_id_type=MESH,
        ).wait_recv()

    def local(src, dst):
        k = used_local[0]
        used_local[0] += 1
        copy = pltpu.make_async_copy(src, dst, local_sems.at[k])
        copy.start()
        return copy

    lens = ref.lens
    ends, run = [], 0
    for i in range(lens.shape[1]):
        run = run + lens[0, i]
        ends.append(run)

    def kept(k):
        start = 0
        for i, end in enumerate(ends):
            start = start + jnp.where(end <= k * CHUNK, lens[0, i], 0)
        return jnp.where(k * CHUNK - start == 0, 0.0, 1.0)

    def live_rows(r, size):
        places = r + lax.broadcasted_iota(jnp.int32, (size, 1), 0)
        return (places < ends[-1]).astype(F32)

    small_all, packed = ref.small_all, ref.packed
    states_at = ref.ema_params.shape[1]
    params = jnp.zeros((states_at, 128), F32)
    for p in range(4):
        v = ref.ema_params[p].astype(F32)
        v = jnp.concatenate([v, jnp.zeros((states_at, 128 - v.shape[1]), F32)], axis=1)
        params = params + (pltpu.roll(v, p * 32, 1) if p else v)
    packed[0:states_at, :] = params.astype(LOW)
    singles = [ref.norm_gains[p : p + 1, :] for p in range(3)] + [ref.attn_params[...]]
    row = jnp.zeros((1, 128), F32)
    for p, v in enumerate(singles):
        v = jnp.concatenate([v.astype(F32), jnp.zeros((1, 128 - v.shape[1]), F32)], axis=1)
        row = row + (pltpu.roll(v, p * 32, 1) if p else v)
    packed[16:32, :] = jnp.broadcast_to(row, (16, 128)).astype(LOW)
    lane_group = lax.broadcasted_iota(jnp.int32, (1, 128), 1) // 32

    def slot(pc, py, px, pz):
        return (pc * 4 + py * 2 + px) * depth + pz

    def small_start():
        return [send(packed, small_all.at[slot(c, y, x, z)], zs[d]) for d in range(1, depth)]

    def small_relay(handles):
        for d, handle in enumerate(handles):
            received(handle, small_all.at[slot(c, y, x, (z + depth - 1 - d) % depth)])
        small_all[slot(c, y, x, z)] = packed[...]
        mine = small_all.at[pl.ds(slot(c, y, x, 0), depth)]
        return [send(mine, mine, place(z, *p)) for p in plane]

    def small_finish(handles):
        for handle, p in zip(handles, plane):
            received(handle, small_all.at[pl.ds(slot(*p, 0), depth)])
        states = ema_in.shape[0] // (4 * tiles)
        gains[...] = jnp.zeros_like(gains)
        attn[...] = jnp.zeros_like(attn)
        for t in range(tiles):
            pz, pc = t // 2, t % 2
            got = [small_all[slot(pc, f // 2, f % 2, pz)].astype(F32)[0 : states + 8, :] for f in range(4)]
            for p in range(4):
                v = jnp.zeros_like(got[0])
                for f in range(4):
                    turn = (f - p) * 32 % 128
                    v = jnp.where(lane_group == f, pltpu.roll(got[f], turn, 1) if turn else got[f], v)
                ema_in[pl.ds(p * states * tiles + t, states, stride=tiles), :] = v[0:states]
                row = v[states : states + 1]
                if p < 3:
                    gains[p : p + 1, t * 128 : (t + 1) * 128] = row
                    if p == 2:
                        omega_in[t : t + 1, :] = row
                    continue
                for f in range(4):
                    turn = (t % 2 * 64 - f * 16) % 128
                    mine = lax.broadcasted_iota(jnp.int32, (1, 128), 1) // 16 == t % 2 * 4 + f
                    moved = pltpu.roll(row, turn, 1) if turn else row
                    attn[t // 2 : t // 2 + 1, :] += jnp.where(mine, moved, 0.0)

    lane = lax.broadcasted_iota(jnp.int32, (1, 128), 1)
    shift = fs * 32

    def mix_align():
        raw, win, line_up = ref.s[MIX], ref.mix_win, ref.by_time
        line_up[0 : win.shape[1], :] = jnp.zeros((win.shape[1], 128), F32)

        def load(r):
            line_up[at_rows(shift + r, 32, 32), :] = raw[pl.ds(r, 32), :].astype(F32)

        row_loop(raw.shape[0], 32, load)
        for t in range(win.shape[1] // 128):
            win[:, t * 128 : (t + 1) * 128] = line_up[t * 128 : (t + 1) * 128, :].T.astype(LOW)

    weights = {m: ref.w[m] for m in SHARDED}
    block_shape = {m: (w.shape[0] // depth, w.shape[1] // 2) for m, w in weights.items()}

    def block(m, zz, yy):
        rb, cb = block_shape[m]
        return weights[m].at[at_rows(zz * rb, rb), at_rows(yy * cb, cb, 128)]

    def piece(m, src_c, src_x):
        rb, cb = block_shape[m]
        half = cb // 2
        if m in (VALUE, UP):
            return weights[m].at[at_rows(z * rb + src_c * (rb // 2), rb // 2), at_rows(y * cb + src_x * half, half, 128)]
        return weights[m].at[at_rows(z * rb, rb), at_rows(y * cb + src_x * half, half, 128)]

    def move(src, dst):
        rows_at_once = 32

        def step(r):
            dst[pl.ds(r, rows_at_once), :] = src[pl.ds(r, rows_at_once), :]

        row_loop(src.shape[0], rows_at_once, step)

    spare, near, loads, top = ref.up_low, {MIX: ref.mix_win}, {}, 0
    for m in (VALUE, MERGE, UP, DOWN):
        tall, wide = ref.s[m].shape
        near[m] = spare.at[top : top + tall, 0:wide]
        loads[m] = local(ref.s[m], near[m])
        top += tall
    for k in (TOK, COT):
        loads[k] = local(ref.acts[k - TOK], (tok, cot)[k - TOK])
    barrier = pltpu.get_barrier_semaphore()
    peers = [place(z, *p) for p in plane] + zs[1:]
    for peer in peers:
        pl.semaphore_signal(barrier, inc=1, device_id=peer, device_id_type=MESH)
    pl.semaphore_wait(barrier, len(peers))

    swaps = {m: [] for m in SHARDED}

    def swap_start(m):
        shard = near[m]
        if m in loads:
            loads[m].wait()
        if m == MIX:
            first, last = 1 - (fs + 2) // 3, fs // 3
            middle = 1 - first - last
            for peer, pc, px in mates + ((None, c, x),):
                pq = pc * 2 + px
                tiles_at = (
                    first * 2 * pq,
                    (first + last) * (1 + 2 * pq) + middle * (1 + pq),
                    first * 8 + last * (2 + 2 * pq) + middle * (5 + pq),
                )
                for i, tile in enumerate(tiles_at):
                    src = shard.at[:, at_rows(tile * 128, 128, 128)]
                    dst = ref.mix_in.at[x, at_rows(c * 128, 128), pl.ds(i * 128, 128)]
                    if peer is None:
                        move(src, dst)
                    else:
                        swaps[m].append((send(src, dst, peer), pc, px, i))
            return
        if m in (VALUE, UP):
            wide = shard.shape[1] // 4
            for peer, pc, px in mates + ((None, c, x),):
                src = shard.at[:, at_rows((pc * 2 + px) * wide, wide, 128)]
                if peer is None:
                    move(src, piece(m, c, x))
                else:
                    swaps[m].append((send(src, piece(m, c, x), peer), pc, px, 0))
            return
        tall = shard.shape[0] // 2
        swaps[m].append((send(shard.at[at_rows((1 - x) * tall, tall), :], piece(m, c, x), xn), c, 1 - x, 0))
        move(shard.at[at_rows(x * tall, tall), :], piece(m, c, x))

    z_ids, z_sends, y_sends = {}, {}, {}

    def swap_finish(m):
        for handle, pc, px, i in swaps[m]:
            if m == MIX:
                received(handle, ref.mix_in.at[px, at_rows(pc * 128, 128), pl.ds(i * 128, 128)])
            else:
                received(handle, piece(m, pc, px))
        if m == MIX:
            only = (q == 3).astype(F32)
            low_y = (y == 0).astype(F32)
            lead = jnp.broadcast_to(jnp.maximum(low_y, only), (1, 128))
            rb, cb = block_shape[m]
            a, b, w = ref.mix_in.at[0], ref.mix_in.at[1], weights[m]

            def combine(r):
                at = pl.ds(r, 64)
                to = at_rows(z * rb + r, 64)

                def put(i, v):
                    w[to, at_rows(y * cb + i * 128, 128, 128)] = v.astype(LOW)

                put(0, a[at, 0:128].astype(F32) * lead)
                put(1, a[at, 128:256])
                put(2, a[at, 256:384].astype(F32) + b[at, 0:128].astype(F32) * lead)
                put(3, b[at, 128:256])
                put(4, b[at, 256:384])

            row_loop(rb, 64, combine)

    def y_own(m):
        y_sends[m] = [(3, send(block(m, z, y), block(m, z, y), yn))]

    def z_start(m, far=False):
        own = block(m, z, 1 - y if far else y)
        ids = [new_id() for _ in range(3)]
        z_ids[m, far] = ids
        z_sends.setdefault(m, []).extend(
            [
                send(own, own, place(partner, c, y, x), ids[2]),
                send(own, own, place(far_mid, c, y, x), ids[1], middle),
                send(own, own, place(far_mid, c, y, x), ids[0], outer),
            ]
        )

    def z_received(m, i, far, when):
        there = block(m, line[i], 1 - y if far else y)
        pl.when(when)(functools.partial(received, z_ids[m, far][i], there))
        return there

    def z_pass(m, steps=(1, 0), far=False):
        for i in steps:
            there = z_received(m, i, far, middle)
            z_sends[m].append(send(there, there, place(partner, c, y, x), z_ids[m, far][i], middle))

    def z_far(m):
        received(y_sends[m][0][1], block(m, z, 1 - y))
        z_start(m, True)

    def z_finish(m):
        for far in (False, True):
            received(z_ids[m, far][2], block(m, partner, 1 - y if far else y))
            for i in (1, 0):
                z_received(m, i, far, outer)

    def y_forward(m, steps=(2, 1, 0)):
        for i in steps:
            there = block(m, line[i], y)
            if i == 2:
                received(z_ids[m, False][i], there)
            else:
                z_received(m, i, False, outer)
            y_sends[m].append((i, send(there, there, yn)))

    def y_finish(m):
        for i, handle in y_sends[m]:
            received(handle, block(m, line[i], 1 - y))

    def group_rows(c, x):
        return at_rows((c * 2 + x) * rows, rows)

    def part_rows(c, x, first, count):
        return at_rows((c * 2 + x) * rows + first, count)

    def gather_start(buf, first=0, count=None):
        count = rows if count is None else count
        own = buf.at[part_rows(c, x, first, count), :]
        return [(first, count), send(own, own, xn), send(own, own, sib)]

    def gather_relay(buf, handles):
        other = buf.at[part_rows(c, 1 - x, *handles[0]), :]
        received(handles[1], other)
        handles.append(send(other, other, sib))

    def gather_finish(buf, handles):
        received(handles[2], buf.at[part_rows(1 - c, x, *handles[0]), :])
        received(handles[3], buf.at[part_rows(1 - c, 1 - x, *handles[0]), :])

    total = ref.total
    stage = [ref.stage.at[0], ref.stage.at[1], ref.stage.at[2], ref.hidden_mul]
    staged = [[], [], [], []]

    def stage_out(k, first, count, extra=None):
        def put(r):
            at = pl.ds(r, 32)
            v = total[at, :]
            if extra is not None:
                v = v + extra[at, :].astype(F32)
            stage[k][at, :] = v.astype(LOW)

        row_loop(count, 32, put, first)

    def stage_free(k):
        for handle in staged[k]:
            sent(handle)
        staged[k] = []

    def reduce_first(partial, sibs):
        for k, px in ((0, 1 - x), (1, x)):
            partial(1 - c, px)
            stage_free(k)
            stage_out(k, 0, rows)
            staged[k] = [send(stage[k], sibs[k], sib)]
        return staged[0][0], staged[1][0]

    def reduce_cross(partial, sibs, cross, handles, slot=2):
        halves = (pl.ds(0, rows // 2), pl.ds(rows // 2, rows // 2))
        partial(c, 1 - x)
        received(handles[0], sibs[0])
        stage_free(slot)
        for i, half in enumerate(halves):
            stage_out(slot, i * (rows // 2), rows // 2, sibs[0])
            staged[slot].append(send(stage[slot].at[half, :], cross.at[half, :], xn))
        return handles[1], list(zip(staged[slot], (cross.at[half, :] for half in halves)))

    def reduce_early(partial, sibs, cross):
        return reduce_cross(partial, sibs, cross, reduce_first(partial, sibs))

    def reduce_late(partial, sibs, cross, handles, consume):
        partial(c, x)
        received(handles[0], sibs[1])
        for i, (handle, half) in enumerate(handles[1]):
            received(handle, half)
            consume(i * (rows // 2), rows // 2)

    def reduced(r, size, sibs, cross):
        at = pl.ds(r, size)
        return total[at, :] + sibs[1][at, :].astype(F32) + cross[at, :].astype(F32)

    sibs_a, sibs_b = ((r.at[0], r.at[1]) for r in (ref.sibs_a, ref.sibs_b))
    cross_a, cross_b = ref.cross_a, ref.cross_b
    sibs_c, cross_c = (ref.gc.at[2 * rows : 3 * rows, :], ref.gc.at[3 * rows : 4 * rows, :]), ref.update_in

    w_up = weights[UP]
    y_out = {
        DOWN: ref.mix_pack.at[:, 384 : 384 + block_shape[DOWN][1]],
        UP: ref.yo,
        MERGE: ref.gc.at[0 : weights[MERGE].shape[0], 0 : block_shape[MERGE][1]],
        MIX: w_up.at[:, 0 : block_shape[MIX][1]],
        VALUE: w_up.at[:, block_shape[MIX][1] : block_shape[MIX][1] + block_shape[VALUE][1]],
    }
    y_in = {m: ref.yi[m] for m in SHARDED}
    z_in = {m: ref.zi[m] for m in SHARDED}
    f_in = {m: ref.fi[m] for m in SHARDED}
    gy, gz, gf = {}, {}, {}

    def y_grad_send(m, product, steps=(0, 1, 2, 3)):
        rb, cb = block_shape[m]
        if m not in gy:
            gy[m], gz[m] = {}, [new_id() for _ in range(4)]
        for i in steps:
            at = at_rows(line[i] * rb, rb)
            y_out[m][at, :] = product(line[i], 1 - y).astype(LOW)
            gy[m][i] = send(y_out[m].at[at, :], y_in[m].at[at, :], yn)

    def y_grad_add(m, product, steps=(0, 1, 2, 3)):
        rb, cb = block_shape[m]
        for i in steps:
            at = at_rows(line[i] * rb, rb)
            own = product(line[i], y)
            received(gy[m][i], y_in[m].at[at, :])
            y_in[m][at, :] = (own + y_in[m][at, :].astype(F32)).astype(LOW)
            if i < 3:
                send(
                    y_in[m].at[at, :], z_in[m].at[i], place(partner, c, y, x), gz[m][i], outer if i < 2 else None
                )

    def z_relay(m, steps=(0, 1)):
        rb, cb = block_shape[m]
        for i in steps:
            at = at_rows(line[i] * rb, rb)

            @pl.when(middle)
            def _(i=i, at=at):
                received(gz[m][i], z_in[m].at[i])
                y_in[m][at, :] = (y_in[m][at, :].astype(F32) + z_in[m][i].astype(F32)).astype(LOW)

            send(y_in[m].at[at, :], z_in[m].at[3], place(line[i], c, y, x), gz[m][3], middle)

    def z_grad_add(m):
        rb, cb = block_shape[m]
        for i in (2, 3):
            received(gz[m][i], z_in[m].at[i])

        def add(r):
            at = at_rows(z * rb + r, 64)
            v = y_in[m][at, :].astype(F32)
            for i in (2, 3):
                v = v + z_in[m][i, pl.ds(r, 64), :].astype(F32)
            y_in[m][at, :] = v.astype(LOW)

        row_loop(rb, 64, add)
        to_owners(m)

    far_land = [ref.mix_in.at[i // 2, pl.ds(i % 2 * 128, 128), :] for i in range(4)]
    y_last = ref.mix_win.at[:, 0 : block_shape[MERGE][1]]

    def sides(m):
        return (False, y_in[m], [z_in[m].at[i] for i in range(4)]), (True, y_out[m], far_land)

    def first_send(m, product):
        rb, cb = block_shape[m]
        for far, _, _ in sides(m):
            gz[m, far] = [new_id() for _ in range(4)]
        for i in range(4):
            at = at_rows(line[i] * rb, rb)
            for far, buf, land in sides(m):
                buf[at, :] = product(line[i], 1 - y if far else y).astype(LOW)
                if i < 3:
                    send(
                        buf.at[at, :], land[i], place(partner, c, y, x), gz[m, far][i], outer if i < 2 else None
                    )

    def first_relay(m):
        rb, cb = block_shape[m]
        for i in (0, 1):
            at = at_rows(line[i] * rb, rb)
            for far, buf, land in sides(m):

                @pl.when(middle)
                def _(i=i, at=at, far=far, buf=buf, land=land):
                    received(gz[m, far][i], land[i])
                    buf[at, :] = (buf[at, :].astype(F32) + land[i][...].astype(F32)).astype(LOW)

                send(buf.at[at, :], land[3], place(line[i], c, y, x), gz[m, far][3], middle)

    def first_turn(m):
        rb, cb = block_shape[m]
        at = at_rows(z * rb, rb)
        for far, buf, land in sides(m):
            for i in (2, 3):
                received(gz[m, far][i], land[i])
            buf[at, :] = (buf[at, :].astype(F32) + land[2][...].astype(F32) + land[3][...].astype(F32)).astype(LOW)
        gy[m] = send(y_out[m].at[at, :], y_last, yn)

    def first_finish(m):
        rb, cb = block_shape[m]
        at = at_rows(z * rb, rb)
        received(gy[m], y_last)
        y_in[m][at, :] = (y_in[m][at, :].astype(F32) + y_last[...].astype(F32)).astype(LOW)
        to_owners(m)

    def to_owners(m):
        rb, cb = block_shape[m]
        gf[m] = []
        if m in (MERGE, DOWN):
            land = f_in[m].at[at_rows(x * rb, rb), :]

            def part(px):
                return y_in[m].at[at_rows(z * rb, rb), at_rows(px * (cb // 2), cb // 2, 128)]

            gf[m].append((send(part(1 - x), land, xn), f_in[m].at[at_rows((1 - x) * rb, rb), :]))
            move(part(x), land)
            return
        half = rb // 2

        def land_at(pc, px):
            if m == MIX:
                return f_in[m].at[pc * 2 + px]
            wide = f_in[m].shape[1] // 4
            return f_in[m].at[:, at_rows((pc * 2 + px) * wide, wide, 128)]

        def part(pc, px):
            if m == MIX:
                return y_in[m].at[at_rows(z * rb + pc * half, half), at_rows(px * 256, 384, 128)]
            return y_in[m].at[at_rows(z * rb + pc * half, half), at_rows(px * (cb // 2), cb // 2, 128)]

        for peer, pc, px in mates:
            gf[m].append((send(part(pc, px), land_at(c, x), peer), land_at(pc, px)))
        move(part(c, x), land_at(c, x))

    def grad_out(m):
        for handle, landed in gf[m]:
            received(handle, landed)
        if m != MIX:
            return
        out, src, line_up = ref.g_mix, f_in[MIX], ref.by_time
        first, last = (fs == 0).astype(F32), (fs == 3).astype(F32)
        mid = 1.0 - first - last
        first, last, mid = (jnp.broadcast_to(v, (1, 128)) for v in (first, last, mid))

        def get(p, t):
            return src[p, :, t * 128 : (t + 1) * 128].astype(F32)

        for tile in range(9):
            v = first * (get(tile // 2, tile % 2) if tile < 8 else src[q, :, 256:384].astype(F32))
            if tile == 0:
                v = v + (mid + last) * get(3, 0)
            else:
                v = v + mid * get((tile - 1) % 4, 1 + (tile - 1) // 4)
                v = v + last * get((tile - 1) // 2, 1 + (tile - 1) % 2)
            line_up[tile * 128 : (tile + 1) * 128, :] = v.T

        def write(r):
            out[pl.ds(r, 32), :] = line_up[at_rows(shift + r, 32, 32), :].astype(LOW)

        row_loop(out.shape[0], 32, write)

    h_small = small_start()
    mix_align()
    swap_start(MIX)
    h_small = small_relay(h_small)
    swap_start(VALUE)
    swap_start(MERGE)
    swap_finish(MIX)
    y_own(MIX)
    z_start(MIX)

    nl, ml, n2, gc, gm = (ref.nl, ref.ml, ref.n2, ref.gc, ref.gm)
    by_time, out_time, back_time = ref.by_time, ref.out_time, ref.back_time

    def centre(v):
        cen = v - jnp.mean(v, axis=-1, keepdims=True)
        return cen, lax.rsqrt(jnp.mean(cen * cen, axis=-1, keepdims=True) + 1e-05)

    def norm_one(r):
        cen, rate = centre(tok[pl.ds(r, 16), :].astype(F32))
        v = cen * rate * gains[0:1, :]
        nl[at_rows(q * rows + r, 16), :] = v.astype(LOW)
        for s in range(tiles):
            by_time[pl.ds(r * tiles + s, 16, stride=tiles), :] = v[:, s * 128 : (s + 1) * 128]

    small_finish(h_small)
    loads[TOK].wait()
    row_loop(rows, 16, norm_one)
    swap_finish(VALUE)
    y_own(VALUE)
    z_start(VALUE)

    def cot_low(r):
        at = pl.ds(r, 32)
        gc[at_rows(q * rows + r, 32), :] = (cot[at, :].astype(F32) * live_rows(r, 32)).astype(LOW)

    def load_ema():
        return ema_in[...].reshape(4, -1, tiles, 128)

    _, _, rate_all, weight_all = ema_coefficients(load_ema())
    omega = omega_in[...]
    marks = ref.marks

    def at_time(t):
        return at_rows(t * tiles, tiles, 8)

    def ema_chunk(k, state):
        state = state * kept(k)
        marks[k] = state

        def step(i, state):
            t = k * CHUNK + i
            v = by_time[at_time(t), :]
            state = rate_all * state + v[None]
            out_time[at_time(t), :] = jnp.sum(weight_all * state, axis=0) + omega * v
            return state

        return lax.fori_loop(0, CHUNK, step, state, unroll=4)

    lax.fori_loop(0, rows // CHUNK, ema_chunk, jnp.zeros_like(rate_all))

    def mixed(r):
        for s in range(tiles):
            at = pl.ds(r * tiles + s, 16, stride=tiles)
            v = out_time[at, :]
            gate = jax.nn.sigmoid(v)
            ml[at_rows(q * rows + r, 16), s * 128 : (s + 1) * 128] = (v * gate).astype(LOW)
            out_time[at, :] = slope_of(v, gate)

    row_loop(rows, 16, mixed)
    h_ml = gather_start(ml)
    swap_start(UP)
    h_nl = gather_start(nl)
    swap_finish(MERGE)
    z_start(MERGE)
    z_pass(MIX, (1,))
    y_forward(MIX, [2])
    swap_start(DOWN)
    loads[COT].wait()
    row_loop(rows, 32, cot_low)
    z_pass(MIX, (0,))
    y_forward(MIX, [1])
    z_pass(VALUE)
    gather_relay(ml, h_ml)
    y_forward(MIX, [0])
    y_own(MERGE)
    y_forward(VALUE)
    swap_finish(UP)
    z_start(UP)
    gather_finish(ml, h_ml)
    z_pass(MERGE)

    value_low, value_slope = ref.value_low, ref.value_slope
    vq = value_low.shape[1]

    def value_block(r):
        total[:, :vq] = mm(nl[pl.ds(r, rows), :], weights[VALUE][...])

        def act(s):
            v = total[pl.ds(s, 32), :vq]
            gate = jax.nn.sigmoid(v)
            value_low[at_rows(r + s, 32), :] = (v * gate).astype(LOW)
            value_slope[at_rows(r + s, 32), :] = slope_of(v, gate).astype(LOW)

        row_loop(rows, 32, act)

    y_finish(MIX)

    w_mix, reset_w = weights[MIX], ref.reset_w
    half_mix = w_mix.shape[1] // 2

    def fix_reset(r):
        at = pl.ds(r, 64)
        reset_w[at, 0:128] = w_mix[at, 384:512]
        reset_w[at, 128:256] = (w_mix[at, 512:640].astype(F32) + w_mix[at, half_mix : half_mix + 128].astype(F32)).astype(LOW)

    row_loop(width, 64, fix_reset)

    def w_update():
        return w_mix[:, 0:256]

    def w_shared():
        return w_mix[:, 256:384]

    def w_late():
        return w_mix[:, half_mix + 128 : half_mix + 384]

    def w_hidden():
        return w_mix[:, half_mix + 384 : half_mix + 640]

    scale = float(STRETCH) ** -0.5
    stretch = STRETCH
    shared_pre, query, key, probs = ref.shared_pre, ref.query, ref.key, ref.probs
    probs_low = ref.probs_low
    shared_pre[...] = mm(ml[group_rows(c, x), :], w_shared())
    sv = shared_pre[...]
    shared = sv * jax.nn.sigmoid(sv)
    query[...] = (shared * attn[0:1, :] + attn[1:2, :]).astype(LOW)
    key[...] = (shared * attn[2:3, :]).astype(LOW)
    bias = pltpu.roll(jnp.broadcast_to(attn[3:4, :], (stretch, stretch)), 0, 1, stride=1, stride_axis=0).T
    row_id = lax.broadcasted_iota(jnp.int32, (stretch, stretch), 0)
    col_id = lax.broadcasted_iota(jnp.int32, (stretch, stretch), 1)
    for n in range(rows // stretch):
        at = pl.ds(n * stretch, stretch)
        scores = mm_nt(query[at, :], key[at, :]) * scale + bias
        scores = jnp.where(row_id >= col_id, scores, -1000000000.0)
        ex = jnp.exp(scores - jnp.max(scores, axis=-1, keepdims=True))
        pr = ex / jnp.sum(ex, axis=-1, keepdims=True)
        probs[at, :] = pr
        probs_low[at_rows(q * rows + n * stretch, stretch), :] = pr.astype(LOW)
    own_probs = probs_low.at[group_rows(c, x), :]
    h_probs = [send(own_probs, own_probs, peer) for peer, _, _ in mates]

    mix_pack, update_in = ref.mix_pack, ref.update_in
    hidden_at = pl.ds(mix_pack.shape[1] - 256, 256)
    update_out = mix_pack.at[:, hidden_at]

    def update_block(r):
        update_out[pl.ds(r, rows), :] = mm(ml[pl.ds(r, rows), :], w_update()).astype(LOW)

    row_loop(4 * rows, rows, update_block)
    part_w = width // 4
    own_cols = at_rows(q * part_w, part_w, 128)
    h_update = [
        send(update_out.at[group_rows(pc, px), :], update_in.at[:, own_cols], peer) for peer, pc, px in mates
    ]
    update_in[:, own_cols] = update_out[group_rows(c, x), :]
    gather_relay(nl, h_nl)
    h_gc = gather_start(gc)

    reset_gate, reset_slope = ref.reset_gate, ref.reset_slope

    def reset_block(r):
        at = pl.ds(r, rows)
        total[:, 0:256] = mm(ml[at, :], reset_w[...])
        total[:, 256:512] = mm(ml[at, :], w_late())

        def act(s):
            v = total[pl.ds(s, 32), :vq]
            gate = jax.nn.sigmoid(v)
            reset_gate[at_rows(r + s, 32), :] = (v * gate).astype(LOW)
            reset_slope[at_rows(r + s, 32), :] = slope_of(v, gate).astype(LOW)

        row_loop(rows, 32, act)

    row_loop(4 * rows, rows, reset_block)
    y_forward(MERGE)
    swap_finish(DOWN)
    z_start(DOWN)
    y_own(DOWN)
    z_pass(UP, (1,))
    gather_finish(nl, h_nl)
    y_finish(VALUE)
    row_loop(4 * rows, rows, value_block)
    z_pass(UP, (0,))
    y_own(UP)
    y_forward(UP, [2])
    for handle, (_, pc, px) in zip(h_probs, mates):
        received(handle, probs_low.at[group_rows(pc, px), :])

    gated = ref.gated

    def attend(r):
        at = pl.ds(r, stretch)
        total[0:stretch, :vq] = mm(probs_low[at, :], value_low[at, :])

        def act(s):
            v = total[pl.ds(s, 32), :vq]
            to = at_rows(r + s, 32)
            gated[to, :] = (v * reset_gate[to, :].astype(F32)).astype(LOW)
            reset_slope[to, :] = (v * reset_slope[to, :].astype(F32)).astype(LOW)

        row_loop(stretch, 32, act)

    row_loop(4 * rows, stretch, attend)
    z_pass(DOWN, (1,))
    y_forward(UP, [1])
    y_finish(MERGE)

    def merge_partial(c, x):
        at = group_rows(c, x)
        total[...] = mm(gated[at, :], weights[MERGE][...])
        total[:, own_cols] += mm(ml[at, :], w_hidden())

    h_red = reduce_early(merge_partial, sibs_a, cross_a)
    z_pass(DOWN, (0,))
    y_forward(UP, [0])
    for handle, (_, pc, px) in zip(h_update, mates):
        received(handle, update_in.at[:, at_rows((pc * 2 + px) * part_w, part_w, 128)])
    gather_relay(gc, h_gc)
    z_far(DOWN)

    after, hidden_mul, update_mul = ref.after, ref.hidden_mul, ref.update_mul

    def norm_two(r):
        at = pl.ds(r, 16)
        v = reduced(r, 16, sibs_a, cross_a)
        gate = jax.nn.sigmoid(v)
        hidden = v * gate
        u = jax.nn.sigmoid(update_in[at, :].astype(F32))
        xv = tok[at, :].astype(F32)
        av = u * hidden + (1.0 - u) * xv
        after[at, :] = av
        hidden_mul[at, :] = (u * slope_of(v, gate)).astype(LOW)
        update_mul[at, :] = ((hidden - xv) * u * (1.0 - u)).astype(LOW)
        cen, rate = centre(av)
        n2[at_rows(q * rows + r, 16), :] = (cen * rate * gains[1:2, :]).astype(LOW)

    h_n2 = []

    def take_merge(first, count):
        row_loop(count, 16, norm_two, first, 2)
        h_n2.append(gather_start(n2, first, count))

    reduce_late(merge_partial, sibs_a, cross_a, h_red, take_merge)
    z_pass(DOWN, (1,), True)
    gather_relay(n2, h_n2[0])
    z_pass(DOWN, (0,), True)
    gather_relay(n2, h_n2[1])
    for handles in h_n2:
        gather_finish(n2, handles)
    gather_finish(gc, h_gc)
    y_finish(UP)

    up_low, up_slope = ref.up_low, ref.up_slope
    for m in SHARDED:
        for swap in swaps[m]:
            sent(swap[0])

    def up_block(r):
        total[...] = mm(n2[pl.ds(r, rows), :], weights[UP][...])

        def act(s):
            v = total[pl.ds(s, 16), :]
            gate = jax.nn.sigmoid(v)
            up_low[at_rows(r + s, 16), :] = (v * gate).astype(LOW)
            up_slope[at_rows(r + s, 16), :] = slope_of(v, gate).astype(LOW)

        row_loop(rows, 16, act)

    row_loop(4 * rows, rows, up_block)

    def cols_of(m, yy):
        cb = block_shape[m][1]
        return at_rows(yy * cb, cb, 128)

    def rows_of(m, zz):
        rb = block_shape[m][0]
        return at_rows(zz * rb, rb, 128)

    def down_product(zz, yy):
        return mm_tn(up_low[:, rows_of(DOWN, zz)], gc[:, cols_of(DOWN, yy)])

    y_grad_send(DOWN, down_product)
    z_finish(DOWN)

    def down_partial(c, x):
        total[...] = mm(up_low[group_rows(c, x), :], weights[DOWN][...])

    def up_back(r):
        at = pl.ds(r, rows)
        total[...] = mm_nt(gc[at, :], weights[DOWN][...])

        def act(s):
            to = at_rows(r + s, 16)
            up_slope[to, :] = (total[pl.ds(s, 16), :] * up_slope[to, :].astype(F32)).astype(LOW)

        row_loop(rows, 16, act)

    row_loop(4 * rows, rows, up_back)
    grad_up = up_slope

    def two_partial(c, x):
        total[...] = mm_nt(grad_up[group_rows(c, x), :], weights[UP][...])

    def up_product(zz, yy):
        return mm_tn(n2[:, rows_of(UP, zz)], grad_up[:, cols_of(UP, yy)])

    h_red = reduce_early(two_partial, sibs_a, cross_a)
    y_grad_send(UP, up_product)
    y_grad_add(DOWN, down_product, (0, 1))
    for handle in h_gc[1:]:
        sent(handle)

    gain_sum, update_back = ref.gain_sum, hidden_mul
    gain_sum[...] = jnp.zeros_like(gain_sum)

    def norm_two_back(r):
        at = pl.ds(r, 16)
        g = reduced(r, 16, sibs_a, cross_a)
        cen, rate = centre(after[at, :])
        unit = cen * rate
        gain_sum[1] += g * unit
        g = g * gains[1:2, :]
        back = rate * (g - jnp.mean(g, axis=-1, keepdims=True) - unit * jnp.mean(g * unit, axis=-1, keepdims=True))
        back = back + cot[at, :].astype(F32) * live_rows(r, 16)
        gm[at_rows(q * rows + r, 16), :] = (back * hidden_mul[at, :].astype(F32)).astype(LOW)
        hidden_mul[at, :] = (back * update_mul[at, :].astype(F32)).astype(LOW)
        u = jax.nn.sigmoid(update_in[at, :].astype(F32))
        update_mul[at, :] = (back * (1.0 - u)).astype(LOW)

    h_gm = []

    def take_two(first, count):
        row_loop(count, 16, norm_two_back, first, 2)
        h_gm.append(gather_start(gm, first, count))

    reduce_late(two_partial, sibs_a, cross_a, h_red, take_two)
    for handle in h_update:
        sent(handle)
    update_grad = mix_pack.at[:, 0:256]
    own_rows = group_rows(c, x)
    h_update = [
        send(update_back.at[:, at_rows((pc * 2 + px) * part_w, part_w, 128)], update_grad.at[own_rows, :], peer)
        for peer, pc, px in mates
    ]
    update_grad[own_rows, :] = update_back[:, own_cols]

    y_grad_add(DOWN, down_product, (2, 3))
    z_relay(DOWN)
    gather_relay(gm, h_gm[0])
    y_grad_add(UP, up_product, (0,))
    gather_relay(gm, h_gm[1])
    y_grad_add(UP, up_product, (1,))
    for handles in h_gm:
        gather_finish(gm, handles)

    def merge_product(zz, yy):
        return mm_tn(gated[:, rows_of(MERGE, zz)], gm[:, cols_of(MERGE, yy)])

    for handle in z_sends[UP] + [h for _, h in y_sends[UP]]:
        sent(handle)
    grad_probs, probs_in = ref.grad_probs, ref.probs_in

    def gated_back(r):
        at = pl.ds(r, rows)
        total[:, :vq] = mm_nt(gm[at, :], weights[MERGE][...])

        def act(s):
            to = at_rows(r + s, 32)
            g = total[pl.ds(s, 32), :vq]
            back = (g * reset_slope[to, :].astype(F32)).astype(LOW)
            mix_pack[to, 384:640] = back[:, 0:256]
            mix_pack[to, 640:768] = back[:, 128:256]
            mix_pack[to, 768:1024] = back[:, 256:512]
            mix_pack[to, hidden_at] = gm[to, own_cols]
            reset_gate[to, :] = (g * reset_gate[to, :].astype(F32)).astype(LOW)

        row_loop(rows, 32, act)

    for handle in gy[DOWN].values():
        sent(handle)
    row_loop(4 * rows, rows, gated_back)
    grad_att = reset_gate

    def probs_back(r):
        at = pl.ds(r, stretch)
        grad_probs[at, :] = mm_nt(grad_att[at, :], value_low[at, :]).astype(LOW)

    row_loop(4 * rows, stretch, probs_back)
    h_probs = [
        send(grad_probs.at[group_rows(pc, px), :], probs_in.at[i], peer) for i, (peer, pc, px) in enumerate(mates)
    ]
    first_send(MERGE, merge_product)
    for handle, (_, pc, px) in zip(h_update, mates):
        received(handle, update_grad.at[group_rows(pc, px), :])

    shared_grad = mix_pack.at[:, 256:384]

    def mixed_partial(cc, xx):
        at = group_rows(cc, xx)
        total[...] = (
            mm_nt(update_grad[at, :], w_update())
            + mm_nt(mix_pack[at, 384:640], reset_w[...])
            + mm_nt(mix_pack[at, 768:1024], w_late())
            + mm_nt(mix_pack[at, hidden_at], w_hidden())
        )


    def value_back(r):
        at = pl.ds(r, stretch)
        total[0:stretch, :vq] = mm_tn(probs_low[at, :], grad_att[at, :])

        def act(s):
            to = at_rows(r + s, 32)
            value_slope[to, :] = (total[pl.ds(s, 32), :vq] * value_slope[to, :].astype(F32)).astype(LOW)

        row_loop(stretch, 32, act)

    row_loop(4 * rows, stretch, value_back)
    grad_value = value_slope

    def value_product(zz, yy):
        return mm_tn(nl[:, rows_of(VALUE, zz)], grad_value[:, cols_of(VALUE, yy)])

    y_grad_send(VALUE, value_product, (0, 1))
    y_grad_add(UP, up_product, (2, 3))
    z_relay(UP)

    for i, handle in enumerate(h_probs):
        received(handle, probs_in.at[i])
    anti = (row_id + col_id == stretch - 1).astype(LOW)
    lag_sum = jnp.zeros((1, stretch), F32)
    grads_q = jnp.zeros((1, stretch), F32)
    grads_o = jnp.zeros((1, stretch), F32)
    grads_k = jnp.zeros((1, stretch), F32)
    for n in range(rows // stretch):
        at = pl.ds(n * stretch, stretch)
        to = at_rows(q * rows + n * stretch, stretch)
        g = grad_probs[to, :].astype(F32)
        for i in range(3):
            g = g + probs_in[i, at, :].astype(F32)
        pr = probs[at, :]
        gs = (pr * (g - jnp.sum(pr * g, axis=-1, keepdims=True))).astype(LOW)
        gq = mm(gs, key[at, :]) * scale
        gk = mm_tn(gs, query[at, :]) * scale
        lags = pltpu.roll(mm_nt(anti, gs), 1, 1, stride=1, stride_axis=0)
        lag_sum += jnp.sum(lags, axis=0, keepdims=True)
        sv = shared_pre[at, :]
        gate = jax.nn.sigmoid(sv)
        sh = sv * gate
        grads_q += jnp.sum(gq * sh, axis=0, keepdims=True)
        grads_o += jnp.sum(gq, axis=0, keepdims=True)
        grads_k += jnp.sum(gk * sh, axis=0, keepdims=True)
        gsh = gq * attn[0:1, :] + gk * attn[2:3, :]
        shared_grad[to, :] = (gsh * slope_of(sv, gate)).astype(LOW)
    attn_rows = (grads_q, grads_o, grads_k, lag_sum)
    own_shared = shared_grad.at[own_rows, :]
    h_shared = [send(own_shared, own_shared, peer) for peer, _, _ in mates]
    h_mixed = reduce_early(mixed_partial, sibs_a, cross_a)


    for handle, (_, pc, px) in zip(h_shared, mates):
        received(handle, shared_grad.at[group_rows(pc, px), :])

    def mix_product(zz, yy):
        return mm_tn(ml[:, rows_of(MIX, zz)], mix_pack[:, cols_of(MIX, yy)])

    y_grad_send(MIX, mix_product)
    first_relay(MERGE)
    y_grad_send(VALUE, value_product, (2, 3))
    y_grad_add(VALUE, value_product, (0, 1))
    z_grad_add(DOWN)
    for handle in h_update:
        sent(handle)
    h_down = reduce_first(down_partial, sibs_c)

    def mixed_own(cc, xx):
        mixed_partial(cc, xx)
        total[...] += mm_nt(shared_grad[own_rows, :], w_shared())


    def to_time(r):
        v = reduced(r, 16, sibs_a, cross_a)
        for s in range(tiles):
            at = pl.ds(r * tiles + s, 16, stride=tiles)
            out_time[at, :] = out_time[at, :] * v[:, s * 128 : (s + 1) * 128]

    reduce_late(mixed_own, sibs_a, cross_a, h_mixed, lambda first, count: row_loop(count, 16, to_time, first, 2))

    def value_partial(cc, xx):
        total[...] = mm_nt(grad_value[group_rows(cc, xx), :], weights[VALUE][...])

    h_red = reduce_early(value_partial, sibs_b, cross_b)
    y_grad_add(MIX, mix_product, (0,))

    held = ref.held
    ema = load_ema()
    damping, decay_gate, rate_all, weight_all = ema_coefficients(ema)
    omega = omega_in[...]
    half = rate_all.shape[0] // 2
    chunks = rows // CHUNK
    sums = []
    for part in range(2):
        js = slice(part * half, (part + 1) * half)
        rate, weight = rate_all[js], weight_all[js]

        def chunk(m, carry, js=js, rate=rate, weight=weight, part=part):
            k = chunks - 1 - m
            held[0] = marks[k, js]

            def ahead(i, state):
                state = rate * state + by_time[at_time(k * CHUNK + i), :][None]
                held[i + 1] = state
                return state

            lax.fori_loop(0, CHUNK, ahead, held[0], unroll=4)

            def back(n, carry):
                s, dw, dr, dom = carry
                i = CHUNK - 1 - n
                t = at_time(k * CHUNK + i)
                g = out_time[t, :]
                s = rate * s + g[None]
                dx = jnp.sum(weight * s, axis=0)
                if part == 0:
                    back_time[t, :] = dx + omega * g
                    dom = dom + g * by_time[t, :]
                else:
                    back_time[t, :] = back_time[t, :] + dx
                return s, dw + held[i + 1] * g[None], dr + held[i] * s, dom

            s, dw, dr, dom = lax.fori_loop(0, CHUNK, back, carry, unroll=2)
            return s * kept(k), dw, dr, dom

        zero = jnp.zeros_like(rate)
        carry = lax.fori_loop(0, chunks // 2, chunk, (zero, zero, zero, jnp.zeros_like(omega)))
        if part:
            y_grad_add(MIX, mix_product, (2,))
        else:
            y_grad_add(MIX, mix_product, (1,))
            z_relay(VALUE)
        sums.append(lax.fori_loop(chunks // 2, chunks, chunk, carry))
        if not part:
            h_down = reduce_cross(down_partial, sibs_c, cross_c, h_down, 3)
            z_relay(MIX, (0,))
            first_turn(MERGE)
    small = ref.by_time
    rate_scale = ema.shape[1] ** (-0.5)
    for part in range(2):
        js = slice(part * half, (part + 1) * half)
        dw, dr = sums[part][1], sums[part][2] * weight_all[js]
        d_damp = dw * ema[2, js] * ema[3, js] * rate_scale - dr * decay_gate[js]
        parts = (
            d_damp * damping[js] * (1.0 - damping[js]),
            -dr * damping[js] * decay_gate[js] * (1.0 - decay_gate[js]),
            dw * damping[js] * ema[3, js] * rate_scale,
            dw * damping[js] * ema[2, js] * rate_scale,
        )
        for p in range(4):
            for j in range(half):
                small[pl.ds((p * 2 * half + part * half + j) * tiles, tiles), :] = parts[p][j]

    tile_rows = ref.tile_rows
    states = 4 * ema.shape[1]
    gain_two = jnp.sum(gain_sum[1], axis=0, keepdims=True)
    for t in range(tiles):
        at = (t % 2) * depth + t // 2
        tile_rows[at, 0:states, :] = small[pl.ds(t, states, stride=tiles), :]
        tail = jnp.concatenate(
            [
                jnp.zeros((1, 128), F32),
                gain_two[:, t * 128 : (t + 1) * 128],
                sums[0][3][t : t + 1],
                attn_rows[t // 2],
                jnp.zeros((4, 128), F32),
            ],
            axis=0,
        )
        tile_rows[at, states : states + 8, :] = tail
    sib_in, z_small, x_small, y_small = ref.sib_in, ref.z_small, ref.x_small, ref.y_small
    h_sib = send(tile_rows.at[pl.ds((1 - c) * depth, depth)], sib_in, sib)
    z_relay(MIX, (1,))
    received(h_sib, sib_in)
    sib_in[...] += tile_rows[pl.ds(c * depth, depth)]
    h_zs = [send(sib_in.at[(z + d) % depth], z_small.at[d - 1], zs[d]) for d in range(1, depth)]

    def norm_one_back(r):
        at = pl.ds(r, 16)
        ema_part = jnp.concatenate(
            [back_time[pl.ds(r * tiles + s, 16, stride=tiles), :] for s in range(tiles)], axis=1
        )
        g = reduced(r, 16, sibs_b, cross_b) + ema_part
        cen, rate = centre(tok[at, :].astype(F32))
        unit = cen * rate
        gain_sum[0] += g * unit
        g = g * gains[0:1, :]
        back = rate * (g - jnp.mean(g, axis=-1, keepdims=True) - unit * jnp.mean(g * unit, axis=-1, keepdims=True))
        ref.grad_tokens[at, :] = (back + update_mul[at, :].astype(F32)).astype(LOW)

    reduce_late(
        value_partial, sibs_b, cross_b, h_red, lambda first, count: row_loop(count, 16, norm_one_back, first, 2)
    )
    one_rows, one_z, one_sum, one_plane = ref.one_rows, ref.one_z, ref.one_sum, ref.one_plane
    gain_one = jnp.sum(gain_sum[0], axis=0, keepdims=True)
    for t in range(tiles):
        one_rows[t] = jnp.broadcast_to(gain_one[:, t * 128 : (t + 1) * 128], (8, 128))
    h_one = [send(one_rows.at[pl.ds((z + d) % depth * 2, 2)], one_z.at[d - 1], zs[d]) for d in range(1, depth)]
    y_grad_add(MIX, mix_product, (3,))
    z_grad_add(UP)
    first_finish(MERGE)
    y_grad_add(VALUE, value_product, (2, 3))
    for d, handle in enumerate(h_zs):
        received(handle, z_small.at[d])
    x_small[0] = sib_in[z] + z_small[0] + z_small[1] + z_small[2]
    h_x = send(x_small.at[0], x_small.at[1], xn)
    z_grad_add(MIX)
    for d, handle in enumerate(h_one):
        received(handle, one_z.at[d])
    one_sum[...] = one_rows[pl.ds(z * 2, 2)] + one_z[0] + one_z[1] + one_z[2]
    h_one = [send(one_sum.at[p[0]], one_plane.at[i], place(z, *p)) for i, p in enumerate(plane)]
    received(h_x, x_small.at[1])
    y_small[0] = x_small[0] + x_small[1]
    h_y = send(y_small.at[0], y_small.at[1], yn)
    z_grad_add(VALUE)

    def finish(r):
        at = pl.ds(r, 16)
        ref.result[at, :] = (after[at, :] + reduced(r, 16, sibs_c, cross_c)).astype(LOW)

    reduce_late(down_partial, sibs_c, cross_c, h_down, lambda first, count: row_loop(count, 16, finish, first, 2))
    for m in (DOWN, UP, MERGE):
        grad_out(m)
    received(h_y, y_small.at[1])
    totals = y_small[0] + y_small[1]
    ref.small_out[...] = pltpu.roll(totals, (128 - shift) % 128, 1)
    one = one_sum[c]
    for i, handle in enumerate(h_one):
        received(handle, one_plane.at[i])
        one = one + one_plane[i]
    ref.small_out[states : states + 1, :] = pltpu.roll(one, (128 - shift) % 128, 1)[0:1]
    for m in (MIX, VALUE):
        grad_out(m)
    ref.attn_out[...] = pltpu.roll(totals[states : states + 8], (128 - c * 64 - fs * 16) % 128, 1)
    for handle in pending:
        sent(handle)
    assert used[0] <= COPIES


def finish_kernel(result, grad_tokens, value, mix, merge, up, down, small, attn, *outs):
    for src, out in zip((result, grad_tokens, value, mix, merge, up, down), outs):

        def widen(r, src=src, out=out):
            out[pl.ds(r, 32), :] = src[pl.ds(r, 32), :].astype(out.dtype)

        row_loop(out.shape[0], 32, widen)
    gains, ema, per = outs[7:]
    states, mine = ema.shape[1:]
    gains[...] = small[4 * states : 4 * states + 3, :mine]
    for p in range(4):
        ema[p] = small[p * states : (p + 1) * states, :mine]
    per[...] = attn[3:4, : per.shape[1]]


def layer_on_device(depth, tokens, cotangent, lengths, value_proj, mix_proj, merge_proj, up_proj, down_proj, norm_gains, ema_params, attn_params):
    rows, width = tokens.shape
    fs = lax.axis_index(FS)
    window = -(-mix_proj.shape[1] // 128) * 128
    group = 4 * rows
    vq = value_proj.shape[1]
    fq = up_proj.shape[1]
    quarters = ((width, vq), (width, 10 * STRIP), (vq, width), (width, fq), (fq, width))
    tiles = width // 128
    states = ema_params.shape[2]
    small_rows = 4 * states + 8
    shape = jax.ShapeDtypeStruct
    mix_turned = mix_proj.T
    ema_turned = jnp.swapaxes(ema_params, 1, 2)
    shards = (value_proj, mix_turned, merge_proj, up_proj, down_proj)
    inputs = dict(
        acts=(tokens, cotangent),
        lens=lengths,
        norm_gains=norm_gains,
        ema_params=ema_turned,
        attn_params=attn_params[None],
        s=shards,
    )
    landings = [w.shape for w in shards]
    landings[MIX] = (4, mix_proj.shape[0], 3 * STRIP)
    outputs = dict(
        result=shape((rows, width), LOW),
        grad_tokens=shape((rows, width), LOW),
        fi=tuple(shape(d, LOW) for d in landings),
        g_mix=shape(mix_turned.shape, LOW),
        small_out=shape((small_rows, 128), F32),
        attn_out=shape((8, 128), F32),
    )
    copies = pltpu.SemaphoreType.DMA((COPIES,))

    def low(*dims):
        return pltpu.VMEM(dims, LOW)

    def full(*dims):
        return pltpu.VMEM(dims, F32)

    scratch = dict(
        send_sems=copies,
        recv_sems=copies,
        local_sems=pltpu.SemaphoreType.DMA((32,)),
        w=tuple(low(*d) for d in quarters),
        yo=low(width, fq // 2),
        yi=tuple(low(r, k // 2) for r, k in quarters),
        zi=tuple(low(4, r // depth, k // 2) for r, k in quarters),
        mix_win=low(mix_proj.shape[0], window),
        small_all=low(8 * depth, 32, 128),
        packed=low(32, 128),
        ema_in=full(4 * states * tiles, 128),
        omega_in=full(tiles, 128),
        gains=full(8, width),
        attn=full(8, 128),
        tok=low(rows, width),
        cot=low(rows, width),
        nl=low(group, width),
        ml=low(group, width),
        n2=low(group, width),
        gc=low(group, width),
        gm=low(group, width),
        mix_in=low(2, 2 * mix_proj.shape[0], 4 * STRIP),
        reset_w=low(width, 256),
        value_low=low(group, vq),
        value_slope=low(group, vq),
        reset_gate=low(group, vq),
        reset_slope=low(group, vq),
        gated=low(group, vq),
        up_low=low(group, fq),
        up_slope=low(group, fq),
        update_in=low(rows, width),
        probs_low=low(group, STRETCH),
        probs=full(rows, STRETCH),
        shared_pre=full(rows, Z),
        query=low(rows, Z),
        key=low(rows, Z),
        grad_probs=low(group, STRETCH),
        probs_in=low(3, rows, STRETCH),
        mix_pack=low(group, 10 * STRIP),
        by_time=full(rows * tiles, 128),
        out_time=full(rows * tiles, 128),
        back_time=full(rows * tiles, 128),
        marks=full(rows // CHUNK, states, tiles, 128),
        held=full(CHUNK + 1, states // 2, tiles, 128),
        total=full(rows, width),
        stage=low(3, rows, width),
        sibs_a=low(2, rows, width),
        sibs_b=low(2, rows, width),
        cross_a=low(rows, width),
        cross_b=low(rows, width),
        after=full(rows, width),
        hidden_mul=low(rows, width),
        update_mul=low(rows, width),
        gain_sum=full(2, 16, width),
        tile_rows=full(tiles, small_rows, 128),
        sib_in=full(depth, small_rows, 128),
        z_small=full(depth - 1, small_rows, 128),
        x_small=full(2, small_rows, 128),
        y_small=full(2, small_rows, 128),
        one_rows=full(tiles, 8, 128),
        one_z=full(depth - 1, 2, 8, 128),
        one_sum=full(2, 8, 128),
        one_plane=full(7, 8, 128),
    )
    in_vmem = pl.BlockSpec(memory_space=pltpu.VMEM)
    specs = jax.tree.map(lambda _: in_vmem, inputs)
    anywhere = pl.BlockSpec(memory_space=pl.ANY)
    specs.update(
        lens=pl.BlockSpec(memory_space=pltpu.SMEM), acts=(anywhere,) * 2, s=tuple(in_vmem if m == MIX else anywhere for m in SHARDED)
    )
    in_leaves, in_tree = jax.tree.flatten(inputs)
    out_leaves, out_tree = jax.tree.flatten(outputs)
    scratch_leaves, scratch_tree = jax.tree.flatten(scratch, is_leaf=lambda v: not isinstance(v, (dict, tuple)))
    outs = pl.pallas_call(
        functools.partial(layer_kernel, (in_tree, out_tree, scratch_tree), depth),
        out_shape=tuple(out_leaves),
        in_specs=jax.tree.leaves(specs),
        out_specs=tuple(in_vmem for _ in out_leaves),
        scratch_shapes=scratch_leaves,
        compiler_params=pltpu.CompilerParams(collective_id=0, has_side_effects=True, vmem_limit_bytes=VMEM_BYTES),
        name="layer",
    )(*in_leaves)
    by = types.SimpleNamespace(**jax.tree.unflatten(out_tree, outs))
    grads = list(by.fi)
    grads[MIX] = by.g_mix
    wide = [shape(g.shape, F32) for g in (*grads, norm_gains, ema_turned)]
    *finals, attn_grad = pl.pallas_call(
        finish_kernel,
        out_shape=(shape((rows, width), LOW), shape((rows, width), LOW), *wide, shape((1, attn_params.shape[0]), F32)),
        in_specs=[in_vmem] * 9,
        out_specs=(in_vmem,) * 10,
        compiler_params=pltpu.CompilerParams(vmem_limit_bytes=VMEM_BYTES),
        name="finish",
    )(by.result, by.grad_tokens, *grads, by.small_out, by.attn_out)
    finals[2 + MIX] = finals[2 + MIX].T
    finals[-1] = jnp.swapaxes(finals[-1], 1, 2)
    return (*finals, attn_grad[0])


VMEM_BYTES = 64 << 20
COPIES = 256


def solution(mesh):
    in_specs = (
        P((DP, FS), None),
        P((DP, FS), None),
        P((DP, FS), None),
        P(DP, FS),
        P(DP, FS),
        P(DP, FS),
        P(DP, FS),
        P(DP, FS),
        P(None, (DP, FS)),
        P(None, (DP, FS), None),
        P((DP, FS)),
    )
    out_specs = (
        P((DP, FS), None),
        P((DP, FS), None),
        P(DP, FS),
        P(DP, FS),
        P(DP, FS),
        P(DP, FS),
        P(DP, FS),
        P(None, (DP, FS)),
        P(None, (DP, FS), None),
        P((DP, FS)),
    )
    fits = mesh.shape[DP] == 8 and mesh.shape[DP] // 2 * 4 * STRIP == V and mesh.shape[FS] * 4 * STRIP == V
    body = functools.partial(layer_on_device, mesh.shape[DP] // 2) if fits else on_device
    return jax.shard_map(body, mesh=mesh, in_specs=in_specs, out_specs=out_specs, check_vma=False)
```

```python
import functools
import types

import jax
import jax.numpy as jnp
from jax import lax
from jax.experimental import pallas as pl
from jax.experimental.pallas import tpu as pltpu
from jax.sharding import PartitionSpec as P

D = 1024
Z = 128
V = 2048
STRETCH = 128


DP, FS = "dp", "fsdp"
highest = lax.Precision.HIGHEST


def layer_norm(values, gain):
    centred = values - jnp.mean(values, axis=-1, keepdims=True)
    spread_sq = jnp.mean(centred * centred, axis=-1, keepdims=True)
    return centred * lax.rsqrt(spread_sq + 1e-05) * gain


def token_layout(length_row, row_count):
    places = jnp.arange(row_count, dtype=jnp.int32)
    running = jnp.cumsum(length_row)
    before = (running[None, :] <= places[:, None]).astype(jnp.int32)
    starts = jnp.sum(before * length_row[None, :], axis=1)
    return (places - starts, places < running[-1])


def ema_coefficients(ema):
    damping = jax.nn.sigmoid(ema[0])
    decay_gate = jax.nn.sigmoid(ema[1])
    keep_rate = 1.0 - damping * decay_gate
    weights_out = damping * ema[2] * ema[3] * ema.shape[1] ** (-0.5)
    return damping, decay_gate, keep_rate, weights_out


CHUNK = 32


def ema_forward_kernel(x_ref, ema_ref, omega_ref, keep_ref, y_ref, mark_ref):
    _, _, rate, weight = ema_coefficients(ema_ref[...])
    omega = omega_ref[...]

    def chunk(k, state):
        state = state * keep_ref[k][None]
        mark_ref[k] = state

        def step(i, state):
            t = k * CHUNK + i
            x = x_ref[t]
            state = rate * state + x[None]
            y_ref[t] = jnp.sum(weight * state, axis=0) + omega * x
            return state

        return lax.fori_loop(0, CHUNK, step, state, unroll=4)

    lax.fori_loop(0, x_ref.shape[0] // CHUNK, chunk, jnp.zeros_like(rate))


def ema_backward_kernel(x_ref, g_ref, ema_ref, omega_ref, keep_ref, mark_ref, dx_ref, dema_ref, domega_ref, h_ref):
    ema = ema_ref[...]
    damping, decay_gate, rate_all, weight_all = ema_coefficients(ema)
    omega = omega_ref[...]
    half = rate_all.shape[0] // 2
    chunks = x_ref.shape[0] // CHUNK
    sums = []
    for part in range(2):
        js = slice(part * half, (part + 1) * half)
        rate, weight = rate_all[js], weight_all[js]
        zero = jnp.zeros_like(rate)

        def chunk(m, carry, js=js, rate=rate, weight=weight, part=part):
            k = chunks - 1 - m
            h_ref[0] = mark_ref[k, js]

            def ahead(i, state):
                state = rate * state + x_ref[k * CHUNK + i][None]
                h_ref[i + 1] = state
                return state

            lax.fori_loop(0, CHUNK, ahead, h_ref[0], unroll=4)

            def back(n, carry):
                s, dw, dr, dom = carry
                i = CHUNK - 1 - n
                t = k * CHUNK + i
                g = g_ref[t]
                s = rate * s + g[None]
                dx = jnp.sum(weight * s, axis=0)
                if part == 0:
                    dx_ref[t] = dx + omega * g
                    dom = dom + g * x_ref[t]
                else:
                    dx_ref[t] = dx_ref[t] + dx
                dw = dw + h_ref[i + 1] * g[None]
                dr = dr + h_ref[i] * s
                return s, dw, dr, dom

            s, dw, dr, dom = lax.fori_loop(0, CHUNK, back, carry, unroll=2)
            return s * keep_ref[k][None], dw, dr, dom

        out = lax.fori_loop(0, chunks, chunk, (zero, zero, zero, jnp.zeros_like(omega)))
        sums.append(out)
    dw = jnp.concatenate([sums[0][1], sums[1][1]], axis=0)
    dr = jnp.concatenate([sums[0][2], sums[1][2]], axis=0) * weight_all
    scale = ema.shape[1] ** (-0.5)
    d_damp = dw * ema[2] * ema[3] * scale - dr * decay_gate
    dema_ref[0] = d_damp * damping * (1.0 - damping)
    dema_ref[1] = -dr * damping * decay_gate * (1.0 - decay_gate)
    dema_ref[2] = dw * damping * ema[3] * scale
    dema_ref[3] = dw * damping * ema[2] * scale
    domega_ref[...] = sums[0][3]


def ema_keep(position):
    starts = position.reshape(-1, CHUNK)[:, 0] != 0
    return jnp.broadcast_to(starts.astype(jnp.float32)[:, None, None], (starts.shape[0], 8, 128))


def ema_apply(x, ema, omega, keep):
    f32 = jnp.float32
    shape = jax.ShapeDtypeStruct
    return pl.pallas_call(
        ema_forward_kernel,
        out_shape=(shape(x.shape, f32), shape((keep.shape[0],) + ema.shape[1:], f32)),
        compiler_params=pltpu.CompilerParams(vmem_limit_bytes=32 << 20),
    )(x, ema, omega, keep)


def ema_reverse(x, g, ema, omega, keep, mark):
    f32 = jnp.float32
    shape = jax.ShapeDtypeStruct
    return pl.pallas_call(
        ema_backward_kernel,
        out_shape=(shape(x.shape, f32), shape(ema.shape, f32), shape(omega.shape, f32)),
        scratch_shapes=[pltpu.VMEM((CHUNK + 1, ema.shape[1] // 2) + ema.shape[2:], f32)],
        compiler_params=pltpu.CompilerParams(vmem_limit_bytes=32 << 20),
    )(x, g, ema, omega, keep, mark)


def silu_slope(values):
    logistic = jax.nn.sigmoid(values)
    return logistic * (1.0 + values * (1.0 - logistic))


def relative_table(rel_bias):
    lag_grid = (
        jnp.arange(STRETCH, dtype=jnp.int32)[:, None]
        - jnp.arange(STRETCH, dtype=jnp.int32)[None, :]
    )
    one_hot = (lag_grid[:, :, None] == jnp.arange(STRETCH, dtype=jnp.int32)[None, None, :]).astype(
        jnp.float32
    )
    bias_grid = jnp.einsum("ijl,l->ij", one_hot, rel_bias, precision=highest)
    return (lag_grid, one_hot, bias_grid)


def gather_forward(value_proj, mix_proj, merge_proj, up_proj, down_proj):
    first = (
        lax.all_gather(value_proj, DP, axis=0, tiled=True),
        lax.all_gather(mix_proj, DP, axis=0, tiled=True),
        lax.all_gather(merge_proj, DP, axis=0, tiled=True),
        lax.all_gather(up_proj, DP, axis=0, tiled=True),
        lax.all_gather(down_proj, DP, axis=0, tiled=True),
    )
    return (
        lax.all_gather(first[0], FS, axis=1, tiled=True),
        lax.all_gather(first[1], FS, axis=1, tiled=True),
        lax.all_gather(first[2], FS, axis=1, tiled=True),
        lax.all_gather(first[3], FS, axis=1, tiled=True),
        lax.all_gather(first[4], FS, axis=1, tiled=True),
    )


def reduce_gradients(value_grad, mix_grad, merge_grad, up_grad, down_grad):
    first = (
        lax.psum_scatter(
            value_grad.astype(jnp.bfloat16), DP, scatter_dimension=0, tiled=True
        ).astype(jnp.float32),
        lax.psum_scatter(
            mix_grad.astype(jnp.bfloat16), DP, scatter_dimension=0, tiled=True
        ).astype(jnp.float32),
        lax.psum_scatter(
            merge_grad.astype(jnp.bfloat16), DP, scatter_dimension=0, tiled=True
        ).astype(jnp.float32),
        lax.psum_scatter(
            up_grad.astype(jnp.bfloat16), DP, scatter_dimension=0, tiled=True
        ).astype(jnp.float32),
        lax.psum_scatter(
            down_grad.astype(jnp.bfloat16), DP, scatter_dimension=0, tiled=True
        ).astype(jnp.float32),
    )
    return (
        lax.psum_scatter(
            first[0].astype(jnp.bfloat16), FS, scatter_dimension=1, tiled=True
        ).astype(jnp.float32),
        lax.psum_scatter(
            first[1].astype(jnp.bfloat16), FS, scatter_dimension=1, tiled=True
        ).astype(jnp.float32),
        lax.psum_scatter(
            first[2].astype(jnp.bfloat16), FS, scatter_dimension=1, tiled=True
        ).astype(jnp.float32),
        lax.psum_scatter(
            first[3].astype(jnp.bfloat16), FS, scatter_dimension=1, tiled=True
        ).astype(jnp.float32),
        lax.psum_scatter(
            first[4].astype(jnp.bfloat16), FS, scatter_dimension=1, tiled=True
        ).astype(jnp.float32),
    )


def on_device(
    tokens,
    cotangent,
    lengths,
    value_proj,
    mix_proj,
    merge_proj,
    up_proj,
    down_proj,
    norm_gains,
    ema_params,
    attn_params,
):
    gains_full, ema_full, attn_full = (
        lax.all_gather(norm_gains, (DP, FS), axis=1, tiled=True),
        lax.all_gather(ema_params, (DP, FS), axis=1, tiled=True),
        lax.all_gather(attn_params, (DP, FS), axis=0, tiled=True),
    )
    value_full, mix_full, merge_full, up_full, down_full = gather_forward(
        value_proj, mix_proj, merge_proj, up_proj, down_proj
    )
    gains_float = gains_full.astype(jnp.float32)
    ema_float = ema_full.astype(jnp.float32)
    attn_float = attn_full.astype(jnp.float32)
    row_count = tokens.shape[0]
    position, live_rows = token_layout(lengths[0], row_count)
    tokens_float = tokens.astype(jnp.float32)
    normed, norm_back = jax.vjp(layer_norm, tokens_float, gains_float[0])
    normed_low = normed.astype(jnp.bfloat16)
    value_pre = jnp.dot(normed_low, value_full, preferred_element_type=jnp.float32)
    value_low = jax.nn.silu(value_pre).astype(jnp.bfloat16)

    lanes = (8, tokens.shape[1] // 8)
    ema_by_state = jnp.swapaxes(ema_float, 1, 2).reshape(4, -1, *lanes)
    omega = gains_float[2].reshape(lanes)
    keep = ema_keep(position)
    normed_rows = normed.reshape(row_count, *lanes)
    ema_rows, ema_marks = ema_apply(normed_rows, ema_by_state, omega, keep)
    ema_out = ema_rows.reshape(row_count, -1)
    mixed_low = jax.nn.silu(ema_out).astype(jnp.bfloat16)
    projected = jnp.dot(mixed_low, mix_full, preferred_element_type=jnp.float32)
    update_gate = jax.nn.sigmoid(projected[:, :D])
    shared_pre = projected[:, D : D + Z]
    reset_pre = projected[:, D + Z : D + Z + V]
    hidden_x = projected[:, D + Z + V :]
    shared = jax.nn.silu(shared_pre)
    reset_gate = jax.nn.silu(reset_pre)
    query_low = (shared * attn_float[:Z] + attn_float[Z : 2 * Z]).astype(jnp.bfloat16)
    key_low = (shared * attn_float[2 * Z : 3 * Z]).astype(jnp.bfloat16)
    block_count = row_count // STRETCH
    lag_grid, one_hot, bias_grid = relative_table(attn_float[3 * Z :])
    query_blocks = query_low.reshape(block_count, STRETCH, Z)
    key_blocks = key_low.reshape(block_count, STRETCH, Z)
    value_blocks = value_low.reshape(block_count, STRETCH, V)
    score_scale = Z ** (-0.5)

    def block_scores():
        raw_scores = (
            jnp.einsum("nik,njk->nij", query_blocks, key_blocks, preferred_element_type=jnp.float32)
            * score_scale
            + bias_grid
        )
        return jnp.where(lag_grid >= 0, raw_scores, -1000000000.0)

    scores = block_scores()
    row_max = jnp.max(scores, axis=-1, keepdims=True)
    log_total = row_max + jnp.log(jnp.sum(jnp.exp(scores - row_max), axis=-1, keepdims=True))
    probs_low = jnp.exp(scores - log_total).astype(jnp.bfloat16)
    attended = jnp.einsum(
        "nij,njv->niv", probs_low, value_blocks, preferred_element_type=jnp.float32
    ).reshape(row_count, V)
    gated_low = (attended * reset_gate).astype(jnp.bfloat16)
    hidden_in = jnp.dot(gated_low, merge_full, preferred_element_type=jnp.float32) + hidden_x
    hidden = jax.nn.silu(hidden_in)
    after_mixer = update_gate * hidden + (1.0 - update_gate) * tokens_float
    normed_two, norm_two_back = jax.vjp(layer_norm, after_mixer, gains_float[1])
    normed_two_low = normed_two.astype(jnp.bfloat16)
    up_pre = jnp.dot(normed_two_low, up_full, preferred_element_type=jnp.float32)
    up_low = jax.nn.silu(up_pre).astype(jnp.bfloat16)
    result = (after_mixer + jnp.dot(up_low, down_full, preferred_element_type=jnp.float32)).astype(
        jnp.bfloat16
    )
    value_back, mix_back, merge_back, up_back, down_back = (
        value_full, mix_full, merge_full, up_full, down_full
    )
    grad_rows = cotangent.astype(jnp.float32) * live_rows[:, None].astype(jnp.float32)
    grad_down_low = grad_rows.astype(jnp.bfloat16)
    down_grad = jnp.einsum("tf,td->fd", up_low, grad_down_low, preferred_element_type=jnp.float32)
    grad_up_act = jnp.einsum(
        "td,fd->tf", grad_down_low, down_back, preferred_element_type=jnp.float32
    )
    grad_up_low = (grad_up_act * silu_slope(up_pre)).astype(jnp.bfloat16)
    up_grad = jnp.einsum(
        "td,tf->df", normed_two_low, grad_up_low, preferred_element_type=jnp.float32
    )
    grad_normed_two = jnp.einsum(
        "tf,df->td", grad_up_low, up_back, preferred_element_type=jnp.float32
    )
    grad_after_norm, gain_two_grad = norm_two_back(grad_normed_two)
    grad_after = grad_after_norm + grad_rows
    grad_hidden_in = grad_after * update_gate * silu_slope(hidden_in)
    grad_merge_low = grad_hidden_in.astype(jnp.bfloat16)
    merge_grad = jnp.einsum(
        "tv,td->vd", gated_low, grad_merge_low, preferred_element_type=jnp.float32
    )
    grad_gated = jnp.einsum(
        "td,vd->tv", grad_merge_low, merge_back, preferred_element_type=jnp.float32
    )
    grad_reset = grad_gated * attended
    grad_attended_low = (
        (grad_gated * reset_gate).astype(jnp.bfloat16).reshape(block_count, STRETCH, V)
    )
    grad_probs = jnp.einsum(
        "niv,njv->nij", grad_attended_low, value_blocks, preferred_element_type=jnp.float32
    )
    soft_probs = jnp.exp(block_scores() - log_total)
    grad_scores_low = (
        soft_probs * (grad_probs - jnp.sum(soft_probs * grad_probs, axis=-1, keepdims=True))
    ).astype(jnp.bfloat16)
    grad_query = (
        jnp.einsum(
            "nij,njk->nik", grad_scores_low, key_blocks, preferred_element_type=jnp.float32
        ).reshape(row_count, Z)
        * score_scale
    )
    grad_key = (
        jnp.einsum(
            "nij,nik->njk", grad_scores_low, query_blocks, preferred_element_type=jnp.float32
        ).reshape(row_count, Z)
        * score_scale
    )
    grad_value_act = jnp.einsum(
        "nij,niv->njv",
        soft_probs.astype(jnp.bfloat16),
        grad_attended_low,
        preferred_element_type=jnp.float32,
    ).reshape(row_count, V)
    rel_grad = jnp.einsum(
        "ij,ijl->l",
        jnp.sum(grad_scores_low.astype(jnp.float32), axis=0),
        one_hot,
        precision=highest,
    )
    attn_grad = jnp.concatenate(
        [
            jnp.sum(grad_query * shared, axis=0),
            jnp.sum(grad_query, axis=0),
            jnp.sum(grad_key * shared, axis=0),
            rel_grad,
        ]
    )
    grad_shared = grad_query * attn_float[:Z] + grad_key * attn_float[2 * Z : 3 * Z]
    grad_projected_low = jnp.concatenate(
        [
            grad_after * (hidden - tokens_float) * update_gate * (1.0 - update_gate),
            grad_shared * silu_slope(shared_pre),
            grad_reset * silu_slope(reset_pre),
            grad_hidden_in,
        ],
        axis=1,
    ).astype(jnp.bfloat16)
    mix_grad = jnp.einsum(
        "td,tm->dm", mixed_low, grad_projected_low, preferred_element_type=jnp.float32
    )
    grad_mixed = jnp.einsum(
        "tm,dm->td", grad_projected_low, mix_back, preferred_element_type=jnp.float32
    )
    grad_ema_rows = (grad_mixed * silu_slope(ema_out)).reshape(row_count, *lanes)
    grad_normed_rows, ema_grad_rows, omega_grad = ema_reverse(
        normed_rows, grad_ema_rows, ema_by_state, omega, keep, ema_marks
    )
    grad_normed_ema = grad_normed_rows.reshape(row_count, -1)
    ema_grad = jnp.swapaxes(ema_grad_rows.reshape(4, -1, tokens.shape[1]), 1, 2)
    omega_grad = omega_grad.reshape(-1)
    grad_value_low = (grad_value_act * silu_slope(value_pre)).astype(jnp.bfloat16)
    value_grad = jnp.einsum(
        "td,tv->dv", normed_low, grad_value_low, preferred_element_type=jnp.float32
    )
    grad_normed = grad_normed_ema + jnp.einsum(
        "tv,dv->td", grad_value_low, value_back, preferred_element_type=jnp.float32
    )
    grad_input, gain_one_grad = norm_back(grad_normed)
    grad_tokens = (grad_input + grad_after * (1.0 - update_gate)).astype(jnp.bfloat16)
    gains_grad = jnp.stack([gain_one_grad, gain_two_grad, omega_grad])
    small_totals = (
        lax.psum_scatter(gains_grad, (DP, FS), scatter_dimension=1, tiled=True),
        lax.psum_scatter(ema_grad, (DP, FS), scatter_dimension=1, tiled=True),
        lax.psum_scatter(attn_grad, (DP, FS), scatter_dimension=0, tiled=True),
    )
    totals = reduce_gradients(value_grad, mix_grad, merge_grad, up_grad, down_grad)
    return (
        result,
        grad_tokens,
        totals[0],
        totals[1],
        totals[2],
        totals[3],
        totals[4],
        small_totals[0],
        small_totals[1],
        small_totals[2],
    )


STRIP = 128
MESH = pl.DeviceIdType.MESH
F32 = jnp.float32
LOW = jnp.bfloat16
SHARDED = VALUE, MIX, MERGE, UP, DOWN = range(5)
TOK, COT = 5, 6


def mm(a, b):
    return lax.dot_general(a, b, (((1,), (0,)), ((), ())), preferred_element_type=F32)


def mm_nt(a, b):
    return lax.dot_general(a, b, (((1,), (1,)), ((), ())), preferred_element_type=F32)


def mm_tn(a, b):
    return lax.dot_general(a, b, (((0,), (0,)), ((), ())), preferred_element_type=F32)


def at_rows(start, size, unit=16):
    return pl.ds(pl.multiple_of(start, unit), size)


def row_loop(count, size, body, first=0, unroll=1):
    def step(i, carry):
        body(pl.multiple_of(first + i * size, size))
        return carry

    lax.fori_loop(0, count // size, step, 0, unroll=unroll)


def slope_of(value, gate):
    return gate * (1.0 + value * (1.0 - gate))


def layer_kernel(trees, depth, *refs):
    ref, at = types.SimpleNamespace(), 0
    for tree in trees:
        ref.__dict__.update(jax.tree.unflatten(tree, refs[at : at + tree.num_leaves]))
        at += tree.num_leaves
    tok, cot, gains, ema_in, omega_in, attn = ref.tok, ref.cot, ref.gains, ref.ema_in, ref.omega_in, ref.attn
    rows, width = tok.shape
    tiles = width // 128
    dp, fs = lax.axis_index(DP), lax.axis_index(FS)
    z, c, y, x = dp // 2, dp % 2, fs // 2, fs % 2
    q = c * 2 + x

    def place(z, c, y, x):
        return (z * 2 + c, y * 2 + x)

    sib, xn, xc, yn = place(z, 1 - c, y, x), place(z, c, y, 1 - x), place(z, 1 - c, y, 1 - x), place(z, c, 1 - y, x)
    half_z = z // 2
    partner, far_mid, far_end = z + 1 - 2 * (z % 2), 2 - half_z, 3 * (1 - half_z)
    middle = (z % 2 + half_z) % 2 == 1
    outer = (z % 2 + half_z) % 2 == 0
    line = (far_end, far_mid, partner, z)
    zs = [None] + [place((z + d) % depth, c, y, x) for d in range(1, depth)]
    mates = ((sib, 1 - c, x), (xn, c, 1 - x), (xc, 1 - c, 1 - x))
    plane = [(pc, py, px) for pc in range(2) for py in range(2) for px in range(2)][1:]
    plane = [((c + pc) % 2, (y + py) % 2, (x + px) % 2) for pc, py, px in plane]

    send_sems, recv_sems, local_sems = ref.send_sems, ref.recv_sems, ref.local_sems
    used, used_local, pending = [0], [0], []

    def new_id():
        used[0] += 1
        return used[0] - 1

    def send(src, dst, peer, arrives=None, when=None):
        k = new_id()
        copy = pltpu.make_async_remote_copy(
            src_ref=src, dst_ref=dst, send_sem=send_sems.at[k], recv_sem=recv_sems.at[k if arrives is None else arrives],
            device_id=peer, device_id_type=MESH,
        )
        if when is None:
            copy.start()
        else:
            pl.when(when)(copy.start)
        handle = [k, copy, False, when]
        pending.append(handle)
        return handle

    def sent(handle):
        if not handle[2]:
            if handle[3] is None:
                handle[1].wait_send()
            else:
                pl.when(handle[3])(handle[1].wait_send)
            handle[2] = True

    def received(handle, landed):
        k = handle if isinstance(handle, int) else handle[0]
        pltpu.make_async_remote_copy(
            src_ref=landed, dst_ref=landed, send_sem=send_sems.at[k], recv_sem=recv_sems.at[k],
            device_id=sib, device_id_type=MESH,
        ).wait_recv()

    def local(src, dst):
        k = used_local[0]
        used_local[0] += 1
        copy = pltpu.make_async_copy(src, dst, local_sems.at[k])
        copy.start()
        return copy

    lens = ref.lens
    ends, run = [], 0
    for i in range(lens.shape[1]):
        run = run + lens[0, i]
        ends.append(run)

    def kept(k):
        start = 0
        for i, end in enumerate(ends):
            start = start + jnp.where(end <= k * CHUNK, lens[0, i], 0)
        return jnp.where(k * CHUNK - start == 0, 0.0, 1.0)

    def live_rows(r, size):
        places = r + lax.broadcasted_iota(jnp.int32, (size, 1), 0)
        return (places < ends[-1]).astype(F32)

    small_all, packed = ref.small_all, ref.packed
    states_at = ref.ema_params.shape[1]
    params = jnp.zeros((states_at, 128), F32)
    for p in range(4):
        v = ref.ema_params[p].astype(F32)
        v = jnp.concatenate([v, jnp.zeros((states_at, 128 - v.shape[1]), F32)], axis=1)
        params = params + (pltpu.roll(v, p * 32, 1) if p else v)
    packed[0:states_at, :] = params.astype(LOW)
    singles = [ref.norm_gains[p : p + 1, :] for p in range(3)] + [ref.attn_params[...]]
    row = jnp.zeros((1, 128), F32)
    for p, v in enumerate(singles):
        v = jnp.concatenate([v.astype(F32), jnp.zeros((1, 128 - v.shape[1]), F32)], axis=1)
        row = row + (pltpu.roll(v, p * 32, 1) if p else v)
    packed[16:32, :] = jnp.broadcast_to(row, (16, 128)).astype(LOW)
    lane_group = lax.broadcasted_iota(jnp.int32, (1, 128), 1) // 32

    def slot(pc, py, px, pz):
        return (pc * 4 + py * 2 + px) * depth + pz

    def small_start():
        return [send(packed, small_all.at[slot(c, y, x, z)], zs[d]) for d in range(1, depth)]

    def small_relay(handles):
        for d, handle in enumerate(handles):
            received(handle, small_all.at[slot(c, y, x, (z + depth - 1 - d) % depth)])
        small_all[slot(c, y, x, z)] = packed[...]
        mine = small_all.at[pl.ds(slot(c, y, x, 0), depth)]
        return [send(mine, mine, place(z, *p)) for p in plane]

    def small_finish(handles):
        for handle, p in zip(handles, plane):
            received(handle, small_all.at[pl.ds(slot(*p, 0), depth)])
        states = ema_in.shape[0] // (4 * tiles)
        gains[...] = jnp.zeros_like(gains)
        attn[...] = jnp.zeros_like(attn)
        for t in range(tiles):
            pz, pc = t // 2, t % 2
            got = [small_all[slot(pc, f // 2, f % 2, pz)].astype(F32)[0 : states + 8, :] for f in range(4)]
            for p in range(4):
                v = jnp.zeros_like(got[0])
                for f in range(4):
                    turn = (f - p) * 32 % 128
                    v = jnp.where(lane_group == f, pltpu.roll(got[f], turn, 1) if turn else got[f], v)
                ema_in[pl.ds(p * states * tiles + t, states, stride=tiles), :] = v[0:states]
                row = v[states : states + 1]
                if p < 3:
                    gains[p : p + 1, t * 128 : (t + 1) * 128] = row
                    if p == 2:
                        omega_in[t : t + 1, :] = row
                    continue
                for f in range(4):
                    turn = (t % 2 * 64 - f * 16) % 128
                    mine = lax.broadcasted_iota(jnp.int32, (1, 128), 1) // 16 == t % 2 * 4 + f
                    moved = pltpu.roll(row, turn, 1) if turn else row
                    attn[t // 2 : t // 2 + 1, :] += jnp.where(mine, moved, 0.0)

    lane = lax.broadcasted_iota(jnp.int32, (1, 128), 1)
    shift = fs * 32

    def mix_align():
        raw, win, line_up = ref.s[MIX], ref.mix_win, ref.by_time
        line_up[0 : win.shape[1], :] = jnp.zeros((win.shape[1], 128), F32)

        def load(r):
            line_up[at_rows(shift + r, 32, 32), :] = raw[pl.ds(r, 32), :].astype(F32)

        row_loop(raw.shape[0], 32, load)
        for t in range(win.shape[1] // 128):
            win[:, t * 128 : (t + 1) * 128] = line_up[t * 128 : (t + 1) * 128, :].T.astype(LOW)

    weights = {m: ref.w[m] for m in SHARDED}
    block_shape = {m: (w.shape[0] // depth, w.shape[1] // 2) for m, w in weights.items()}

    def block(m, zz, yy):
        rb, cb = block_shape[m]
        return weights[m].at[at_rows(zz * rb, rb), at_rows(yy * cb, cb, 128)]

    def piece(m, src_c, src_x):
        rb, cb = block_shape[m]
        half = cb // 2
        if m in (VALUE, UP):
            return weights[m].at[at_rows(z * rb + src_c * (rb // 2), rb // 2), at_rows(y * cb + src_x * half, half, 128)]
        return weights[m].at[at_rows(z * rb, rb), at_rows(y * cb + src_x * half, half, 128)]

    def move(src, dst):
        rows_at_once = 32

        def step(r):
            dst[pl.ds(r, rows_at_once), :] = src[pl.ds(r, rows_at_once), :]

        row_loop(src.shape[0], rows_at_once, step)

    spare, near, loads, top = ref.up_low, {MIX: ref.mix_win}, {}, 0
    for m in (VALUE, MERGE, UP, DOWN):
        tall, wide = ref.s[m].shape
        near[m] = spare.at[top : top + tall, 0:wide]
        loads[m] = local(ref.s[m], near[m])
        top += tall
    for k in (TOK, COT):
        loads[k] = local(ref.acts[k - TOK], (tok, cot)[k - TOK])
    barrier = pltpu.get_barrier_semaphore()
    peers = [place(z, *p) for p in plane] + zs[1:]
    for peer in peers:
        pl.semaphore_signal(barrier, inc=1, device_id=peer, device_id_type=MESH)
    pl.semaphore_wait(barrier, len(peers))

    swaps = {m: [] for m in SHARDED}

    def swap_start(m):
        shard = near[m]
        if m in loads:
            loads[m].wait()
        if m == MIX:
            first, last = 1 - (fs + 2) // 3, fs // 3
            middle = 1 - first - last
            for peer, pc, px in mates + ((None, c, x),):
                pq = pc * 2 + px
                tiles_at = (
                    first * 2 * pq,
                    (first + last) * (1 + 2 * pq) + middle * (1 + pq),
                    first * 8 + last * (2 + 2 * pq) + middle * (5 + pq),
                )
                for i, tile in enumerate(tiles_at):
                    src = shard.at[:, at_rows(tile * 128, 128, 128)]
                    dst = ref.mix_in.at[x, at_rows(c * 128, 128), pl.ds(i * 128, 128)]
                    if peer is None:
                        move(src, dst)
                    else:
                        swaps[m].append((send(src, dst, peer), pc, px, i))
            return
        if m in (VALUE, UP):
            wide = shard.shape[1] // 4
            for peer, pc, px in mates + ((None, c, x),):
                src = shard.at[:, at_rows((pc * 2 + px) * wide, wide, 128)]
                if peer is None:
                    move(src, piece(m, c, x))
                else:
                    swaps[m].append((send(src, piece(m, c, x), peer), pc, px, 0))
            return
        tall = shard.shape[0] // 2
        swaps[m].append((send(shard.at[at_rows((1 - x) * tall, tall), :], piece(m, c, x), xn), c, 1 - x, 0))
        move(shard.at[at_rows(x * tall, tall), :], piece(m, c, x))

    z_ids, z_sends, y_sends = {}, {}, {}

    def swap_finish(m):
        for handle, pc, px, i in swaps[m]:
            if m == MIX:
                received(handle, ref.mix_in.at[px, at_rows(pc * 128, 128), pl.ds(i * 128, 128)])
            else:
                received(handle, piece(m, pc, px))
        if m == MIX:
            only = (q == 3).astype(F32)
            low_y = (y == 0).astype(F32)
            lead = jnp.broadcast_to(jnp.maximum(low_y, only), (1, 128))
            rb, cb = block_shape[m]
            a, b, w = ref.mix_in.at[0], ref.mix_in.at[1], weights[m]

            def combine(r):
                at = pl.ds(r, 64)
                to = at_rows(z * rb + r, 64)

                def put(i, v):
                    w[to, at_rows(y * cb + i * 128, 128, 128)] = v.astype(LOW)

                put(0, a[at, 0:128].astype(F32) * lead)
                put(1, a[at, 128:256])
                put(2, a[at, 256:384].astype(F32) + b[at, 0:128].astype(F32) * lead)
                put(3, b[at, 128:256])
                put(4, b[at, 256:384])

            row_loop(rb, 64, combine)

    def y_own(m):
        y_sends[m] = [(3, send(block(m, z, y), block(m, z, y), yn))]

    def z_start(m, far=False):
        own = block(m, z, 1 - y if far else y)
        ids = [new_id() for _ in range(3)]
        z_ids[m, far] = ids
        z_sends.setdefault(m, []).extend(
            [
                send(own, own, place(partner, c, y, x), ids[2]),
                send(own, own, place(far_mid, c, y, x), ids[1], middle),
                send(own, own, place(far_mid, c, y, x), ids[0], outer),
            ]
        )

    def z_received(m, i, far, when):
        there = block(m, line[i], 1 - y if far else y)
        pl.when(when)(functools.partial(received, z_ids[m, far][i], there))
        return there

    def z_pass(m, steps=(1, 0), far=False):
        for i in steps:
            there = z_received(m, i, far, middle)
            z_sends[m].append(send(there, there, place(partner, c, y, x), z_ids[m, far][i], middle))

    def z_far(m):
        received(y_sends[m][0][1], block(m, z, 1 - y))
        z_start(m, True)

    def z_finish(m):
        for far in (False, True):
            received(z_ids[m, far][2], block(m, partner, 1 - y if far else y))
            for i in (1, 0):
                z_received(m, i, far, outer)

    def y_forward(m, steps=(2, 1, 0)):
        for i in steps:
            there = block(m, line[i], y)
            if i == 2:
                received(z_ids[m, False][i], there)
            else:
                z_received(m, i, False, outer)
            y_sends[m].append((i, send(there, there, yn)))

    def y_finish(m):
        for i, handle in y_sends[m]:
            received(handle, block(m, line[i], 1 - y))

    def group_rows(c, x):
        return at_rows((c * 2 + x) * rows, rows)

    def part_rows(c, x, first, count):
        return at_rows((c * 2 + x) * rows + first, count)

    def gather_start(buf, first=0, count=None):
        count = rows if count is None else count
        own = buf.at[part_rows(c, x, first, count), :]
        return [(first, count), send(own, own, xn), send(own, own, sib)]

    def gather_relay(buf, handles):
        other = buf.at[part_rows(c, 1 - x, *handles[0]), :]
        received(handles[1], other)
        handles.append(send(other, other, sib))

    def gather_finish(buf, handles):
        received(handles[2], buf.at[part_rows(1 - c, x, *handles[0]), :])
        received(handles[3], buf.at[part_rows(1 - c, 1 - x, *handles[0]), :])

    total = ref.total
    stage = [ref.stage.at[0], ref.stage.at[1], ref.stage.at[2], ref.hidden_mul]
    staged = [[], [], [], []]

    def stage_out(k, first, count, extra=None):
        def put(r):
            at = pl.ds(r, 32)
            v = total[at, :]
            if extra is not None:
                v = v + extra[at, :].astype(F32)
            stage[k][at, :] = v.astype(LOW)

        row_loop(count, 32, put, first)

    def stage_free(k):
        for handle in staged[k]:
            sent(handle)
        staged[k] = []

    def reduce_first(partial, sibs):
        for k, px in ((0, 1 - x), (1, x)):
            partial(1 - c, px)
            stage_free(k)
            stage_out(k, 0, rows)
            staged[k] = [send(stage[k], sibs[k], sib)]
        return staged[0][0], staged[1][0]

    def reduce_cross(partial, sibs, cross, handles, slot=2):
        halves = (pl.ds(0, rows // 2), pl.ds(rows // 2, rows // 2))
        partial(c, 1 - x)
        received(handles[0], sibs[0])
        stage_free(slot)
        for i, half in enumerate(halves):
            stage_out(slot, i * (rows // 2), rows // 2, sibs[0])
            staged[slot].append(send(stage[slot].at[half, :], cross.at[half, :], xn))
        return handles[1], list(zip(staged[slot], (cross.at[half, :] for half in halves)))

    def reduce_early(partial, sibs, cross):
        return reduce_cross(partial, sibs, cross, reduce_first(partial, sibs))

    def reduce_late(partial, sibs, cross, handles, consume):
        partial(c, x)
        received(handles[0], sibs[1])
        for i, (handle, half) in enumerate(handles[1]):
            received(handle, half)
            consume(i * (rows // 2), rows // 2)

    def reduced(r, size, sibs, cross):
        at = pl.ds(r, size)
        return total[at, :] + sibs[1][at, :].astype(F32) + cross[at, :].astype(F32)

    sibs_a, sibs_b = ((r.at[0], r.at[1]) for r in (ref.sibs_a, ref.sibs_b))
    cross_a, cross_b = ref.cross_a, ref.cross_b
    sibs_c, cross_c = (ref.gc.at[2 * rows : 3 * rows, :], ref.gc.at[3 * rows : 4 * rows, :]), ref.update_in

    w_up = weights[UP]
    y_out = {
        DOWN: ref.mix_pack.at[:, 384 : 384 + block_shape[DOWN][1]],
        UP: ref.yo,
        MERGE: ref.gc.at[0 : weights[MERGE].shape[0], 0 : block_shape[MERGE][1]],
        MIX: w_up.at[:, 0 : block_shape[MIX][1]],
        VALUE: w_up.at[:, block_shape[MIX][1] : block_shape[MIX][1] + block_shape[VALUE][1]],
    }
    y_in = {m: ref.yi[m] for m in SHARDED}
    z_in = {m: ref.zi[m] for m in SHARDED}
    f_in = {m: ref.fi[m] for m in SHARDED}
    gy, gz, gf = {}, {}, {}

    def y_grad_send(m, product, steps=(0, 1, 2, 3)):
        rb, cb = block_shape[m]
        if m not in gy:
            gy[m], gz[m] = {}, [new_id() for _ in range(4)]
        for i in steps:
            at = at_rows(line[i] * rb, rb)
            y_out[m][at, :] = product(line[i], 1 - y).astype(LOW)
            gy[m][i] = send(y_out[m].at[at, :], y_in[m].at[at, :], yn)

    def y_grad_add(m, product, steps=(0, 1, 2, 3)):
        rb, cb = block_shape[m]
        for i in steps:
            at = at_rows(line[i] * rb, rb)
            own = product(line[i], y)
            received(gy[m][i], y_in[m].at[at, :])
            y_in[m][at, :] = (own + y_in[m][at, :].astype(F32)).astype(LOW)
            if i < 3:
                send(
                    y_in[m].at[at, :], z_in[m].at[i], place(partner, c, y, x), gz[m][i], outer if i < 2 else None
                )

    def z_relay(m, steps=(0, 1)):
        rb, cb = block_shape[m]
        for i in steps:
            at = at_rows(line[i] * rb, rb)

            @pl.when(middle)
            def _(i=i, at=at):
                received(gz[m][i], z_in[m].at[i])
                y_in[m][at, :] = (y_in[m][at, :].astype(F32) + z_in[m][i].astype(F32)).astype(LOW)

            send(y_in[m].at[at, :], z_in[m].at[3], place(line[i], c, y, x), gz[m][3], middle)

    def z_grad_add(m):
        rb, cb = block_shape[m]
        for i in (2, 3):
            received(gz[m][i], z_in[m].at[i])

        def add(r):
            at = at_rows(z * rb + r, 64)
            v = y_in[m][at, :].astype(F32)
            for i in (2, 3):
                v = v + z_in[m][i, pl.ds(r, 64), :].astype(F32)
            y_in[m][at, :] = v.astype(LOW)

        row_loop(rb, 64, add)
        to_owners(m)

    far_land = [ref.mix_in.at[i // 2, pl.ds(i % 2 * 128, 128), :] for i in range(4)]
    y_last = ref.mix_win.at[:, 0 : block_shape[MERGE][1]]

    def sides(m):
        return (False, y_in[m], [z_in[m].at[i] for i in range(4)]), (True, y_out[m], far_land)

    def first_send(m, product):
        rb, cb = block_shape[m]
        for far, _, _ in sides(m):
            gz[m, far] = [new_id() for _ in range(4)]
        for i in range(4):
            at = at_rows(line[i] * rb, rb)
            for far, buf, land in sides(m):
                buf[at, :] = product(line[i], 1 - y if far else y).astype(LOW)
                if i < 3:
                    send(
                        buf.at[at, :], land[i], place(partner, c, y, x), gz[m, far][i], outer if i < 2 else None
                    )

    def first_relay(m):
        rb, cb = block_shape[m]
        for i in (0, 1):
            at = at_rows(line[i] * rb, rb)
            for far, buf, land in sides(m):

                @pl.when(middle)
                def _(i=i, at=at, far=far, buf=buf, land=land):
                    received(gz[m, far][i], land[i])
                    buf[at, :] = (buf[at, :].astype(F32) + land[i][...].astype(F32)).astype(LOW)

                send(buf.at[at, :], land[3], place(line[i], c, y, x), gz[m, far][3], middle)

    def first_turn(m):
        rb, cb = block_shape[m]
        at = at_rows(z * rb, rb)
        for far, buf, land in sides(m):
            for i in (2, 3):
                received(gz[m, far][i], land[i])
            buf[at, :] = (buf[at, :].astype(F32) + land[2][...].astype(F32) + land[3][...].astype(F32)).astype(LOW)
        gy[m] = send(y_out[m].at[at, :], y_last, yn)

    def first_finish(m):
        rb, cb = block_shape[m]
        at = at_rows(z * rb, rb)
        received(gy[m], y_last)
        y_in[m][at, :] = (y_in[m][at, :].astype(F32) + y_last[...].astype(F32)).astype(LOW)
        to_owners(m)

    def to_owners(m):
        rb, cb = block_shape[m]
        gf[m] = []
        if m in (MERGE, DOWN):
            land = f_in[m].at[at_rows(x * rb, rb), :]

            def part(px):
                return y_in[m].at[at_rows(z * rb, rb), at_rows(px * (cb // 2), cb // 2, 128)]

            gf[m].append((send(part(1 - x), land, xn), f_in[m].at[at_rows((1 - x) * rb, rb), :]))
            move(part(x), land)
            return
        half = rb // 2

        def land_at(pc, px):
            if m == MIX:
                return f_in[m].at[pc * 2 + px]
            wide = f_in[m].shape[1] // 4
            return f_in[m].at[:, at_rows((pc * 2 + px) * wide, wide, 128)]

        def part(pc, px):
            if m == MIX:
                return y_in[m].at[at_rows(z * rb + pc * half, half), at_rows(px * 256, 384, 128)]
            return y_in[m].at[at_rows(z * rb + pc * half, half), at_rows(px * (cb // 2), cb // 2, 128)]

        for peer, pc, px in mates:
            gf[m].append((send(part(pc, px), land_at(c, x), peer), land_at(pc, px)))
        move(part(c, x), land_at(c, x))

    def grad_out(m):
        for handle, landed in gf[m]:
            received(handle, landed)
        if m != MIX:
            return
        out, src, line_up = ref.g_mix, f_in[MIX], ref.by_time
        first, last = (fs == 0).astype(F32), (fs == 3).astype(F32)
        mid = 1.0 - first - last
        first, last, mid = (jnp.broadcast_to(v, (1, 128)) for v in (first, last, mid))

        def get(p, t):
            return src[p, :, t * 128 : (t + 1) * 128].astype(F32)

        for tile in range(9):
            v = first * (get(tile // 2, tile % 2) if tile < 8 else src[q, :, 256:384].astype(F32))
            if tile == 0:
                v = v + (mid + last) * get(3, 0)
            else:
                v = v + mid * get((tile - 1) % 4, 1 + (tile - 1) // 4)
                v = v + last * get((tile - 1) // 2, 1 + (tile - 1) % 2)
            line_up[tile * 128 : (tile + 1) * 128, :] = v.T

        def write(r):
            out[pl.ds(r, 32), :] = line_up[at_rows(shift + r, 32, 32), :].astype(LOW)

        row_loop(out.shape[0], 32, write)

    h_small = small_start()
    mix_align()
    swap_start(MIX)
    h_small = small_relay(h_small)
    swap_start(VALUE)
    swap_start(MERGE)
    swap_finish(MIX)
    y_own(MIX)
    z_start(MIX)

    nl, ml, n2, gc, gm = (ref.nl, ref.ml, ref.n2, ref.gc, ref.gm)
    by_time, out_time, back_time = ref.by_time, ref.out_time, ref.back_time

    def centre(v):
        cen = v - jnp.mean(v, axis=-1, keepdims=True)
        return cen, lax.rsqrt(jnp.mean(cen * cen, axis=-1, keepdims=True) + 1e-05)

    def norm_one(r):
        cen, rate = centre(tok[pl.ds(r, 16), :].astype(F32))
        v = cen * rate * gains[0:1, :]
        nl[at_rows(q * rows + r, 16), :] = v.astype(LOW)
        for s in range(tiles):
            by_time[pl.ds(r * tiles + s, 16, stride=tiles), :] = v[:, s * 128 : (s + 1) * 128]

    small_finish(h_small)
    loads[TOK].wait()
    row_loop(rows, 16, norm_one)
    swap_finish(VALUE)
    y_own(VALUE)
    z_start(VALUE)

    def cot_low(r):
        at = pl.ds(r, 32)
        gc[at_rows(q * rows + r, 32), :] = (cot[at, :].astype(F32) * live_rows(r, 32)).astype(LOW)

    def load_ema():
        return ema_in[...].reshape(4, -1, tiles, 128)

    _, _, rate_all, weight_all = ema_coefficients(load_ema())
    omega = omega_in[...]
    marks = ref.marks

    def at_time(t):
        return at_rows(t * tiles, tiles, 8)

    def ema_chunk(k, state):
        state = state * kept(k)
        marks[k] = state

        def step(i, state):
            t = k * CHUNK + i
            v = by_time[at_time(t), :]
            state = rate_all * state + v[None]
            out_time[at_time(t), :] = jnp.sum(weight_all * state, axis=0) + omega * v
            return state

        return lax.fori_loop(0, CHUNK, step, state, unroll=4)

    lax.fori_loop(0, rows // CHUNK, ema_chunk, jnp.zeros_like(rate_all))

    def mixed(r):
        for s in range(tiles):
            at = pl.ds(r * tiles + s, 16, stride=tiles)
            v = out_time[at, :]
            gate = jax.nn.sigmoid(v)
            ml[at_rows(q * rows + r, 16), s * 128 : (s + 1) * 128] = (v * gate).astype(LOW)
            out_time[at, :] = slope_of(v, gate)

    row_loop(rows, 16, mixed)
    h_ml = gather_start(ml)
    swap_start(UP)
    h_nl = gather_start(nl)
    swap_finish(MERGE)
    z_start(MERGE)
    z_pass(MIX, (1,))
    y_forward(MIX, [2])
    swap_start(DOWN)
    loads[COT].wait()
    row_loop(rows, 32, cot_low)
    z_pass(MIX, (0,))
    y_forward(MIX, [1])
    z_pass(VALUE)
    gather_relay(ml, h_ml)
    y_forward(MIX, [0])
    y_own(MERGE)
    y_forward(VALUE)
    swap_finish(UP)
    z_start(UP)
    gather_finish(ml, h_ml)
    z_pass(MERGE)

    value_low, value_slope = ref.value_low, ref.value_slope
    vq = value_low.shape[1]

    def value_block(r):
        total[:, :vq] = mm(nl[pl.ds(r, rows), :], weights[VALUE][...])

        def act(s):
            v = total[pl.ds(s, 32), :vq]
            gate = jax.nn.sigmoid(v)
            value_low[at_rows(r + s, 32), :] = (v * gate).astype(LOW)
            value_slope[at_rows(r + s, 32), :] = slope_of(v, gate).astype(LOW)

        row_loop(rows, 32, act)

    y_finish(MIX)

    w_mix, reset_w = weights[MIX], ref.reset_w
    half_mix = w_mix.shape[1] // 2

    def fix_reset(r):
        at = pl.ds(r, 64)
        reset_w[at, 0:128] = w_mix[at, 384:512]
        reset_w[at, 128:256] = (w_mix[at, 512:640].astype(F32) + w_mix[at, half_mix : half_mix + 128].astype(F32)).astype(LOW)

    row_loop(width, 64, fix_reset)

    def w_update():
        return w_mix[:, 0:256]

    def w_shared():
        return w_mix[:, 256:384]

    def w_late():
        return w_mix[:, half_mix + 128 : half_mix + 384]

    def w_hidden():
        return w_mix[:, half_mix + 384 : half_mix + 640]

    scale = float(STRETCH) ** -0.5
    stretch = STRETCH
    shared_pre, query, key, probs = ref.shared_pre, ref.query, ref.key, ref.probs
    probs_low = ref.probs_low
    shared_pre[...] = mm(ml[group_rows(c, x), :], w_shared())
    sv = shared_pre[...]
    shared = sv * jax.nn.sigmoid(sv)
    query[...] = (shared * attn[0:1, :] + attn[1:2, :]).astype(LOW)
    key[...] = (shared * attn[2:3, :]).astype(LOW)
    bias = pltpu.roll(jnp.broadcast_to(attn[3:4, :], (stretch, stretch)), 0, 1, stride=1, stride_axis=0).T
    row_id = lax.broadcasted_iota(jnp.int32, (stretch, stretch), 0)
    col_id = lax.broadcasted_iota(jnp.int32, (stretch, stretch), 1)
    for n in range(rows // stretch):
        at = pl.ds(n * stretch, stretch)
        scores = mm_nt(query[at, :], key[at, :]) * scale + bias
        scores = jnp.where(row_id >= col_id, scores, -1000000000.0)
        ex = jnp.exp(scores - jnp.max(scores, axis=-1, keepdims=True))
        pr = ex / jnp.sum(ex, axis=-1, keepdims=True)
        probs[at, :] = pr
        probs_low[at_rows(q * rows + n * stretch, stretch), :] = pr.astype(LOW)
    own_probs = probs_low.at[group_rows(c, x), :]
    h_probs = [send(own_probs, own_probs, peer) for peer, _, _ in mates]

    mix_pack, update_in = ref.mix_pack, ref.update_in
    hidden_at = pl.ds(mix_pack.shape[1] - 256, 256)
    update_out = mix_pack.at[:, hidden_at]

    def update_block(r):
        update_out[pl.ds(r, rows), :] = mm(ml[pl.ds(r, rows), :], w_update()).astype(LOW)

    row_loop(4 * rows, rows, update_block)
    part_w = width // 4
    own_cols = at_rows(q * part_w, part_w, 128)
    h_update = [
        send(update_out.at[group_rows(pc, px), :], update_in.at[:, own_cols], peer) for peer, pc, px in mates
    ]
    update_in[:, own_cols] = update_out[group_rows(c, x), :]
    gather_relay(nl, h_nl)
    h_gc = gather_start(gc)

    reset_gate, reset_slope = ref.reset_gate, ref.reset_slope

    def reset_block(r):
        at = pl.ds(r, rows)
        total[:, 0:256] = mm(ml[at, :], reset_w[...])
        total[:, 256:512] = mm(ml[at, :], w_late())

        def act(s):
            v = total[pl.ds(s, 32), :vq]
            gate = jax.nn.sigmoid(v)
            reset_gate[at_rows(r + s, 32), :] = (v * gate).astype(LOW)
            reset_slope[at_rows(r + s, 32), :] = slope_of(v, gate).astype(LOW)

        row_loop(rows, 32, act)

    row_loop(4 * rows, rows, reset_block)
    y_forward(MERGE)
    swap_finish(DOWN)
    z_start(DOWN)
    y_own(DOWN)
    z_pass(UP, (1,))
    gather_finish(nl, h_nl)
    y_finish(VALUE)
    row_loop(4 * rows, rows, value_block)
    z_pass(UP, (0,))
    y_own(UP)
    y_forward(UP, [2])
    for handle, (_, pc, px) in zip(h_probs, mates):
        received(handle, probs_low.at[group_rows(pc, px), :])

    gated = ref.gated

    def attend(r):
        at = pl.ds(r, stretch)
        total[0:stretch, :vq] = mm(probs_low[at, :], value_low[at, :])

        def act(s):
            v = total[pl.ds(s, 32), :vq]
            to = at_rows(r + s, 32)
            gated[to, :] = (v * reset_gate[to, :].astype(F32)).astype(LOW)
            reset_slope[to, :] = (v * reset_slope[to, :].astype(F32)).astype(LOW)

        row_loop(stretch, 32, act)

    row_loop(4 * rows, stretch, attend)
    z_pass(DOWN, (1,))
    y_forward(UP, [1])
    y_finish(MERGE)

    def merge_partial(c, x):
        at = group_rows(c, x)
        total[...] = mm(gated[at, :], weights[MERGE][...])
        total[:, own_cols] += mm(ml[at, :], w_hidden())

    h_red = reduce_early(merge_partial, sibs_a, cross_a)
    z_pass(DOWN, (0,))
    y_forward(UP, [0])
    for handle, (_, pc, px) in zip(h_update, mates):
        received(handle, update_in.at[:, at_rows((pc * 2 + px) * part_w, part_w, 128)])
    gather_relay(gc, h_gc)
    z_far(DOWN)

    after, hidden_mul, update_mul = ref.after, ref.hidden_mul, ref.update_mul

    def norm_two(r):
        at = pl.ds(r, 16)
        v = reduced(r, 16, sibs_a, cross_a)
        gate = jax.nn.sigmoid(v)
        hidden = v * gate
        u = jax.nn.sigmoid(update_in[at, :].astype(F32))
        xv = tok[at, :].astype(F32)
        av = u * hidden + (1.0 - u) * xv
        after[at, :] = av
        hidden_mul[at, :] = (u * slope_of(v, gate)).astype(LOW)
        update_mul[at, :] = ((hidden - xv) * u * (1.0 - u)).astype(LOW)
        cen, rate = centre(av)
        n2[at_rows(q * rows + r, 16), :] = (cen * rate * gains[1:2, :]).astype(LOW)

    h_n2 = []

    def take_merge(first, count):
        row_loop(count, 16, norm_two, first, 2)
        h_n2.append(gather_start(n2, first, count))

    reduce_late(merge_partial, sibs_a, cross_a, h_red, take_merge)
    z_pass(DOWN, (1,), True)
    up_low, up_slope = ref.up_low, ref.up_slope
    for m in SHARDED:
        for swap in swaps[m]:
            sent(swap[0])

    def up_block(r):
        total[...] = mm(n2[at_rows(r, rows), :], weights[UP][...])

        def act(s):
            v = total[pl.ds(s, 16), :]
            gate = jax.nn.sigmoid(v)
            up_low[at_rows(r + s, 16), :] = (v * gate).astype(LOW)
            up_slope[at_rows(r + s, 16), :] = slope_of(v, gate).astype(LOW)

        row_loop(rows, 16, act)

    def up_rows(c, x):
        up_block(pl.multiple_of((c * 2 + x) * rows, rows))

    gather_relay(n2, h_n2[0])
    z_pass(DOWN, (0,), True)
    y_finish(UP)
    up_rows(c, x)
    for handles in h_n2:
        received(handles[2], n2.at[part_rows(1 - c, x, *handles[0]), :])
    up_rows(1 - c, x)
    gather_relay(n2, h_n2[1])
    up_rows(c, 1 - x)
    for handles in h_n2:
        received(handles[3], n2.at[part_rows(1 - c, 1 - x, *handles[0]), :])
    up_rows(1 - c, 1 - x)
    gather_finish(gc, h_gc)

    def cols_of(m, yy):
        cb = block_shape[m][1]
        return at_rows(yy * cb, cb, 128)

    def rows_of(m, zz):
        rb = block_shape[m][0]
        return at_rows(zz * rb, rb, 128)

    def down_product(zz, yy):
        return mm_tn(up_low[:, rows_of(DOWN, zz)], gc[:, cols_of(DOWN, yy)])

    y_grad_send(DOWN, down_product)
    z_finish(DOWN)

    def down_partial(c, x):
        total[...] = mm(up_low[group_rows(c, x), :], weights[DOWN][...])

    def up_back(r):
        at = pl.ds(r, rows)
        total[...] = mm_nt(gc[at, :], weights[DOWN][...])

        def act(s):
            to = at_rows(r + s, 16)
            up_slope[to, :] = (total[pl.ds(s, 16), :] * up_slope[to, :].astype(F32)).astype(LOW)

        row_loop(rows, 16, act)

    row_loop(4 * rows, rows, up_back)
    grad_up = up_slope

    def two_partial(c, x):
        total[...] = mm_nt(grad_up[group_rows(c, x), :], weights[UP][...])

    def up_product(zz, yy):
        return mm_tn(n2[:, rows_of(UP, zz)], grad_up[:, cols_of(UP, yy)])

    h_red = reduce_early(two_partial, sibs_a, cross_a)
    y_grad_send(UP, up_product)
    y_grad_add(DOWN, down_product, (0, 1))
    for handle in h_gc[1:]:
        sent(handle)

    gain_sum, update_back = ref.gain_sum, hidden_mul
    gain_sum[...] = jnp.zeros_like(gain_sum)

    def norm_two_back(r):
        at = pl.ds(r, 16)
        g = reduced(r, 16, sibs_a, cross_a)
        cen, rate = centre(after[at, :])
        unit = cen * rate
        gain_sum[1] += g * unit
        g = g * gains[1:2, :]
        back = rate * (g - jnp.mean(g, axis=-1, keepdims=True) - unit * jnp.mean(g * unit, axis=-1, keepdims=True))
        back = back + cot[at, :].astype(F32) * live_rows(r, 16)
        gm[at_rows(q * rows + r, 16), :] = (back * hidden_mul[at, :].astype(F32)).astype(LOW)
        hidden_mul[at, :] = (back * update_mul[at, :].astype(F32)).astype(LOW)
        u = jax.nn.sigmoid(update_in[at, :].astype(F32))
        update_mul[at, :] = (back * (1.0 - u)).astype(LOW)

    h_gm = []

    def take_two(first, count):
        row_loop(count, 16, norm_two_back, first, 2)
        h_gm.append(gather_start(gm, first, count))

    reduce_late(two_partial, sibs_a, cross_a, h_red, take_two)
    for handle in h_update:
        sent(handle)
    update_grad = mix_pack.at[:, 0:256]
    own_rows = group_rows(c, x)
    h_update = [
        send(update_back.at[:, at_rows((pc * 2 + px) * part_w, part_w, 128)], update_grad.at[own_rows, :], peer)
        for peer, pc, px in mates
    ]
    update_grad[own_rows, :] = update_back[:, own_cols]

    y_grad_add(DOWN, down_product, (2, 3))
    z_relay(DOWN)
    def merge_product(zz, yy):
        return mm_tn(gated[:, rows_of(MERGE, zz)], gm[:, cols_of(MERGE, yy)])

    for handle in z_sends[UP] + [h for _, h in y_sends[UP]] + list(gy[DOWN].values()):
        sent(handle)
    grad_probs, probs_in = ref.grad_probs, ref.probs_in
    grad_att = reset_gate

    def gated_back(c, x):
        first = (c * 2 + x) * rows
        total[:, :vq] = mm_nt(gm[at_rows(first, rows), :], weights[MERGE][...])

        def act(s):
            to = at_rows(first + s, 32)
            g = total[pl.ds(s, 32), :vq]
            back = (g * reset_slope[to, :].astype(F32)).astype(LOW)
            mix_pack[to, 384:640] = back[:, 0:256]
            mix_pack[to, 640:768] = back[:, 128:256]
            mix_pack[to, 768:1024] = back[:, 256:512]
            mix_pack[to, hidden_at] = gm[to, own_cols]
            reset_gate[to, :] = (g * reset_gate[to, :].astype(F32)).astype(LOW)

        row_loop(rows, 32, act)

        def probs_back(r):
            at = at_rows(first + r, stretch)
            grad_probs[at, :] = mm_nt(grad_att[at, :], value_low[at, :]).astype(LOW)

        row_loop(rows, stretch, probs_back)

    gated_back(c, x)
    gather_relay(gm, h_gm[0])
    y_grad_add(UP, up_product, (0,))
    for handles in h_gm:
        received(handles[2], gm.at[part_rows(1 - c, x, *handles[0]), :])
    gated_back(1 - c, x)
    gather_relay(gm, h_gm[1])
    gated_back(c, 1 - x)
    for handles in h_gm:
        received(handles[3], gm.at[part_rows(1 - c, 1 - x, *handles[0]), :])
    gated_back(1 - c, 1 - x)
    h_probs = [
        send(grad_probs.at[group_rows(pc, px), :], probs_in.at[i], peer) for i, (peer, pc, px) in enumerate(mates)
    ]
    y_grad_add(UP, up_product, (1,))
    first_send(MERGE, merge_product)
    for handle, (_, pc, px) in zip(h_update, mates):
        received(handle, update_grad.at[group_rows(pc, px), :])

    shared_grad = mix_pack.at[:, 256:384]

    def mixed_partial(cc, xx):
        at = group_rows(cc, xx)
        total[...] = (
            mm_nt(update_grad[at, :], w_update())
            + mm_nt(mix_pack[at, 384:640], reset_w[...])
            + mm_nt(mix_pack[at, 768:1024], w_late())
            + mm_nt(mix_pack[at, hidden_at], w_hidden())
        )


    def value_back(r):
        at = pl.ds(r, stretch)
        total[0:stretch, :vq] = mm_tn(probs_low[at, :], grad_att[at, :])

        def act(s):
            to = at_rows(r + s, 32)
            value_slope[to, :] = (total[pl.ds(s, 32), :vq] * value_slope[to, :].astype(F32)).astype(LOW)

        row_loop(stretch, 32, act)

    row_loop(4 * rows, stretch, value_back)
    grad_value = value_slope

    def value_product(zz, yy):
        return mm_tn(nl[:, rows_of(VALUE, zz)], grad_value[:, cols_of(VALUE, yy)])

    y_grad_send(VALUE, value_product, (0, 1))
    y_grad_add(UP, up_product, (2, 3))

    for i, handle in enumerate(h_probs):
        received(handle, probs_in.at[i])
    anti = (row_id + col_id == stretch - 1).astype(LOW)
    lag_sum = jnp.zeros((1, stretch), F32)
    grads_q = jnp.zeros((1, stretch), F32)
    grads_o = jnp.zeros((1, stretch), F32)
    grads_k = jnp.zeros((1, stretch), F32)
    for n in range(rows // stretch):
        at = pl.ds(n * stretch, stretch)
        to = at_rows(q * rows + n * stretch, stretch)
        g = grad_probs[to, :].astype(F32)
        for i in range(3):
            g = g + probs_in[i, at, :].astype(F32)
        pr = probs[at, :]
        gs = (pr * (g - jnp.sum(pr * g, axis=-1, keepdims=True))).astype(LOW)
        gq = mm(gs, key[at, :]) * scale
        gk = mm_tn(gs, query[at, :]) * scale
        lags = pltpu.roll(mm_nt(anti, gs), 1, 1, stride=1, stride_axis=0)
        lag_sum += jnp.sum(lags, axis=0, keepdims=True)
        sv = shared_pre[at, :]
        gate = jax.nn.sigmoid(sv)
        sh = sv * gate
        grads_q += jnp.sum(gq * sh, axis=0, keepdims=True)
        grads_o += jnp.sum(gq, axis=0, keepdims=True)
        grads_k += jnp.sum(gk * sh, axis=0, keepdims=True)
        gsh = gq * attn[0:1, :] + gk * attn[2:3, :]
        shared_grad[to, :] = (gsh * slope_of(sv, gate)).astype(LOW)
    attn_rows = (grads_q, grads_o, grads_k, lag_sum)
    own_shared = shared_grad.at[own_rows, :]
    h_shared = [send(own_shared, own_shared, peer) for peer, _, _ in mates]
    h_mixed = reduce_early(mixed_partial, sibs_a, cross_a)


    for handle, (_, pc, px) in zip(h_shared, mates):
        received(handle, shared_grad.at[group_rows(pc, px), :])

    def mix_product(zz, yy):
        return mm_tn(ml[:, rows_of(MIX, zz)], mix_pack[:, cols_of(MIX, yy)])

    y_grad_send(MIX, mix_product)
    z_relay(UP)
    first_relay(MERGE)
    y_grad_send(VALUE, value_product, (2, 3))
    y_grad_add(VALUE, value_product, (0, 1))
    z_grad_add(DOWN)
    for handle in h_update:
        sent(handle)
    h_down = reduce_first(down_partial, sibs_c)

    def mixed_own(cc, xx):
        mixed_partial(cc, xx)
        total[...] += mm_nt(shared_grad[own_rows, :], w_shared())


    def to_time(r):
        v = reduced(r, 16, sibs_a, cross_a)
        for s in range(tiles):
            at = pl.ds(r * tiles + s, 16, stride=tiles)
            out_time[at, :] = out_time[at, :] * v[:, s * 128 : (s + 1) * 128]

    reduce_late(mixed_own, sibs_a, cross_a, h_mixed, lambda first, count: row_loop(count, 16, to_time, first, 2))

    def value_partial(cc, xx):
        total[...] = mm_nt(grad_value[group_rows(cc, xx), :], weights[VALUE][...])

    h_red = reduce_early(value_partial, sibs_b, cross_b)
    y_grad_add(MIX, mix_product, (0,))

    held = ref.held
    ema = load_ema()
    damping, decay_gate, rate_all, weight_all = ema_coefficients(ema)
    omega = omega_in[...]
    half = rate_all.shape[0] // 2
    chunks = rows // CHUNK
    sums = []
    for part in range(2):
        js = slice(part * half, (part + 1) * half)
        rate, weight = rate_all[js], weight_all[js]

        def chunk(m, carry, js=js, rate=rate, weight=weight, part=part):
            k = chunks - 1 - m
            held[0] = marks[k, js]

            def ahead(i, state):
                state = rate * state + by_time[at_time(k * CHUNK + i), :][None]
                held[i + 1] = state
                return state

            lax.fori_loop(0, CHUNK, ahead, held[0], unroll=4)

            def back(n, carry):
                s, dw, dr, dom = carry
                i = CHUNK - 1 - n
                t = at_time(k * CHUNK + i)
                g = out_time[t, :]
                s = rate * s + g[None]
                dx = jnp.sum(weight * s, axis=0)
                if part == 0:
                    back_time[t, :] = dx + omega * g
                    dom = dom + g * by_time[t, :]
                else:
                    back_time[t, :] = back_time[t, :] + dx
                return s, dw + held[i + 1] * g[None], dr + held[i] * s, dom

            s, dw, dr, dom = lax.fori_loop(0, CHUNK, back, carry, unroll=2)
            return s * kept(k), dw, dr, dom

        zero = jnp.zeros_like(rate)
        carry = lax.fori_loop(0, chunks // 2, chunk, (zero, zero, zero, jnp.zeros_like(omega)))
        if part:
            y_grad_add(MIX, mix_product, (2,))
        else:
            y_grad_add(MIX, mix_product, (1,))
            z_relay(VALUE)
        sums.append(lax.fori_loop(chunks // 2, chunks, chunk, carry))
        if not part:
            h_down = reduce_cross(down_partial, sibs_c, cross_c, h_down, 3)
            z_relay(MIX, (0,))
            first_turn(MERGE)
    small = ref.by_time
    rate_scale = ema.shape[1] ** (-0.5)
    for part in range(2):
        js = slice(part * half, (part + 1) * half)
        dw, dr = sums[part][1], sums[part][2] * weight_all[js]
        d_damp = dw * ema[2, js] * ema[3, js] * rate_scale - dr * decay_gate[js]
        parts = (
            d_damp * damping[js] * (1.0 - damping[js]),
            -dr * damping[js] * decay_gate[js] * (1.0 - decay_gate[js]),
            dw * damping[js] * ema[3, js] * rate_scale,
            dw * damping[js] * ema[2, js] * rate_scale,
        )
        for p in range(4):
            for j in range(half):
                small[pl.ds((p * 2 * half + part * half + j) * tiles, tiles), :] = parts[p][j]

    tile_rows = ref.tile_rows
    states = 4 * ema.shape[1]
    gain_two = jnp.sum(gain_sum[1], axis=0, keepdims=True)
    for t in range(tiles):
        at = (t % 2) * depth + t // 2
        tile_rows[at, 0:states, :] = small[pl.ds(t, states, stride=tiles), :]
        tail = jnp.concatenate(
            [
                jnp.zeros((1, 128), F32),
                gain_two[:, t * 128 : (t + 1) * 128],
                sums[0][3][t : t + 1],
                attn_rows[t // 2],
                jnp.zeros((4, 128), F32),
            ],
            axis=0,
        )
        tile_rows[at, states : states + 8, :] = tail
    sib_in, z_small, x_small, y_small = ref.sib_in, ref.z_small, ref.x_small, ref.y_small
    h_sib = send(tile_rows.at[pl.ds((1 - c) * depth, depth)], sib_in, sib)
    z_relay(MIX, (1,))
    received(h_sib, sib_in)
    sib_in[...] += tile_rows[pl.ds(c * depth, depth)]
    h_zs = [send(sib_in.at[(z + d) % depth], z_small.at[d - 1], zs[d]) for d in range(1, depth)]

    def norm_one_back(r):
        at = pl.ds(r, 16)
        ema_part = jnp.concatenate(
            [back_time[pl.ds(r * tiles + s, 16, stride=tiles), :] for s in range(tiles)], axis=1
        )
        g = reduced(r, 16, sibs_b, cross_b) + ema_part
        cen, rate = centre(tok[at, :].astype(F32))
        unit = cen * rate
        gain_sum[0] += g * unit
        g = g * gains[0:1, :]
        back = rate * (g - jnp.mean(g, axis=-1, keepdims=True) - unit * jnp.mean(g * unit, axis=-1, keepdims=True))
        ref.grad_tokens[at, :] = (back + update_mul[at, :].astype(F32)).astype(LOW)

    reduce_late(
        value_partial, sibs_b, cross_b, h_red, lambda first, count: row_loop(count, 16, norm_one_back, first, 2)
    )
    one_rows, one_z, one_sum, one_plane = ref.one_rows, ref.one_z, ref.one_sum, ref.one_plane
    gain_one = jnp.sum(gain_sum[0], axis=0, keepdims=True)
    for t in range(tiles):
        one_rows[t] = jnp.broadcast_to(gain_one[:, t * 128 : (t + 1) * 128], (8, 128))
    h_one = [send(one_rows.at[pl.ds((z + d) % depth * 2, 2)], one_z.at[d - 1], zs[d]) for d in range(1, depth)]
    y_grad_add(MIX, mix_product, (3,))
    z_grad_add(UP)
    first_finish(MERGE)
    y_grad_add(VALUE, value_product, (2, 3))
    for d, handle in enumerate(h_zs):
        received(handle, z_small.at[d])
    x_small[0] = sib_in[z] + z_small[0] + z_small[1] + z_small[2]
    h_x = send(x_small.at[0], x_small.at[1], xn)
    z_grad_add(MIX)
    for d, handle in enumerate(h_one):
        received(handle, one_z.at[d])
    one_sum[...] = one_rows[pl.ds(z * 2, 2)] + one_z[0] + one_z[1] + one_z[2]
    h_one = [send(one_sum.at[p[0]], one_plane.at[i], place(z, *p)) for i, p in enumerate(plane)]
    received(h_x, x_small.at[1])
    y_small[0] = x_small[0] + x_small[1]
    h_y = send(y_small.at[0], y_small.at[1], yn)
    z_grad_add(VALUE)

    def finish(r):
        at = pl.ds(r, 16)
        ref.result[at, :] = (after[at, :] + reduced(r, 16, sibs_c, cross_c)).astype(LOW)

    reduce_late(down_partial, sibs_c, cross_c, h_down, lambda first, count: row_loop(count, 16, finish, first, 2))
    for m in (DOWN, UP, MERGE):
        grad_out(m)
    received(h_y, y_small.at[1])
    totals = y_small[0] + y_small[1]
    ref.small_out[...] = pltpu.roll(totals, (128 - shift) % 128, 1)
    one = one_sum[c]
    for i, handle in enumerate(h_one):
        received(handle, one_plane.at[i])
        one = one + one_plane[i]
    ref.small_out[states : states + 1, :] = pltpu.roll(one, (128 - shift) % 128, 1)[0:1]
    for m in (MIX, VALUE):
        grad_out(m)
    ref.attn_out[...] = pltpu.roll(totals[states : states + 8], (128 - c * 64 - fs * 16) % 128, 1)
    for handle in pending:
        sent(handle)
    assert used[0] <= COPIES


def finish_kernel(result, grad_tokens, value, mix, merge, up, down, small, attn, *outs):
    for src, out in zip((result, grad_tokens, value, mix, merge, up, down), outs):

        def widen(r, src=src, out=out):
            out[pl.ds(r, 32), :] = src[pl.ds(r, 32), :].astype(out.dtype)

        row_loop(out.shape[0], 32, widen)
    gains, ema, per = outs[7:]
    states, mine = ema.shape[1:]
    gains[...] = small[4 * states : 4 * states + 3, :mine]
    for p in range(4):
        ema[p] = small[p * states : (p + 1) * states, :mine]
    per[...] = attn[3:4, : per.shape[1]]


def layer_on_device(depth, tokens, cotangent, lengths, value_proj, mix_proj, merge_proj, up_proj, down_proj, norm_gains, ema_params, attn_params):
    rows, width = tokens.shape
    fs = lax.axis_index(FS)
    window = -(-mix_proj.shape[1] // 128) * 128
    group = 4 * rows
    vq = value_proj.shape[1]
    fq = up_proj.shape[1]
    quarters = ((width, vq), (width, 10 * STRIP), (vq, width), (width, fq), (fq, width))
    tiles = width // 128
    states = ema_params.shape[2]
    small_rows = 4 * states + 8
    shape = jax.ShapeDtypeStruct
    mix_turned = mix_proj.T
    ema_turned = jnp.swapaxes(ema_params, 1, 2)
    shards = (value_proj, mix_turned, merge_proj, up_proj, down_proj)
    inputs = dict(
        acts=(tokens, cotangent),
        lens=lengths,
        norm_gains=norm_gains,
        ema_params=ema_turned,
        attn_params=attn_params[None],
        s=shards,
    )
    landings = [w.shape for w in shards]
    landings[MIX] = (4, mix_proj.shape[0], 3 * STRIP)
    outputs = dict(
        result=shape((rows, width), LOW),
        grad_tokens=shape((rows, width), LOW),
        fi=tuple(shape(d, LOW) for d in landings),
        g_mix=shape(mix_turned.shape, LOW),
        small_out=shape((small_rows, 128), F32),
        attn_out=shape((8, 128), F32),
    )
    copies = pltpu.SemaphoreType.DMA((COPIES,))

    def low(*dims):
        return pltpu.VMEM(dims, LOW)

    def full(*dims):
        return pltpu.VMEM(dims, F32)

    scratch = dict(
        send_sems=copies,
        recv_sems=copies,
        local_sems=pltpu.SemaphoreType.DMA((32,)),
        w=tuple(low(*d) for d in quarters),
        yo=low(width, fq // 2),
        yi=tuple(low(r, k // 2) for r, k in quarters),
        zi=tuple(low(4, r // depth, k // 2) for r, k in quarters),
        mix_win=low(mix_proj.shape[0], window),
        small_all=low(8 * depth, 32, 128),
        packed=low(32, 128),
        ema_in=full(4 * states * tiles, 128),
        omega_in=full(tiles, 128),
        gains=full(8, width),
        attn=full(8, 128),
        tok=low(rows, width),
        cot=low(rows, width),
        nl=low(group, width),
        ml=low(group, width),
        n2=low(group, width),
        gc=low(group, width),
        gm=low(group, width),
        mix_in=low(2, 2 * mix_proj.shape[0], 4 * STRIP),
        reset_w=low(width, 256),
        value_low=low(group, vq),
        value_slope=low(group, vq),
        reset_gate=low(group, vq),
        reset_slope=low(group, vq),
        gated=low(group, vq),
        up_low=low(group, fq),
        up_slope=low(group, fq),
        update_in=low(rows, width),
        probs_low=low(group, STRETCH),
        probs=full(rows, STRETCH),
        shared_pre=full(rows, Z),
        query=low(rows, Z),
        key=low(rows, Z),
        grad_probs=low(group, STRETCH),
        probs_in=low(3, rows, STRETCH),
        mix_pack=low(group, 10 * STRIP),
        by_time=full(rows * tiles, 128),
        out_time=full(rows * tiles, 128),
        back_time=full(rows * tiles, 128),
        marks=full(rows // CHUNK, states, tiles, 128),
        held=full(CHUNK + 1, states // 2, tiles, 128),
        total=full(rows, width),
        stage=low(3, rows, width),
        sibs_a=low(2, rows, width),
        sibs_b=low(2, rows, width),
        cross_a=low(rows, width),
        cross_b=low(rows, width),
        after=full(rows, width),
        hidden_mul=low(rows, width),
        update_mul=low(rows, width),
        gain_sum=full(2, 16, width),
        tile_rows=full(tiles, small_rows, 128),
        sib_in=full(depth, small_rows, 128),
        z_small=full(depth - 1, small_rows, 128),
        x_small=full(2, small_rows, 128),
        y_small=full(2, small_rows, 128),
        one_rows=full(tiles, 8, 128),
        one_z=full(depth - 1, 2, 8, 128),
        one_sum=full(2, 8, 128),
        one_plane=full(7, 8, 128),
    )
    in_vmem = pl.BlockSpec(memory_space=pltpu.VMEM)
    specs = jax.tree.map(lambda _: in_vmem, inputs)
    anywhere = pl.BlockSpec(memory_space=pl.ANY)
    specs.update(
        lens=pl.BlockSpec(memory_space=pltpu.SMEM), acts=(anywhere,) * 2, s=tuple(in_vmem if m == MIX else anywhere for m in SHARDED)
    )
    in_leaves, in_tree = jax.tree.flatten(inputs)
    out_leaves, out_tree = jax.tree.flatten(outputs)
    scratch_leaves, scratch_tree = jax.tree.flatten(scratch, is_leaf=lambda v: not isinstance(v, (dict, tuple)))
    outs = pl.pallas_call(
        functools.partial(layer_kernel, (in_tree, out_tree, scratch_tree), depth),
        out_shape=tuple(out_leaves),
        in_specs=jax.tree.leaves(specs),
        out_specs=tuple(in_vmem for _ in out_leaves),
        scratch_shapes=scratch_leaves,
        compiler_params=pltpu.CompilerParams(collective_id=0, has_side_effects=True, vmem_limit_bytes=VMEM_BYTES),
        name="layer",
    )(*in_leaves)
    by = types.SimpleNamespace(**jax.tree.unflatten(out_tree, outs))
    grads = list(by.fi)
    grads[MIX] = by.g_mix
    wide = [shape(g.shape, F32) for g in (*grads, norm_gains, ema_turned)]
    *finals, attn_grad = pl.pallas_call(
        finish_kernel,
        out_shape=(shape((rows, width), LOW), shape((rows, width), LOW), *wide, shape((1, attn_params.shape[0]), F32)),
        in_specs=[in_vmem] * 9,
        out_specs=(in_vmem,) * 10,
        compiler_params=pltpu.CompilerParams(vmem_limit_bytes=VMEM_BYTES),
        name="finish",
    )(by.result, by.grad_tokens, *grads, by.small_out, by.attn_out)
    finals[2 + MIX] = finals[2 + MIX].T
    finals[-1] = jnp.swapaxes(finals[-1], 1, 2)
    return (*finals, attn_grad[0])


VMEM_BYTES = 64 << 20
COPIES = 256


def solution(mesh):
    in_specs = (
        P((DP, FS), None),
        P((DP, FS), None),
        P((DP, FS), None),
        P(DP, FS),
        P(DP, FS),
        P(DP, FS),
        P(DP, FS),
        P(DP, FS),
        P(None, (DP, FS)),
        P(None, (DP, FS), None),
        P((DP, FS)),
    )
    out_specs = (
        P((DP, FS), None),
        P((DP, FS), None),
        P(DP, FS),
        P(DP, FS),
        P(DP, FS),
        P(DP, FS),
        P(DP, FS),
        P(None, (DP, FS)),
        P(None, (DP, FS), None),
        P((DP, FS)),
    )
    fits = mesh.shape[DP] == 8 and mesh.shape[DP] // 2 * 4 * STRIP == V and mesh.shape[FS] * 4 * STRIP == V
    body = functools.partial(layer_on_device, mesh.shape[DP] // 2) if fits else on_device
    return jax.shard_map(body, mesh=mesh, in_specs=in_specs, out_specs=out_specs, check_vma=False)
```

```python
import functools
import types

import jax
import jax.numpy as jnp
from jax import lax
from jax.experimental import pallas as pl
from jax.experimental.pallas import tpu as pltpu
from jax.sharding import PartitionSpec as P

D = 1024
Z = 128
V = 2048
STRETCH = 128


DP, FS = "dp", "fsdp"
highest = lax.Precision.HIGHEST


def layer_norm(values, gain):
    centred = values - jnp.mean(values, axis=-1, keepdims=True)
    spread_sq = jnp.mean(centred * centred, axis=-1, keepdims=True)
    return centred * lax.rsqrt(spread_sq + 1e-05) * gain


def token_layout(length_row, row_count):
    places = jnp.arange(row_count, dtype=jnp.int32)
    running = jnp.cumsum(length_row)
    before = (running[None, :] <= places[:, None]).astype(jnp.int32)
    starts = jnp.sum(before * length_row[None, :], axis=1)
    return (places - starts, places < running[-1])


def ema_coefficients(ema):
    damping = jax.nn.sigmoid(ema[0])
    decay_gate = jax.nn.sigmoid(ema[1])
    keep_rate = 1.0 - damping * decay_gate
    weights_out = damping * ema[2] * ema[3] * ema.shape[1] ** (-0.5)
    return damping, decay_gate, keep_rate, weights_out


CHUNK = 32


def ema_forward_kernel(x_ref, ema_ref, omega_ref, keep_ref, y_ref, mark_ref):
    _, _, rate, weight = ema_coefficients(ema_ref[...])
    omega = omega_ref[...]

    def chunk(k, state):
        state = state * keep_ref[k][None]
        mark_ref[k] = state

        def step(i, state):
            t = k * CHUNK + i
            x = x_ref[t]
            state = rate * state + x[None]
            y_ref[t] = jnp.sum(weight * state, axis=0) + omega * x
            return state

        return lax.fori_loop(0, CHUNK, step, state, unroll=4)

    lax.fori_loop(0, x_ref.shape[0] // CHUNK, chunk, jnp.zeros_like(rate))


def ema_backward_kernel(x_ref, g_ref, ema_ref, omega_ref, keep_ref, mark_ref, dx_ref, dema_ref, domega_ref, h_ref):
    ema = ema_ref[...]
    damping, decay_gate, rate_all, weight_all = ema_coefficients(ema)
    omega = omega_ref[...]
    half = rate_all.shape[0] // 2
    chunks = x_ref.shape[0] // CHUNK
    sums = []
    for part in range(2):
        js = slice(part * half, (part + 1) * half)
        rate, weight = rate_all[js], weight_all[js]
        zero = jnp.zeros_like(rate)

        def chunk(m, carry, js=js, rate=rate, weight=weight, part=part):
            k = chunks - 1 - m
            h_ref[0] = mark_ref[k, js]

            def ahead(i, state):
                state = rate * state + x_ref[k * CHUNK + i][None]
                h_ref[i + 1] = state
                return state

            lax.fori_loop(0, CHUNK, ahead, h_ref[0], unroll=4)

            def back(n, carry):
                s, dw, dr, dom = carry
                i = CHUNK - 1 - n
                t = k * CHUNK + i
                g = g_ref[t]
                s = rate * s + g[None]
                dx = jnp.sum(weight * s, axis=0)
                if part == 0:
                    dx_ref[t] = dx + omega * g
                    dom = dom + g * x_ref[t]
                else:
                    dx_ref[t] = dx_ref[t] + dx
                dw = dw + h_ref[i + 1] * g[None]
                dr = dr + h_ref[i] * s
                return s, dw, dr, dom

            s, dw, dr, dom = lax.fori_loop(0, CHUNK, back, carry, unroll=2)
            return s * keep_ref[k][None], dw, dr, dom

        out = lax.fori_loop(0, chunks, chunk, (zero, zero, zero, jnp.zeros_like(omega)))
        sums.append(out)
    dw = jnp.concatenate([sums[0][1], sums[1][1]], axis=0)
    dr = jnp.concatenate([sums[0][2], sums[1][2]], axis=0) * weight_all
    scale = ema.shape[1] ** (-0.5)
    d_damp = dw * ema[2] * ema[3] * scale - dr * decay_gate
    dema_ref[0] = d_damp * damping * (1.0 - damping)
    dema_ref[1] = -dr * damping * decay_gate * (1.0 - decay_gate)
    dema_ref[2] = dw * damping * ema[3] * scale
    dema_ref[3] = dw * damping * ema[2] * scale
    domega_ref[...] = sums[0][3]


def ema_keep(position):
    starts = position.reshape(-1, CHUNK)[:, 0] != 0
    return jnp.broadcast_to(starts.astype(jnp.float32)[:, None, None], (starts.shape[0], 8, 128))


def ema_apply(x, ema, omega, keep):
    f32 = jnp.float32
    shape = jax.ShapeDtypeStruct
    return pl.pallas_call(
        ema_forward_kernel,
        out_shape=(shape(x.shape, f32), shape((keep.shape[0],) + ema.shape[1:], f32)),
        compiler_params=pltpu.CompilerParams(vmem_limit_bytes=32 << 20),
    )(x, ema, omega, keep)


def ema_reverse(x, g, ema, omega, keep, mark):
    f32 = jnp.float32
    shape = jax.ShapeDtypeStruct
    return pl.pallas_call(
        ema_backward_kernel,
        out_shape=(shape(x.shape, f32), shape(ema.shape, f32), shape(omega.shape, f32)),
        scratch_shapes=[pltpu.VMEM((CHUNK + 1, ema.shape[1] // 2) + ema.shape[2:], f32)],
        compiler_params=pltpu.CompilerParams(vmem_limit_bytes=32 << 20),
    )(x, g, ema, omega, keep, mark)


def silu_slope(values):
    logistic = jax.nn.sigmoid(values)
    return logistic * (1.0 + values * (1.0 - logistic))


def relative_table(rel_bias):
    lag_grid = (
        jnp.arange(STRETCH, dtype=jnp.int32)[:, None]
        - jnp.arange(STRETCH, dtype=jnp.int32)[None, :]
    )
    one_hot = (lag_grid[:, :, None] == jnp.arange(STRETCH, dtype=jnp.int32)[None, None, :]).astype(
        jnp.float32
    )
    bias_grid = jnp.einsum("ijl,l->ij", one_hot, rel_bias, precision=highest)
    return (lag_grid, one_hot, bias_grid)


def gather_forward(value_proj, mix_proj, merge_proj, up_proj, down_proj):
    first = (
        lax.all_gather(value_proj, DP, axis=0, tiled=True),
        lax.all_gather(mix_proj, DP, axis=0, tiled=True),
        lax.all_gather(merge_proj, DP, axis=0, tiled=True),
        lax.all_gather(up_proj, DP, axis=0, tiled=True),
        lax.all_gather(down_proj, DP, axis=0, tiled=True),
    )
    return (
        lax.all_gather(first[0], FS, axis=1, tiled=True),
        lax.all_gather(first[1], FS, axis=1, tiled=True),
        lax.all_gather(first[2], FS, axis=1, tiled=True),
        lax.all_gather(first[3], FS, axis=1, tiled=True),
        lax.all_gather(first[4], FS, axis=1, tiled=True),
    )


def reduce_gradients(value_grad, mix_grad, merge_grad, up_grad, down_grad):
    first = (
        lax.psum_scatter(
            value_grad.astype(jnp.bfloat16), DP, scatter_dimension=0, tiled=True
        ).astype(jnp.float32),
        lax.psum_scatter(
            mix_grad.astype(jnp.bfloat16), DP, scatter_dimension=0, tiled=True
        ).astype(jnp.float32),
        lax.psum_scatter(
            merge_grad.astype(jnp.bfloat16), DP, scatter_dimension=0, tiled=True
        ).astype(jnp.float32),
        lax.psum_scatter(
            up_grad.astype(jnp.bfloat16), DP, scatter_dimension=0, tiled=True
        ).astype(jnp.float32),
        lax.psum_scatter(
            down_grad.astype(jnp.bfloat16), DP, scatter_dimension=0, tiled=True
        ).astype(jnp.float32),
    )
    return (
        lax.psum_scatter(
            first[0].astype(jnp.bfloat16), FS, scatter_dimension=1, tiled=True
        ).astype(jnp.float32),
        lax.psum_scatter(
            first[1].astype(jnp.bfloat16), FS, scatter_dimension=1, tiled=True
        ).astype(jnp.float32),
        lax.psum_scatter(
            first[2].astype(jnp.bfloat16), FS, scatter_dimension=1, tiled=True
        ).astype(jnp.float32),
        lax.psum_scatter(
            first[3].astype(jnp.bfloat16), FS, scatter_dimension=1, tiled=True
        ).astype(jnp.float32),
        lax.psum_scatter(
            first[4].astype(jnp.bfloat16), FS, scatter_dimension=1, tiled=True
        ).astype(jnp.float32),
    )


def on_device(
    tokens,
    cotangent,
    lengths,
    value_proj,
    mix_proj,
    merge_proj,
    up_proj,
    down_proj,
    norm_gains,
    ema_params,
    attn_params,
):
    gains_full, ema_full, attn_full = (
        lax.all_gather(norm_gains, (DP, FS), axis=1, tiled=True),
        lax.all_gather(ema_params, (DP, FS), axis=1, tiled=True),
        lax.all_gather(attn_params, (DP, FS), axis=0, tiled=True),
    )
    value_full, mix_full, merge_full, up_full, down_full = gather_forward(
        value_proj, mix_proj, merge_proj, up_proj, down_proj
    )
    gains_float = gains_full.astype(jnp.float32)
    ema_float = ema_full.astype(jnp.float32)
    attn_float = attn_full.astype(jnp.float32)
    row_count = tokens.shape[0]
    position, live_rows = token_layout(lengths[0], row_count)
    tokens_float = tokens.astype(jnp.float32)
    normed, norm_back = jax.vjp(layer_norm, tokens_float, gains_float[0])
    normed_low = normed.astype(jnp.bfloat16)
    value_pre = jnp.dot(normed_low, value_full, preferred_element_type=jnp.float32)
    value_low = jax.nn.silu(value_pre).astype(jnp.bfloat16)

    lanes = (8, tokens.shape[1] // 8)
    ema_by_state = jnp.swapaxes(ema_float, 1, 2).reshape(4, -1, *lanes)
    omega = gains_float[2].reshape(lanes)
    keep = ema_keep(position)
    normed_rows = normed.reshape(row_count, *lanes)
    ema_rows, ema_marks = ema_apply(normed_rows, ema_by_state, omega, keep)
    ema_out = ema_rows.reshape(row_count, -1)
    mixed_low = jax.nn.silu(ema_out).astype(jnp.bfloat16)
    projected = jnp.dot(mixed_low, mix_full, preferred_element_type=jnp.float32)
    update_gate = jax.nn.sigmoid(projected[:, :D])
    shared_pre = projected[:, D : D + Z]
    reset_pre = projected[:, D + Z : D + Z + V]
    hidden_x = projected[:, D + Z + V :]
    shared = jax.nn.silu(shared_pre)
    reset_gate = jax.nn.silu(reset_pre)
    query_low = (shared * attn_float[:Z] + attn_float[Z : 2 * Z]).astype(jnp.bfloat16)
    key_low = (shared * attn_float[2 * Z : 3 * Z]).astype(jnp.bfloat16)
    block_count = row_count // STRETCH
    lag_grid, one_hot, bias_grid = relative_table(attn_float[3 * Z :])
    query_blocks = query_low.reshape(block_count, STRETCH, Z)
    key_blocks = key_low.reshape(block_count, STRETCH, Z)
    value_blocks = value_low.reshape(block_count, STRETCH, V)
    score_scale = Z ** (-0.5)

    def block_scores():
        raw_scores = (
            jnp.einsum("nik,njk->nij", query_blocks, key_blocks, preferred_element_type=jnp.float32)
            * score_scale
            + bias_grid
        )
        return jnp.where(lag_grid >= 0, raw_scores, -1000000000.0)

    scores = block_scores()
    row_max = jnp.max(scores, axis=-1, keepdims=True)
    log_total = row_max + jnp.log(jnp.sum(jnp.exp(scores - row_max), axis=-1, keepdims=True))
    probs_low = jnp.exp(scores - log_total).astype(jnp.bfloat16)
    attended = jnp.einsum(
        "nij,njv->niv", probs_low, value_blocks, preferred_element_type=jnp.float32
    ).reshape(row_count, V)
    gated_low = (attended * reset_gate).astype(jnp.bfloat16)
    hidden_in = jnp.dot(gated_low, merge_full, preferred_element_type=jnp.float32) + hidden_x
    hidden = jax.nn.silu(hidden_in)
    after_mixer = update_gate * hidden + (1.0 - update_gate) * tokens_float
    normed_two, norm_two_back = jax.vjp(layer_norm, after_mixer, gains_float[1])
    normed_two_low = normed_two.astype(jnp.bfloat16)
    up_pre = jnp.dot(normed_two_low, up_full, preferred_element_type=jnp.float32)
    up_low = jax.nn.silu(up_pre).astype(jnp.bfloat16)
    result = (after_mixer + jnp.dot(up_low, down_full, preferred_element_type=jnp.float32)).astype(
        jnp.bfloat16
    )
    value_back, mix_back, merge_back, up_back, down_back = (
        value_full, mix_full, merge_full, up_full, down_full
    )
    grad_rows = cotangent.astype(jnp.float32) * live_rows[:, None].astype(jnp.float32)
    grad_down_low = grad_rows.astype(jnp.bfloat16)
    down_grad = jnp.einsum("tf,td->fd", up_low, grad_down_low, preferred_element_type=jnp.float32)
    grad_up_act = jnp.einsum(
        "td,fd->tf", grad_down_low, down_back, preferred_element_type=jnp.float32
    )
    grad_up_low = (grad_up_act * silu_slope(up_pre)).astype(jnp.bfloat16)
    up_grad = jnp.einsum(
        "td,tf->df", normed_two_low, grad_up_low, preferred_element_type=jnp.float32
    )
    grad_normed_two = jnp.einsum(
        "tf,df->td", grad_up_low, up_back, preferred_element_type=jnp.float32
    )
    grad_after_norm, gain_two_grad = norm_two_back(grad_normed_two)
    grad_after = grad_after_norm + grad_rows
    grad_hidden_in = grad_after * update_gate * silu_slope(hidden_in)
    grad_merge_low = grad_hidden_in.astype(jnp.bfloat16)
    merge_grad = jnp.einsum(
        "tv,td->vd", gated_low, grad_merge_low, preferred_element_type=jnp.float32
    )
    grad_gated = jnp.einsum(
        "td,vd->tv", grad_merge_low, merge_back, preferred_element_type=jnp.float32
    )
    grad_reset = grad_gated * attended
    grad_attended_low = (
        (grad_gated * reset_gate).astype(jnp.bfloat16).reshape(block_count, STRETCH, V)
    )
    grad_probs = jnp.einsum(
        "niv,njv->nij", grad_attended_low, value_blocks, preferred_element_type=jnp.float32
    )
    soft_probs = jnp.exp(block_scores() - log_total)
    grad_scores_low = (
        soft_probs * (grad_probs - jnp.sum(soft_probs * grad_probs, axis=-1, keepdims=True))
    ).astype(jnp.bfloat16)
    grad_query = (
        jnp.einsum(
            "nij,njk->nik", grad_scores_low, key_blocks, preferred_element_type=jnp.float32
        ).reshape(row_count, Z)
        * score_scale
    )
    grad_key = (
        jnp.einsum(
            "nij,nik->njk", grad_scores_low, query_blocks, preferred_element_type=jnp.float32
        ).reshape(row_count, Z)
        * score_scale
    )
    grad_value_act = jnp.einsum(
        "nij,niv->njv",
        soft_probs.astype(jnp.bfloat16),
        grad_attended_low,
        preferred_element_type=jnp.float32,
    ).reshape(row_count, V)
    rel_grad = jnp.einsum(
        "ij,ijl->l",
        jnp.sum(grad_scores_low.astype(jnp.float32), axis=0),
        one_hot,
        precision=highest,
    )
    attn_grad = jnp.concatenate(
        [
            jnp.sum(grad_query * shared, axis=0),
            jnp.sum(grad_query, axis=0),
            jnp.sum(grad_key * shared, axis=0),
            rel_grad,
        ]
    )
    grad_shared = grad_query * attn_float[:Z] + grad_key * attn_float[2 * Z : 3 * Z]
    grad_projected_low = jnp.concatenate(
        [
            grad_after * (hidden - tokens_float) * update_gate * (1.0 - update_gate),
            grad_shared * silu_slope(shared_pre),
            grad_reset * silu_slope(reset_pre),
            grad_hidden_in,
        ],
        axis=1,
    ).astype(jnp.bfloat16)
    mix_grad = jnp.einsum(
        "td,tm->dm", mixed_low, grad_projected_low, preferred_element_type=jnp.float32
    )
    grad_mixed = jnp.einsum(
        "tm,dm->td", grad_projected_low, mix_back, preferred_element_type=jnp.float32
    )
    grad_ema_rows = (grad_mixed * silu_slope(ema_out)).reshape(row_count, *lanes)
    grad_normed_rows, ema_grad_rows, omega_grad = ema_reverse(
        normed_rows, grad_ema_rows, ema_by_state, omega, keep, ema_marks
    )
    grad_normed_ema = grad_normed_rows.reshape(row_count, -1)
    ema_grad = jnp.swapaxes(ema_grad_rows.reshape(4, -1, tokens.shape[1]), 1, 2)
    omega_grad = omega_grad.reshape(-1)
    grad_value_low = (grad_value_act * silu_slope(value_pre)).astype(jnp.bfloat16)
    value_grad = jnp.einsum(
        "td,tv->dv", normed_low, grad_value_low, preferred_element_type=jnp.float32
    )
    grad_normed = grad_normed_ema + jnp.einsum(
        "tv,dv->td", grad_value_low, value_back, preferred_element_type=jnp.float32
    )
    grad_input, gain_one_grad = norm_back(grad_normed)
    grad_tokens = (grad_input + grad_after * (1.0 - update_gate)).astype(jnp.bfloat16)
    gains_grad = jnp.stack([gain_one_grad, gain_two_grad, omega_grad])
    small_totals = (
        lax.psum_scatter(gains_grad, (DP, FS), scatter_dimension=1, tiled=True),
        lax.psum_scatter(ema_grad, (DP, FS), scatter_dimension=1, tiled=True),
        lax.psum_scatter(attn_grad, (DP, FS), scatter_dimension=0, tiled=True),
    )
    totals = reduce_gradients(value_grad, mix_grad, merge_grad, up_grad, down_grad)
    return (
        result,
        grad_tokens,
        totals[0],
        totals[1],
        totals[2],
        totals[3],
        totals[4],
        small_totals[0],
        small_totals[1],
        small_totals[2],
    )


STRIP = 128
MESH = pl.DeviceIdType.MESH
F32 = jnp.float32
LOW = jnp.bfloat16
SHARDED = VALUE, MIX, MERGE, UP, DOWN = range(5)
TOK, COT = 5, 6


def mm(a, b):
    return lax.dot_general(a, b, (((1,), (0,)), ((), ())), preferred_element_type=F32)


def mm_nt(a, b):
    return lax.dot_general(a, b, (((1,), (1,)), ((), ())), preferred_element_type=F32)


def mm_tn(a, b):
    return lax.dot_general(a, b, (((0,), (0,)), ((), ())), preferred_element_type=F32)


def at_rows(start, size, unit=16):
    return pl.ds(pl.multiple_of(start, unit), size)


def row_loop(count, size, body, first=0, unroll=1):
    def step(i, carry):
        body(pl.multiple_of(first + i * size, size))
        return carry

    lax.fori_loop(0, count // size, step, 0, unroll=unroll)


def slope_of(value, gate):
    return gate * (1.0 + value * (1.0 - gate))


def layer_kernel(trees, depth, *refs):
    ref, at = types.SimpleNamespace(), 0
    for tree in trees:
        ref.__dict__.update(jax.tree.unflatten(tree, refs[at : at + tree.num_leaves]))
        at += tree.num_leaves
    tok, cot, gains, ema_in, omega_in, attn = ref.tok, ref.cot, ref.gains, ref.ema_in, ref.omega_in, ref.attn
    rows, width = tok.shape
    tiles = width // 128
    dp, fs = lax.axis_index(DP), lax.axis_index(FS)
    z, c, y, x = dp // 2, dp % 2, fs // 2, fs % 2
    q = c * 2 + x

    def place(z, c, y, x):
        return (z * 2 + c, y * 2 + x)

    sib, xn, xc, yn = place(z, 1 - c, y, x), place(z, c, y, 1 - x), place(z, 1 - c, y, 1 - x), place(z, c, 1 - y, x)
    half_z = z // 2
    partner, far_mid, far_end = z + 1 - 2 * (z % 2), 2 - half_z, 3 * (1 - half_z)
    middle = (z % 2 + half_z) % 2 == 1
    outer = (z % 2 + half_z) % 2 == 0
    line = (far_end, far_mid, partner, z)
    zs = [None] + [place((z + d) % depth, c, y, x) for d in range(1, depth)]
    mates = ((sib, 1 - c, x), (xn, c, 1 - x), (xc, 1 - c, 1 - x))
    plane = [(pc, py, px) for pc in range(2) for py in range(2) for px in range(2)][1:]
    plane = [((c + pc) % 2, (y + py) % 2, (x + px) % 2) for pc, py, px in plane]

    send_sems, recv_sems, local_sems = ref.send_sems, ref.recv_sems, ref.local_sems
    used, used_local, pending = [0], [0], []

    def new_id():
        used[0] += 1
        return used[0] - 1

    def send(src, dst, peer, arrives=None, when=None):
        k = new_id()
        copy = pltpu.make_async_remote_copy(
            src_ref=src, dst_ref=dst, send_sem=send_sems.at[k], recv_sem=recv_sems.at[k if arrives is None else arrives],
            device_id=peer, device_id_type=MESH,
        )
        if when is None:
            copy.start()
        else:
            pl.when(when)(copy.start)
        handle = [k, copy, False, when]
        pending.append(handle)
        return handle

    def sent(handle):
        if not handle[2]:
            if handle[3] is None:
                handle[1].wait_send()
            else:
                pl.when(handle[3])(handle[1].wait_send)
            handle[2] = True

    def received(handle, landed):
        k = handle if isinstance(handle, int) else handle[0]
        pltpu.make_async_remote_copy(
            src_ref=landed, dst_ref=landed, send_sem=send_sems.at[k], recv_sem=recv_sems.at[k],
            device_id=sib, device_id_type=MESH,
        ).wait_recv()

    def local(src, dst):
        k = used_local[0]
        used_local[0] += 1
        copy = pltpu.make_async_copy(src, dst, local_sems.at[k])
        copy.start()
        return copy

    lens = ref.lens
    ends, run = [], 0
    for i in range(lens.shape[1]):
        run = run + lens[0, i]
        ends.append(run)

    def kept(k):
        start = 0
        for i, end in enumerate(ends):
            start = start + jnp.where(end <= k * CHUNK, lens[0, i], 0)
        return jnp.where(k * CHUNK - start == 0, 0.0, 1.0)

    def live_rows(r, size):
        places = r + lax.broadcasted_iota(jnp.int32, (size, 1), 0)
        return (places < ends[-1]).astype(F32)

    small_all, packed = ref.small_all, ref.packed
    states_at = ref.ema_params.shape[1]
    params = jnp.zeros((states_at, 128), F32)
    for p in range(4):
        v = ref.ema_params[p].astype(F32)
        v = jnp.concatenate([v, jnp.zeros((states_at, 128 - v.shape[1]), F32)], axis=1)
        params = params + (pltpu.roll(v, p * 32, 1) if p else v)
    packed[0:states_at, :] = params.astype(LOW)
    singles = [ref.norm_gains[p : p + 1, :] for p in range(3)] + [ref.attn_params[...]]
    row = jnp.zeros((1, 128), F32)
    for p, v in enumerate(singles):
        v = jnp.concatenate([v.astype(F32), jnp.zeros((1, 128 - v.shape[1]), F32)], axis=1)
        row = row + (pltpu.roll(v, p * 32, 1) if p else v)
    packed[16:32, :] = jnp.broadcast_to(row, (16, 128)).astype(LOW)
    lane_group = lax.broadcasted_iota(jnp.int32, (1, 128), 1) // 32

    def slot(pc, py, px, pz):
        return (pc * 4 + py * 2 + px) * depth + pz

    def small_start():
        return [send(packed, small_all.at[slot(c, y, x, z)], zs[d]) for d in range(1, depth)]

    def small_relay(handles):
        for d, handle in enumerate(handles):
            received(handle, small_all.at[slot(c, y, x, (z + depth - 1 - d) % depth)])
        small_all[slot(c, y, x, z)] = packed[...]
        mine = small_all.at[pl.ds(slot(c, y, x, 0), depth)]
        return [send(mine, mine, place(z, *p)) for p in plane]

    def small_finish(handles):
        for handle, p in zip(handles, plane):
            received(handle, small_all.at[pl.ds(slot(*p, 0), depth)])
        states = ema_in.shape[0] // (4 * tiles)
        gains[...] = jnp.zeros_like(gains)
        attn[...] = jnp.zeros_like(attn)
        for t in range(tiles):
            pz, pc = t // 2, t % 2
            got = [small_all[slot(pc, f // 2, f % 2, pz)].astype(F32)[0 : states + 8, :] for f in range(4)]
            for p in range(4):
                v = jnp.zeros_like(got[0])
                for f in range(4):
                    turn = (f - p) * 32 % 128
                    v = jnp.where(lane_group == f, pltpu.roll(got[f], turn, 1) if turn else got[f], v)
                ema_in[pl.ds(p * states * tiles + t, states, stride=tiles), :] = v[0:states]
                row = v[states : states + 1]
                if p < 3:
                    gains[p : p + 1, t * 128 : (t + 1) * 128] = row
                    if p == 2:
                        omega_in[t : t + 1, :] = row
                    continue
                for f in range(4):
                    turn = (t % 2 * 64 - f * 16) % 128
                    mine = lax.broadcasted_iota(jnp.int32, (1, 128), 1) // 16 == t % 2 * 4 + f
                    moved = pltpu.roll(row, turn, 1) if turn else row
                    attn[t // 2 : t // 2 + 1, :] += jnp.where(mine, moved, 0.0)

    lane = lax.broadcasted_iota(jnp.int32, (1, 128), 1)
    shift = fs * 32

    def mix_align():
        raw, win, line_up = ref.s[MIX], ref.mix_win, ref.by_time
        line_up[0 : win.shape[1], :] = jnp.zeros((win.shape[1], 128), F32)

        def load(r):
            line_up[at_rows(shift + r, 32, 32), :] = raw[pl.ds(r, 32), :].astype(F32)

        row_loop(raw.shape[0], 32, load)
        for t in range(win.shape[1] // 128):
            win[:, t * 128 : (t + 1) * 128] = line_up[t * 128 : (t + 1) * 128, :].T.astype(LOW)

    weights = {m: ref.w[m] for m in SHARDED}
    block_shape = {m: (w.shape[0] // depth, w.shape[1] // 2) for m, w in weights.items()}

    def block(m, zz, yy):
        rb, cb = block_shape[m]
        return weights[m].at[at_rows(zz * rb, rb), at_rows(yy * cb, cb, 128)]

    def piece(m, src_c, src_x):
        rb, cb = block_shape[m]
        half = cb // 2
        if m in (VALUE, UP):
            return weights[m].at[at_rows(z * rb + src_c * (rb // 2), rb // 2), at_rows(y * cb + src_x * half, half, 128)]
        return weights[m].at[at_rows(z * rb, rb), at_rows(y * cb + src_x * half, half, 128)]

    def move(src, dst):
        rows_at_once = 32

        def step(r):
            dst[pl.ds(r, rows_at_once), :] = src[pl.ds(r, rows_at_once), :]

        row_loop(src.shape[0], rows_at_once, step)

    spare, near, loads, top = ref.up_low, {MIX: ref.mix_win}, {}, 0
    for m in (VALUE, MERGE, UP, DOWN):
        tall, wide = ref.s[m].shape
        near[m] = spare.at[top : top + tall, 0:wide]
        loads[m] = local(ref.s[m], near[m])
        top += tall
    for k in (TOK, COT):
        loads[k] = local(ref.acts[k - TOK], (tok, cot)[k - TOK])
    barrier = pltpu.get_barrier_semaphore()
    peers = [place(z, *p) for p in plane] + zs[1:]
    for peer in peers:
        pl.semaphore_signal(barrier, inc=1, device_id=peer, device_id_type=MESH)
    pl.semaphore_wait(barrier, len(peers))

    swaps = {m: [] for m in SHARDED}

    def swap_start(m):
        shard = near[m]
        if m in loads:
            loads[m].wait()
        if m == MIX:
            first, last = 1 - (fs + 2) // 3, fs // 3
            middle = 1 - first - last
            for peer, pc, px in mates + ((None, c, x),):
                pq = pc * 2 + px
                tiles_at = (
                    first * 2 * pq,
                    (first + last) * (1 + 2 * pq) + middle * (1 + pq),
                    first * 8 + last * (2 + 2 * pq) + middle * (5 + pq),
                )
                for i, tile in enumerate(tiles_at):
                    src = shard.at[:, at_rows(tile * 128, 128, 128)]
                    dst = ref.mix_in.at[x, at_rows(c * 128, 128), pl.ds(i * 128, 128)]
                    if peer is None:
                        move(src, dst)
                    else:
                        swaps[m].append((send(src, dst, peer), pc, px, i))
            return
        if m in (VALUE, UP):
            wide = shard.shape[1] // 4
            for peer, pc, px in mates + ((None, c, x),):
                src = shard.at[:, at_rows((pc * 2 + px) * wide, wide, 128)]
                if peer is None:
                    move(src, piece(m, c, x))
                else:
                    swaps[m].append((send(src, piece(m, c, x), peer), pc, px, 0))
            return
        tall = shard.shape[0] // 2
        swaps[m].append((send(shard.at[at_rows((1 - x) * tall, tall), :], piece(m, c, x), xn), c, 1 - x, 0))
        move(shard.at[at_rows(x * tall, tall), :], piece(m, c, x))

    z_ids, z_sends, y_sends = {}, {}, {}

    def swap_finish(m):
        for handle, pc, px, i in swaps[m]:
            if m == MIX:
                received(handle, ref.mix_in.at[px, at_rows(pc * 128, 128), pl.ds(i * 128, 128)])
            else:
                received(handle, piece(m, pc, px))
        if m == MIX:
            only = (q == 3).astype(F32)
            low_y = (y == 0).astype(F32)
            lead = jnp.broadcast_to(jnp.maximum(low_y, only), (1, 128))
            rb, cb = block_shape[m]
            a, b, w = ref.mix_in.at[0], ref.mix_in.at[1], weights[m]

            def combine(r):
                at = pl.ds(r, 64)
                to = at_rows(z * rb + r, 64)

                def put(i, v):
                    w[to, at_rows(y * cb + i * 128, 128, 128)] = v.astype(LOW)

                put(0, a[at, 0:128].astype(F32) * lead)
                put(1, a[at, 128:256])
                put(2, a[at, 256:384].astype(F32) + b[at, 0:128].astype(F32) * lead)
                put(3, b[at, 128:256])
                put(4, b[at, 256:384])

            row_loop(rb, 64, combine)

    def y_own(m):
        y_sends[m] = [(3, send(block(m, z, y), block(m, z, y), yn))]

    def z_start(m, far=False):
        own = block(m, z, 1 - y if far else y)
        ids = [new_id() for _ in range(3)]
        z_ids[m, far] = ids
        z_sends.setdefault(m, []).extend(
            [
                send(own, own, place(partner, c, y, x), ids[2]),
                send(own, own, place(far_mid, c, y, x), ids[1], middle),
                send(own, own, place(far_mid, c, y, x), ids[0], outer),
            ]
        )

    def z_received(m, i, far, when):
        there = block(m, line[i], 1 - y if far else y)
        pl.when(when)(functools.partial(received, z_ids[m, far][i], there))
        return there

    def z_pass(m, steps=(1, 0), far=False):
        for i in steps:
            there = z_received(m, i, far, middle)
            z_sends[m].append(send(there, there, place(partner, c, y, x), z_ids[m, far][i], middle))

    def z_far(m):
        received(y_sends[m][0][1], block(m, z, 1 - y))
        z_start(m, True)

    def z_finish(m):
        for far in (False, True):
            received(z_ids[m, far][2], block(m, partner, 1 - y if far else y))
            for i in (1, 0):
                z_received(m, i, far, outer)

    def y_forward(m, steps=(2, 1, 0)):
        for i in steps:
            there = block(m, line[i], y)
            if i == 2:
                received(z_ids[m, False][i], there)
            else:
                z_received(m, i, False, outer)
            y_sends[m].append((i, send(there, there, yn)))

    def y_finish(m):
        for i, handle in y_sends[m]:
            received(handle, block(m, line[i], 1 - y))

    def group_rows(c, x):
        return at_rows((c * 2 + x) * rows, rows)

    def part_rows(c, x, first, count):
        return at_rows((c * 2 + x) * rows + first, count)

    def gather_start(buf, first=0, count=None):
        count = rows if count is None else count
        own = buf.at[part_rows(c, x, first, count), :]
        return [(first, count), send(own, own, xn), send(own, own, sib)]

    def gather_relay(buf, handles):
        other = buf.at[part_rows(c, 1 - x, *handles[0]), :]
        received(handles[1], other)
        handles.append(send(other, other, sib))

    def gather_finish(buf, handles):
        received(handles[2], buf.at[part_rows(1 - c, x, *handles[0]), :])
        received(handles[3], buf.at[part_rows(1 - c, 1 - x, *handles[0]), :])

    total = ref.total
    stage = [ref.stage.at[0], ref.stage.at[1], ref.stage.at[2], ref.hidden_mul]
    staged = [[], [], [], []]

    def stage_out(k, first, count, extra=None):
        def put(r):
            at = pl.ds(r, 32)
            v = total[at, :]
            if extra is not None:
                v = v + extra[at, :].astype(F32)
            stage[k][at, :] = v.astype(LOW)

        row_loop(count, 32, put, first, 2)

    def stage_free(k):
        for handle in staged[k]:
            sent(handle)
        staged[k] = []

    def reduce_first(partial, sibs):
        for k, px in ((0, 1 - x), (1, x)):
            partial(1 - c, px)
            stage_free(k)
            stage_out(k, 0, rows)
            staged[k] = [send(stage[k], sibs[k], sib)]
        return staged[0][0], staged[1][0]

    def reduce_cross(partial, sibs, cross, handles, slot=2):
        halves = (pl.ds(0, rows // 2), pl.ds(rows // 2, rows // 2))
        partial(c, 1 - x)
        received(handles[0], sibs[0])
        stage_free(slot)
        for i, half in enumerate(halves):
            stage_out(slot, i * (rows // 2), rows // 2, sibs[0])
            staged[slot].append(send(stage[slot].at[half, :], cross.at[half, :], xn))
        return handles[1], list(zip(staged[slot], (cross.at[half, :] for half in halves)))

    def reduce_early(partial, sibs, cross):
        return reduce_cross(partial, sibs, cross, reduce_first(partial, sibs))

    def reduce_late(partial, sibs, cross, handles, consume):
        partial(c, x)
        received(handles[0], sibs[1])
        for i, (handle, half) in enumerate(handles[1]):
            received(handle, half)
            consume(i * (rows // 2), rows // 2)

    def reduced(r, size, sibs, cross):
        at = pl.ds(r, size)
        return total[at, :] + sibs[1][at, :].astype(F32) + cross[at, :].astype(F32)

    sibs_a, sibs_b = ((r.at[0], r.at[1]) for r in (ref.sibs_a, ref.sibs_b))
    cross_a, cross_b = ref.cross_a, ref.cross_b
    sibs_c, cross_c = (ref.gc.at[2 * rows : 3 * rows, :], ref.gc.at[3 * rows : 4 * rows, :]), ref.update_in

    w_up = weights[UP]
    y_out = {
        DOWN: ref.mix_pack.at[:, 384 : 384 + block_shape[DOWN][1]],
        UP: ref.yo,
        MERGE: ref.gc.at[0 : weights[MERGE].shape[0], 0 : block_shape[MERGE][1]],
        MIX: w_up.at[:, 0 : block_shape[MIX][1]],
        VALUE: w_up.at[:, block_shape[MIX][1] : block_shape[MIX][1] + block_shape[VALUE][1]],
    }
    y_in = {m: ref.yi[m] for m in SHARDED}
    z_in = {m: ref.zi[m] for m in SHARDED}
    f_in = {m: ref.fi[m] for m in SHARDED}
    gy, gz, gf = {}, {}, {}

    def y_grad_send(m, product, steps=(0, 1, 2, 3)):
        rb, cb = block_shape[m]
        if m not in gy:
            gy[m], gz[m] = {}, [new_id() for _ in range(4)]
        for i in steps:
            at = at_rows(line[i] * rb, rb)
            y_out[m][at, :] = product(line[i], 1 - y).astype(LOW)
            gy[m][i] = send(y_out[m].at[at, :], y_in[m].at[at, :], yn)

    def y_grad_add(m, product, steps=(0, 1, 2, 3)):
        rb, cb = block_shape[m]
        for i in steps:
            at = at_rows(line[i] * rb, rb)
            own = product(line[i], y)
            received(gy[m][i], y_in[m].at[at, :])
            y_in[m][at, :] = (own + y_in[m][at, :].astype(F32)).astype(LOW)
            if i < 3:
                send(
                    y_in[m].at[at, :], z_in[m].at[i], place(partner, c, y, x), gz[m][i], outer if i < 2 else None
                )

    def z_relay(m, steps=(0, 1)):
        rb, cb = block_shape[m]
        for i in steps:
            at = at_rows(line[i] * rb, rb)

            @pl.when(middle)
            def _(i=i, at=at):
                received(gz[m][i], z_in[m].at[i])
                y_in[m][at, :] = (y_in[m][at, :].astype(F32) + z_in[m][i].astype(F32)).astype(LOW)

            send(y_in[m].at[at, :], z_in[m].at[3], place(line[i], c, y, x), gz[m][3], middle)

    def z_grad_add(m):
        rb, cb = block_shape[m]
        for i in (2, 3):
            received(gz[m][i], z_in[m].at[i])

        def add(r):
            at = at_rows(z * rb + r, 64)
            v = y_in[m][at, :].astype(F32)
            for i in (2, 3):
                v = v + z_in[m][i, pl.ds(r, 64), :].astype(F32)
            y_in[m][at, :] = v.astype(LOW)

        row_loop(rb, 64, add)
        to_owners(m)

    far_land = [ref.mix_in.at[i // 2, pl.ds(i % 2 * 128, 128), :] for i in range(4)]
    y_last = ref.mix_win.at[:, 0 : block_shape[MERGE][1]]

    def sides(m):
        return (False, y_in[m], [z_in[m].at[i] for i in range(4)]), (True, y_out[m], far_land)

    def first_send(m, product):
        rb, cb = block_shape[m]
        for far, _, _ in sides(m):
            gz[m, far] = [new_id() for _ in range(4)]
        for i in range(4):
            at = at_rows(line[i] * rb, rb)
            for far, buf, land in sides(m):
                buf[at, :] = product(line[i], 1 - y if far else y).astype(LOW)
                if i < 3:
                    send(
                        buf.at[at, :], land[i], place(partner, c, y, x), gz[m, far][i], outer if i < 2 else None
                    )

    def first_relay(m):
        rb, cb = block_shape[m]
        for i in (0, 1):
            at = at_rows(line[i] * rb, rb)
            for far, buf, land in sides(m):

                @pl.when(middle)
                def _(i=i, at=at, far=far, buf=buf, land=land):
                    received(gz[m, far][i], land[i])
                    buf[at, :] = (buf[at, :].astype(F32) + land[i][...].astype(F32)).astype(LOW)

                send(buf.at[at, :], land[3], place(line[i], c, y, x), gz[m, far][3], middle)

    def first_turn(m):
        rb, cb = block_shape[m]
        at = at_rows(z * rb, rb)
        for far, buf, land in sides(m):
            for i in (2, 3):
                received(gz[m, far][i], land[i])
            buf[at, :] = (buf[at, :].astype(F32) + land[2][...].astype(F32) + land[3][...].astype(F32)).astype(LOW)
        gy[m] = send(y_out[m].at[at, :], y_last, yn)

    def first_finish(m):
        rb, cb = block_shape[m]
        at = at_rows(z * rb, rb)
        received(gy[m], y_last)
        y_in[m][at, :] = (y_in[m][at, :].astype(F32) + y_last[...].astype(F32)).astype(LOW)
        to_owners(m)

    def to_owners(m):
        rb, cb = block_shape[m]
        gf[m] = []
        if m in (MERGE, DOWN):
            land = f_in[m].at[at_rows(x * rb, rb), :]

            def part(px):
                return y_in[m].at[at_rows(z * rb, rb), at_rows(px * (cb // 2), cb // 2, 128)]

            gf[m].append((send(part(1 - x), land, xn), f_in[m].at[at_rows((1 - x) * rb, rb), :]))
            move(part(x), land)
            return
        half = rb // 2

        def land_at(pc, px):
            if m == MIX:
                return f_in[m].at[pc * 2 + px]
            wide = f_in[m].shape[1] // 4
            return f_in[m].at[:, at_rows((pc * 2 + px) * wide, wide, 128)]

        def part(pc, px):
            if m == MIX:
                return y_in[m].at[at_rows(z * rb + pc * half, half), at_rows(px * 256, 384, 128)]
            return y_in[m].at[at_rows(z * rb + pc * half, half), at_rows(px * (cb // 2), cb // 2, 128)]

        for peer, pc, px in mates:
            gf[m].append((send(part(pc, px), land_at(c, x), peer), land_at(pc, px)))
        move(part(c, x), land_at(c, x))

    def grad_out(m):
        for handle, landed in gf[m]:
            received(handle, landed)
        if m != MIX:
            return
        out, src, line_up = ref.g_mix, f_in[MIX], ref.by_time
        first, last = (fs == 0).astype(F32), (fs == 3).astype(F32)
        mid = 1.0 - first - last
        first, last, mid = (jnp.broadcast_to(v, (1, 128)) for v in (first, last, mid))

        def get(p, t):
            return src[p, :, t * 128 : (t + 1) * 128].astype(F32)

        for tile in range(9):
            v = first * (get(tile // 2, tile % 2) if tile < 8 else src[q, :, 256:384].astype(F32))
            if tile == 0:
                v = v + (mid + last) * get(3, 0)
            else:
                v = v + mid * get((tile - 1) % 4, 1 + (tile - 1) // 4)
                v = v + last * get((tile - 1) // 2, 1 + (tile - 1) % 2)
            line_up[tile * 128 : (tile + 1) * 128, :] = v.T

        def write(r):
            out[pl.ds(r, 32), :] = line_up[at_rows(shift + r, 32, 32), :].astype(LOW)

        row_loop(out.shape[0], 32, write)

    h_small = small_start()
    mix_align()
    swap_start(MIX)
    h_small = small_relay(h_small)
    swap_start(VALUE)
    swap_start(MERGE)
    swap_finish(MIX)
    y_own(MIX)
    z_start(MIX)

    nl, ml, n2, gc, gm = (ref.nl, ref.ml, ref.n2, ref.gc, ref.gm)
    by_time, out_time, back_time = ref.by_time, ref.out_time, ref.back_time

    def centre(v):
        cen = v - jnp.mean(v, axis=-1, keepdims=True)
        return cen, lax.rsqrt(jnp.mean(cen * cen, axis=-1, keepdims=True) + 1e-05)

    def norm_one(r):
        cen, rate = centre(tok[pl.ds(r, 16), :].astype(F32))
        v = cen * rate * gains[0:1, :]
        nl[at_rows(q * rows + r, 16), :] = v.astype(LOW)
        for s in range(tiles):
            by_time[pl.ds(r * tiles + s, 16, stride=tiles), :] = v[:, s * 128 : (s + 1) * 128]

    small_finish(h_small)
    loads[TOK].wait()
    row_loop(rows, 16, norm_one, 0, 2)
    swap_finish(VALUE)
    y_own(VALUE)
    z_start(VALUE)

    def cot_low(r):
        at = pl.ds(r, 32)
        gc[at_rows(q * rows + r, 32), :] = (cot[at, :].astype(F32) * live_rows(r, 32)).astype(LOW)

    def load_ema():
        return ema_in[...].reshape(4, -1, tiles, 128)

    _, _, rate_all, weight_all = ema_coefficients(load_ema())
    omega = omega_in[...]
    marks = ref.marks

    def at_time(t):
        return at_rows(t * tiles, tiles, 8)

    def ema_chunk(k, state):
        state = state * kept(k)
        marks[k] = state

        def step(i, state):
            t = k * CHUNK + i
            v = by_time[at_time(t), :]
            state = rate_all * state + v[None]
            out_time[at_time(t), :] = jnp.sum(weight_all * state, axis=0) + omega * v
            return state

        return lax.fori_loop(0, CHUNK, step, state, unroll=4)

    lax.fori_loop(0, rows // CHUNK, ema_chunk, jnp.zeros_like(rate_all))

    def mixed(r):
        for s in range(tiles):
            at = pl.ds(r * tiles + s, 16, stride=tiles)
            v = out_time[at, :]
            gate = jax.nn.sigmoid(v)
            ml[at_rows(q * rows + r, 16), s * 128 : (s + 1) * 128] = (v * gate).astype(LOW)
            out_time[at, :] = slope_of(v, gate)

    row_loop(rows, 16, mixed)
    h_ml = gather_start(ml)
    swap_start(UP)
    h_nl = gather_start(nl)
    swap_finish(MERGE)
    z_start(MERGE)
    z_pass(MIX, (1,))
    y_forward(MIX, [2])
    swap_start(DOWN)
    loads[COT].wait()
    row_loop(rows, 32, cot_low)
    z_pass(MIX, (0,))
    y_forward(MIX, [1])
    z_pass(VALUE)
    gather_relay(ml, h_ml)
    y_forward(MIX, [0])
    y_own(MERGE)
    y_forward(VALUE)
    swap_finish(UP)
    z_start(UP)
    gather_finish(ml, h_ml)
    z_pass(MERGE)

    value_low, value_slope = ref.value_low, ref.value_slope
    vq = value_low.shape[1]

    def value_block(r):
        total[:, :vq] = mm(nl[pl.ds(r, rows), :], weights[VALUE][...])

        def act(s):
            v = total[pl.ds(s, 32), :vq]
            gate = jax.nn.sigmoid(v)
            value_low[at_rows(r + s, 32), :] = (v * gate).astype(LOW)
            value_slope[at_rows(r + s, 32), :] = slope_of(v, gate).astype(LOW)

        row_loop(rows, 32, act)

    y_finish(MIX)

    w_mix, reset_w = weights[MIX], ref.reset_w
    half_mix = w_mix.shape[1] // 2

    def fix_reset(r):
        at = pl.ds(r, 64)
        reset_w[at, 0:128] = w_mix[at, 384:512]
        reset_w[at, 128:256] = (w_mix[at, 512:640].astype(F32) + w_mix[at, half_mix : half_mix + 128].astype(F32)).astype(LOW)

    row_loop(width, 64, fix_reset)

    def w_update():
        return w_mix[:, 0:256]

    def w_shared():
        return w_mix[:, 256:384]

    def w_late():
        return w_mix[:, half_mix + 128 : half_mix + 384]

    def w_hidden():
        return w_mix[:, half_mix + 384 : half_mix + 640]

    scale = float(STRETCH) ** -0.5
    stretch = STRETCH
    shared_pre, query, key, probs = ref.shared_pre, ref.query, ref.key, ref.probs
    probs_low = ref.probs_low
    shared_pre[...] = mm(ml[group_rows(c, x), :], w_shared())
    sv = shared_pre[...]
    shared = sv * jax.nn.sigmoid(sv)
    query[...] = (shared * attn[0:1, :] + attn[1:2, :]).astype(LOW)
    key[...] = (shared * attn[2:3, :]).astype(LOW)
    bias = pltpu.roll(jnp.broadcast_to(attn[3:4, :], (stretch, stretch)), 0, 1, stride=1, stride_axis=0).T
    row_id = lax.broadcasted_iota(jnp.int32, (stretch, stretch), 0)
    col_id = lax.broadcasted_iota(jnp.int32, (stretch, stretch), 1)
    for n in range(rows // stretch):
        at = pl.ds(n * stretch, stretch)
        scores = mm_nt(query[at, :], key[at, :]) * scale + bias
        scores = jnp.where(row_id >= col_id, scores, -1000000000.0)
        ex = jnp.exp(scores - jnp.max(scores, axis=-1, keepdims=True))
        pr = ex / jnp.sum(ex, axis=-1, keepdims=True)
        probs[at, :] = pr
        probs_low[at_rows(q * rows + n * stretch, stretch), :] = pr.astype(LOW)
    own_probs = probs_low.at[group_rows(c, x), :]
    h_probs = [send(own_probs, own_probs, peer) for peer, _, _ in mates]

    mix_pack, update_in = ref.mix_pack, ref.update_in
    hidden_at = pl.ds(mix_pack.shape[1] - 256, 256)
    update_out = mix_pack.at[:, hidden_at]

    def update_block(r):
        update_out[pl.ds(r, rows), :] = mm(ml[pl.ds(r, rows), :], w_update()).astype(LOW)

    row_loop(4 * rows, rows, update_block)
    part_w = width // 4
    own_cols = at_rows(q * part_w, part_w, 128)
    h_update = [
        send(update_out.at[group_rows(pc, px), :], update_in.at[:, own_cols], peer) for peer, pc, px in mates
    ]
    update_in[:, own_cols] = update_out[group_rows(c, x), :]
    gather_relay(nl, h_nl)
    h_gc = gather_start(gc)

    reset_gate, reset_slope = ref.reset_gate, ref.reset_slope

    def reset_block(r):
        at = pl.ds(r, rows)
        total[:, 0:256] = mm(ml[at, :], reset_w[...])
        total[:, 256:512] = mm(ml[at, :], w_late())

        def act(s):
            v = total[pl.ds(s, 32), :vq]
            gate = jax.nn.sigmoid(v)
            reset_gate[at_rows(r + s, 32), :] = (v * gate).astype(LOW)
            reset_slope[at_rows(r + s, 32), :] = slope_of(v, gate).astype(LOW)

        row_loop(rows, 32, act)

    row_loop(4 * rows, rows, reset_block)
    y_forward(MERGE)
    swap_finish(DOWN)
    z_start(DOWN)
    y_own(DOWN)
    z_pass(UP, (1,))
    gather_finish(nl, h_nl)
    y_finish(VALUE)
    row_loop(4 * rows, rows, value_block)
    z_pass(UP, (0,))
    y_own(UP)
    y_forward(UP, [2])
    for handle, (_, pc, px) in zip(h_probs, mates):
        received(handle, probs_low.at[group_rows(pc, px), :])

    gated = ref.gated

    def attend(r):
        at = pl.ds(r, stretch)
        total[0:stretch, :vq] = mm(probs_low[at, :], value_low[at, :])

        def act(s):
            v = total[pl.ds(s, 32), :vq]
            to = at_rows(r + s, 32)
            gated[to, :] = (v * reset_gate[to, :].astype(F32)).astype(LOW)
            reset_slope[to, :] = (v * reset_slope[to, :].astype(F32)).astype(LOW)

        row_loop(stretch, 32, act)

    row_loop(4 * rows, stretch, attend)
    z_pass(DOWN, (1,))
    y_forward(UP, [1])
    y_finish(MERGE)

    def merge_partial(c, x):
        at = group_rows(c, x)
        total[...] = mm(gated[at, :], weights[MERGE][...])
        total[:, own_cols] += mm(ml[at, :], w_hidden())

    h_red = reduce_early(merge_partial, sibs_a, cross_a)
    z_pass(DOWN, (0,))
    y_forward(UP, [0])
    for handle, (_, pc, px) in zip(h_update, mates):
        received(handle, update_in.at[:, at_rows((pc * 2 + px) * part_w, part_w, 128)])
    gather_relay(gc, h_gc)
    z_far(DOWN)

    after, hidden_mul, update_mul = ref.after, ref.hidden_mul, ref.update_mul

    def norm_two(r):
        at = pl.ds(r, 16)
        v = reduced(r, 16, sibs_a, cross_a)
        gate = jax.nn.sigmoid(v)
        hidden = v * gate
        u = jax.nn.sigmoid(update_in[at, :].astype(F32))
        xv = tok[at, :].astype(F32)
        av = u * hidden + (1.0 - u) * xv
        after[at, :] = av
        hidden_mul[at, :] = (u * slope_of(v, gate)).astype(LOW)
        update_mul[at, :] = ((hidden - xv) * u * (1.0 - u)).astype(LOW)
        cen, rate = centre(av)
        n2[at_rows(q * rows + r, 16), :] = (cen * rate * gains[1:2, :]).astype(LOW)

    h_n2 = []

    def take_merge(first, count):
        row_loop(count, 16, norm_two, first, 2)
        h_n2.append(gather_start(n2, first, count))

    reduce_late(merge_partial, sibs_a, cross_a, h_red, take_merge)
    z_pass(DOWN, (1,), True)
    up_low, up_slope = ref.up_low, ref.up_slope
    for m in SHARDED:
        for swap in swaps[m]:
            sent(swap[0])

    def up_block(r):
        total[...] = mm(n2[at_rows(r, rows), :], weights[UP][...])

        def act(s):
            v = total[pl.ds(s, 16), :]
            gate = jax.nn.sigmoid(v)
            up_low[at_rows(r + s, 16), :] = (v * gate).astype(LOW)
            up_slope[at_rows(r + s, 16), :] = slope_of(v, gate).astype(LOW)

        row_loop(rows, 16, act)

    def up_rows(c, x):
        up_block(pl.multiple_of((c * 2 + x) * rows, rows))

    gather_relay(n2, h_n2[0])
    z_pass(DOWN, (0,), True)
    y_finish(UP)
    up_rows(c, x)
    for handles in h_n2:
        received(handles[2], n2.at[part_rows(1 - c, x, *handles[0]), :])
    up_rows(1 - c, x)
    gather_relay(n2, h_n2[1])
    up_rows(c, 1 - x)
    for handles in h_n2:
        received(handles[3], n2.at[part_rows(1 - c, 1 - x, *handles[0]), :])
    up_rows(1 - c, 1 - x)
    gather_finish(gc, h_gc)

    def cols_of(m, yy):
        cb = block_shape[m][1]
        return at_rows(yy * cb, cb, 128)

    def rows_of(m, zz):
        rb = block_shape[m][0]
        return at_rows(zz * rb, rb, 128)

    def down_product(zz, yy):
        return mm_tn(up_low[:, rows_of(DOWN, zz)], gc[:, cols_of(DOWN, yy)])

    y_grad_send(DOWN, down_product)
    z_finish(DOWN)

    def down_partial(c, x):
        total[...] = mm(up_low[group_rows(c, x), :], weights[DOWN][...])

    def up_back(r):
        at = pl.ds(r, rows)
        total[...] = mm_nt(gc[at, :], weights[DOWN][...])

        def act(s):
            to = at_rows(r + s, 16)
            up_slope[to, :] = (total[pl.ds(s, 16), :] * up_slope[to, :].astype(F32)).astype(LOW)

        row_loop(rows, 16, act)

    row_loop(4 * rows, rows, up_back)
    grad_up = up_slope

    def two_partial(c, x):
        total[...] = mm_nt(grad_up[group_rows(c, x), :], weights[UP][...])

    def up_product(zz, yy):
        return mm_tn(n2[:, rows_of(UP, zz)], grad_up[:, cols_of(UP, yy)])

    h_red = reduce_early(two_partial, sibs_a, cross_a)
    y_grad_send(UP, up_product)
    y_grad_add(DOWN, down_product, (0, 1))
    for handle in h_gc[1:]:
        sent(handle)

    gain_sum, update_back = ref.gain_sum, hidden_mul
    gain_sum[...] = jnp.zeros_like(gain_sum)

    def norm_two_back(r):
        at = pl.ds(r, 16)
        g = reduced(r, 16, sibs_a, cross_a)
        cen, rate = centre(after[at, :])
        unit = cen * rate
        gain_sum[1] += g * unit
        g = g * gains[1:2, :]
        back = rate * (g - jnp.mean(g, axis=-1, keepdims=True) - unit * jnp.mean(g * unit, axis=-1, keepdims=True))
        back = back + cot[at, :].astype(F32) * live_rows(r, 16)
        gm[at_rows(q * rows + r, 16), :] = (back * hidden_mul[at, :].astype(F32)).astype(LOW)
        hidden_mul[at, :] = (back * update_mul[at, :].astype(F32)).astype(LOW)
        u = jax.nn.sigmoid(update_in[at, :].astype(F32))
        update_mul[at, :] = (back * (1.0 - u)).astype(LOW)

    h_gm = []

    def take_two(first, count):
        row_loop(count, 16, norm_two_back, first, 2)
        h_gm.append(gather_start(gm, first, count))

    reduce_late(two_partial, sibs_a, cross_a, h_red, take_two)
    for handle in h_update:
        sent(handle)
    update_grad = mix_pack.at[:, 0:256]
    own_rows = group_rows(c, x)
    h_update = [
        send(update_back.at[:, at_rows((pc * 2 + px) * part_w, part_w, 128)], update_grad.at[own_rows, :], peer)
        for peer, pc, px in mates
    ]
    update_grad[own_rows, :] = update_back[:, own_cols]

    y_grad_add(DOWN, down_product, (2, 3))
    z_relay(DOWN)
    def merge_product(zz, yy):
        return mm_tn(gated[:, rows_of(MERGE, zz)], gm[:, cols_of(MERGE, yy)])

    for handle in z_sends[UP] + [h for _, h in y_sends[UP]] + list(gy[DOWN].values()):
        sent(handle)
    grad_probs, probs_in = ref.grad_probs, ref.probs_in
    grad_att = reset_gate

    def gated_back(c, x):
        first = (c * 2 + x) * rows
        total[:, :vq] = mm_nt(gm[at_rows(first, rows), :], weights[MERGE][...])

        def act(s):
            to = at_rows(first + s, 32)
            g = total[pl.ds(s, 32), :vq]
            back = (g * reset_slope[to, :].astype(F32)).astype(LOW)
            mix_pack[to, 384:640] = back[:, 0:256]
            mix_pack[to, 640:768] = back[:, 128:256]
            mix_pack[to, 768:1024] = back[:, 256:512]
            mix_pack[to, hidden_at] = gm[to, own_cols]
            reset_gate[to, :] = (g * reset_gate[to, :].astype(F32)).astype(LOW)

        row_loop(rows, 32, act)

        def probs_back(r):
            at = at_rows(first + r, stretch)
            grad_probs[at, :] = mm_nt(grad_att[at, :], value_low[at, :]).astype(LOW)

        row_loop(rows, stretch, probs_back)

    gated_back(c, x)
    gather_relay(gm, h_gm[0])
    y_grad_add(UP, up_product, (0,))
    for handles in h_gm:
        received(handles[2], gm.at[part_rows(1 - c, x, *handles[0]), :])
    gated_back(1 - c, x)
    gather_relay(gm, h_gm[1])
    gated_back(c, 1 - x)
    for handles in h_gm:
        received(handles[3], gm.at[part_rows(1 - c, 1 - x, *handles[0]), :])
    gated_back(1 - c, 1 - x)
    h_probs = [
        send(grad_probs.at[group_rows(pc, px), :], probs_in.at[i], peer) for i, (peer, pc, px) in enumerate(mates)
    ]
    y_grad_add(UP, up_product, (1,))
    first_send(MERGE, merge_product)
    for handle, (_, pc, px) in zip(h_update, mates):
        received(handle, update_grad.at[group_rows(pc, px), :])

    shared_grad = mix_pack.at[:, 256:384]

    def mixed_partial(cc, xx):
        at = group_rows(cc, xx)
        total[...] = (
            mm_nt(update_grad[at, :], w_update())
            + mm_nt(mix_pack[at, 384:640], reset_w[...])
            + mm_nt(mix_pack[at, 768:1024], w_late())
            + mm_nt(mix_pack[at, hidden_at], w_hidden())
        )


    def value_back(r):
        at = pl.ds(r, stretch)
        total[0:stretch, :vq] = mm_tn(probs_low[at, :], grad_att[at, :])

        def act(s):
            to = at_rows(r + s, 32)
            value_slope[to, :] = (total[pl.ds(s, 32), :vq] * value_slope[to, :].astype(F32)).astype(LOW)

        row_loop(stretch, 32, act)

    row_loop(4 * rows, stretch, value_back)
    grad_value = value_slope

    def value_product(zz, yy):
        return mm_tn(nl[:, rows_of(VALUE, zz)], grad_value[:, cols_of(VALUE, yy)])

    y_grad_send(VALUE, value_product, (0, 1))
    y_grad_add(UP, up_product, (2, 3))

    for i, handle in enumerate(h_probs):
        received(handle, probs_in.at[i])
    anti = (row_id + col_id == stretch - 1).astype(LOW)
    lag_sum = jnp.zeros((1, stretch), F32)
    grads_q = jnp.zeros((1, stretch), F32)
    grads_o = jnp.zeros((1, stretch), F32)
    grads_k = jnp.zeros((1, stretch), F32)
    for n in range(rows // stretch):
        at = pl.ds(n * stretch, stretch)
        to = at_rows(q * rows + n * stretch, stretch)
        g = grad_probs[to, :].astype(F32)
        for i in range(3):
            g = g + probs_in[i, at, :].astype(F32)
        pr = probs[at, :]
        gs = (pr * (g - jnp.sum(pr * g, axis=-1, keepdims=True))).astype(LOW)
        gq = mm(gs, key[at, :]) * scale
        gk = mm_tn(gs, query[at, :]) * scale
        lags = pltpu.roll(mm_nt(anti, gs), 1, 1, stride=1, stride_axis=0)
        lag_sum += jnp.sum(lags, axis=0, keepdims=True)
        sv = shared_pre[at, :]
        gate = jax.nn.sigmoid(sv)
        sh = sv * gate
        grads_q += jnp.sum(gq * sh, axis=0, keepdims=True)
        grads_o += jnp.sum(gq, axis=0, keepdims=True)
        grads_k += jnp.sum(gk * sh, axis=0, keepdims=True)
        gsh = gq * attn[0:1, :] + gk * attn[2:3, :]
        shared_grad[to, :] = (gsh * slope_of(sv, gate)).astype(LOW)
    attn_rows = (grads_q, grads_o, grads_k, lag_sum)
    own_shared = shared_grad.at[own_rows, :]
    h_shared = [send(own_shared, own_shared, peer) for peer, _, _ in mates]
    h_mixed = reduce_early(mixed_partial, sibs_a, cross_a)


    for handle, (_, pc, px) in zip(h_shared, mates):
        received(handle, shared_grad.at[group_rows(pc, px), :])

    def mix_product(zz, yy):
        return mm_tn(ml[:, rows_of(MIX, zz)], mix_pack[:, cols_of(MIX, yy)])

    y_grad_send(MIX, mix_product)
    z_relay(UP)
    first_relay(MERGE)
    y_grad_send(VALUE, value_product, (2, 3))
    y_grad_add(VALUE, value_product, (0, 1))
    z_grad_add(DOWN)
    for handle in h_update:
        sent(handle)
    h_down = reduce_first(down_partial, sibs_c)

    def mixed_own(cc, xx):
        mixed_partial(cc, xx)
        total[...] += mm_nt(shared_grad[own_rows, :], w_shared())


    def to_time(r):
        v = reduced(r, 16, sibs_a, cross_a)
        for s in range(tiles):
            at = pl.ds(r * tiles + s, 16, stride=tiles)
            out_time[at, :] = out_time[at, :] * v[:, s * 128 : (s + 1) * 128]

    reduce_late(mixed_own, sibs_a, cross_a, h_mixed, lambda first, count: row_loop(count, 16, to_time, first, 2))

    def value_partial(cc, xx):
        total[...] = mm_nt(grad_value[group_rows(cc, xx), :], weights[VALUE][...])

    h_red = reduce_early(value_partial, sibs_b, cross_b)
    y_grad_add(MIX, mix_product, (0,))

    held = ref.held
    ema = load_ema()
    damping, decay_gate, rate_all, weight_all = ema_coefficients(ema)
    omega = omega_in[...]
    half = rate_all.shape[0] // 2
    chunks = rows // CHUNK
    sums = []
    for part in range(2):
        js = slice(part * half, (part + 1) * half)
        rate, weight = rate_all[js], weight_all[js]

        def chunk(m, carry, js=js, rate=rate, weight=weight, part=part):
            k = chunks - 1 - m
            held[0] = marks[k, js]

            def ahead(i, state):
                state = rate * state + by_time[at_time(k * CHUNK + i), :][None]
                held[i + 1] = state
                return state

            lax.fori_loop(0, CHUNK, ahead, held[0], unroll=4)

            def back(n, carry):
                s, dw, dr, dom = carry
                i = CHUNK - 1 - n
                t = at_time(k * CHUNK + i)
                g = out_time[t, :]
                s = rate * s + g[None]
                dx = jnp.sum(weight * s, axis=0)
                if part == 0:
                    back_time[t, :] = dx + omega * g
                    dom = dom + g * by_time[t, :]
                else:
                    back_time[t, :] = back_time[t, :] + dx
                return s, dw + held[i + 1] * g[None], dr + held[i] * s, dom

            s, dw, dr, dom = lax.fori_loop(0, CHUNK, back, carry, unroll=2)
            return s * kept(k), dw, dr, dom

        zero = jnp.zeros_like(rate)
        carry = lax.fori_loop(0, chunks // 2, chunk, (zero, zero, zero, jnp.zeros_like(omega)))
        if part:
            y_grad_add(MIX, mix_product, (2,))
        else:
            y_grad_add(MIX, mix_product, (1,))
            z_relay(VALUE)
        sums.append(lax.fori_loop(chunks // 2, chunks, chunk, carry))
        if not part:
            h_down = reduce_cross(down_partial, sibs_c, cross_c, h_down, 3)
            z_relay(MIX, (0,))
            first_turn(MERGE)
    small = ref.by_time
    rate_scale = ema.shape[1] ** (-0.5)
    for part in range(2):
        js = slice(part * half, (part + 1) * half)
        dw, dr = sums[part][1], sums[part][2] * weight_all[js]
        d_damp = dw * ema[2, js] * ema[3, js] * rate_scale - dr * decay_gate[js]
        parts = (
            d_damp * damping[js] * (1.0 - damping[js]),
            -dr * damping[js] * decay_gate[js] * (1.0 - decay_gate[js]),
            dw * damping[js] * ema[3, js] * rate_scale,
            dw * damping[js] * ema[2, js] * rate_scale,
        )
        for p in range(4):
            for j in range(half):
                small[pl.ds((p * 2 * half + part * half + j) * tiles, tiles), :] = parts[p][j]

    tile_rows = ref.tile_rows
    states = 4 * ema.shape[1]
    gain_two = jnp.sum(gain_sum[1], axis=0, keepdims=True)
    for t in range(tiles):
        at = (t % 2) * depth + t // 2
        tile_rows[at, 0:states, :] = small[pl.ds(t, states, stride=tiles), :]
        tail = jnp.concatenate(
            [
                jnp.zeros((1, 128), F32),
                gain_two[:, t * 128 : (t + 1) * 128],
                sums[0][3][t : t + 1],
                attn_rows[t // 2],
                jnp.zeros((4, 128), F32),
            ],
            axis=0,
        )
        tile_rows[at, states : states + 8, :] = tail
    sib_in, z_small, x_small, y_small = ref.sib_in, ref.z_small, ref.x_small, ref.y_small
    h_sib = send(tile_rows.at[pl.ds((1 - c) * depth, depth)], sib_in, sib)
    z_relay(MIX, (1,))
    received(h_sib, sib_in)
    sib_in[...] += tile_rows[pl.ds(c * depth, depth)]
    h_zs = [send(sib_in.at[(z + d) % depth], z_small.at[d - 1], zs[d]) for d in range(1, depth)]

    def norm_one_back(r):
        at = pl.ds(r, 16)
        ema_part = jnp.concatenate(
            [back_time[pl.ds(r * tiles + s, 16, stride=tiles), :] for s in range(tiles)], axis=1
        )
        g = reduced(r, 16, sibs_b, cross_b) + ema_part
        cen, rate = centre(tok[at, :].astype(F32))
        unit = cen * rate
        gain_sum[0] += g * unit
        g = g * gains[0:1, :]
        back = rate * (g - jnp.mean(g, axis=-1, keepdims=True) - unit * jnp.mean(g * unit, axis=-1, keepdims=True))
        ref.grad_tokens[at, :] = (back + update_mul[at, :].astype(F32)).astype(LOW)

    reduce_late(
        value_partial, sibs_b, cross_b, h_red, lambda first, count: row_loop(count, 16, norm_one_back, first, 2)
    )
    one_rows, one_z, one_sum, one_plane = ref.one_rows, ref.one_z, ref.one_sum, ref.one_plane
    gain_one = jnp.sum(gain_sum[0], axis=0, keepdims=True)
    for t in range(tiles):
        one_rows[t] = jnp.broadcast_to(gain_one[:, t * 128 : (t + 1) * 128], (8, 128))
    h_one = [send(one_rows.at[pl.ds((z + d) % depth * 2, 2)], one_z.at[d - 1], zs[d]) for d in range(1, depth)]
    y_grad_add(MIX, mix_product, (3,))
    z_grad_add(UP)
    first_finish(MERGE)
    y_grad_add(VALUE, value_product, (2, 3))
    for d, handle in enumerate(h_zs):
        received(handle, z_small.at[d])
    x_small[0] = sib_in[z] + z_small[0] + z_small[1] + z_small[2]
    h_x = send(x_small.at[0], x_small.at[1], xn)
    z_grad_add(MIX)
    for d, handle in enumerate(h_one):
        received(handle, one_z.at[d])
    one_sum[...] = one_rows[pl.ds(z * 2, 2)] + one_z[0] + one_z[1] + one_z[2]
    h_one = [send(one_sum.at[p[0]], one_plane.at[i], place(z, *p)) for i, p in enumerate(plane)]
    received(h_x, x_small.at[1])
    y_small[0] = x_small[0] + x_small[1]
    h_y = send(y_small.at[0], y_small.at[1], yn)
    z_grad_add(VALUE)

    def finish(r):
        at = pl.ds(r, 16)
        ref.result[at, :] = (after[at, :] + reduced(r, 16, sibs_c, cross_c)).astype(LOW)

    reduce_late(down_partial, sibs_c, cross_c, h_down, lambda first, count: row_loop(count, 16, finish, first, 2))
    for m in (DOWN, UP, MERGE):
        grad_out(m)
    received(h_y, y_small.at[1])
    totals = y_small[0] + y_small[1]
    ref.small_out[...] = pltpu.roll(totals, (128 - shift) % 128, 1)
    one = one_sum[c]
    for i, handle in enumerate(h_one):
        received(handle, one_plane.at[i])
        one = one + one_plane[i]
    ref.small_out[states : states + 1, :] = pltpu.roll(one, (128 - shift) % 128, 1)[0:1]
    for m in (MIX, VALUE):
        grad_out(m)
    ref.attn_out[...] = pltpu.roll(totals[states : states + 8], (128 - c * 64 - fs * 16) % 128, 1)
    for handle in pending:
        sent(handle)
    assert used[0] <= COPIES


def finish_kernel(result, grad_tokens, value, mix, merge, up, down, small, attn, *outs):
    for src, out in zip((result, grad_tokens, value, mix, merge, up, down), outs):

        def widen(r, src=src, out=out):
            out[pl.ds(r, 32), :] = src[pl.ds(r, 32), :].astype(out.dtype)

        row_loop(out.shape[0], 32, widen)
    gains, ema, per = outs[7:]
    states, mine = ema.shape[1:]
    gains[...] = small[4 * states : 4 * states + 3, :mine]
    for p in range(4):
        ema[p] = small[p * states : (p + 1) * states, :mine]
    per[...] = attn[3:4, : per.shape[1]]


def layer_on_device(depth, tokens, cotangent, lengths, value_proj, mix_proj, merge_proj, up_proj, down_proj, norm_gains, ema_params, attn_params):
    rows, width = tokens.shape
    fs = lax.axis_index(FS)
    window = -(-mix_proj.shape[1] // 128) * 128
    group = 4 * rows
    vq = value_proj.shape[1]
    fq = up_proj.shape[1]
    quarters = ((width, vq), (width, 10 * STRIP), (vq, width), (width, fq), (fq, width))
    tiles = width // 128
    states = ema_params.shape[2]
    small_rows = 4 * states + 8
    shape = jax.ShapeDtypeStruct
    mix_turned = mix_proj.T
    ema_turned = jnp.swapaxes(ema_params, 1, 2)
    shards = (value_proj, mix_turned, merge_proj, up_proj, down_proj)
    inputs = dict(
        acts=(tokens, cotangent),
        lens=lengths,
        norm_gains=norm_gains,
        ema_params=ema_turned,
        attn_params=attn_params[None],
        s=shards,
    )
    landings = [w.shape for w in shards]
    landings[MIX] = (4, mix_proj.shape[0], 3 * STRIP)
    outputs = dict(
        result=shape((rows, width), LOW),
        grad_tokens=shape((rows, width), LOW),
        fi=tuple(shape(d, LOW) for d in landings),
        g_mix=shape(mix_turned.shape, LOW),
        small_out=shape((small_rows, 128), F32),
        attn_out=shape((8, 128), F32),
    )
    copies = pltpu.SemaphoreType.DMA((COPIES,))

    def low(*dims):
        return pltpu.VMEM(dims, LOW)

    def full(*dims):
        return pltpu.VMEM(dims, F32)

    scratch = dict(
        send_sems=copies,
        recv_sems=copies,
        local_sems=pltpu.SemaphoreType.DMA((32,)),
        w=tuple(low(*d) for d in quarters),
        yo=low(width, fq // 2),
        yi=tuple(low(r, k // 2) for r, k in quarters),
        zi=tuple(low(4, r // depth, k // 2) for r, k in quarters),
        mix_win=low(mix_proj.shape[0], window),
        small_all=low(8 * depth, 32, 128),
        packed=low(32, 128),
        ema_in=full(4 * states * tiles, 128),
        omega_in=full(tiles, 128),
        gains=full(8, width),
        attn=full(8, 128),
        tok=low(rows, width),
        cot=low(rows, width),
        nl=low(group, width),
        ml=low(group, width),
        n2=low(group, width),
        gc=low(group, width),
        gm=low(group, width),
        mix_in=low(2, 2 * mix_proj.shape[0], 4 * STRIP),
        reset_w=low(width, 256),
        value_low=low(group, vq),
        value_slope=low(group, vq),
        reset_gate=low(group, vq),
        reset_slope=low(group, vq),
        gated=low(group, vq),
        up_low=low(group, fq),
        up_slope=low(group, fq),
        update_in=low(rows, width),
        probs_low=low(group, STRETCH),
        probs=full(rows, STRETCH),
        shared_pre=full(rows, Z),
        query=low(rows, Z),
        key=low(rows, Z),
        grad_probs=low(group, STRETCH),
        probs_in=low(3, rows, STRETCH),
        mix_pack=low(group, 10 * STRIP),
        by_time=full(rows * tiles, 128),
        out_time=full(rows * tiles, 128),
        back_time=full(rows * tiles, 128),
        marks=full(rows // CHUNK, states, tiles, 128),
        held=full(CHUNK + 1, states // 2, tiles, 128),
        total=full(rows, width),
        stage=low(3, rows, width),
        sibs_a=low(2, rows, width),
        sibs_b=low(2, rows, width),
        cross_a=low(rows, width),
        cross_b=low(rows, width),
        after=full(rows, width),
        hidden_mul=low(rows, width),
        update_mul=low(rows, width),
        gain_sum=full(2, 16, width),
        tile_rows=full(tiles, small_rows, 128),
        sib_in=full(depth, small_rows, 128),
        z_small=full(depth - 1, small_rows, 128),
        x_small=full(2, small_rows, 128),
        y_small=full(2, small_rows, 128),
        one_rows=full(tiles, 8, 128),
        one_z=full(depth - 1, 2, 8, 128),
        one_sum=full(2, 8, 128),
        one_plane=full(7, 8, 128),
    )
    in_vmem = pl.BlockSpec(memory_space=pltpu.VMEM)
    specs = jax.tree.map(lambda _: in_vmem, inputs)
    anywhere = pl.BlockSpec(memory_space=pl.ANY)
    specs.update(
        lens=pl.BlockSpec(memory_space=pltpu.SMEM), acts=(anywhere,) * 2, s=tuple(in_vmem if m == MIX else anywhere for m in SHARDED)
    )
    in_leaves, in_tree = jax.tree.flatten(inputs)
    out_leaves, out_tree = jax.tree.flatten(outputs)
    scratch_leaves, scratch_tree = jax.tree.flatten(scratch, is_leaf=lambda v: not isinstance(v, (dict, tuple)))
    outs = pl.pallas_call(
        functools.partial(layer_kernel, (in_tree, out_tree, scratch_tree), depth),
        out_shape=tuple(out_leaves),
        in_specs=jax.tree.leaves(specs),
        out_specs=tuple(in_vmem for _ in out_leaves),
        scratch_shapes=scratch_leaves,
        compiler_params=pltpu.CompilerParams(collective_id=0, has_side_effects=True, vmem_limit_bytes=VMEM_BYTES),
        name="layer",
    )(*in_leaves)
    by = types.SimpleNamespace(**jax.tree.unflatten(out_tree, outs))
    grads = list(by.fi)
    grads[MIX] = by.g_mix
    wide = [shape(g.shape, F32) for g in (*grads, norm_gains, ema_turned)]
    *finals, attn_grad = pl.pallas_call(
        finish_kernel,
        out_shape=(shape((rows, width), LOW), shape((rows, width), LOW), *wide, shape((1, attn_params.shape[0]), F32)),
        in_specs=[in_vmem] * 9,
        out_specs=(in_vmem,) * 10,
        compiler_params=pltpu.CompilerParams(vmem_limit_bytes=VMEM_BYTES),
        name="finish",
    )(by.result, by.grad_tokens, *grads, by.small_out, by.attn_out)
    finals[2 + MIX] = finals[2 + MIX].T
    finals[-1] = jnp.swapaxes(finals[-1], 1, 2)
    return (*finals, attn_grad[0])


VMEM_BYTES = 64 << 20
COPIES = 256


def solution(mesh):
    in_specs = (
        P((DP, FS), None),
        P((DP, FS), None),
        P((DP, FS), None),
        P(DP, FS),
        P(DP, FS),
        P(DP, FS),
        P(DP, FS),
        P(DP, FS),
        P(None, (DP, FS)),
        P(None, (DP, FS), None),
        P((DP, FS)),
    )
    out_specs = (
        P((DP, FS), None),
        P((DP, FS), None),
        P(DP, FS),
        P(DP, FS),
        P(DP, FS),
        P(DP, FS),
        P(DP, FS),
        P(None, (DP, FS)),
        P(None, (DP, FS), None),
        P((DP, FS)),
    )
    fits = mesh.shape[DP] == 8 and mesh.shape[DP] // 2 * 4 * STRIP == V and mesh.shape[FS] * 4 * STRIP == V
    body = functools.partial(layer_on_device, mesh.shape[DP] // 2) if fits else on_device
    return jax.shard_map(body, mesh=mesh, in_specs=in_specs, out_specs=out_specs, check_vma=False)
```
